32 devices in a mesh: dp: 16 (over z, y, core), blk: 2 (over x).
Axes of the slice: x: 2, y: 2, z: 4, core: 2. Of those that a mesh axis runs over, the one named last changes fastest.
Arguments:
- tokens: bfloat16 [16, 1024, 768], P('dp', 'blk'), may hold values from -6 to 6
- segments: int32 [16, 1024], P('dp'), may hold values from 0 to 15, never falling along the last dimension, each value on 1 to 198 neighbouring positions
- cotangent: bfloat16 [16, 1024, 768], P('dp', 'blk'), may hold values from -6 to 6
- qkv_weight: float32 [768, 2304], P(('dp', 'blk')), may hold values from -0.21875 to 0.21875
- proj_weight: float32 [768, 768], P(('dp', 'blk')), may hold values from -0.875 to 0.875
- up_weight: float32 [768, 3072], P(('dp', 'blk')), may hold values from -0.21875 to 0.21875
- down_weight: float32 [3072, 768], P(('dp', 'blk')), may hold values from -0.109375 to 0.109375
- vec_params: float32 [12, 768], P(None, ('dp', 'blk')), may hold values from -1.25 to 1.25
- qkv_velocity: float32 [768, 2304], P(('dp', 'blk')), may hold values from -80 to 80
- proj_velocity: float32 [768, 768], P(('dp', 'blk')), may hold values from -40 to 40
- up_velocity: float32 [768, 3072], P(('dp', 'blk')), may hold values from -40 to 40
- down_velocity: float32 [3072, 768], P(('dp', 'blk')), may hold values from -40 to 40
- vec_velocity: float32 [12, 768], P(None, ('dp', 'blk')), may hold values from -80 to 80
- qkv_average: float32 [768, 2304], P(('dp', 'blk')), may hold values from -0.109375 to 0.109375
- proj_average: float32 [768, 768], P(('dp', 'blk')), may hold values from -0.4375 to 0.4375
- up_average: float32 [768, 3072], P(('dp', 'blk')), may hold values from -0.109375 to 0.109375
- down_average: float32 [3072, 768], P(('dp', 'blk')), may hold values from -0.0546875 to 0.0546875
- vec_average: float32 [12, 768], P(None, ('dp', 'blk')), may hold values from -0.625 to 0.625
Outputs:
- output: bfloat16 [16, 1024, 768], P('dp', 'blk')
- tokens_grad: bfloat16 [16, 1024, 768], P('dp', 'blk')
- qkv_grad: float32 [768, 2304], P(('dp', 'blk'))
- proj_grad: float32 [768, 768], P(('dp', 'blk'))
- up_grad: float32 [768, 3072], P(('dp', 'blk'))
- down_grad: float32 [3072, 768], P(('dp', 'blk'))
- vec_grad: float32 [12, 768], P(None, ('dp', 'blk'))
- qkv_master: float32 [768, 2304], P(('dp', 'blk'))
- proj_master: float32 [768, 768], P(('dp', 'blk'))
- up_master: float32 [768, 3072], P(('dp', 'blk'))
- down_master: float32 [3072, 768], P(('dp', 'blk'))
- vec_master: float32 [12, 768], P(None, ('dp', 'blk'))
- qkv_velocity_out: float32 [768, 2304], P(('dp', 'blk'))
- proj_velocity_out: float32 [768, 768], P(('dp', 'blk'))
- up_velocity_out: float32 [768, 3072], P(('dp', 'blk'))
- down_velocity_out: float32 [3072, 768], P(('dp', 'blk'))
- vec_velocity_out: float32 [12, 768], P(None, ('dp', 'blk'))
- qkv_average_out: float32 [768, 2304], P(('dp', 'blk'))
- proj_average_out: float32 [768, 768], P(('dp', 'blk'))
- up_average_out: float32 [768, 3072], P(('dp', 'blk'))
- down_average_out: float32 [3072, 768], P(('dp', 'blk'))
- vec_average_out: float32 [12, 768], P(None, ('dp', 'blk'))
- qkv_copy: bfloat16 [768, 2304], P(('dp', 'blk'))
- proj_copy: bfloat16 [768, 768], P(('dp', 'blk'))
- up_copy: bfloat16 [768, 3072], P(('dp', 'blk'))
- down_copy: bfloat16 [3072, 768], P(('dp', 'blk'))
- vec_copy: bfloat16 [12, 768], P(None, ('dp', 'blk'))
The draws below stay inside these ranges and needn't reach their ends.
Inputs may be any that keep to these rules, and one draw needn't show every extreme that they name: `segments`: in each row the ids never fall; each image holds 1 to 198 consecutive positions, and some image holds exactly 198; every id from 0 to the largest occurs.
All inputs are finite; a program needn't handle non-finite values.
Results may differ from the reference program's by a relative error of at most 0.014.
Values may be sent and summed in bfloat16 or wider, within the bound.
A program may use at most 256 MiB of HBM per device.

```python
import math
import jax
import jax.numpy as jnp
import numpy as np
from jax import lax

D = 768
FF = 3072
HEADS = 12
HEAD_DIM = 64
SEQ = 1024
IMG_MAX = 198
ROWS = 16


def levels(rng, extent, pieces, least, top_value):
    level, own = 1.0, jax.random.fold_in(rng, 6)
    for position, parts in pieces:
        draws = jnp.exp(jax.random.uniform(jax.random.fold_in(own, position), (parts,), jnp.float32, least / len(pieces), top_value / len(pieces)))
        level = level * jnp.repeat(draws, extent[position] // parts).reshape([-1 if axis == position else 1 for axis in range(len(extent))])
    return level


def length_profile(amount, total, bound, lean):
    weights = [(1 << 20) // math.isqrt(standing ** lean) + 1 for standing in range(2, amount + 1)]
    rest, counts = total - bound - (amount - 1), [1] * (amount - 1)
    while rest > 0:
        candidates = [i for i in range(amount - 1) if counts[i] < bound]
        whole, left = sum([weights[i] for i in candidates]), rest
        for i in candidates:
            addition = min(bound - counts[i], max(1, left * weights[i] // whole), rest)
            counts[i] = counts[i] + addition
            rest = rest - addition
    return np.array([bound] + counts)


def uneven(stream_key, number_of, total, limit, lean):
    if number_of == 2:
        one = jax.random.randint(stream_key, (), max(1, total - limit), min(limit, total - 1) + 1)
        return jnp.stack([one, total - one])
    sizes = jnp.asarray(length_profile(number_of, total, limit, lean), jnp.int32)
    couples = (number_of - 1) // 2
    donor, sink = sizes[1:1 + 2 * couples:2], sizes[2:2 + 2 * couples:2]
    slack = jnp.minimum(donor - 1, limit - sink)
    moved = jax.random.randint(jax.random.fold_in(stream_key, 1), (couples,), 0, 1 << 20) % (slack + 1)
    sizes = sizes.at[1:1 + 2 * couples:2].set(donor - moved).at[2:2 + 2 * couples:2].set(sink + moved)
    return sizes[jax.random.permutation(jax.random.fold_in(stream_key, 2), number_of)]


def normal_values(key, extent, spread, reach, cuts=(), dtype=jnp.bfloat16):
    level = levels(key, extent, cuts, -0.22, 0.18) if cuts else 1.0
    values = jax.random.normal(key, extent, jnp.float32) * spread * level
    return jnp.minimum(jnp.maximum(values, -reach), reach).astype(dtype)


def setup_inputs(seed: int = 0) -> dict:
    key_list = jax.random.split(jax.random.key(seed), 19)
    return {
        "tokens": normal_values(key_list[0], (ROWS, SEQ, D), 1.0, 6.0, ((0, 16), (1, 2))),
        "segments": jax.vmap(lambda own: jnp.searchsorted(jnp.cumsum(uneven(own, SEQ * 3 // IMG_MAX + 1, SEQ, IMG_MAX, 1)), jnp.arange(SEQ), side="right"))(jax.random.split(key_list[1], ROWS)).reshape((ROWS, SEQ)).astype(jnp.int32),
        "cotangent": normal_values(key_list[2], (ROWS, SEQ, D), 1.0, 6.0, ((0, 16), (1, 2))),
        "qkv_weight": normal_values(key_list[3], (D, 3 * D), D ** -0.5, 0.21875, ((0, 32),), jnp.float32),
        "proj_weight": normal_values(key_list[4], (D, D), (D // 16) ** -0.5, 0.875, ((0, 32),), jnp.float32),
        "up_weight": normal_values(key_list[5], (D, FF), D ** -0.5, 0.21875, ((0, 32),), jnp.float32),
        "down_weight": normal_values(key_list[6], (FF, D), FF ** -0.5, 0.109375, ((0, 32),), jnp.float32),
        "vec_params": normal_values(key_list[7], (12, D), 0.2, 1.25, ((1, 32),), jnp.float32),
        "qkv_velocity": normal_values(key_list[8], (D, 3 * D), (0.1 * (ROWS * SEQ) ** 0.5), 80.0, ((0, 32),), jnp.float32),
        "proj_velocity": normal_values(key_list[9], (D, D), (0.05 * (ROWS * SEQ) ** 0.5), 40.0, ((0, 32),), jnp.float32),
        "up_velocity": normal_values(key_list[10], (D, FF), (0.05 * (ROWS * SEQ) ** 0.5), 40.0, ((0, 32),), jnp.float32),
        "down_velocity": normal_values(key_list[11], (FF, D), (0.05 * (ROWS * SEQ) ** 0.5), 40.0, ((0, 32),), jnp.float32),
        "vec_velocity": normal_values(key_list[12], (12, D), (0.1 * (ROWS * SEQ) ** 0.5), 80.0, ((1, 32),), jnp.float32),
        "qkv_average": normal_values(key_list[13], (D, 3 * D), (4 * D) ** -0.5, 0.109375, ((0, 32),), jnp.float32),
        "proj_average": normal_values(key_list[14], (D, D), (D // 4) ** -0.5, 0.4375, ((0, 32),), jnp.float32),
        "up_average": normal_values(key_list[15], (D, FF), (4 * D) ** -0.5, 0.109375, ((0, 32),), jnp.float32),
        "down_average": normal_values(key_list[16], (FF, D), (4 * FF) ** -0.5, 0.0546875, ((0, 32),), jnp.float32),
        "vec_average": normal_values(key_list[17], (12, D), 0.1, 0.625, ((1, 32),), jnp.float32),
    }


@jax.custom_vjp
def low(v):
    return lax.optimization_barrier(v.astype(jnp.bfloat16)).astype(jnp.float32)

@jax.custom_vjp
def low_back(v):
    return v

def low_keep(v):
    return (low(v), None)

def low_pass(kept, grad):
    return (grad,)

def back_keep(v):
    return (v, None)

def back_low(kept, grad):
    return (low(grad),)
low.defvjp(low_keep, low_pass)
low_back.defvjp(back_keep, back_low)
HIGH = lax.Precision.HIGHEST

def layer_norm(value, gain, shift):
    mean = lax.optimization_barrier(jnp.mean(value, axis=-1, keepdims=True))
    cent = value - mean
    var = lax.optimization_barrier(jnp.mean(cent * cent, axis=-1, keepdims=True))
    return cent * lax.rsqrt(var + 1e-06) * (1.0 + gain) + shift

def layer(params, inputs, seg):
    wq, wp, wu, wd, vec = params
    groups, length = (inputs.shape[0], inputs.shape[1])
    bias_u = vec[8:12].reshape(-1)
    a_one = low(layer_norm(inputs, vec[0], vec[1]))
    zero_bias = jnp.zeros_like(vec[2])
    pre = jnp.einsum('gsd,de->gse', a_one, wq, precision=HIGH) + jnp.concatenate([vec[2], zero_bias, vec[3]])
    qkv = low(low_back(pre))
    query = qkv[..., :D].reshape(groups, length, HEADS, HEAD_DIM)
    keys = qkv[..., D:2 * D].reshape(groups, length, HEADS, HEAD_DIM)
    values = qkv[..., 2 * D:].reshape(groups, length, HEADS, HEAD_DIM)
    scores = low_back(jnp.einsum('gqhd,gkhd->ghqk', query, keys, precision=HIGH) * HEAD_DIM ** (-0.5))
    allowed = (seg[:, :, None] == seg[:, None, :])[:, None]
    probs = low(jax.nn.softmax(jnp.where(allowed, scores, -1e+30), axis=-1))
    mixed = jnp.einsum('ghqk,gkhd->gqhd', probs, values, precision=HIGH).reshape(groups, length, D)
    mixed = low(low_back(mixed))
    second = inputs + low_back(jnp.einsum('gsd,de->gse', mixed, wp, precision=HIGH) + vec[4])
    a_two = low(layer_norm(second, vec[5], vec[6]))
    hidden = low_back(jnp.einsum('gsd,df->gsf', a_two, wu, precision=HIGH) + bias_u)
    act = low(jax.nn.gelu(hidden, approximate=False))
    return second + low_back(jnp.einsum('gsf,fd->gsd', act, wd, precision=HIGH) + vec[7])

def update(weight, grad, velocity, average, rate):
    step_value = grad + 0.0005 * weight
    velocity_new = 0.9 * velocity + step_value
    weight_new = weight - rate * (step_value + 0.9 * velocity_new)
    average_new = 0.9 * average + 0.1 * weight_new
    return (weight_new, velocity_new, average_new)

def reference(tokens, segments, cotangent, qkv_weight, proj_weight, up_weight, down_weight, vec_params, qkv_velocity, proj_velocity, up_velocity, down_velocity, vec_velocity, qkv_average, proj_average, up_average, down_average, vec_average):
    masters = (qkv_weight, proj_weight, up_weight, down_weight, vec_params)
    used = tuple((lax.optimization_barrier(w.astype(jnp.bfloat16)).astype(jnp.float32) for w in masters))
    group = math.gcd(ROWS, max(1, 4096 // SEQ))
    count = ROWS // group
    inputs = tokens.astype(jnp.float32).reshape(count, group, SEQ, D)
    cots = cotangent.astype(jnp.float32).reshape(count, group, SEQ, D)
    segs = segments.reshape(count, group, SEQ)

    def one_group(total, item):
        value, seg, cot = item
        outval, back = jax.vjp(lambda p, v: layer(p, v, seg), used, value)
        grads, value_grad = back(cot)
        total = jax.tree.map(lambda a, b: a + b, total, grads)
        return (total, (outval.astype(jnp.bfloat16), value_grad.astype(jnp.bfloat16)))
    start = tuple((jnp.zeros(w.shape, jnp.float32) for w in masters))
    grads, (outs, value_grads) = lax.scan(one_group, start, (inputs, segs, cots))
    output = outs.reshape(ROWS, SEQ, D)
    tokens_grad = value_grads.reshape(ROWS, SEQ, D)
    rate = 0.05 / math.sqrt(ROWS * SEQ)
    velocities = (qkv_velocity, proj_velocity, up_velocity, down_velocity, vec_velocity)
    averages = (qkv_average, proj_average, up_average, down_average, vec_average)
    news = [update(w, g, m, e, rate) for w, g, m, e in zip(masters, grads, velocities, averages)]
    return (output, tokens_grad, grads[0], grads[1], grads[2], grads[3], grads[4], news[0][0], news[1][0], news[2][0], news[3][0], news[4][0], news[0][1], news[1][1], news[2][1], news[3][1], news[4][1], news[0][2], news[1][2], news[2][2], news[3][2], news[4][2], news[0][0].astype(jnp.bfloat16), news[1][0].astype(jnp.bfloat16), news[2][0].astype(jnp.bfloat16), news[3][0].astype(jnp.bfloat16), news[4][0].astype(jnp.bfloat16))
```

```python
import math

import jax
import jax.numpy as jnp
from jax import lax
from jax.experimental import pallas as pl
from jax.experimental.pallas import tpu as pltpu
from jax.sharding import PartitionSpec as P

D = 768
HEADS = 12
HEAD_DIM = 64


def layer_norm(value, gain, shift):
    mean = jnp.mean(value, axis=-1, keepdims=True)
    cent = value - mean
    var = jnp.mean(cent * cent, axis=-1, keepdims=True)
    return cent * lax.rsqrt(var + 1e-06) * (1.0 + gain) + shift


def gelu_exact(value):
    return jax.nn.gelu(value, approximate=False)


def contract_tokens(left, right):
    return lax.dot_general(
        left.reshape(-1, left.shape[-1]),
        right.reshape(-1, right.shape[-1]),
        (((0,), (0,)), ((), ())),
        preferred_element_type=jnp.float32,
    )


def times_transpose(left, weight):
    return lax.dot_general(
        left, weight, (((left.ndim - 1,), (1,)), ((), ())), preferred_element_type=jnp.float32
    )


def group_size(rows, block):
    limit = max(1, 512 // block)
    best = 1
    for cand in range(1, rows + 1):
        if rows % cand == 0 and cand <= limit:
            best = cand
    return best


def scores_of(query, keys, seg_query, seg_keys):
    scores = jnp.einsum(
        "gqhd,gkhd->ghqk", query, keys, preferred_element_type=jnp.float32
    ) * HEAD_DIM ** (-0.5)
    allowed = (seg_query[:, :, None] == seg_keys[:, None, :])[:, None]
    return (scores, allowed)


def attend_back(query, kv_all, grad_out, seg_query, segments, group):
    rows, block = (query.shape[0], query.shape[1])
    length = kv_all.shape[1]
    keys = kv_all[0:group, :, :D].reshape(group, length, HEADS, HEAD_DIM)
    values = kv_all[0:group, :, D:].reshape(group, length, HEADS, HEAD_DIM)
    scores, allowed = scores_of(query, keys, seg_query, segments)
    probs = jax.nn.softmax(jnp.where(allowed, scores, -1e30), axis=-1)
    probs_low = probs.astype(jnp.bfloat16)
    prob_grad = jnp.einsum("gqhd,gkhd->ghqk", grad_out, values, preferred_element_type=jnp.float32)
    score_grad = probs * (prob_grad - jnp.sum(probs * prob_grad, axis=-1, keepdims=True))
    score_low = score_grad.astype(jnp.bfloat16)
    dq_part = jnp.einsum(
        "ghqk,gkhd->gqhd", score_low, keys, preferred_element_type=jnp.float32
    ) * HEAD_DIM ** (-0.5)
    dk_part = jnp.einsum(
        "ghqk,gqhd->gkhd", score_low, query, preferred_element_type=jnp.float32
    ) * HEAD_DIM ** (-0.5)
    dv_part = jnp.einsum("ghqk,gqhd->gkhd", probs_low, grad_out, preferred_element_type=jnp.float32)
    dq_parts = dq_part.reshape(group, block, D)
    dkv_parts = jnp.concatenate(
        [dk_part.reshape(group, length, D), dv_part.reshape(group, length, D)], axis=-1
    )
    return (dq_parts, dkv_parts)


def update(weight, grad, velocity, average, rate):
    step_value = grad + 0.0005 * weight
    velocity_new = 0.9 * velocity + step_value
    weight_new = weight - rate * (step_value + 0.9 * velocity_new)
    average_new = 0.9 * average + 0.1 * weight_new
    return (weight_new, velocity_new, average_new)


def on_device(
    tokens,
    segments,
    cotangent,
    qkv_weight,
    proj_weight,
    up_weight,
    down_weight,
    vec_params,
    qkv_velocity,
    proj_velocity,
    up_velocity,
    down_velocity,
    vec_velocity,
    qkv_average,
    proj_average,
    up_average,
    down_average,
    vec_average,
):
    rows, block = (tokens.shape[0], tokens.shape[1])
    length = segments.shape[1]
    total_tokens = rows * lax.axis_size("dp") * length
    rate = 0.05 / math.sqrt(total_tokens)
    group = group_size(rows, block)
    gathered = (
        lax.all_gather(qkv_weight.astype(jnp.bfloat16), ("dp", "blk"), axis=0, tiled=True),
        lax.all_gather(proj_weight.astype(jnp.bfloat16), ("dp", "blk"), axis=0, tiled=True),
        lax.all_gather(up_weight.astype(jnp.bfloat16), ("dp", "blk"), axis=0, tiled=True),
        lax.all_gather(down_weight.astype(jnp.bfloat16), ("dp", "blk"), axis=0, tiled=True),
        lax.all_gather(vec_params.astype(jnp.bfloat16), ("dp", "blk"), axis=1, tiled=True),
    )
    w_query, w_proj, w_up, w_down, vec_low = gathered
    vec = vec_low.astype(jnp.float32)
    bias_up = vec[8:12].reshape(-1)
    position = lax.axis_index("blk")
    seg_query = lax.dynamic_slice_in_dim(segments, position * block, block, 1)
    inputs = tokens.astype(jnp.float32)
    a_one = layer_norm(inputs, vec[0], vec[1]).astype(jnp.bfloat16)
    zero_bias = jnp.zeros_like(vec[2])
    pre = jnp.dot(a_one, w_query, preferred_element_type=jnp.float32) + jnp.concatenate(
        [vec[2], zero_bias, vec[3]]
    )
    qkv = pre.astype(jnp.bfloat16)
    query = qkv[..., :D].reshape(rows, block, HEADS, HEAD_DIM)
    key_value = qkv[..., D:]
    piece = lax.all_gather(key_value, "blk", axis=1, tiled=True)
    top = jnp.full((rows, HEADS, block), -1e30, jnp.float32)
    count = piece.shape[1]
    keys = piece[0:group, :, :D].reshape(group, count, HEADS, HEAD_DIM)
    values = piece[0:group, :, D:].reshape(group, count, HEADS, HEAD_DIM)
    scores, allowed = scores_of(query, keys, seg_query, segments)
    scores = jnp.where(allowed, scores, -1e30)
    new_top = jnp.maximum(top, jnp.max(scores, axis=-1))
    weights = jnp.where(allowed, jnp.exp(scores - new_top[..., None]), 0.0)
    denoms = jnp.sum(weights, axis=-1)
    added = jnp.einsum(
        "ghqk,gkhd->gqhd", weights.astype(jnp.bfloat16), values, preferred_element_type=jnp.float32
    )
    mixed = (added / jnp.transpose(denoms, (0, 2, 1))[..., None]).reshape(rows, block, D)
    mixed_low = mixed.astype(jnp.bfloat16)
    second = inputs + jnp.dot(mixed_low, w_proj, preferred_element_type=jnp.float32) + vec[4]
    second_norm, norm_two_back = jax.vjp(layer_norm, second, vec[5], vec[6])
    a_two = second_norm.astype(jnp.bfloat16)
    hidden = jnp.dot(a_two, w_up, preferred_element_type=jnp.float32) + bias_up
    act_value, gelu_back = jax.vjp(gelu_exact, hidden)
    act = act_value.astype(jnp.bfloat16)
    result = second + jnp.dot(act, w_down, preferred_element_type=jnp.float32) + vec[7]
    output = result.astype(jnp.bfloat16)
    out_grad = cotangent.astype(jnp.float32)
    grad_down = contract_tokens(act, cotangent)
    bias_down_grad = jnp.sum(out_grad, axis=(0, 1))
    act_grad = times_transpose(cotangent, w_down)
    hidden_grad = gelu_back(act_grad)[0].astype(jnp.bfloat16)
    bias_up_grad = jnp.sum(hidden_grad.astype(jnp.float32), axis=(0, 1))
    grad_up = contract_tokens(a_two, hidden_grad)
    a_two_grad = times_transpose(hidden_grad, w_up)
    second_part, gain_two_grad, shift_two_grad = norm_two_back(a_two_grad)
    second_grad = out_grad + second_part
    attn_grad = second_grad.astype(jnp.bfloat16)
    bias_proj_grad = jnp.sum(attn_grad.astype(jnp.float32), axis=(0, 1))
    grad_proj = contract_tokens(mixed_low, attn_grad)
    mixed_grad = (
        times_transpose(attn_grad, w_proj)
        .astype(jnp.bfloat16)
        .reshape(rows, block, HEADS, HEAD_DIM)
    )
    kv_again = lax.all_gather(key_value, "blk", axis=1, tiled=True)
    query_grad, kv_terms = attend_back(query, kv_again, mixed_grad, seg_query, segments, group)
    kv_grad = lax.psum_scatter(
        kv_terms.astype(jnp.bfloat16), "blk", scatter_dimension=1, tiled=True
    ).astype(jnp.float32)
    qkv_grad_low = jnp.concatenate([query_grad, kv_grad], axis=-1).astype(jnp.bfloat16)
    qkv_sums = jnp.sum(qkv_grad_low.astype(jnp.float32), axis=(0, 1))
    grad_query = contract_tokens(a_one, qkv_grad_low)
    a_one_grad = times_transpose(qkv_grad_low, w_query)
    norm_one_back = jax.vjp(layer_norm, inputs, vec[0], vec[1])[1]
    first_part, gain_one_grad, shift_one_grad = norm_one_back(a_one_grad)
    tokens_grad = (second_grad + first_part).astype(jnp.bfloat16)
    vec_local = jnp.concatenate(
        [
            jnp.stack(
                [
                    gain_one_grad,
                    shift_one_grad,
                    qkv_sums[:D],
                    qkv_sums[2 * D :],
                    bias_proj_grad,
                    gain_two_grad,
                    shift_two_grad,
                    bias_down_grad,
                ]
            ),
            bias_up_grad.reshape(4, D),
        ],
        axis=0,
    )
    query_share, proj_share, up_share, down_share, vec_share = (
        lax.psum_scatter(grad_query, ("dp", "blk"), scatter_dimension=0, tiled=True),
        lax.psum_scatter(grad_proj, ("dp", "blk"), scatter_dimension=0, tiled=True),
        lax.psum_scatter(grad_up, ("dp", "blk"), scatter_dimension=0, tiled=True),
        lax.psum_scatter(grad_down, ("dp", "blk"), scatter_dimension=0, tiled=True),
        lax.psum_scatter(vec_local, ("dp", "blk"), scatter_dimension=1, tiled=True),
    )
    qkv_new = update(qkv_weight, query_share, qkv_velocity, qkv_average, rate)
    proj_new = update(proj_weight, proj_share, proj_velocity, proj_average, rate)
    up_new = update(up_weight, up_share, up_velocity, up_average, rate)
    down_new = update(down_weight, down_share, down_velocity, down_average, rate)
    vec_new = update(vec_params, vec_share, vec_velocity, vec_average, rate)
    return (
        output,
        tokens_grad,
        query_share,
        proj_share,
        up_share,
        down_share,
        vec_share,
        qkv_new[0],
        proj_new[0],
        up_new[0],
        down_new[0],
        vec_new[0],
        qkv_new[1],
        proj_new[1],
        up_new[1],
        down_new[1],
        vec_new[1],
        qkv_new[2],
        proj_new[2],
        up_new[2],
        down_new[2],
        vec_new[2],
        qkv_new[0].astype(jnp.bfloat16),
        proj_new[0].astype(jnp.bfloat16),
        up_new[0].astype(jnp.bfloat16),
        down_new[0].astype(jnp.bfloat16),
        vec_new[0].astype(jnp.bfloat16),
    )


PIECE = (48, 384)
NP = 12
Z, Y, X, C = 4, 2, 2, 2
MESH = pl.DeviceIdType.MESH


def place():
    d, x = lax.axis_index("dp"), lax.axis_index("blk")
    return d // (2 * Y), (d // 2) % Y, d % 2, x


def ident(z, y, c, x):
    return ((z * Y + y) * 2 + c, x)


def greet(z, y, c, x):
    barrier = pltpu.get_barrier_semaphore()
    peers = [ident((z + k) % Z, y, c, x) for k in range(1, Z)]
    peers += [ident(z, 1 - y, c, x), ident(z, y, c, 1 - x), ident(z, y, 1 - c, x)]
    for peer in peers:
        pl.semaphore_signal(barrier, inc=1, device_id=peer, device_id_type=MESH)
    pl.semaphore_wait(barrier, len(peers))


def remote(src, dst, send, recv, peer):
    return pltpu.make_async_remote_copy(
        src_ref=src, dst_ref=dst, send_sem=send, recv_sem=recv, device_id=peer, device_id_type=MESH
    )


def vec_steps(z, y, c, x):
    return [
        [ident(z, y, 1 - c, x)],
        [ident(z, y, c, 1 - x)],
        [ident(z, 1 - y, c, x)],
        [ident((z + k) % Z, y, c, x) for k in range(1, Z)],
    ]


def vec_copies(step, now, got, send, recv, at):
    peers = vec_steps(*at)[step]
    return [
        remote(now.at[step], got.at[step + k], send.at[step + k], recv.at[step + k], peer)
        for k, peer in enumerate(peers)
    ]


def gather_kernel(unit, vec_in, full, vec_out, vec_now, vec_got, own_sem, send, recv, vsend, vrecv):
    z, y, c, x = at = place()
    own = pltpu.make_async_copy(unit, full.at[c, y, x, z], own_sem)
    own.start()
    vec_now[0] = vec_in[...]
    greet(*at)

    def first(t):
        return [
            remote(unit.at[t], full.at[c, y, x, z, t], send.at[t, k - 1], recv.at[t, k - 1], ident((z + k) % Z, y, c, x))
            for k in range(1, Z)
        ]

    def second(t):
        low, high = full.at[c, y, x, 0:2, t], full.at[c, y, x, 2:4, t]
        return [
            remote(low, low, send.at[t, 3], recv.at[t, 3], ident(z, y, c, 1 - x)),
            remote(high, high, send.at[t, 4], recv.at[t, 4], ident(z, 1 - y, c, x)),
        ]

    def third(t):
        low, high = full.at[c, y, :, 0:2, t], full.at[c, :, x, 2:4, t]
        return [
            remote(low, low, send.at[t, 5], recv.at[t, 5], ident(z, 1 - y, c, x)),
            remote(high, high, send.at[t, 6], recv.at[t, 6], ident(z, y, c, 1 - x)),
        ]

    def last(t):
        block = full.at[c, :, :, :, t]
        return [remote(block, block, send.at[t, 7], recv.at[t, 7], ident(z, y, 1 - c, x))]

    def begin(copies):
        for copy in copies:
            copy.start()

    def arrive(copies):
        for copy in copies:
            copy.wait_recv()

    for step in range(4):
        copies = vec_copies(step, vec_now, vec_got, vsend, vrecv, at)
        begin(copies)
        if step < AHEAD:
            begin(first(step))
        arrive(copies)
        total = vec_now[step]
        for k in range(len(copies)):
            total = total + vec_got[step + k]
        if step < 3:
            vec_now[step + 1] = total
        else:
            vec_out[...] = total
    own.wait()

    def body(i, _):
        @pl.when(i + AHEAD < NP)
        def _():
            begin(first(i + AHEAD))

        @pl.when(i < NP)
        def _():
            arrive(first(i))
            begin(second(i))

        @pl.when(jnp.logical_and(i >= 1, i < NP + 1))
        def _():
            arrive(second(i - 1))
            begin(third(i - 1))

        @pl.when(jnp.logical_and(i >= 2, i < NP + 2))
        def _():
            arrive(third(i - 2))
            begin(last(i - 2))

        return 0

    lax.fori_loop(0, NP + 2, body, 0)

    def done(t, _):
        arrive(last(t))
        for copy in first(t) + second(t) + third(t) + last(t):
            copy.wait_send()
        return 0

    lax.fori_loop(0, NP, done, 0)
    for step in range(4):
        for copy in vec_copies(step, vec_now, vec_got, vsend, vrecv, at):
            copy.wait_send()


AHEAD = 3


def gather_all(unit, vec_placed):
    return pl.pallas_call(
        gather_kernel,
        out_shape=(
            jax.ShapeDtypeStruct((C, Y, X, Z, NP) + PIECE, jnp.bfloat16),
            jax.ShapeDtypeStruct(vec_placed.shape, jnp.bfloat16),
        ),
        in_specs=[pl.BlockSpec(memory_space=pl.ANY), pl.BlockSpec(memory_space=pltpu.VMEM)],
        out_specs=(pl.BlockSpec(memory_space=pl.ANY), pl.BlockSpec(memory_space=pltpu.VMEM)),
        scratch_shapes=[
            pltpu.VMEM((4,) + vec_placed.shape, jnp.bfloat16),
            pltpu.VMEM((6,) + vec_placed.shape, jnp.bfloat16),
            pltpu.SemaphoreType.DMA,
            pltpu.SemaphoreType.DMA((NP, 8)),
            pltpu.SemaphoreType.DMA((NP, 8)),
            pltpu.SemaphoreType.DMA((6,)),
            pltpu.SemaphoreType.DMA((6,)),
        ],
        compiler_params=pltpu.CompilerParams(
            collective_id=0, has_side_effects=True, vmem_limit_bytes=56 << 20
        ),
        name="gather_all",
    )(unit, vec_placed)


def scatter_kernel(
    local_in, vec_in, out, vec_out, local, got_core, got_two, got_one, got_z, vec_now, vec_got, own_sem, send, recv, vsend, vrecv
):
    z, y, c, x = at = place()
    own = pltpu.make_async_copy(local_in, local, own_sem)
    own.start()
    vec_now[0] = vec_in[...]
    greet(*at)

    def core(t):
        return [
            remote(local.at[1 - c, :, :, :, t], got_core.at[t], send.at[t, 0], recv.at[t, 0], ident(z, y, 1 - c, x))
        ]

    def two(t):
        return [
            remote(local.at[c, 1 - y, :, 0:2, t], got_two.at[t, 0], send.at[t, 1], recv.at[t, 1], ident(z, 1 - y, c, x)),
            remote(local.at[c, :, 1 - x, 2:4, t], got_two.at[t, 1], send.at[t, 2], recv.at[t, 2], ident(z, y, c, 1 - x)),
        ]

    def one(t):
        return [
            remote(local.at[c, y, 1 - x, 0:2, t], got_one.at[t, 0], send.at[t, 3], recv.at[t, 3], ident(z, y, c, 1 - x)),
            remote(local.at[c, 1 - y, x, 2:4, t], got_one.at[t, 1], send.at[t, 4], recv.at[t, 4], ident(z, 1 - y, c, x)),
        ]

    def along(t):
        return [
            remote(local.at[c, y, x, (z + k) % Z, t], got_z.at[t, k - 1], send.at[t, 4 + k], recv.at[t, 4 + k], ident((z + k) % Z, y, c, x))
            for k in range(1, Z)
        ]

    def begin(copies):
        for copy in copies:
            copy.start()

    def arrive(copies):
        for copy in copies:
            copy.wait_recv()

    def add(a, b):
        return (a.astype(jnp.float32) + b.astype(jnp.float32)).astype(jnp.bfloat16)

    own.wait()

    def vec_step(step):
        begin(vec_copies(step, vec_now, vec_got, vsend, vrecv, at))

    def vec_sum(step):
        copies = vec_copies(step, vec_now, vec_got, vsend, vrecv, at)
        arrive(copies)
        total = vec_now[step]
        for k in range(len(copies)):
            total = total + vec_got[step + k]
        if step < 3:
            vec_now[step + 1] = total
            vec_step(step + 1)
        else:
            vec_out[...] = total

    vec_step(0)
    for t in range(2):
        begin(core(t))

    def body(i, _):
        @pl.when(i + 2 < NP)
        def _():
            begin(core(i + 2))

        @pl.when(i < NP)
        def _():
            arrive(core(i))
            for a in range(Y):
                for b in range(X):
                    local[c, a, b, :, i] = add(local[c, a, b, :, i], got_core[i, a, b])
            begin(two(i))

        @pl.when(jnp.logical_and(i >= 1, i < NP + 1))
        def _():
            t = i - 1
            arrive(two(t))
            for b in range(X):
                local[c, y, b, 0:2, t] = add(local[c, y, b, 0:2, t], got_two[t, 0, b])
                local[c, b, x, 2:4, t] = add(local[c, b, x, 2:4, t], got_two[t, 1, b])
            begin(one(t))

        @pl.when(jnp.logical_and(i >= 2, i < NP + 2))
        def _():
            t = i - 2
            arrive(one(t))
            for b in range(2):
                local[c, y, x, 2 * b : 2 * b + 2, t] = add(local[c, y, x, 2 * b : 2 * b + 2, t], got_one[t, b])
            begin(along(t))

        @pl.when(i >= 3)
        def _():
            t = i - 3
            arrive(along(t))
            total = local[c, y, x, z, t].astype(jnp.float32)
            for k in range(Z - 1):
                total = total + got_z[t, k].astype(jnp.float32)
            out[t] = total

        for step in range(4):
            @pl.when(i == 2 * step)
            def _():
                vec_sum(step)

        return 0

    lax.fori_loop(0, NP + 3, body, 0)

    def done(t, _):
        for copy in core(t) + two(t) + one(t) + along(t):
            copy.wait_send()
        return 0

    lax.fori_loop(0, NP, done, 0)
    for step in range(4):
        for copy in vec_copies(step, vec_now, vec_got, vsend, vrecv, at):
            copy.wait_send()


def scatter_all(local, vec_local):
    return pl.pallas_call(
        scatter_kernel,
        out_shape=(
            jax.ShapeDtypeStruct((NP,) + PIECE, jnp.float32),
            jax.ShapeDtypeStruct(vec_local.shape, jnp.float32),
        ),
        in_specs=[pl.BlockSpec(memory_space=pl.ANY), pl.BlockSpec(memory_space=pltpu.VMEM)],
        out_specs=(pl.BlockSpec(memory_space=pltpu.VMEM), pl.BlockSpec(memory_space=pltpu.VMEM)),
        scratch_shapes=[
            pltpu.VMEM((C, Y, X, Z, NP) + PIECE, jnp.bfloat16),
            pltpu.VMEM((NP, Y, X, Z) + PIECE, jnp.bfloat16),
            pltpu.VMEM((NP, 2, 2, 2) + PIECE, jnp.bfloat16),
            pltpu.VMEM((NP, 2, 2) + PIECE, jnp.bfloat16),
            pltpu.VMEM((NP, Z - 1) + PIECE, jnp.bfloat16),
            pltpu.VMEM((4,) + vec_local.shape, jnp.float32),
            pltpu.VMEM((6,) + vec_local.shape, jnp.float32),
            pltpu.SemaphoreType.DMA,
            pltpu.SemaphoreType.DMA((NP, 8)),
            pltpu.SemaphoreType.DMA((NP, 8)),
            pltpu.SemaphoreType.DMA((6,)),
            pltpu.SemaphoreType.DMA((6,)),
        ],
        compiler_params=pltpu.CompilerParams(
            collective_id=1, has_side_effects=True, vmem_limit_bytes=56 << 20
        ),
        name="scatter_all",
    )(local, vec_local)


def to_pieces(weight):
    if weight.shape[1] == D and weight.shape[0] != D // (Z * Y * X * C):
        return weight.reshape(2, 48, 2, 384).transpose(0, 2, 1, 3).reshape(4, 48, 384)
    rows, cols = weight.shape
    return weight.reshape(rows, cols // 768, 2, 384).transpose(1, 2, 0, 3).reshape(cols // 768, 48, 384)


def from_pieces(pieces, down):
    if down:
        return pieces.reshape(2, 2, 48, 384).transpose(0, 2, 1, 3).reshape(96, 768)
    count = pieces.shape[0]
    return pieces.reshape(count, 2, 24, 384).transpose(2, 0, 1, 3).reshape(24, count * 768)


def whole_of(full, lo, hi):
    count = hi - lo
    part = full[:, :, :, :, lo:hi].reshape(C, Y, X, Z, count, 2, 24, 384)
    return part.transpose(3, 1, 0, 2, 6, 4, 5, 7).reshape(768, count * 768)


def whole_down(full):
    part = full[:, :, :, :, 8:12].reshape(C, Y, X, Z, 2, 2, 48, 384)
    return part.transpose(3, 1, 0, 2, 4, 6, 5, 7).reshape(3072, 768)


def split_of(grad):
    count = grad.shape[1] // 768
    part = grad.reshape(Z, Y, C, X, 24, count, 2, 384)
    return part.transpose(2, 1, 3, 0, 5, 6, 4, 7).reshape(C, Y, X, Z, count, 48, 384)


def split_down(grad):
    part = grad.reshape(Z, Y, C, X, 2, 48, 2, 384)
    return part.transpose(2, 1, 3, 0, 4, 6, 5, 7).reshape(C, Y, X, Z, 4, 48, 384)

REACH = 256


def swap_blk(value):
    return lax.ppermute(value, "blk", [(0, 1), (1, 0)])


def on_device_fast(
    tokens,
    segments,
    cotangent,
    qkv_weight,
    proj_weight,
    up_weight,
    down_weight,
    vec_params,
    qkv_velocity,
    proj_velocity,
    up_velocity,
    down_velocity,
    vec_velocity,
    qkv_average,
    proj_average,
    up_average,
    down_average,
    vec_average,
):
    rows, block = (tokens.shape[0], tokens.shape[1])
    length = segments.shape[1]
    total_tokens = rows * lax.axis_size("dp") * length
    rate = 0.05 / math.sqrt(total_tokens)
    position = lax.axis_index("blk")
    shard = lax.axis_index("dp") * lax.axis_size("blk") + position
    masters = [w.astype(jnp.bfloat16) for w in (qkv_weight, proj_weight, up_weight, down_weight)]
    unit = jnp.concatenate([to_pieces(w) for w in masters], axis=0)
    vec_placed = lax.dynamic_update_slice(
        jnp.zeros((16, D), jnp.bfloat16), vec_params.astype(jnp.bfloat16), (0, shard * vec_params.shape[1])
    )
    full, vec_low = gather_all(unit, vec_placed)
    w_query, w_proj, w_up = whole_of(full, 0, 3), whole_of(full, 3, 4), whole_of(full, 4, 8)
    w_down = whole_down(full)
    vec = vec_low.astype(jnp.float32)
    bias_up = vec[8:12].reshape(-1)
    seg_query = lax.dynamic_slice_in_dim(segments, position * block, block, 1)
    inputs = tokens.astype(jnp.float32)
    a_one = layer_norm(inputs, vec[0], vec[1]).astype(jnp.bfloat16)
    zero_bias = jnp.zeros_like(vec[2])
    pre = jnp.dot(a_one, w_query, preferred_element_type=jnp.float32) + jnp.concatenate(
        [vec[2], zero_bias, vec[3]]
    )
    qkv = pre.astype(jnp.bfloat16)
    query = qkv[..., :D].reshape(rows, block, HEADS, HEAD_DIM)
    key_value = qkv[..., D:]
    halo = swap_blk(lax.dynamic_slice_in_dim(key_value, (1 - position) * REACH, REACH, 1))
    near = jnp.where(
        position == 0,
        jnp.concatenate([key_value, halo], axis=1),
        jnp.concatenate([halo, key_value], axis=1),
    )
    seg_near = lax.dynamic_slice_in_dim(segments, position * REACH, block + REACH, 1)
    count = near.shape[1]
    keys = near[..., :D].reshape(rows, count, HEADS, HEAD_DIM)
    values = near[..., D:].reshape(rows, count, HEADS, HEAD_DIM)
    scores, allowed = scores_of(query, keys, seg_query, seg_near)
    scores = jnp.where(allowed, scores, -1e30)
    new_top = jnp.max(scores, axis=-1)
    weights = jnp.where(allowed, jnp.exp(scores - new_top[..., None]), 0.0)
    denoms = jnp.sum(weights, axis=-1)
    added = jnp.einsum(
        "ghqk,gkhd->gqhd", weights.astype(jnp.bfloat16), values, preferred_element_type=jnp.float32
    )
    mixed = (added / jnp.transpose(denoms, (0, 2, 1))[..., None]).reshape(rows, block, D)
    mixed_low = mixed.astype(jnp.bfloat16)
    second = inputs + jnp.dot(mixed_low, w_proj, preferred_element_type=jnp.float32) + vec[4]
    second_norm, norm_two_back = jax.vjp(layer_norm, second, vec[5], vec[6])
    a_two = second_norm.astype(jnp.bfloat16)
    hidden = jnp.dot(a_two, w_up, preferred_element_type=jnp.float32) + bias_up
    act_value, gelu_back = jax.vjp(gelu_exact, hidden)
    act = act_value.astype(jnp.bfloat16)
    result = second + jnp.dot(act, w_down, preferred_element_type=jnp.float32) + vec[7]
    output = result.astype(jnp.bfloat16)
    out_grad = cotangent.astype(jnp.float32)
    grad_down = contract_tokens(act, cotangent).astype(jnp.bfloat16)
    bias_down_grad = jnp.sum(out_grad, axis=(0, 1))
    act_grad = times_transpose(cotangent, w_down)
    hidden_grad = gelu_back(act_grad)[0].astype(jnp.bfloat16)
    bias_up_grad = jnp.sum(hidden_grad.astype(jnp.float32), axis=(0, 1))
    grad_up = contract_tokens(a_two, hidden_grad).astype(jnp.bfloat16)
    a_two_grad = times_transpose(hidden_grad, w_up)
    second_part, gain_two_grad, shift_two_grad = norm_two_back(a_two_grad)
    second_grad = out_grad + second_part
    attn_grad = second_grad.astype(jnp.bfloat16)
    bias_proj_grad = jnp.sum(attn_grad.astype(jnp.float32), axis=(0, 1))
    grad_proj = contract_tokens(mixed_low, attn_grad).astype(jnp.bfloat16)
    mixed_grad = (
        times_transpose(attn_grad, w_proj)
        .astype(jnp.bfloat16)
        .reshape(rows, block, HEADS, HEAD_DIM)
    )
    query_grad, kv_terms = attend_back(query, near, mixed_grad, seg_query, seg_near, rows)
    away = swap_blk(
        lax.dynamic_slice_in_dim(kv_terms, (1 - position) * block, REACH, 1).astype(jnp.bfloat16)
    ).astype(jnp.float32)
    kv_own = lax.dynamic_slice_in_dim(kv_terms, position * REACH, block, 1)
    padded = jnp.where(
        position == 0,
        jnp.pad(away, ((0, 0), (block - REACH, 0), (0, 0))),
        jnp.pad(away, ((0, 0), (0, block - REACH), (0, 0))),
    )
    kv_grad = kv_own + padded
    qkv_grad_low = jnp.concatenate([query_grad, kv_grad], axis=-1).astype(jnp.bfloat16)
    qkv_sums = jnp.sum(qkv_grad_low.astype(jnp.float32), axis=(0, 1))
    grad_query = contract_tokens(a_one, qkv_grad_low).astype(jnp.bfloat16)
    a_one_grad = times_transpose(qkv_grad_low, w_query)
    norm_one_back = jax.vjp(layer_norm, inputs, vec[0], vec[1])[1]
    first_part, gain_one_grad, shift_one_grad = norm_one_back(a_one_grad)
    tokens_grad = (second_grad + first_part).astype(jnp.bfloat16)
    vec_local = jnp.concatenate(
        [
            jnp.stack(
                [
                    gain_one_grad,
                    shift_one_grad,
                    qkv_sums[:D],
                    qkv_sums[2 * D :],
                    bias_proj_grad,
                    gain_two_grad,
                    shift_two_grad,
                    bias_down_grad,
                ]
            ),
            bias_up_grad.reshape(4, D),
            jnp.zeros((4, D), jnp.float32),
        ],
        axis=0,
    )
    local = jnp.concatenate(
        [split_of(grad_query), split_of(grad_proj), split_of(grad_up), split_down(grad_down)], axis=4
    )
    pieces, vec_sum = scatter_all(local, vec_local)
    query_share = from_pieces(pieces[0:3], False)
    proj_share = from_pieces(pieces[3:4], False)
    up_share = from_pieces(pieces[4:8], False)
    down_share = from_pieces(pieces[8:12], True)
    vec_share = lax.dynamic_slice(
        vec_sum, (0, shard * vec_params.shape[1]), vec_params.shape
    )
    qkv_new = update(qkv_weight, query_share, qkv_velocity, qkv_average, rate)
    proj_new = update(proj_weight, proj_share, proj_velocity, proj_average, rate)
    up_new = update(up_weight, up_share, up_velocity, up_average, rate)
    down_new = update(down_weight, down_share, down_velocity, down_average, rate)
    vec_new = update(vec_params, vec_share, vec_velocity, vec_average, rate)
    return (
        output,
        tokens_grad,
        query_share,
        proj_share,
        up_share,
        down_share,
        vec_share,
        qkv_new[0],
        proj_new[0],
        up_new[0],
        down_new[0],
        vec_new[0],
        qkv_new[1],
        proj_new[1],
        up_new[1],
        down_new[1],
        vec_new[1],
        qkv_new[2],
        proj_new[2],
        up_new[2],
        down_new[2],
        vec_new[2],
        qkv_new[0].astype(jnp.bfloat16),
        proj_new[0].astype(jnp.bfloat16),
        up_new[0].astype(jnp.bfloat16),
        down_new[0].astype(jnp.bfloat16),
        vec_new[0].astype(jnp.bfloat16),
    )


def solution(mesh):
    fits = mesh.shape["dp"] == Z * Y * C and mesh.shape["blk"] == X
    return jax.shard_map(
        on_device_fast if fits else on_device,
        mesh=mesh,
        in_specs=(
            P("dp", "blk", None),
            P("dp", None),
            P("dp", "blk", None),
            P(("dp", "blk"), None),
            P(("dp", "blk"), None),
            P(("dp", "blk"), None),
            P(("dp", "blk"), None),
            P(None, ("dp", "blk")),
            P(("dp", "blk"), None),
            P(("dp", "blk"), None),
            P(("dp", "blk"), None),
            P(("dp", "blk"), None),
            P(None, ("dp", "blk")),
            P(("dp", "blk"), None),
            P(("dp", "blk"), None),
            P(("dp", "blk"), None),
            P(("dp", "blk"), None),
            P(None, ("dp", "blk")),
        ),
        out_specs=(
            P("dp", "blk", None),
            P("dp", "blk", None),
            P(("dp", "blk"), None),
            P(("dp", "blk"), None),
            P(("dp", "blk"), None),
            P(("dp", "blk"), None),
            P(None, ("dp", "blk")),
            P(("dp", "blk"), None),
            P(("dp", "blk"), None),
            P(("dp", "blk"), None),
            P(("dp", "blk"), None),
            P(None, ("dp", "blk")),
            P(("dp", "blk"), None),
            P(("dp", "blk"), None),
            P(("dp", "blk"), None),
            P(("dp", "blk"), None),
            P(None, ("dp", "blk")),
            P(("dp", "blk"), None),
            P(("dp", "blk"), None),
            P(("dp", "blk"), None),
            P(("dp", "blk"), None),
            P(None, ("dp", "blk")),
            P(("dp", "blk"), None),
            P(("dp", "blk"), None),
            P(("dp", "blk"), None),
            P(("dp", "blk"), None),
            P(None, ("dp", "blk")),
        ),
        check_vma=False,
    )
```

```python
import math

import jax
import jax.numpy as jnp
from jax import lax
from jax.experimental import pallas as pl
from jax.experimental.pallas import tpu as pltpu
from jax.sharding import PartitionSpec as P

D = 768
HEADS = 12
HEAD_DIM = 64


def layer_norm(value, gain, shift):
    mean = jnp.mean(value, axis=-1, keepdims=True)
    cent = value - mean
    var = jnp.mean(cent * cent, axis=-1, keepdims=True)
    return cent * lax.rsqrt(var + 1e-06) * (1.0 + gain) + shift


def gelu_exact(value):
    return jax.nn.gelu(value, approximate=False)


def contract_tokens(left, right):
    return lax.dot_general(
        left.reshape(-1, left.shape[-1]),
        right.reshape(-1, right.shape[-1]),
        (((0,), (0,)), ((), ())),
        preferred_element_type=jnp.float32,
    )


def times_transpose(left, weight):
    return lax.dot_general(
        left, weight, (((left.ndim - 1,), (1,)), ((), ())), preferred_element_type=jnp.float32
    )


def group_size(rows, block):
    limit = max(1, 512 // block)
    best = 1
    for cand in range(1, rows + 1):
        if rows % cand == 0 and cand <= limit:
            best = cand
    return best


def scores_of(query, keys, seg_query, seg_keys):
    scores = jnp.einsum(
        "gqhd,gkhd->ghqk", query, keys, preferred_element_type=jnp.float32
    ) * HEAD_DIM ** (-0.5)
    allowed = (seg_query[:, :, None] == seg_keys[:, None, :])[:, None]
    return (scores, allowed)


def attend_back(query, kv_all, grad_out, seg_query, segments, group):
    rows, block = (query.shape[0], query.shape[1])
    length = kv_all.shape[1]
    keys = kv_all[0:group, :, :D].reshape(group, length, HEADS, HEAD_DIM)
    values = kv_all[0:group, :, D:].reshape(group, length, HEADS, HEAD_DIM)
    scores, allowed = scores_of(query, keys, seg_query, segments)
    probs = jax.nn.softmax(jnp.where(allowed, scores, -1e30), axis=-1)
    probs_low = probs.astype(jnp.bfloat16)
    prob_grad = jnp.einsum("gqhd,gkhd->ghqk", grad_out, values, preferred_element_type=jnp.float32)
    score_grad = probs * (prob_grad - jnp.sum(probs * prob_grad, axis=-1, keepdims=True))
    score_low = score_grad.astype(jnp.bfloat16)
    dq_part = jnp.einsum(
        "ghqk,gkhd->gqhd", score_low, keys, preferred_element_type=jnp.float32
    ) * HEAD_DIM ** (-0.5)
    dk_part = jnp.einsum(
        "ghqk,gqhd->gkhd", score_low, query, preferred_element_type=jnp.float32
    ) * HEAD_DIM ** (-0.5)
    dv_part = jnp.einsum("ghqk,gqhd->gkhd", probs_low, grad_out, preferred_element_type=jnp.float32)
    dq_parts = dq_part.reshape(group, block, D)
    dkv_parts = jnp.concatenate(
        [dk_part.reshape(group, length, D), dv_part.reshape(group, length, D)], axis=-1
    )
    return (dq_parts, dkv_parts)


def update(weight, grad, velocity, average, rate):
    step_value = grad + 0.0005 * weight
    velocity_new = 0.9 * velocity + step_value
    weight_new = weight - rate * (step_value + 0.9 * velocity_new)
    average_new = 0.9 * average + 0.1 * weight_new
    return (weight_new, velocity_new, average_new)


def on_device(
    tokens,
    segments,
    cotangent,
    qkv_weight,
    proj_weight,
    up_weight,
    down_weight,
    vec_params,
    qkv_velocity,
    proj_velocity,
    up_velocity,
    down_velocity,
    vec_velocity,
    qkv_average,
    proj_average,
    up_average,
    down_average,
    vec_average,
):
    rows, block = (tokens.shape[0], tokens.shape[1])
    length = segments.shape[1]
    total_tokens = rows * lax.axis_size("dp") * length
    rate = 0.05 / math.sqrt(total_tokens)
    group = group_size(rows, block)
    gathered = (
        lax.all_gather(qkv_weight.astype(jnp.bfloat16), ("dp", "blk"), axis=0, tiled=True),
        lax.all_gather(proj_weight.astype(jnp.bfloat16), ("dp", "blk"), axis=0, tiled=True),
        lax.all_gather(up_weight.astype(jnp.bfloat16), ("dp", "blk"), axis=0, tiled=True),
        lax.all_gather(down_weight.astype(jnp.bfloat16), ("dp", "blk"), axis=0, tiled=True),
        lax.all_gather(vec_params.astype(jnp.bfloat16), ("dp", "blk"), axis=1, tiled=True),
    )
    w_query, w_proj, w_up, w_down, vec_low = gathered
    vec = vec_low.astype(jnp.float32)
    bias_up = vec[8:12].reshape(-1)
    position = lax.axis_index("blk")
    seg_query = lax.dynamic_slice_in_dim(segments, position * block, block, 1)
    inputs = tokens.astype(jnp.float32)
    a_one = layer_norm(inputs, vec[0], vec[1]).astype(jnp.bfloat16)
    zero_bias = jnp.zeros_like(vec[2])
    pre = jnp.dot(a_one, w_query, preferred_element_type=jnp.float32) + jnp.concatenate(
        [vec[2], zero_bias, vec[3]]
    )
    qkv = pre.astype(jnp.bfloat16)
    query = qkv[..., :D].reshape(rows, block, HEADS, HEAD_DIM)
    key_value = qkv[..., D:]
    piece = lax.all_gather(key_value, "blk", axis=1, tiled=True)
    top = jnp.full((rows, HEADS, block), -1e30, jnp.float32)
    count = piece.shape[1]
    keys = piece[0:group, :, :D].reshape(group, count, HEADS, HEAD_DIM)
    values = piece[0:group, :, D:].reshape(group, count, HEADS, HEAD_DIM)
    scores, allowed = scores_of(query, keys, seg_query, segments)
    scores = jnp.where(allowed, scores, -1e30)
    new_top = jnp.maximum(top, jnp.max(scores, axis=-1))
    weights = jnp.where(allowed, jnp.exp(scores - new_top[..., None]), 0.0)
    denoms = jnp.sum(weights, axis=-1)
    added = jnp.einsum(
        "ghqk,gkhd->gqhd", weights.astype(jnp.bfloat16), values, preferred_element_type=jnp.float32
    )
    mixed = (added / jnp.transpose(denoms, (0, 2, 1))[..., None]).reshape(rows, block, D)
    mixed_low = mixed.astype(jnp.bfloat16)
    second = inputs + jnp.dot(mixed_low, w_proj, preferred_element_type=jnp.float32) + vec[4]
    second_norm, norm_two_back = jax.vjp(layer_norm, second, vec[5], vec[6])
    a_two = second_norm.astype(jnp.bfloat16)
    hidden = jnp.dot(a_two, w_up, preferred_element_type=jnp.float32) + bias_up
    act_value, gelu_back = jax.vjp(gelu_exact, hidden)
    act = act_value.astype(jnp.bfloat16)
    result = second + jnp.dot(act, w_down, preferred_element_type=jnp.float32) + vec[7]
    output = result.astype(jnp.bfloat16)
    out_grad = cotangent.astype(jnp.float32)
    grad_down = contract_tokens(act, cotangent)
    bias_down_grad = jnp.sum(out_grad, axis=(0, 1))
    act_grad = times_transpose(cotangent, w_down)
    hidden_grad = gelu_back(act_grad)[0].astype(jnp.bfloat16)
    bias_up_grad = jnp.sum(hidden_grad.astype(jnp.float32), axis=(0, 1))
    grad_up = contract_tokens(a_two, hidden_grad)
    a_two_grad = times_transpose(hidden_grad, w_up)
    second_part, gain_two_grad, shift_two_grad = norm_two_back(a_two_grad)
    second_grad = out_grad + second_part
    attn_grad = second_grad.astype(jnp.bfloat16)
    bias_proj_grad = jnp.sum(attn_grad.astype(jnp.float32), axis=(0, 1))
    grad_proj = contract_tokens(mixed_low, attn_grad)
    mixed_grad = (
        times_transpose(attn_grad, w_proj)
        .astype(jnp.bfloat16)
        .reshape(rows, block, HEADS, HEAD_DIM)
    )
    kv_again = lax.all_gather(key_value, "blk", axis=1, tiled=True)
    query_grad, kv_terms = attend_back(query, kv_again, mixed_grad, seg_query, segments, group)
    kv_grad = lax.psum_scatter(
        kv_terms.astype(jnp.bfloat16), "blk", scatter_dimension=1, tiled=True
    ).astype(jnp.float32)
    qkv_grad_low = jnp.concatenate([query_grad, kv_grad], axis=-1).astype(jnp.bfloat16)
    qkv_sums = jnp.sum(qkv_grad_low.astype(jnp.float32), axis=(0, 1))
    grad_query = contract_tokens(a_one, qkv_grad_low)
    a_one_grad = times_transpose(qkv_grad_low, w_query)
    norm_one_back = jax.vjp(layer_norm, inputs, vec[0], vec[1])[1]
    first_part, gain_one_grad, shift_one_grad = norm_one_back(a_one_grad)
    tokens_grad = (second_grad + first_part).astype(jnp.bfloat16)
    vec_local = jnp.concatenate(
        [
            jnp.stack(
                [
                    gain_one_grad,
                    shift_one_grad,
                    qkv_sums[:D],
                    qkv_sums[2 * D :],
                    bias_proj_grad,
                    gain_two_grad,
                    shift_two_grad,
                    bias_down_grad,
                ]
            ),
            bias_up_grad.reshape(4, D),
        ],
        axis=0,
    )
    query_share, proj_share, up_share, down_share, vec_share = (
        lax.psum_scatter(grad_query, ("dp", "blk"), scatter_dimension=0, tiled=True),
        lax.psum_scatter(grad_proj, ("dp", "blk"), scatter_dimension=0, tiled=True),
        lax.psum_scatter(grad_up, ("dp", "blk"), scatter_dimension=0, tiled=True),
        lax.psum_scatter(grad_down, ("dp", "blk"), scatter_dimension=0, tiled=True),
        lax.psum_scatter(vec_local, ("dp", "blk"), scatter_dimension=1, tiled=True),
    )
    qkv_new = update(qkv_weight, query_share, qkv_velocity, qkv_average, rate)
    proj_new = update(proj_weight, proj_share, proj_velocity, proj_average, rate)
    up_new = update(up_weight, up_share, up_velocity, up_average, rate)
    down_new = update(down_weight, down_share, down_velocity, down_average, rate)
    vec_new = update(vec_params, vec_share, vec_velocity, vec_average, rate)
    return (
        output,
        tokens_grad,
        query_share,
        proj_share,
        up_share,
        down_share,
        vec_share,
        qkv_new[0],
        proj_new[0],
        up_new[0],
        down_new[0],
        vec_new[0],
        qkv_new[1],
        proj_new[1],
        up_new[1],
        down_new[1],
        vec_new[1],
        qkv_new[2],
        proj_new[2],
        up_new[2],
        down_new[2],
        vec_new[2],
        qkv_new[0].astype(jnp.bfloat16),
        proj_new[0].astype(jnp.bfloat16),
        up_new[0].astype(jnp.bfloat16),
        down_new[0].astype(jnp.bfloat16),
        vec_new[0].astype(jnp.bfloat16),
    )


PIECE = (48, 384)
NP = 12
Z, Y, X, C = 4, 2, 2, 2
AHEAD = 2
REACH = 256
TILE = 128
SPAN = TILE + 2 * REACH
PAIRS = HEADS // 2
MESH = pl.DeviceIdType.MESH
F32, BF16 = jnp.float32, jnp.bfloat16
NT = (((1,), (1,)), ((), ()))
TN = (((0,), (0,)), ((), ()))


def place():
    d, x = lax.axis_index("dp"), lax.axis_index("blk")
    return d // (2 * Y), (d // 2) % Y, d % 2, x


def ident(z, y, c, x):
    return ((z * Y + y) * 2 + c, x)


def greet(z, y, c, x):
    barrier = pltpu.get_barrier_semaphore()
    peers = [ident((z + k) % Z, y, c, x) for k in range(1, Z)]
    peers += [ident(z, 1 - y, c, x), ident(z, y, c, 1 - x), ident(z, y, 1 - c, x)]
    for peer in peers:
        pl.semaphore_signal(barrier, inc=1, device_id=peer, device_id_type=MESH)
    pl.semaphore_wait(barrier, len(peers))


def remote(src, dst, send, recv, peer):
    return pltpu.make_async_remote_copy(
        src_ref=src, dst_ref=dst, send_sem=send, recv_sem=recv, device_id=peer, device_id_type=MESH
    )


def begin(copies):
    for copy in copies:
        copy.start()


def arrive(copies):
    for copy in copies:
        copy.wait_recv()


def within(index, low, high, run):
    if isinstance(index, int):
        if low <= index < high:
            run()
    else:
        pl.when(jnp.logical_and(index >= low, index < high))(run)


def loop(count, body):
    def step(i, carry):
        body(i)
        return carry

    lax.fori_loop(0, count, step, 0)


def cols(j, width):
    return pl.ds(pl.multiple_of(j * width, width), width)


def dot(a, b, dims=None):
    dims = (((1,), (0,)), ((), ())) if dims is None else dims
    return lax.dot_general(a, b, dims, preferred_element_type=F32)


class Vec:
    def __init__(self, at, now, got, send, recv):
        self.at, self.now, self.got, self.send, self.recv = at, now, got, send, recv

    def copies(self, step):
        z, y, c, x = self.at
        peers = [
            [ident(z, y, 1 - c, x)],
            [ident(z, y, c, 1 - x)],
            [ident(z, 1 - y, c, x)],
            [ident((z + k) % Z, y, c, x) for k in range(1, Z)],
        ][step]
        return [
            remote(self.now.at[step], self.got.at[step + k], self.send.at[step + k], self.recv.at[step + k], peer)
            for k, peer in enumerate(peers)
        ]

    def begin(self, step):
        begin(self.copies(step))

    def total(self, step):
        copies = self.copies(step)
        arrive(copies)
        total = self.now[step]
        for k in range(len(copies)):
            total = total + self.got[step + k]
        return total

    def sent(self):
        for step in range(4):
            for copy in self.copies(step):
                copy.wait_send()


def normal(value):
    mean = jnp.mean(value, axis=-1, keepdims=True)
    cent = value - mean
    var = jnp.mean(cent * cent, axis=-1, keepdims=True)
    scale = lax.rsqrt(var + 1e-06)
    return cent * scale, scale


def window(tile, x):
    first = jnp.where(x == 0, jnp.maximum(tile - 2, 0), jnp.minimum(tile, 1))
    return pl.ds(pl.multiple_of(first * TILE, TILE), SPAN)


def mask_fill(seg_col, seg_row, bias, x, tiles):
    def one(tile):
        column = seg_col[window(tile, x), :]
        row = seg_row[0:1, cols(tile, TILE)]
        bias[tile] = jnp.where(column == row, 0.0, -1e30).astype(F32)

    loop(tiles, one)


def split_heads(pair_block):
    lane = lax.broadcasted_iota(jnp.int32, pair_block.shape, 1)
    zero = jnp.zeros_like(pair_block)
    return jnp.concatenate(
        [jnp.where(lane < HEAD_DIM, pair_block, zero), jnp.where(lane < HEAD_DIM, zero, pair_block)], axis=0
    )


def join_heads(both):
    own = jnp.concatenate([both[:HEAD_DIM, :TILE], both[HEAD_DIM:, TILE:]], axis=0)
    return jnp.transpose(own)


def rows_from_stage(stage, target, col):
    def group(g):
        parts = [stage[c, g % Y, x, g // Y].astype(F32) for c in range(C) for x in range(X)]
        rows = pl.ds(pl.multiple_of(g * 96, 96), 96)
        target[rows, col : col + 384] = jnp.concatenate([p[:24] for p in parts], axis=0).astype(BF16)
        target[rows, col + 384 : col + 768] = jnp.concatenate([p[24:] for p in parts], axis=0).astype(BF16)

    loop(Z * Y, group)


def down_from_stage(stage, target, half, col):
    def group(g):
        for c in range(C):
            for x in range(X):
                start = pl.multiple_of(g * 384 + (c * X + x) * 96 + half * 48, 16)
                target[pl.ds(start, 48), col * 384 : col * 384 + 384] = stage[c, g % Y, x, g // Y]

    loop(Z * Y, group)


class Gather:
    def __init__(self, at, unit, full, own, send, recv):
        self.at, self.unit, self.full, self.own, self.send, self.recv = at, unit, full, own, send, recv

    def mine(self, t):
        z, y, c, x = self.at
        return pltpu.make_async_copy(self.unit.at[t], self.full.at[c, y, x, z, t], self.own.at[t])

    def first(self, t):
        z, y, c, x = self.at
        return [
            remote(
                self.unit.at[t], self.full.at[c, y, x, z, t], self.send.at[t, k - 1], self.recv.at[t, k - 1],
                ident((z + k) % Z, y, c, x),
            )
            for k in range(1, Z)
        ]

    def second(self, t):
        z, y, c, x = self.at
        low, high = self.full.at[c, y, x, 0:2, t], self.full.at[c, y, x, 2:4, t]
        return [
            remote(low, low, self.send.at[t, 3], self.recv.at[t, 3], ident(z, y, c, 1 - x)),
            remote(high, high, self.send.at[t, 4], self.recv.at[t, 4], ident(z, 1 - y, c, x)),
        ]

    def third(self, t):
        z, y, c, x = self.at
        low, high = self.full.at[c, y, :, 0:2, t], self.full.at[c, :, x, 2:4, t]
        return [
            remote(low, low, self.send.at[t, 5], self.recv.at[t, 5], ident(z, 1 - y, c, x)),
            remote(high, high, self.send.at[t, 6], self.recv.at[t, 6], ident(z, y, c, 1 - x)),
        ]

    def last(self, t):
        z, y, c, x = self.at
        block = self.full.at[c, :, :, :, t]
        return [remote(block, block, self.send.at[t, 7], self.recv.at[t, 7], ident(z, y, 1 - c, x))]

    def start(self):
        loop(NP, lambda t: self.mine(t).start())
        loop(AHEAD, lambda t: begin(self.first(t)))

    def progress(self, i):
        def to_second():
            self.mine(i).wait()
            arrive(self.first(i))
            begin(self.second(i))

        def to_third():
            arrive(self.second(i - 1))
            begin(self.third(i - 1))

        def to_last():
            arrive(self.third(i - 2))
            begin(self.last(i - 2))

        within(i, 0, NP, to_second)
        within(i, 1, NP + 1, to_third)
        within(i, 2, NP + 2, to_last)
        within(i, 0, NP - AHEAD, lambda: begin(self.first(i + AHEAD)))

    def sent(self):
        def one(t):
            for copy in self.first(t) + self.second(t) + self.third(t) + self.last(t):
                copy.wait_send()

        loop(NP, one)


def forward_kernel(
    unit, vec_in, tok, seg_col, seg_row,
    full, vec_out, out_o, q_o, k_o, v_o, o_o, stat_o, x2_o, a2_o, z_o, slope_o,
    near, a1, wbig, wdown, stage, vecf, bias, out_s, q_s, k_s, v_s, o_s, stat_s, x2_s, a2_s, z_s, slope_s,
    vec_now, vec_got, own, send, recv, vsend, vrecv, hsem, ssem, osem,
):
    z, y, c, x = at = place()
    block = tok.shape[0]
    tiles = block // TILE
    offset = pl.multiple_of(x * REACH, REACH)
    vec_now[0] = vec_in[...]
    greet(*at)
    gather = Gather(at, unit, full, own, send, recv)
    gather.start()
    vec = Vec(at, vec_now, vec_got, vsend, vrecv)
    vec.begin(0)
    away = pl.multiple_of((1 - x) * REACH, REACH)
    land = pl.multiple_of(x * block, REACH)
    halo = remote(
        tok.at[pl.ds(away, REACH)], near.at[pl.ds(land, REACH)], hsem.at[0], hsem.at[1], ident(z, y, c, 1 - x)
    )
    halo.start()
    near[pl.ds(offset, block), :] = tok[...]

    def put(k, src, dst):
        return pltpu.make_async_copy(src, dst, osem.at[k])

    def vec_step(step):
        total = vec.total(step)
        if step < 3:
            vec_now[step + 1] = total
            vec.begin(step + 1)
        else:
            vec_out[...] = total
            vecf[...] = total.astype(F32)

    def load(t):
        arrive(gather.last(t))
        copy = pltpu.make_async_copy(full.at[:, :, :, :, t], stage, ssem)
        copy.start()
        copy.wait()

    vec_step(0)
    vec_step(1)
    gather.progress(0)
    vec_step(2)
    vec_step(3)
    gather.progress(1)
    halo.wait_recv()

    def norm_one(i):
        rows = pl.ds(pl.multiple_of(i * 256, 256), 256)
        value = normal(near[rows, :].astype(F32))[0]
        a1[rows, :] = (value * (1.0 + vecf[0:1, :]) + vecf[1:2, :]).astype(BF16)

    loop(near.shape[0] // 256, norm_one)
    mask_fill(seg_col, seg_row, bias, x, tiles)
    gather.progress(2)
    gather.progress(3)
    load(0)
    rows_from_stage(stage, wbig, D)

    def keys(j):
        k_s[:, cols(j, 256)] = dot(a1[...], wbig[:, pl.ds(pl.multiple_of(D + j * 256, 256), 256)]).astype(BF16)

    loop(3, keys)
    gather.progress(4)
    load(1)
    rows_from_stage(stage, wbig, 2 * D)

    def values(j):
        value = dot(a1[...], wbig[:, pl.ds(pl.multiple_of(2 * D + j * 256, 256), 256)])
        v_s[:, cols(j, 256)] = (value + vecf[3:4, cols(j, 256)]).astype(BF16)

    loop(3, values)
    load(2)
    rows_from_stage(stage, wbig, 0)

    def queries(j):
        value = dot(a1[pl.ds(offset, block), :], wbig[:, cols(j, 256)]) + vecf[2:3, cols(j, 256)]
        q_s[:, cols(j, 256)] = value.astype(BF16) * HEAD_DIM ** (-0.5)

    loop(3, queries)
    put(0, k_s, k_o).start()
    put(1, v_s, v_o).start()
    put(2, q_s, q_o).start()

    def attend(pair):
        gather.progress(pair + 5)
        lanes = cols(pair, 128)

        def one(tile):
            rows = cols(tile, TILE)
            span = window(tile, x)
            both = split_heads(q_s[rows, lanes])
            fill = bias[tile]
            scores = dot(k_s[span, lanes], both, NT) + jnp.concatenate([fill, fill], axis=1)
            top = jnp.max(scores, axis=0, keepdims=True)
            weights = jnp.exp(scores - top)
            total = jnp.sum(weights, axis=0, keepdims=True)
            mixed = dot(v_s[span, lanes], weights.astype(BF16), TN) / total
            o_s[rows, lanes] = join_heads(mixed).astype(BF16)
            stat_s[pair * tiles + tile] = jnp.broadcast_to(top + jnp.log(total), (8, 2 * TILE))

        loop(tiles, one)

    loop(PAIRS, attend)
    put(3, o_s, o_o).start()
    put(4, stat_s, stat_o).start()
    load(3)
    rows_from_stage(stage, wbig, 3 * D)

    def project(j):
        value = dot(o_s[...], wbig[:, pl.ds(pl.multiple_of(3 * D + j * 256, 256), 256)])
        x2_s[:, cols(j, 256)] = tok[:, cols(j, 256)].astype(F32) + value + vecf[4:5, cols(j, 256)]

    loop(3, project)

    def norm_two(i):
        rows = pl.ds(pl.multiple_of(i * 256, 256), 256)
        value = normal(x2_s[rows, :])[0]
        a2_s[rows, :] = (value * (1.0 + vecf[5:6, :]) + vecf[6:7, :]).astype(BF16)

    loop(block // 256, norm_two)
    put(5, x2_s, x2_o).start()
    put(6, a2_s, a2_o).start()
    gather.progress(11)

    def expand(j):
        col = pl.multiple_of(j * 256, 256)
        u = dot(a2_s[...], wbig[:, pl.ds(pl.multiple_of(4 * D + col, 256), 256)])
        u = u + vecf[pl.ds(8 + j // 3, 1), pl.ds(pl.multiple_of((j % 3) * 256, 256), 256)]
        half = 0.5 + 0.5 * lax.erf(u * math.sqrt(0.5))
        z_s[:, cols(j, 256)] = (u * half).astype(BF16)
        slope = half + u * (jnp.exp(-0.5 * u * u) * (1.0 / math.sqrt(2.0 * math.pi)))
        slope_s[:, cols(j, 256)] = slope.astype(BF16)

    for t in range(4):
        load(4 + t)
        rows_from_stage(stage, wbig, (4 + t) * D)
        loop(3, lambda j: expand(j + 3 * t))
        if t == 1:
            gather.progress(12)
    put(7, z_s, z_o).start()
    put(8, slope_s, slope_o).start()
    gather.progress(13)
    for t in range(4):
        load(8 + t)
        down_from_stage(stage, wdown, t % 2, t // 2)
        if t % 2 == 1:
            col = slice(t // 2 * 384, t // 2 * 384 + 384)
            value = dot(z_s[...], wdown[:, col])
            out_s[:, col] = (x2_s[:, col] + value + vecf[7:8, col]).astype(BF16)
    put(9, out_s, out_o).start()
    pairs = [(k_s, k_o), (v_s, v_o), (q_s, q_o), (o_s, o_o), (stat_s, stat_o), (x2_s, x2_o), (a2_s, a2_o)]
    for k, (src, dst) in enumerate(pairs + [(z_s, z_o), (slope_s, slope_o), (out_s, out_o)]):
        put(k, src, dst).wait()
    gather.sent()
    vec.sent()
    halo.wait_send()


def forward_all(unit, vec_placed, tok, seg_col, seg_row):
    block, near = tok.shape[0], seg_col.shape[0]
    ff = 4 * D
    tiles = block // TILE
    shapes = [
        ((block, D), BF16),
        ((block, D), BF16),
        ((near, D), BF16),
        ((near, D), BF16),
        ((block, D), BF16),
        ((PAIRS * tiles, 8, 2 * TILE), F32),
        ((block, D), F32),
        ((block, D), BF16),
        ((block, ff), BF16),
        ((block, ff), BF16),
    ]
    hbm, vmem = pl.BlockSpec(memory_space=pl.ANY), pl.BlockSpec(memory_space=pltpu.VMEM)
    outs = [((C, Y, X, Z, NP) + PIECE, BF16), (vec_placed.shape, BF16)] + shapes
    return pl.pallas_call(
        forward_kernel,
        out_shape=tuple(jax.ShapeDtypeStruct(*one) for one in outs),
        in_specs=[vmem] * 5,
        out_specs=tuple([hbm, vmem] + [hbm] * len(shapes)),
        scratch_shapes=[
            pltpu.VMEM((near, D), BF16),
            pltpu.VMEM((near, D), BF16),
            pltpu.VMEM((D, 8 * D), BF16),
            pltpu.VMEM((ff, D), BF16),
            pltpu.VMEM((C, Y, X, Z) + PIECE, BF16),
            pltpu.VMEM(vec_placed.shape, F32),
            pltpu.VMEM((tiles, SPAN, TILE), F32),
            *[pltpu.VMEM(*one) for one in shapes],
            pltpu.VMEM((4,) + vec_placed.shape, BF16),
            pltpu.VMEM((6,) + vec_placed.shape, BF16),
            pltpu.SemaphoreType.DMA((NP,)),
            pltpu.SemaphoreType.DMA((NP, 8)),
            pltpu.SemaphoreType.DMA((NP, 8)),
            pltpu.SemaphoreType.DMA((6,)),
            pltpu.SemaphoreType.DMA((6,)),
            pltpu.SemaphoreType.DMA((2,)),
            pltpu.SemaphoreType.DMA,
            pltpu.SemaphoreType.DMA((10,)),
        ],
        compiler_params=pltpu.CompilerParams(
            collective_id=0, has_side_effects=True, vmem_limit_bytes=60 << 20
        ),
        name="forward_all",
    )(unit, vec_placed, tok, seg_col, seg_row)


def to_unit(qkv, proj, up, down):
    def split(weight):
        rows, width = weight.shape
        count = width // 768
        return weight.reshape(rows, count, 2, 384).transpose(1, 2, 0, 3).reshape(count, 48, 384)

    three = split(qkv)
    four = down.reshape(2, 48, 2, 384).transpose(2, 0, 1, 3).reshape(4, 48, 384)
    return jnp.concatenate([three[1:], three[:1], split(proj), split(up), four], axis=0)


def vec_steps(z, y, c, x):
    return [
        [ident(z, y, 1 - c, x)],
        [ident(z, y, c, 1 - x)],
        [ident(z, 1 - y, c, x)],
        [ident((z + k) % Z, y, c, x) for k in range(1, Z)],
    ]


def vec_copies(step, now, got, send, recv, at):
    peers = vec_steps(*at)[step]
    return [
        remote(now.at[step], got.at[step + k], send.at[step + k], recv.at[step + k], peer)
        for k, peer in enumerate(peers)
    ]


def scatter_kernel(
    local_in, vec_in, out, vec_out, local, got_core, got_two, got_one, got_z, vec_now, vec_got, own_sem, send, recv, vsend, vrecv
):
    z, y, c, x = at = place()
    own = pltpu.make_async_copy(local_in, local, own_sem)
    own.start()
    vec_now[0] = vec_in[...]
    greet(*at)

    def core(t):
        return [
            remote(local.at[1 - c, :, :, :, t], got_core.at[t], send.at[t, 0], recv.at[t, 0], ident(z, y, 1 - c, x))
        ]

    def two(t):
        return [
            remote(local.at[c, 1 - y, :, 0:2, t], got_two.at[t, 0], send.at[t, 1], recv.at[t, 1], ident(z, 1 - y, c, x)),
            remote(local.at[c, :, 1 - x, 2:4, t], got_two.at[t, 1], send.at[t, 2], recv.at[t, 2], ident(z, y, c, 1 - x)),
        ]

    def one(t):
        return [
            remote(local.at[c, y, 1 - x, 0:2, t], got_one.at[t, 0], send.at[t, 3], recv.at[t, 3], ident(z, y, c, 1 - x)),
            remote(local.at[c, 1 - y, x, 2:4, t], got_one.at[t, 1], send.at[t, 4], recv.at[t, 4], ident(z, 1 - y, c, x)),
        ]

    def along(t):
        return [
            remote(local.at[c, y, x, (z + k) % Z, t], got_z.at[t, k - 1], send.at[t, 4 + k], recv.at[t, 4 + k], ident((z + k) % Z, y, c, x))
            for k in range(1, Z)
        ]

    def begin(copies):
        for copy in copies:
            copy.start()

    def arrive(copies):
        for copy in copies:
            copy.wait_recv()

    def add(a, b):
        return (a.astype(jnp.float32) + b.astype(jnp.float32)).astype(jnp.bfloat16)

    own.wait()

    def vec_step(step):
        begin(vec_copies(step, vec_now, vec_got, vsend, vrecv, at))

    def vec_sum(step):
        copies = vec_copies(step, vec_now, vec_got, vsend, vrecv, at)
        arrive(copies)
        total = vec_now[step]
        for k in range(len(copies)):
            total = total + vec_got[step + k]
        if step < 3:
            vec_now[step + 1] = total
            vec_step(step + 1)
        else:
            vec_out[...] = total

    vec_step(0)
    for t in range(2):
        begin(core(t))

    def body(i, _):
        @pl.when(i + 2 < NP)
        def _():
            begin(core(i + 2))

        @pl.when(i < NP)
        def _():
            arrive(core(i))
            for a in range(Y):
                for b in range(X):
                    local[c, a, b, :, i] = add(local[c, a, b, :, i], got_core[i, a, b])
            begin(two(i))

        @pl.when(jnp.logical_and(i >= 1, i < NP + 1))
        def _():
            t = i - 1
            arrive(two(t))
            for b in range(X):
                local[c, y, b, 0:2, t] = add(local[c, y, b, 0:2, t], got_two[t, 0, b])
                local[c, b, x, 2:4, t] = add(local[c, b, x, 2:4, t], got_two[t, 1, b])
            begin(one(t))

        @pl.when(jnp.logical_and(i >= 2, i < NP + 2))
        def _():
            t = i - 2
            arrive(one(t))
            for b in range(2):
                local[c, y, x, 2 * b : 2 * b + 2, t] = add(local[c, y, x, 2 * b : 2 * b + 2, t], got_one[t, b])
            begin(along(t))

        @pl.when(i >= 3)
        def _():
            t = i - 3
            arrive(along(t))
            total = local[c, y, x, z, t].astype(jnp.float32)
            for k in range(Z - 1):
                total = total + got_z[t, k].astype(jnp.float32)
            out[t] = total

        for step in range(4):
            @pl.when(i == 2 * step)
            def _():
                vec_sum(step)

        return 0

    lax.fori_loop(0, NP + 3, body, 0)

    def done(t, _):
        for copy in core(t) + two(t) + one(t) + along(t):
            copy.wait_send()
        return 0

    lax.fori_loop(0, NP, done, 0)
    for step in range(4):
        for copy in vec_copies(step, vec_now, vec_got, vsend, vrecv, at):
            copy.wait_send()


def scatter_all(local, vec_local):
    return pl.pallas_call(
        scatter_kernel,
        out_shape=(
            jax.ShapeDtypeStruct((NP,) + PIECE, jnp.float32),
            jax.ShapeDtypeStruct(vec_local.shape, jnp.float32),
        ),
        in_specs=[pl.BlockSpec(memory_space=pl.ANY), pl.BlockSpec(memory_space=pltpu.VMEM)],
        out_specs=(pl.BlockSpec(memory_space=pltpu.VMEM), pl.BlockSpec(memory_space=pltpu.VMEM)),
        scratch_shapes=[
            pltpu.VMEM((C, Y, X, Z, NP) + PIECE, jnp.bfloat16),
            pltpu.VMEM((NP, Y, X, Z) + PIECE, jnp.bfloat16),
            pltpu.VMEM((NP, 2, 2, 2) + PIECE, jnp.bfloat16),
            pltpu.VMEM((NP, 2, 2) + PIECE, jnp.bfloat16),
            pltpu.VMEM((NP, Z - 1) + PIECE, jnp.bfloat16),
            pltpu.VMEM((4,) + vec_local.shape, jnp.float32),
            pltpu.VMEM((6,) + vec_local.shape, jnp.float32),
            pltpu.SemaphoreType.DMA,
            pltpu.SemaphoreType.DMA((NP, 8)),
            pltpu.SemaphoreType.DMA((NP, 8)),
            pltpu.SemaphoreType.DMA((6,)),
            pltpu.SemaphoreType.DMA((6,)),
        ],
        compiler_params=pltpu.CompilerParams(
            collective_id=1, has_side_effects=True, vmem_limit_bytes=56 << 20
        ),
        name="scatter_all",
    )(local, vec_local)


def to_pieces(weight):
    if weight.shape[1] == D and weight.shape[0] != D // (Z * Y * X * C):
        return weight.reshape(2, 48, 2, 384).transpose(0, 2, 1, 3).reshape(4, 48, 384)
    rows, cols = weight.shape
    return weight.reshape(rows, cols // 768, 2, 384).transpose(1, 2, 0, 3).reshape(cols // 768, 48, 384)


def from_pieces(pieces, down):
    if down:
        return pieces.reshape(2, 2, 48, 384).transpose(0, 2, 1, 3).reshape(96, 768)
    count = pieces.shape[0]
    return pieces.reshape(count, 2, 24, 384).transpose(2, 0, 1, 3).reshape(24, count * 768)


def whole_of(full, lo, hi):
    count = hi - lo
    part = full[:, :, :, :, lo:hi].reshape(C, Y, X, Z, count, 2, 24, 384)
    return part.transpose(3, 1, 0, 2, 6, 4, 5, 7).reshape(768, count * 768)


def whole_down(full):
    part = full[:, :, :, :, 8:12].reshape(C, Y, X, Z, 2, 2, 48, 384)
    return part.transpose(3, 1, 0, 2, 4, 6, 5, 7).reshape(3072, 768)


def split_of(grad):
    count = grad.shape[1] // 768
    part = grad.reshape(Z, Y, C, X, 24, count, 2, 384)
    return part.transpose(2, 1, 3, 0, 5, 6, 4, 7).reshape(C, Y, X, Z, count, 48, 384)


def split_down(grad):
    part = grad.reshape(Z, Y, C, X, 2, 48, 2, 384)
    return part.transpose(2, 1, 3, 0, 4, 6, 5, 7).reshape(C, Y, X, Z, 4, 48, 384)


def swap_blk(value):
    return lax.ppermute(value, "blk", [(0, 1), (1, 0)])


def on_device_fast(
    tokens,
    segments,
    cotangent,
    qkv_weight,
    proj_weight,
    up_weight,
    down_weight,
    vec_params,
    qkv_velocity,
    proj_velocity,
    up_velocity,
    down_velocity,
    vec_velocity,
    qkv_average,
    proj_average,
    up_average,
    down_average,
    vec_average,
):
    rows, block = (tokens.shape[0], tokens.shape[1])
    length = segments.shape[1]
    total_tokens = rows * lax.axis_size("dp") * length
    rate = 0.05 / math.sqrt(total_tokens)
    position = lax.axis_index("blk")
    shard = lax.axis_index("dp") * lax.axis_size("blk") + position
    masters = [w.astype(jnp.bfloat16) for w in (qkv_weight, proj_weight, up_weight, down_weight)]
    unit = to_unit(*masters)
    vec_placed = lax.dynamic_update_slice(
        jnp.zeros((16, D), jnp.bfloat16), vec_params.astype(jnp.bfloat16), (0, shard * vec_params.shape[1])
    )
    seg_near = lax.dynamic_slice_in_dim(segments, position * REACH, block + REACH, 1)
    seg_query = lax.dynamic_slice_in_dim(segments, position * block, block, 1)
    seg_col = jnp.broadcast_to(seg_near[0][:, None], (block + REACH, TILE))
    seg_row = jnp.broadcast_to(seg_query, (8, block))
    full, vec_low, out_f, q_f, k_f, v_f, o_f, stat, x2_f, a2_f, z_f, slope_f = forward_all(
        unit, vec_placed, tokens[0], seg_col, seg_row
    )
    order = full.reshape(C, Y, X, Z, NP, 48, 384)
    full = jnp.concatenate([order[:, :, :, :, 2:3], order[:, :, :, :, 0:2], order[:, :, :, :, 3:8], order[:, :, :, :, 8:9], order[:, :, :, :, 10:11], order[:, :, :, :, 9:10], order[:, :, :, :, 11:12]], axis=4)
    w_query, w_proj, w_up = whole_of(full, 0, 3), whole_of(full, 3, 4), whole_of(full, 4, 8)
    w_down = whole_down(full)
    vec = vec_low.astype(jnp.float32)
    inputs = tokens.astype(jnp.float32)
    a_one = layer_norm(inputs, vec[0], vec[1]).astype(jnp.bfloat16)
    query = (q_f * 8).reshape(rows, block, HEADS, HEAD_DIM)
    near = jnp.concatenate([k_f, v_f], axis=1)[None]
    mixed_low = o_f[None]
    second = x2_f[None]
    norm_two_back = jax.vjp(layer_norm, second, vec[5], vec[6])[1]
    a_two = a2_f[None]
    act = z_f[None]
    output = out_f[None]
    out_grad = cotangent.astype(jnp.float32)
    grad_down = contract_tokens(act, cotangent).astype(jnp.bfloat16)
    bias_down_grad = jnp.sum(out_grad, axis=(0, 1))
    act_grad = times_transpose(cotangent, w_down)
    hidden_grad = (act_grad * slope_f[None].astype(jnp.float32)).astype(jnp.bfloat16)
    bias_up_grad = jnp.sum(hidden_grad.astype(jnp.float32), axis=(0, 1))
    grad_up = contract_tokens(a_two, hidden_grad).astype(jnp.bfloat16)
    a_two_grad = times_transpose(hidden_grad, w_up)
    second_part, gain_two_grad, shift_two_grad = norm_two_back(a_two_grad)
    second_grad = out_grad + second_part
    attn_grad = second_grad.astype(jnp.bfloat16)
    bias_proj_grad = jnp.sum(attn_grad.astype(jnp.float32), axis=(0, 1))
    grad_proj = contract_tokens(mixed_low, attn_grad).astype(jnp.bfloat16)
    mixed_grad = (
        times_transpose(attn_grad, w_proj)
        .astype(jnp.bfloat16)
        .reshape(rows, block, HEADS, HEAD_DIM)
    )
    query_grad, kv_terms = attend_back(query, near, mixed_grad, seg_query, seg_near, rows)
    away = swap_blk(
        lax.dynamic_slice_in_dim(kv_terms, (1 - position) * block, REACH, 1).astype(jnp.bfloat16)
    ).astype(jnp.float32)
    kv_own = lax.dynamic_slice_in_dim(kv_terms, position * REACH, block, 1)
    padded = jnp.where(
        position == 0,
        jnp.pad(away, ((0, 0), (block - REACH, 0), (0, 0))),
        jnp.pad(away, ((0, 0), (0, block - REACH), (0, 0))),
    )
    kv_grad = kv_own + padded
    qkv_grad_low = jnp.concatenate([query_grad, kv_grad], axis=-1).astype(jnp.bfloat16)
    qkv_sums = jnp.sum(qkv_grad_low.astype(jnp.float32), axis=(0, 1))
    grad_query = contract_tokens(a_one, qkv_grad_low).astype(jnp.bfloat16)
    a_one_grad = times_transpose(qkv_grad_low, w_query)
    norm_one_back = jax.vjp(layer_norm, inputs, vec[0], vec[1])[1]
    first_part, gain_one_grad, shift_one_grad = norm_one_back(a_one_grad)
    tokens_grad = (second_grad + first_part).astype(jnp.bfloat16)
    vec_local = jnp.concatenate(
        [
            jnp.stack(
                [
                    gain_one_grad,
                    shift_one_grad,
                    qkv_sums[:D],
                    qkv_sums[2 * D :],
                    bias_proj_grad,
                    gain_two_grad,
                    shift_two_grad,
                    bias_down_grad,
                ]
            ),
            bias_up_grad.reshape(4, D),
            jnp.zeros((4, D), jnp.float32),
        ],
        axis=0,
    )
    local = jnp.concatenate(
        [split_of(grad_query), split_of(grad_proj), split_of(grad_up), split_down(grad_down)], axis=4
    )
    pieces, vec_sum = scatter_all(local, vec_local)
    query_share = from_pieces(pieces[0:3], False)
    proj_share = from_pieces(pieces[3:4], False)
    up_share = from_pieces(pieces[4:8], False)
    down_share = from_pieces(pieces[8:12], True)
    vec_share = lax.dynamic_slice(
        vec_sum, (0, shard * vec_params.shape[1]), vec_params.shape
    )
    qkv_new = update(qkv_weight, query_share, qkv_velocity, qkv_average, rate)
    proj_new = update(proj_weight, proj_share, proj_velocity, proj_average, rate)
    up_new = update(up_weight, up_share, up_velocity, up_average, rate)
    down_new = update(down_weight, down_share, down_velocity, down_average, rate)
    vec_new = update(vec_params, vec_share, vec_velocity, vec_average, rate)
    return (
        output,
        tokens_grad,
        query_share,
        proj_share,
        up_share,
        down_share,
        vec_share,
        qkv_new[0],
        proj_new[0],
        up_new[0],
        down_new[0],
        vec_new[0],
        qkv_new[1],
        proj_new[1],
        up_new[1],
        down_new[1],
        vec_new[1],
        qkv_new[2],
        proj_new[2],
        up_new[2],
        down_new[2],
        vec_new[2],
        qkv_new[0].astype(jnp.bfloat16),
        proj_new[0].astype(jnp.bfloat16),
        up_new[0].astype(jnp.bfloat16),
        down_new[0].astype(jnp.bfloat16),
        vec_new[0].astype(jnp.bfloat16),
    )


def solution(mesh):
    fits = mesh.shape["dp"] == Z * Y * C and mesh.shape["blk"] == X
    return jax.shard_map(
        on_device_fast if fits else on_device,
        mesh=mesh,
        in_specs=(
            P("dp", "blk", None),
            P("dp", None),
            P("dp", "blk", None),
            P(("dp", "blk"), None),
            P(("dp", "blk"), None),
            P(("dp", "blk"), None),
            P(("dp", "blk"), None),
            P(None, ("dp", "blk")),
            P(("dp", "blk"), None),
            P(("dp", "blk"), None),
            P(("dp", "blk"), None),
            P(("dp", "blk"), None),
            P(None, ("dp", "blk")),
            P(("dp", "blk"), None),
            P(("dp", "blk"), None),
            P(("dp", "blk"), None),
            P(("dp", "blk"), None),
            P(None, ("dp", "blk")),
        ),
        out_specs=(
            P("dp", "blk", None),
            P("dp", "blk", None),
            P(("dp", "blk"), None),
            P(("dp", "blk"), None),
            P(("dp", "blk"), None),
            P(("dp", "blk"), None),
            P(None, ("dp", "blk")),
            P(("dp", "blk"), None),
            P(("dp", "blk"), None),
            P(("dp", "blk"), None),
            P(("dp", "blk"), None),
            P(None, ("dp", "blk")),
            P(("dp", "blk"), None),
            P(("dp", "blk"), None),
            P(("dp", "blk"), None),
            P(("dp", "blk"), None),
            P(None, ("dp", "blk")),
            P(("dp", "blk"), None),
            P(("dp", "blk"), None),
            P(("dp", "blk"), None),
            P(("dp", "blk"), None),
            P(None, ("dp", "blk")),
            P(("dp", "blk"), None),
            P(("dp", "blk"), None),
            P(("dp", "blk"), None),
            P(("dp", "blk"), None),
            P(None, ("dp", "blk")),
        ),
        check_vma=False,
    )
```

```python
import math

import jax
import jax.numpy as jnp
from jax import lax
from jax.experimental import pallas as pl
from jax.experimental.pallas import tpu as pltpu
from jax.sharding import PartitionSpec as P

D = 768
HEADS = 12
HEAD_DIM = 64


def layer_norm(value, gain, shift):
    mean = jnp.mean(value, axis=-1, keepdims=True)
    cent = value - mean
    var = jnp.mean(cent * cent, axis=-1, keepdims=True)
    return cent * lax.rsqrt(var + 1e-06) * (1.0 + gain) + shift


def gelu_exact(value):
    return jax.nn.gelu(value, approximate=False)


def contract_tokens(left, right):
    return lax.dot_general(
        left.reshape(-1, left.shape[-1]),
        right.reshape(-1, right.shape[-1]),
        (((0,), (0,)), ((), ())),
        preferred_element_type=jnp.float32,
    )


def times_transpose(left, weight):
    return lax.dot_general(
        left, weight, (((left.ndim - 1,), (1,)), ((), ())), preferred_element_type=jnp.float32
    )


def group_size(rows, block):
    limit = max(1, 512 // block)
    best = 1
    for cand in range(1, rows + 1):
        if rows % cand == 0 and cand <= limit:
            best = cand
    return best


def scores_of(query, keys, seg_query, seg_keys):
    scores = jnp.einsum(
        "gqhd,gkhd->ghqk", query, keys, preferred_element_type=jnp.float32
    ) * HEAD_DIM ** (-0.5)
    allowed = (seg_query[:, :, None] == seg_keys[:, None, :])[:, None]
    return (scores, allowed)


def attend_back(query, kv_all, grad_out, seg_query, segments, group):
    rows, block = (query.shape[0], query.shape[1])
    length = kv_all.shape[1]
    keys = kv_all[0:group, :, :D].reshape(group, length, HEADS, HEAD_DIM)
    values = kv_all[0:group, :, D:].reshape(group, length, HEADS, HEAD_DIM)
    scores, allowed = scores_of(query, keys, seg_query, segments)
    probs = jax.nn.softmax(jnp.where(allowed, scores, -1e30), axis=-1)
    probs_low = probs.astype(jnp.bfloat16)
    prob_grad = jnp.einsum("gqhd,gkhd->ghqk", grad_out, values, preferred_element_type=jnp.float32)
    score_grad = probs * (prob_grad - jnp.sum(probs * prob_grad, axis=-1, keepdims=True))
    score_low = score_grad.astype(jnp.bfloat16)
    dq_part = jnp.einsum(
        "ghqk,gkhd->gqhd", score_low, keys, preferred_element_type=jnp.float32
    ) * HEAD_DIM ** (-0.5)
    dk_part = jnp.einsum(
        "ghqk,gqhd->gkhd", score_low, query, preferred_element_type=jnp.float32
    ) * HEAD_DIM ** (-0.5)
    dv_part = jnp.einsum("ghqk,gqhd->gkhd", probs_low, grad_out, preferred_element_type=jnp.float32)
    dq_parts = dq_part.reshape(group, block, D)
    dkv_parts = jnp.concatenate(
        [dk_part.reshape(group, length, D), dv_part.reshape(group, length, D)], axis=-1
    )
    return (dq_parts, dkv_parts)


def update(weight, grad, velocity, average, rate):
    step_value = grad + 0.0005 * weight
    velocity_new = 0.9 * velocity + step_value
    weight_new = weight - rate * (step_value + 0.9 * velocity_new)
    average_new = 0.9 * average + 0.1 * weight_new
    return (weight_new, velocity_new, average_new)


def on_device(
    tokens,
    segments,
    cotangent,
    qkv_weight,
    proj_weight,
    up_weight,
    down_weight,
    vec_params,
    qkv_velocity,
    proj_velocity,
    up_velocity,
    down_velocity,
    vec_velocity,
    qkv_average,
    proj_average,
    up_average,
    down_average,
    vec_average,
):
    rows, block = (tokens.shape[0], tokens.shape[1])
    length = segments.shape[1]
    total_tokens = rows * lax.axis_size("dp") * length
    rate = 0.05 / math.sqrt(total_tokens)
    group = group_size(rows, block)
    gathered = (
        lax.all_gather(qkv_weight.astype(jnp.bfloat16), ("dp", "blk"), axis=0, tiled=True),
        lax.all_gather(proj_weight.astype(jnp.bfloat16), ("dp", "blk"), axis=0, tiled=True),
        lax.all_gather(up_weight.astype(jnp.bfloat16), ("dp", "blk"), axis=0, tiled=True),
        lax.all_gather(down_weight.astype(jnp.bfloat16), ("dp", "blk"), axis=0, tiled=True),
        lax.all_gather(vec_params.astype(jnp.bfloat16), ("dp", "blk"), axis=1, tiled=True),
    )
    w_query, w_proj, w_up, w_down, vec_low = gathered
    vec = vec_low.astype(jnp.float32)
    bias_up = vec[8:12].reshape(-1)
    position = lax.axis_index("blk")
    seg_query = lax.dynamic_slice_in_dim(segments, position * block, block, 1)
    inputs = tokens.astype(jnp.float32)
    a_one = layer_norm(inputs, vec[0], vec[1]).astype(jnp.bfloat16)
    zero_bias = jnp.zeros_like(vec[2])
    pre = jnp.dot(a_one, w_query, preferred_element_type=jnp.float32) + jnp.concatenate(
        [vec[2], zero_bias, vec[3]]
    )
    qkv = pre.astype(jnp.bfloat16)
    query = qkv[..., :D].reshape(rows, block, HEADS, HEAD_DIM)
    key_value = qkv[..., D:]
    piece = lax.all_gather(key_value, "blk", axis=1, tiled=True)
    top = jnp.full((rows, HEADS, block), -1e30, jnp.float32)
    count = piece.shape[1]
    keys = piece[0:group, :, :D].reshape(group, count, HEADS, HEAD_DIM)
    values = piece[0:group, :, D:].reshape(group, count, HEADS, HEAD_DIM)
    scores, allowed = scores_of(query, keys, seg_query, segments)
    scores = jnp.where(allowed, scores, -1e30)
    new_top = jnp.maximum(top, jnp.max(scores, axis=-1))
    weights = jnp.where(allowed, jnp.exp(scores - new_top[..., None]), 0.0)
    denoms = jnp.sum(weights, axis=-1)
    added = jnp.einsum(
        "ghqk,gkhd->gqhd", weights.astype(jnp.bfloat16), values, preferred_element_type=jnp.float32
    )
    mixed = (added / jnp.transpose(denoms, (0, 2, 1))[..., None]).reshape(rows, block, D)
    mixed_low = mixed.astype(jnp.bfloat16)
    second = inputs + jnp.dot(mixed_low, w_proj, preferred_element_type=jnp.float32) + vec[4]
    second_norm, norm_two_back = jax.vjp(layer_norm, second, vec[5], vec[6])
    a_two = second_norm.astype(jnp.bfloat16)
    hidden = jnp.dot(a_two, w_up, preferred_element_type=jnp.float32) + bias_up
    act_value, gelu_back = jax.vjp(gelu_exact, hidden)
    act = act_value.astype(jnp.bfloat16)
    result = second + jnp.dot(act, w_down, preferred_element_type=jnp.float32) + vec[7]
    output = result.astype(jnp.bfloat16)
    out_grad = cotangent.astype(jnp.float32)
    grad_down = contract_tokens(act, cotangent)
    bias_down_grad = jnp.sum(out_grad, axis=(0, 1))
    act_grad = times_transpose(cotangent, w_down)
    hidden_grad = gelu_back(act_grad)[0].astype(jnp.bfloat16)
    bias_up_grad = jnp.sum(hidden_grad.astype(jnp.float32), axis=(0, 1))
    grad_up = contract_tokens(a_two, hidden_grad)
    a_two_grad = times_transpose(hidden_grad, w_up)
    second_part, gain_two_grad, shift_two_grad = norm_two_back(a_two_grad)
    second_grad = out_grad + second_part
    attn_grad = second_grad.astype(jnp.bfloat16)
    bias_proj_grad = jnp.sum(attn_grad.astype(jnp.float32), axis=(0, 1))
    grad_proj = contract_tokens(mixed_low, attn_grad)
    mixed_grad = (
        times_transpose(attn_grad, w_proj)
        .astype(jnp.bfloat16)
        .reshape(rows, block, HEADS, HEAD_DIM)
    )
    kv_again = lax.all_gather(key_value, "blk", axis=1, tiled=True)
    query_grad, kv_terms = attend_back(query, kv_again, mixed_grad, seg_query, segments, group)
    kv_grad = lax.psum_scatter(
        kv_terms.astype(jnp.bfloat16), "blk", scatter_dimension=1, tiled=True
    ).astype(jnp.float32)
    qkv_grad_low = jnp.concatenate([query_grad, kv_grad], axis=-1).astype(jnp.bfloat16)
    qkv_sums = jnp.sum(qkv_grad_low.astype(jnp.float32), axis=(0, 1))
    grad_query = contract_tokens(a_one, qkv_grad_low)
    a_one_grad = times_transpose(qkv_grad_low, w_query)
    norm_one_back = jax.vjp(layer_norm, inputs, vec[0], vec[1])[1]
    first_part, gain_one_grad, shift_one_grad = norm_one_back(a_one_grad)
    tokens_grad = (second_grad + first_part).astype(jnp.bfloat16)
    vec_local = jnp.concatenate(
        [
            jnp.stack(
                [
                    gain_one_grad,
                    shift_one_grad,
                    qkv_sums[:D],
                    qkv_sums[2 * D :],
                    bias_proj_grad,
                    gain_two_grad,
                    shift_two_grad,
                    bias_down_grad,
                ]
            ),
            bias_up_grad.reshape(4, D),
        ],
        axis=0,
    )
    query_share, proj_share, up_share, down_share, vec_share = (
        lax.psum_scatter(grad_query, ("dp", "blk"), scatter_dimension=0, tiled=True),
        lax.psum_scatter(grad_proj, ("dp", "blk"), scatter_dimension=0, tiled=True),
        lax.psum_scatter(grad_up, ("dp", "blk"), scatter_dimension=0, tiled=True),
        lax.psum_scatter(grad_down, ("dp", "blk"), scatter_dimension=0, tiled=True),
        lax.psum_scatter(vec_local, ("dp", "blk"), scatter_dimension=1, tiled=True),
    )
    qkv_new = update(qkv_weight, query_share, qkv_velocity, qkv_average, rate)
    proj_new = update(proj_weight, proj_share, proj_velocity, proj_average, rate)
    up_new = update(up_weight, up_share, up_velocity, up_average, rate)
    down_new = update(down_weight, down_share, down_velocity, down_average, rate)
    vec_new = update(vec_params, vec_share, vec_velocity, vec_average, rate)
    return (
        output,
        tokens_grad,
        query_share,
        proj_share,
        up_share,
        down_share,
        vec_share,
        qkv_new[0],
        proj_new[0],
        up_new[0],
        down_new[0],
        vec_new[0],
        qkv_new[1],
        proj_new[1],
        up_new[1],
        down_new[1],
        vec_new[1],
        qkv_new[2],
        proj_new[2],
        up_new[2],
        down_new[2],
        vec_new[2],
        qkv_new[0].astype(jnp.bfloat16),
        proj_new[0].astype(jnp.bfloat16),
        up_new[0].astype(jnp.bfloat16),
        down_new[0].astype(jnp.bfloat16),
        vec_new[0].astype(jnp.bfloat16),
    )


PIECE = (48, 384)
NP = 12
Z, Y, X, C = 4, 2, 2, 2
AHEAD = 2
REACH = 256
TILE = 128
SPAN = TILE + 2 * REACH
PAIRS = HEADS // 2
MESH = pl.DeviceIdType.MESH
F32, BF16 = jnp.float32, jnp.bfloat16
NT = (((1,), (1,)), ((), ()))
TN = (((0,), (0,)), ((), ()))


def place():
    d, x = lax.axis_index("dp"), lax.axis_index("blk")
    return d // (2 * Y), (d // 2) % Y, d % 2, x


def ident(z, y, c, x):
    return ((z * Y + y) * 2 + c, x)


def greet(z, y, c, x):
    barrier = pltpu.get_barrier_semaphore()
    peers = [ident((z + k) % Z, y, c, x) for k in range(1, Z)]
    peers += [ident(z, 1 - y, c, x), ident(z, y, c, 1 - x), ident(z, y, 1 - c, x)]
    for peer in peers:
        pl.semaphore_signal(barrier, inc=1, device_id=peer, device_id_type=MESH)
    pl.semaphore_wait(barrier, len(peers))


def remote(src, dst, send, recv, peer):
    return pltpu.make_async_remote_copy(
        src_ref=src, dst_ref=dst, send_sem=send, recv_sem=recv, device_id=peer, device_id_type=MESH
    )


def begin(copies):
    for copy in copies:
        copy.start()


def arrive(copies):
    for copy in copies:
        copy.wait_recv()


def within(index, low, high, run):
    if isinstance(index, int):
        if low <= index < high:
            run()
    else:
        pl.when(jnp.logical_and(index >= low, index < high))(run)


def loop(count, body):
    def step(i, carry):
        body(i)
        return carry

    lax.fori_loop(0, count, step, 0)


def cols(j, width):
    return pl.ds(pl.multiple_of(j * width, width), width)


def dot(a, b, dims=None):
    dims = (((1,), (0,)), ((), ())) if dims is None else dims
    return lax.dot_general(a, b, dims, preferred_element_type=F32)


class Vec:
    def __init__(self, at, now, got, send, recv):
        self.at, self.now, self.got, self.send, self.recv = at, now, got, send, recv

    def copies(self, step):
        z, y, c, x = self.at
        peers = [
            [ident(z, y, 1 - c, x)],
            [ident(z, y, c, 1 - x)],
            [ident(z, 1 - y, c, x)],
            [ident((z + k) % Z, y, c, x) for k in range(1, Z)],
        ][step]
        return [
            remote(self.now.at[step], self.got.at[step + k], self.send.at[step + k], self.recv.at[step + k], peer)
            for k, peer in enumerate(peers)
        ]

    def begin(self, step):
        begin(self.copies(step))

    def total(self, step):
        copies = self.copies(step)
        arrive(copies)
        total = self.now[step]
        for k in range(len(copies)):
            total = total + self.got[step + k]
        return total

    def sent(self):
        for step in range(4):
            for copy in self.copies(step):
                copy.wait_send()


def normal(value):
    mean = jnp.mean(value, axis=-1, keepdims=True)
    cent = value - mean
    var = jnp.mean(cent * cent, axis=-1, keepdims=True)
    scale = lax.rsqrt(var + 1e-06)
    return cent * scale, scale


def window(tile, x):
    first = jnp.where(x == 0, jnp.maximum(tile - 2, 0), jnp.minimum(tile, 1))
    return pl.ds(pl.multiple_of(first * TILE, TILE), SPAN)


def mask_fill(seg_col, seg_row, bias, x, tiles):
    def one(tile):
        column = seg_col[window(tile, x), :]
        row = seg_row[0:1, cols(tile, TILE)]
        bias[tile] = jnp.where(column == row, 0.0, -1e30).astype(F32)

    loop(tiles, one)


def split_heads(pair_block):
    lane = lax.broadcasted_iota(jnp.int32, pair_block.shape, 1)
    zero = jnp.zeros_like(pair_block)
    return jnp.concatenate(
        [jnp.where(lane < HEAD_DIM, pair_block, zero), jnp.where(lane < HEAD_DIM, zero, pair_block)], axis=0
    )


def join_heads(both):
    own = jnp.concatenate([both[:HEAD_DIM, :TILE], both[HEAD_DIM:, TILE:]], axis=0)
    return jnp.transpose(own)


def rows_from_stage(stage, target, col):
    def group(g):
        parts = [stage[c, g % Y, x, g // Y].astype(F32) for c in range(C) for x in range(X)]
        rows = pl.ds(pl.multiple_of(g * 96, 96), 96)
        target[rows, col : col + 384] = jnp.concatenate([p[:24] for p in parts], axis=0).astype(BF16)
        target[rows, col + 384 : col + 768] = jnp.concatenate([p[24:] for p in parts], axis=0).astype(BF16)

    loop(Z * Y, group)


def down_from_stage(stage, target, half, col):
    def group(g):
        for c in range(C):
            for x in range(X):
                start = pl.multiple_of(g * 384 + (c * X + x) * 96 + half * 48, 16)
                target[pl.ds(start, 48), col * 384 : col * 384 + 384] = stage[c, g % Y, x, g // Y]

    loop(Z * Y, group)


class Gather:
    def __init__(self, at, unit, full, own, send, recv):
        self.at, self.unit, self.full, self.own, self.send, self.recv = at, unit, full, own, send, recv

    def mine(self, t):
        z, y, c, x = self.at
        return pltpu.make_async_copy(self.unit.at[t], self.full.at[c, y, x, z, t], self.own.at[t])

    def first(self, t):
        z, y, c, x = self.at
        return [
            remote(
                self.unit.at[t], self.full.at[c, y, x, z, t], self.send.at[t, k - 1], self.recv.at[t, k - 1],
                ident((z + k) % Z, y, c, x),
            )
            for k in range(1, Z)
        ]

    def second(self, t):
        z, y, c, x = self.at
        low, high = self.full.at[c, y, x, 0:2, t], self.full.at[c, y, x, 2:4, t]
        return [
            remote(low, low, self.send.at[t, 3], self.recv.at[t, 3], ident(z, y, c, 1 - x)),
            remote(high, high, self.send.at[t, 4], self.recv.at[t, 4], ident(z, 1 - y, c, x)),
        ]

    def third(self, t):
        z, y, c, x = self.at
        low, high = self.full.at[c, y, :, 0:2, t], self.full.at[c, :, x, 2:4, t]
        return [
            remote(low, low, self.send.at[t, 5], self.recv.at[t, 5], ident(z, 1 - y, c, x)),
            remote(high, high, self.send.at[t, 6], self.recv.at[t, 6], ident(z, y, c, 1 - x)),
        ]

    def last(self, t):
        z, y, c, x = self.at
        block = self.full.at[c, :, :, :, t]
        return [remote(block, block, self.send.at[t, 7], self.recv.at[t, 7], ident(z, y, 1 - c, x))]

    def start(self):
        loop(NP, lambda t: self.mine(t).start())
        loop(AHEAD, lambda t: begin(self.first(t)))

    def progress(self, i):
        def to_second():
            self.mine(i).wait()
            arrive(self.first(i))
            begin(self.second(i))

        def to_third():
            arrive(self.second(i - 1))
            begin(self.third(i - 1))

        def to_last():
            arrive(self.third(i - 2))
            begin(self.last(i - 2))

        within(i, 0, NP, to_second)
        within(i, 1, NP + 1, to_third)
        within(i, 2, NP + 2, to_last)
        within(i, 0, NP - AHEAD, lambda: begin(self.first(i + AHEAD)))

    def sent(self):
        def one(t):
            for copy in self.first(t) + self.second(t) + self.third(t) + self.last(t):
                copy.wait_send()

        loop(NP, one)


def forward_kernel(
    unit, vec_in, tok, seg_col, seg_row,
    full, vec_out, out_o, q_o, k_o, v_o, o_o, stat_o, x2_o, a2_o, z_o, slope_o,
    near, a1, wbig, wdown, stage, vecf, bias, out_s, q_s, k_s, v_s, o_s, stat_s, x2_s, a2_s, z_s, slope_s,
    vec_now, vec_got, own, send, recv, vsend, vrecv, hsem, ssem, osem,
):
    z, y, c, x = at = place()
    block = tok.shape[0]
    tiles = block // TILE
    offset = pl.multiple_of(x * REACH, REACH)
    vec_now[0] = vec_in[...]
    greet(*at)
    gather = Gather(at, unit, full, own, send, recv)
    gather.start()
    vec = Vec(at, vec_now, vec_got, vsend, vrecv)
    vec.begin(0)
    away = pl.multiple_of((1 - x) * REACH, REACH)
    land = pl.multiple_of(x * block, REACH)
    halo = remote(
        tok.at[pl.ds(away, REACH)], near.at[pl.ds(land, REACH)], hsem.at[0], hsem.at[1], ident(z, y, c, 1 - x)
    )
    halo.start()
    near[pl.ds(offset, block), :] = tok[...]

    def put(k, src, dst):
        return pltpu.make_async_copy(src, dst, osem.at[k])

    def vec_step(step):
        total = vec.total(step)
        if step < 3:
            vec_now[step + 1] = total
            vec.begin(step + 1)
        else:
            vec_out[...] = total
            vecf[...] = total.astype(F32)

    def load(t):
        arrive(gather.last(t))
        copy = pltpu.make_async_copy(full.at[:, :, :, :, t], stage, ssem)
        copy.start()
        copy.wait()

    vec_step(0)
    vec_step(1)
    gather.progress(0)
    vec_step(2)
    vec_step(3)
    gather.progress(1)
    halo.wait_recv()

    def norm_one(i):
        rows = pl.ds(pl.multiple_of(i * 256, 256), 256)
        value = normal(near[rows, :].astype(F32))[0]
        a1[rows, :] = (value * (1.0 + vecf[0:1, :]) + vecf[1:2, :]).astype(BF16)

    loop(near.shape[0] // 256, norm_one)
    mask_fill(seg_col, seg_row, bias, x, tiles)
    gather.progress(2)
    gather.progress(3)
    load(0)
    rows_from_stage(stage, wbig, D)

    def keys(j):
        k_s[:, cols(j, 256)] = dot(a1[...], wbig[:, pl.ds(pl.multiple_of(D + j * 256, 256), 256)]).astype(BF16)

    loop(3, keys)
    gather.progress(4)
    load(1)
    rows_from_stage(stage, wbig, 2 * D)

    def values(j):
        value = dot(a1[...], wbig[:, pl.ds(pl.multiple_of(2 * D + j * 256, 256), 256)])
        v_s[:, cols(j, 256)] = (value + vecf[3:4, cols(j, 256)]).astype(BF16)

    loop(3, values)
    load(2)
    rows_from_stage(stage, wbig, 0)

    def queries(j):
        value = dot(a1[pl.ds(offset, block), :], wbig[:, cols(j, 256)]) + vecf[2:3, cols(j, 256)]
        q_s[:, cols(j, 256)] = value.astype(BF16) * HEAD_DIM ** (-0.5)

    loop(3, queries)
    put(0, k_s, k_o).start()
    put(1, v_s, v_o).start()
    put(2, q_s, q_o).start()

    def attend(pair):
        gather.progress(pair + 5)
        lanes = cols(pair, 128)

        def one(tile):
            rows = cols(tile, TILE)
            span = window(tile, x)
            both = split_heads(q_s[rows, lanes])
            fill = bias[tile]
            scores = dot(k_s[span, lanes], both, NT) + jnp.concatenate([fill, fill], axis=1)
            top = jnp.max(scores, axis=0, keepdims=True)
            weights = jnp.exp(scores - top)
            total = jnp.sum(weights, axis=0, keepdims=True)
            mixed = dot(v_s[span, lanes], weights.astype(BF16), TN) / total
            o_s[rows, lanes] = join_heads(mixed).astype(BF16)
            stat_s[pair * tiles + tile] = jnp.broadcast_to(top + jnp.log(total), (8, 2 * TILE))

        loop(tiles, one)

    loop(PAIRS, attend)
    put(3, o_s, o_o).start()
    put(4, stat_s, stat_o).start()
    load(3)
    rows_from_stage(stage, wbig, 3 * D)

    def project(j):
        value = dot(o_s[...], wbig[:, pl.ds(pl.multiple_of(3 * D + j * 256, 256), 256)])
        x2_s[:, cols(j, 256)] = tok[:, cols(j, 256)].astype(F32) + value + vecf[4:5, cols(j, 256)]

    loop(3, project)

    def norm_two(i):
        rows = pl.ds(pl.multiple_of(i * 256, 256), 256)
        value = normal(x2_s[rows, :])[0]
        a2_s[rows, :] = (value * (1.0 + vecf[5:6, :]) + vecf[6:7, :]).astype(BF16)

    loop(block // 256, norm_two)
    put(5, x2_s, x2_o).start()
    put(6, a2_s, a2_o).start()
    gather.progress(11)

    def expand(j):
        col = pl.multiple_of(j * 256, 256)
        u = dot(a2_s[...], wbig[:, pl.ds(pl.multiple_of(4 * D + col, 256), 256)])
        u = u + vecf[pl.ds(8 + j // 3, 1), pl.ds(pl.multiple_of((j % 3) * 256, 256), 256)]
        half = 0.5 + 0.5 * lax.erf(u * math.sqrt(0.5))
        z_s[:, cols(j, 256)] = (u * half).astype(BF16)
        slope = half + u * (jnp.exp(-0.5 * u * u) * (1.0 / math.sqrt(2.0 * math.pi)))
        slope_s[:, cols(j, 256)] = slope.astype(BF16)

    for t in range(4):
        load(4 + t)
        rows_from_stage(stage, wbig, (4 + t) * D)
        loop(3, lambda j: expand(j + 3 * t))
        if t == 1:
            gather.progress(12)
    put(7, z_s, z_o).start()
    put(8, slope_s, slope_o).start()
    gather.progress(13)
    for t in range(4):
        load(8 + t)
        down_from_stage(stage, wdown, t % 2, t // 2)
        if t % 2 == 1:
            col = slice(t // 2 * 384, t // 2 * 384 + 384)
            value = dot(z_s[...], wdown[:, col])
            out_s[:, col] = (x2_s[:, col] + value + vecf[7:8, col]).astype(BF16)
    put(9, out_s, out_o).start()
    pairs = [(k_s, k_o), (v_s, v_o), (q_s, q_o), (o_s, o_o), (stat_s, stat_o), (x2_s, x2_o), (a2_s, a2_o)]
    for k, (src, dst) in enumerate(pairs + [(z_s, z_o), (slope_s, slope_o), (out_s, out_o)]):
        put(k, src, dst).wait()
    gather.sent()
    vec.sent()
    halo.wait_send()


def forward_all(unit, vec_placed, tok, seg_col, seg_row):
    block, near = tok.shape[0], seg_col.shape[0]
    ff = 4 * D
    tiles = block // TILE
    shapes = [
        ((block, D), BF16),
        ((block, D), BF16),
        ((near, D), BF16),
        ((near, D), BF16),
        ((block, D), BF16),
        ((PAIRS * tiles, 8, 2 * TILE), F32),
        ((block, D), F32),
        ((block, D), BF16),
        ((block, ff), BF16),
        ((block, ff), BF16),
    ]
    hbm, vmem = pl.BlockSpec(memory_space=pl.ANY), pl.BlockSpec(memory_space=pltpu.VMEM)
    outs = [((C, Y, X, Z, NP) + PIECE, BF16), (vec_placed.shape, BF16)] + shapes
    return pl.pallas_call(
        forward_kernel,
        out_shape=tuple(jax.ShapeDtypeStruct(*one) for one in outs),
        in_specs=[vmem] * 5,
        out_specs=tuple([hbm, vmem] + [hbm] * len(shapes)),
        scratch_shapes=[
            pltpu.VMEM((near, D), BF16),
            pltpu.VMEM((near, D), BF16),
            pltpu.VMEM((D, 8 * D), BF16),
            pltpu.VMEM((ff, D), BF16),
            pltpu.VMEM((C, Y, X, Z) + PIECE, BF16),
            pltpu.VMEM(vec_placed.shape, F32),
            pltpu.VMEM((tiles, SPAN, TILE), F32),
            *[pltpu.VMEM(*one) for one in shapes],
            pltpu.VMEM((4,) + vec_placed.shape, BF16),
            pltpu.VMEM((6,) + vec_placed.shape, BF16),
            pltpu.SemaphoreType.DMA((NP,)),
            pltpu.SemaphoreType.DMA((NP, 8)),
            pltpu.SemaphoreType.DMA((NP, 8)),
            pltpu.SemaphoreType.DMA((6,)),
            pltpu.SemaphoreType.DMA((6,)),
            pltpu.SemaphoreType.DMA((2,)),
            pltpu.SemaphoreType.DMA,
            pltpu.SemaphoreType.DMA((10,)),
        ],
        compiler_params=pltpu.CompilerParams(
            collective_id=0, has_side_effects=True, vmem_limit_bytes=60 << 20
        ),
        name="forward_all",
    )(unit, vec_placed, tok, seg_col, seg_row)


def to_unit(qkv, proj, up, down):
    def split(weight):
        rows, width = weight.shape
        count = width // 768
        return weight.reshape(rows, count, 2, 384).transpose(1, 2, 0, 3).reshape(count, 48, 384)

    three = split(qkv)
    four = down.reshape(2, 48, 2, 384).transpose(2, 0, 1, 3).reshape(4, 48, 384)
    return jnp.concatenate([three[1:], three[:1], split(proj), split(up), four], axis=0)


class Scatter:
    def __init__(self, at, local, got_core, got_two, got_one, got_z, out, send, recv):
        self.at, self.local, self.out, self.send, self.recv = at, local, out, send, recv
        self.got = got_core, got_two, got_one, got_z

    def core(self, t):
        z, y, c, x = self.at
        peer = ident(z, y, 1 - c, x)
        return [remote(self.local.at[1 - c, :, :, :, t], self.got[0].at[t], self.send.at[t, 0], self.recv.at[t, 0], peer)]

    def two(self, t):
        z, y, c, x = self.at
        low, high = self.local.at[c, 1 - y, :, 0:2, t], self.local.at[c, :, 1 - x, 2:4, t]
        return [
            remote(low, self.got[1].at[t, 0], self.send.at[t, 1], self.recv.at[t, 1], ident(z, 1 - y, c, x)),
            remote(high, self.got[1].at[t, 1], self.send.at[t, 2], self.recv.at[t, 2], ident(z, y, c, 1 - x)),
        ]

    def one(self, t):
        z, y, c, x = self.at
        low, high = self.local.at[c, y, 1 - x, 0:2, t], self.local.at[c, 1 - y, x, 2:4, t]
        return [
            remote(low, self.got[2].at[t, 0], self.send.at[t, 3], self.recv.at[t, 3], ident(z, y, c, 1 - x)),
            remote(high, self.got[2].at[t, 1], self.send.at[t, 4], self.recv.at[t, 4], ident(z, 1 - y, c, x)),
        ]

    def along(self, t):
        z, y, c, x = self.at
        return [
            remote(
                self.local.at[c, y, x, (z + k) % Z, t], self.got[3].at[t, k - 1], self.send.at[t, 4 + k],
                self.recv.at[t, 4 + k], ident((z + k) % Z, y, c, x),
            )
            for k in range(1, Z)
        ]

    def add(self, where, value):
        self.local[where] = (self.local[where].astype(F32) + value.astype(F32)).astype(BF16)

    def after_core(self, t):
        c = self.at[2]
        arrive(self.core(t))
        for a in range(Y):
            for b in range(X):
                self.add((c, a, b, slice(None), t), self.got[0][t, a, b])
        begin(self.two(t))

    def after_two(self, t):
        z, y, c, x = self.at
        arrive(self.two(t))
        for b in range(2):
            self.add((c, y, b, slice(0, 2), t), self.got[1][t, 0, b])
            self.add((c, b, x, slice(2, 4), t), self.got[1][t, 1, b])
        begin(self.one(t))

    def after_one(self, t):
        z, y, c, x = self.at
        arrive(self.one(t))
        for b in range(2):
            self.add((c, y, x, slice(2 * b, 2 * b + 2), t), self.got[2][t, b])
        begin(self.along(t))

    def after_z(self, t):
        z, y, c, x = self.at
        arrive(self.along(t))
        total = self.local[c, y, x, z, t].astype(F32)
        for k in range(Z - 1):
            total = total + self.got[3][t, k].astype(F32)
        self.out[t] = total

    def progress(self, i):
        within(i, 0, NP, lambda: self.after_core(i))
        within(i, 1, NP + 1, lambda: self.after_two(i - 1))
        within(i, 2, NP + 2, lambda: self.after_one(i - 2))
        within(i, 3, NP + 3, lambda: self.after_z(i - 3))

    def sent(self):
        def each(t):
            for copy in self.core(t) + self.two(t) + self.one(t) + self.along(t):
                copy.wait_send()

        loop(NP, each)


def total_rows(value):
    return jnp.sum(value.astype(F32), axis=0, keepdims=True)


def norm_back(value, grad, gain):
    unit_value, scale = normal(value)
    inner = grad * (1.0 + gain)
    mean_one = jnp.mean(inner, axis=-1, keepdims=True)
    mean_two = jnp.mean(inner * unit_value, axis=-1, keepdims=True)
    back = scale * (inner - mean_one - unit_value * mean_two)
    return back, total_rows(grad * unit_value), total_rows(grad)


def backward_kernel(
    full, vec_in, tok_o, dy_o, seg_col, seg_row, q_o, k_o, v_o, o_o, stat_o, x2_o, a2_o, z_o, slope_o,
    out, vec_out, tok_grad,
    local, got_core, got_two, got_one, got_z, wbuf, stage, bias, vecf, tok, dy, q_s, k_s, v_s, o_s, stat_s, x2_s, a2_s, z_s,
    slope_s, dx, da, acc_k, acc_v, halo_s, halo_r, vec_now, vec_got, send, recv, vsend, vrecv, hsend, hrecv, isem, ssem,
):
    z, y, c, x = at = place()
    block = tok.shape[0]
    tiles = block // TILE
    offset = pl.multiple_of(x * REACH, REACH)
    away = pl.multiple_of((1 - x) * REACH, REACH)
    outside = pl.multiple_of((1 - x) * block, REACH)
    order = [8, 9, 10, 11, 4, 5, 6, 7, 3, 2, 0, 1]

    def fetch(n):
        return pltpu.make_async_copy(full.at[:, :, :, :, order[n]], stage.at[n % 2], ssem.at[n % 2])

    def take(n, use):
        fetch(n).wait()
        use(stage.at[n % 2])
        if n + 2 < NP:
            fetch(n + 2).start()

    pairs = [
        (z_o, z_s), (dy_o, dy), (slope_o, slope_s), (a2_o, a2_s), (x2_o, x2_s), (o_o, o_s), (k_o, k_s), (v_o, v_s),
        (q_o, q_s), (stat_o, stat_s), (tok_o, tok),
    ]

    def inward(k):
        return pltpu.make_async_copy(pairs[k][0], pairs[k][1], isem.at[k])

    for k in range(2):
        inward(k).start()
    for n in range(2):
        fetch(n).start()
    for k in range(2, len(pairs)):
        inward(k).start()
    greet(*at)
    scatter = Scatter(at, local, got_core, got_two, got_one, got_z, out, send, recv)
    vec = Vec(at, vec_now, vec_got, vsend, vrecv)
    vec_now[0] = jnp.zeros(vec_now.shape[1:], F32)
    vecf[...] = vec_in[...].astype(F32)

    def gain_row(row, where, value):
        vec_now[0, row : row + 1, where] = vec_now[0, row : row + 1, where] + value

    def weight_grad(left, right, t):
        def half(h):
            value = dot(left[:, cols(h, 384)], right[...], TN)
            for g in range(4):
                for k in range(4):
                    part = value[g * 96 + k * 24 : g * 96 + k * 24 + 24]
                    part = jnp.concatenate([part[:, :384], part[:, 384:]], axis=0).astype(BF16)
                    local[k // 2, g % 2, k % 2, 2 * h + g // 2, t] = part

        loop(2, half)
        begin(scatter.core(t))

    inward(0).wait()
    inward(1).wait()
    for col in range(2):
        def down_grad(g):
            value = dot(z_s[:, cols(g, 384)], dy[:, col * 384 : col * 384 + 384], TN).astype(BF16)
            for k in range(4):
                for half in range(2):
                    part = value[k * 96 + half * 48 : k * 96 + half * 48 + 48]
                    local[k // 2, g % Y, k % 2, g // Y, 2 * col + half] = part

        loop(Z * Y, down_grad)
        begin(scatter.core(2 * col))
        begin(scatter.core(2 * col + 1))
    gain_row(7, slice(None), total_rows(dy[...]))
    mask_fill(seg_col, seg_row, bias, x, tiles)
    for n in range(4):
        take(n, lambda part: down_from_stage(part, wbuf, n % 2, n // 2))
    inward(2).wait()
    scatter.progress(0)

    def hidden(n):
        rows = pl.ds(pl.multiple_of(n * 256, 256), 256)
        grad = dot(dy[...], wbuf[rows, :], NT) * slope_s[:, cols(n, 256)].astype(F32)
        low = grad.astype(BF16)
        slope_s[:, cols(n, 256)] = low
        where = pl.ds(pl.multiple_of((n % 3) * 256, 256), 256)
        vec_now[0, pl.ds(8 + n // 3, 1), where] = total_rows(low)

    loop(12, hidden)
    scatter.progress(1)
    inward(3).wait()
    for t in range(4):
        weight_grad(a2_s, slope_s.at[:, t * D : t * D + D], 4 + t)
    scatter.progress(2)
    for n in range(4, 8):
        take(n, lambda part: rows_from_stage(part, wbuf.at[pl.ds((n - 4) * D, D)], 0))

    def inner_grad(n):
        value = None
        for t in range(4):
            rows = pl.ds(pl.multiple_of(t * D + n * 256, 256), 256)
            part = dot(slope_s[:, t * D : t * D + D], wbuf[rows, :], NT)
            value = part if value is None else value + part
        dx[:, cols(n, 256)] = value

    loop(3, inner_grad)
    inward(4).wait()

    def norm_two(i):
        rows = cols(i, 128)
        grad = dx[rows, :]
        back, gain, shift = norm_back(x2_s[rows, :], grad, vecf[5:6, :])
        total = dy[rows, :].astype(F32) + back
        low = total.astype(BF16)
        dx[rows, :] = total
        da[rows, :] = low
        gain_row(5, slice(None), gain)
        gain_row(6, slice(None), shift)
        gain_row(4, slice(None), total_rows(low))

    loop(block // 128, norm_two)
    inward(5).wait()
    weight_grad(o_s, da, 8)
    take(8, lambda part: rows_from_stage(part, wbuf.at[pl.ds(3 * D, D)], 0))

    def mixed_grad(n):
        rows = pl.ds(pl.multiple_of(3 * D + n * 256, 256), 256)
        o_s[:, cols(n, 256)] = dot(da[...], wbuf[rows, :], NT).astype(BF16)

    loop(3, mixed_grad)
    scatter.progress(3)
    for k in range(6, 11):
        inward(k).wait()

    def halo(pair):
        return remote(halo_s.at[pair], halo_r.at[pair], hsend.at[pair], hrecv.at[pair], ident(z, y, c, 1 - x))

    def attend(pair):
        lanes = cols(pair, 128)
        pl.when(pair % 2 == 1)(lambda: scatter.progress(4 + pair // 2))
        acc_k[...] = jnp.zeros(acc_k.shape, F32)
        acc_v[...] = jnp.zeros(acc_v.shape, F32)

        def each(tile):
            rows = cols(tile, TILE)
            span = window(tile, x)
            both, grads = split_heads(q_s[rows, lanes]), split_heads(o_s[rows, lanes])
            fill = bias[tile]
            scores = dot(k_s[span, lanes], both, NT) + jnp.concatenate([fill, fill], axis=1)
            probs = jnp.exp(scores - stat_s[pair * tiles + tile][0:1])
            low = probs.astype(BF16)
            back = dot(v_s[span, lanes], grads, NT)
            mean = jnp.sum(probs * back, axis=0, keepdims=True)
            inner = (probs * (back - mean)).astype(BF16)
            acc_v[span, :] = acc_v[span, :] + dot(low, grads)
            acc_k[span, :] = acc_k[span, :] + dot(inner, both)
            query = join_heads(dot(k_s[span, lanes], inner, TN)) * HEAD_DIM ** (-0.5)
            z_s[rows, lanes] = query.astype(BF16)

        loop(tiles, each)
        for k, acc in ((0, acc_k), (1, acc_v)):
            where = pl.ds(pl.multiple_of((k + 1) * D + pair * 128, 128), 128)
            z_s[:, where] = acc[pl.ds(offset, block), :].astype(BF16)
            halo_s[pair, k] = acc[pl.ds(outside, REACH), :].astype(BF16)
        halo(pair).start()

    loop(PAIRS, attend)

    def norm_one(i):
        rows = cols(i, 128)
        value = normal(tok[rows, :].astype(F32))[0]
        a2_s[rows, :] = (value * (1.0 + vecf[0:1, :]) + vecf[1:2, :]).astype(BF16)

    loop(block // 128, norm_one)
    weight_grad(a2_s, z_s.at[:, 0:D], 9)
    scatter.progress(7)

    def add_halo(pair):
        halo(pair).wait_recv()
        for k in range(2):
            where = pl.ds(pl.multiple_of((k + 1) * D + pair * 128, 128), 128)
            rows = pl.ds(away, REACH)
            z_s[rows, where] = (z_s[rows, where].astype(F32) + halo_r[pair, k].astype(F32)).astype(BF16)

    loop(PAIRS, add_halo)
    weight_grad(a2_s, z_s.at[:, D : 2 * D], 10)
    weight_grad(a2_s, z_s.at[:, 2 * D : 3 * D], 11)
    scatter.progress(8)
    for n in range(9, 12):
        take(n, lambda part: rows_from_stage(part, wbuf.at[pl.ds((n - 9) * D, D)], 0))

    def first_grad(n):
        value = None
        for t in range(3):
            rows = pl.ds(pl.multiple_of(t * D + n * 256, 256), 256)
            part = dot(z_s[:, t * D : t * D + D], wbuf[rows, :], NT)
            value = part if value is None else value + part
        x2_s[:, cols(n, 256)] = value

    loop(3, first_grad)
    scatter.progress(9)
    gain_row(2, slice(None), total_rows(z_s[:, 0:D]))
    gain_row(3, slice(None), total_rows(z_s[:, 2 * D : 3 * D]))

    def norm_first(i):
        rows = cols(i, 128)
        back, gain, shift = norm_back(tok[rows, :].astype(F32), x2_s[rows, :], vecf[0:1, :])
        tok_grad[rows, :] = (dx[rows, :] + back).astype(BF16)
        gain_row(0, slice(None), gain)
        gain_row(1, slice(None), shift)

    loop(block // 128, norm_first)
    vec.begin(0)
    for step in range(4):
        scatter.progress(10 + step)
        total = vec.total(step)
        if step < 3:
            vec_now[step + 1] = total
            vec.begin(step + 1)
        else:
            vec_out[...] = total
    scatter.progress(14)
    scatter.sent()
    vec.sent()
    loop(PAIRS, lambda pair: halo(pair).wait_send())


def backward_all(full, vec_low, tok, dy, seg_col, seg_row, *saved):
    block, near = tok.shape[0], seg_col.shape[0]
    tiles = block // TILE
    hbm, vmem = pl.BlockSpec(memory_space=pl.ANY), pl.BlockSpec(memory_space=pltpu.VMEM)
    vec_shape = vec_low.shape
    rows = (block, D)
    q, k, v, o, stat, x2, a2, act, slope = saved
    buffers = [
        ((C, Y, X, Z, NP) + PIECE, BF16),
        ((NP, Y, X, Z) + PIECE, BF16),
        ((NP, 2, 2, 2) + PIECE, BF16),
        ((NP, 2, 2) + PIECE, BF16),
        ((NP, Z - 1) + PIECE, BF16),
        ((4 * D, D), BF16),
        ((2, C, Y, X, Z) + PIECE, BF16),
        ((tiles, SPAN, TILE), F32),
        (vec_shape, F32),
        (rows, BF16),
        (rows, BF16),
        *[(array.shape, array.dtype) for array in saved],
        (rows, F32),
        (rows, BF16),
        ((near, 128), F32),
        ((near, 128), F32),
        ((PAIRS, 2, REACH, 128), BF16),
        ((PAIRS, 2, REACH, 128), BF16),
        ((4,) + vec_shape, F32),
        ((6,) + vec_shape, F32),
    ]
    semaphores = [(NP, 8), (NP, 8), (6,), (6,), (PAIRS,), (PAIRS,), (11,), (2,)]
    return pl.pallas_call(
        backward_kernel,
        out_shape=(
            jax.ShapeDtypeStruct((NP,) + PIECE, F32),
            jax.ShapeDtypeStruct(vec_shape, F32),
            jax.ShapeDtypeStruct(rows, BF16),
        ),
        in_specs=[hbm, vmem, hbm, hbm, vmem, vmem] + [hbm] * len(saved),
        out_specs=(vmem, vmem, vmem),
        scratch_shapes=[pltpu.VMEM(*one) for one in buffers] + [pltpu.SemaphoreType.DMA(one) for one in semaphores],
        compiler_params=pltpu.CompilerParams(
            collective_id=1, has_side_effects=True, vmem_limit_bytes=60 << 20
        ),
        name="backward_all",
    )(full, vec_low, tok, dy, seg_col, seg_row, *saved)


def from_pieces(pieces):
    count = pieces.shape[0]
    return pieces.reshape(count, 2, 24, 384).transpose(2, 0, 1, 3).reshape(24, count * 768)


def from_down(pieces):
    return pieces.reshape(2, 2, 48, 384).transpose(1, 2, 0, 3).reshape(96, 768)


def on_device_fast(
    tokens,
    segments,
    cotangent,
    qkv_weight,
    proj_weight,
    up_weight,
    down_weight,
    vec_params,
    qkv_velocity,
    proj_velocity,
    up_velocity,
    down_velocity,
    vec_velocity,
    qkv_average,
    proj_average,
    up_average,
    down_average,
    vec_average,
):
    block = tokens.shape[1]
    total_tokens = lax.axis_size("dp") * segments.shape[1]
    rate = 0.05 / math.sqrt(total_tokens)
    position = lax.axis_index("blk")
    shard = lax.axis_index("dp") * lax.axis_size("blk") + position
    unit = to_unit(*[w.astype(jnp.bfloat16) for w in (qkv_weight, proj_weight, up_weight, down_weight)])
    vec_placed = lax.dynamic_update_slice(
        jnp.zeros((16, D), jnp.bfloat16), vec_params.astype(jnp.bfloat16), (0, shard * vec_params.shape[1])
    )
    seg_near = lax.dynamic_slice_in_dim(segments, position * REACH, block + REACH, 1)
    seg_query = lax.dynamic_slice_in_dim(segments, position * block, block, 1)
    seg_col = jnp.broadcast_to(seg_near[0][:, None], (block + REACH, TILE))
    seg_row = jnp.broadcast_to(seg_query, (8, block))
    full, vec_low, result, *saved = forward_all(unit, vec_placed, tokens[0], seg_col, seg_row)
    pieces, vec_sum, back = backward_all(full, vec_low, tokens[0], cotangent[0], seg_col, seg_row, *saved)
    output, tokens_grad = result[None], back[None]
    query_share = from_pieces(pieces[9:12])
    proj_share = from_pieces(pieces[8:9])
    up_share = from_pieces(pieces[4:8])
    down_share = from_down(pieces[0:4])
    vec_share = lax.dynamic_slice(vec_sum, (0, shard * vec_params.shape[1]), vec_params.shape)
    qkv_new = update(qkv_weight, query_share, qkv_velocity, qkv_average, rate)
    proj_new = update(proj_weight, proj_share, proj_velocity, proj_average, rate)
    up_new = update(up_weight, up_share, up_velocity, up_average, rate)
    down_new = update(down_weight, down_share, down_velocity, down_average, rate)
    vec_new = update(vec_params, vec_share, vec_velocity, vec_average, rate)
    return (
        output,
        tokens_grad,
        query_share,
        proj_share,
        up_share,
        down_share,
        vec_share,
        qkv_new[0],
        proj_new[0],
        up_new[0],
        down_new[0],
        vec_new[0],
        qkv_new[1],
        proj_new[1],
        up_new[1],
        down_new[1],
        vec_new[1],
        qkv_new[2],
        proj_new[2],
        up_new[2],
        down_new[2],
        vec_new[2],
        qkv_new[0].astype(jnp.bfloat16),
        proj_new[0].astype(jnp.bfloat16),
        up_new[0].astype(jnp.bfloat16),
        down_new[0].astype(jnp.bfloat16),
        vec_new[0].astype(jnp.bfloat16),
    )


def solution(mesh):
    fits = mesh.shape["dp"] == Z * Y * C and mesh.shape["blk"] == X
    return jax.shard_map(
        on_device_fast if fits else on_device,
        mesh=mesh,
        in_specs=(
            P("dp", "blk", None),
            P("dp", None),
            P("dp", "blk", None),
            P(("dp", "blk"), None),
            P(("dp", "blk"), None),
            P(("dp", "blk"), None),
            P(("dp", "blk"), None),
            P(None, ("dp", "blk")),
            P(("dp", "blk"), None),
            P(("dp", "blk"), None),
            P(("dp", "blk"), None),
            P(("dp", "blk"), None),
            P(None, ("dp", "blk")),
            P(("dp", "blk"), None),
            P(("dp", "blk"), None),
            P(("dp", "blk"), None),
            P(("dp", "blk"), None),
            P(None, ("dp", "blk")),
        ),
        out_specs=(
            P("dp", "blk", None),
            P("dp", "blk", None),
            P(("dp", "blk"), None),
            P(("dp", "blk"), None),
            P(("dp", "blk"), None),
            P(("dp", "blk"), None),
            P(None, ("dp", "blk")),
            P(("dp", "blk"), None),
            P(("dp", "blk"), None),
            P(("dp", "blk"), None),
            P(("dp", "blk"), None),
            P(None, ("dp", "blk")),
            P(("dp", "blk"), None),
            P(("dp", "blk"), None),
            P(("dp", "blk"), None),
            P(("dp", "blk"), None),
            P(None, ("dp", "blk")),
            P(("dp", "blk"), None),
            P(("dp", "blk"), None),
            P(("dp", "blk"), None),
            P(("dp", "blk"), None),
            P(None, ("dp", "blk")),
            P(("dp", "blk"), None),
            P(("dp", "blk"), None),
            P(("dp", "blk"), None),
            P(("dp", "blk"), None),
            P(None, ("dp", "blk")),
        ),
        check_vma=False,
    )
```

```python
import functools
import math

import jax
import jax.numpy as jnp
from jax import lax
from jax.experimental import pallas as pl
from jax.experimental.pallas import tpu as pltpu
from jax.sharding import PartitionSpec as P

D = 768
HEADS = 12
HEAD_DIM = 64


def layer_norm(value, gain, shift):
    mean = jnp.mean(value, axis=-1, keepdims=True)
    cent = value - mean
    var = jnp.mean(cent * cent, axis=-1, keepdims=True)
    return cent * lax.rsqrt(var + 1e-06) * (1.0 + gain) + shift


def gelu_exact(value):
    return jax.nn.gelu(value, approximate=False)


def contract_tokens(left, right):
    return lax.dot_general(
        left.reshape(-1, left.shape[-1]),
        right.reshape(-1, right.shape[-1]),
        (((0,), (0,)), ((), ())),
        preferred_element_type=jnp.float32,
    )


def times_transpose(left, weight):
    return lax.dot_general(
        left, weight, (((left.ndim - 1,), (1,)), ((), ())), preferred_element_type=jnp.float32
    )


def group_size(rows, block):
    limit = max(1, 512 // block)
    best = 1
    for cand in range(1, rows + 1):
        if rows % cand == 0 and cand <= limit:
            best = cand
    return best


def scores_of(query, keys, seg_query, seg_keys):
    scores = jnp.einsum(
        "gqhd,gkhd->ghqk", query, keys, preferred_element_type=jnp.float32
    ) * HEAD_DIM ** (-0.5)
    allowed = (seg_query[:, :, None] == seg_keys[:, None, :])[:, None]
    return (scores, allowed)


def attend_back(query, kv_all, grad_out, seg_query, segments, group):
    rows, block = (query.shape[0], query.shape[1])
    length = kv_all.shape[1]
    keys = kv_all[0:group, :, :D].reshape(group, length, HEADS, HEAD_DIM)
    values = kv_all[0:group, :, D:].reshape(group, length, HEADS, HEAD_DIM)
    scores, allowed = scores_of(query, keys, seg_query, segments)
    probs = jax.nn.softmax(jnp.where(allowed, scores, -1e30), axis=-1)
    probs_low = probs.astype(jnp.bfloat16)
    prob_grad = jnp.einsum("gqhd,gkhd->ghqk", grad_out, values, preferred_element_type=jnp.float32)
    score_grad = probs * (prob_grad - jnp.sum(probs * prob_grad, axis=-1, keepdims=True))
    score_low = score_grad.astype(jnp.bfloat16)
    dq_part = jnp.einsum(
        "ghqk,gkhd->gqhd", score_low, keys, preferred_element_type=jnp.float32
    ) * HEAD_DIM ** (-0.5)
    dk_part = jnp.einsum(
        "ghqk,gqhd->gkhd", score_low, query, preferred_element_type=jnp.float32
    ) * HEAD_DIM ** (-0.5)
    dv_part = jnp.einsum("ghqk,gqhd->gkhd", probs_low, grad_out, preferred_element_type=jnp.float32)
    dq_parts = dq_part.reshape(group, block, D)
    dkv_parts = jnp.concatenate(
        [dk_part.reshape(group, length, D), dv_part.reshape(group, length, D)], axis=-1
    )
    return (dq_parts, dkv_parts)


def update(weight, grad, velocity, average, rate):
    step_value = grad + 0.0005 * weight
    velocity_new = 0.9 * velocity + step_value
    weight_new = weight - rate * (step_value + 0.9 * velocity_new)
    average_new = 0.9 * average + 0.1 * weight_new
    return (weight_new, velocity_new, average_new)


def on_device(
    tokens,
    segments,
    cotangent,
    qkv_weight,
    proj_weight,
    up_weight,
    down_weight,
    vec_params,
    qkv_velocity,
    proj_velocity,
    up_velocity,
    down_velocity,
    vec_velocity,
    qkv_average,
    proj_average,
    up_average,
    down_average,
    vec_average,
):
    rows, block = (tokens.shape[0], tokens.shape[1])
    length = segments.shape[1]
    total_tokens = rows * lax.axis_size("dp") * length
    rate = 0.05 / math.sqrt(total_tokens)
    group = group_size(rows, block)
    gathered = (
        lax.all_gather(qkv_weight.astype(jnp.bfloat16), ("dp", "blk"), axis=0, tiled=True),
        lax.all_gather(proj_weight.astype(jnp.bfloat16), ("dp", "blk"), axis=0, tiled=True),
        lax.all_gather(up_weight.astype(jnp.bfloat16), ("dp", "blk"), axis=0, tiled=True),
        lax.all_gather(down_weight.astype(jnp.bfloat16), ("dp", "blk"), axis=0, tiled=True),
        lax.all_gather(vec_params.astype(jnp.bfloat16), ("dp", "blk"), axis=1, tiled=True),
    )
    w_query, w_proj, w_up, w_down, vec_low = gathered
    vec = vec_low.astype(jnp.float32)
    bias_up = vec[8:12].reshape(-1)
    position = lax.axis_index("blk")
    seg_query = lax.dynamic_slice_in_dim(segments, position * block, block, 1)
    inputs = tokens.astype(jnp.float32)
    a_one = layer_norm(inputs, vec[0], vec[1]).astype(jnp.bfloat16)
    zero_bias = jnp.zeros_like(vec[2])
    pre = jnp.dot(a_one, w_query, preferred_element_type=jnp.float32) + jnp.concatenate(
        [vec[2], zero_bias, vec[3]]
    )
    qkv = pre.astype(jnp.bfloat16)
    query = qkv[..., :D].reshape(rows, block, HEADS, HEAD_DIM)
    key_value = qkv[..., D:]
    piece = lax.all_gather(key_value, "blk", axis=1, tiled=True)
    top = jnp.full((rows, HEADS, block), -1e30, jnp.float32)
    count = piece.shape[1]
    keys = piece[0:group, :, :D].reshape(group, count, HEADS, HEAD_DIM)
    values = piece[0:group, :, D:].reshape(group, count, HEADS, HEAD_DIM)
    scores, allowed = scores_of(query, keys, seg_query, segments)
    scores = jnp.where(allowed, scores, -1e30)
    new_top = jnp.maximum(top, jnp.max(scores, axis=-1))
    weights = jnp.where(allowed, jnp.exp(scores - new_top[..., None]), 0.0)
    denoms = jnp.sum(weights, axis=-1)
    added = jnp.einsum(
        "ghqk,gkhd->gqhd", weights.astype(jnp.bfloat16), values, preferred_element_type=jnp.float32
    )
    mixed = (added / jnp.transpose(denoms, (0, 2, 1))[..., None]).reshape(rows, block, D)
    mixed_low = mixed.astype(jnp.bfloat16)
    second = inputs + jnp.dot(mixed_low, w_proj, preferred_element_type=jnp.float32) + vec[4]
    second_norm, norm_two_back = jax.vjp(layer_norm, second, vec[5], vec[6])
    a_two = second_norm.astype(jnp.bfloat16)
    hidden = jnp.dot(a_two, w_up, preferred_element_type=jnp.float32) + bias_up
    act_value, gelu_back = jax.vjp(gelu_exact, hidden)
    act = act_value.astype(jnp.bfloat16)
    result = second + jnp.dot(act, w_down, preferred_element_type=jnp.float32) + vec[7]
    output = result.astype(jnp.bfloat16)
    out_grad = cotangent.astype(jnp.float32)
    grad_down = contract_tokens(act, cotangent)
    bias_down_grad = jnp.sum(out_grad, axis=(0, 1))
    act_grad = times_transpose(cotangent, w_down)
    hidden_grad = gelu_back(act_grad)[0].astype(jnp.bfloat16)
    bias_up_grad = jnp.sum(hidden_grad.astype(jnp.float32), axis=(0, 1))
    grad_up = contract_tokens(a_two, hidden_grad)
    a_two_grad = times_transpose(hidden_grad, w_up)
    second_part, gain_two_grad, shift_two_grad = norm_two_back(a_two_grad)
    second_grad = out_grad + second_part
    attn_grad = second_grad.astype(jnp.bfloat16)
    bias_proj_grad = jnp.sum(attn_grad.astype(jnp.float32), axis=(0, 1))
    grad_proj = contract_tokens(mixed_low, attn_grad)
    mixed_grad = (
        times_transpose(attn_grad, w_proj)
        .astype(jnp.bfloat16)
        .reshape(rows, block, HEADS, HEAD_DIM)
    )
    kv_again = lax.all_gather(key_value, "blk", axis=1, tiled=True)
    query_grad, kv_terms = attend_back(query, kv_again, mixed_grad, seg_query, segments, group)
    kv_grad = lax.psum_scatter(
        kv_terms.astype(jnp.bfloat16), "blk", scatter_dimension=1, tiled=True
    ).astype(jnp.float32)
    qkv_grad_low = jnp.concatenate([query_grad, kv_grad], axis=-1).astype(jnp.bfloat16)
    qkv_sums = jnp.sum(qkv_grad_low.astype(jnp.float32), axis=(0, 1))
    grad_query = contract_tokens(a_one, qkv_grad_low)
    a_one_grad = times_transpose(qkv_grad_low, w_query)
    norm_one_back = jax.vjp(layer_norm, inputs, vec[0], vec[1])[1]
    first_part, gain_one_grad, shift_one_grad = norm_one_back(a_one_grad)
    tokens_grad = (second_grad + first_part).astype(jnp.bfloat16)
    vec_local = jnp.concatenate(
        [
            jnp.stack(
                [
                    gain_one_grad,
                    shift_one_grad,
                    qkv_sums[:D],
                    qkv_sums[2 * D :],
                    bias_proj_grad,
                    gain_two_grad,
                    shift_two_grad,
                    bias_down_grad,
                ]
            ),
            bias_up_grad.reshape(4, D),
        ],
        axis=0,
    )
    query_share, proj_share, up_share, down_share, vec_share = (
        lax.psum_scatter(grad_query, ("dp", "blk"), scatter_dimension=0, tiled=True),
        lax.psum_scatter(grad_proj, ("dp", "blk"), scatter_dimension=0, tiled=True),
        lax.psum_scatter(grad_up, ("dp", "blk"), scatter_dimension=0, tiled=True),
        lax.psum_scatter(grad_down, ("dp", "blk"), scatter_dimension=0, tiled=True),
        lax.psum_scatter(vec_local, ("dp", "blk"), scatter_dimension=1, tiled=True),
    )
    qkv_new = update(qkv_weight, query_share, qkv_velocity, qkv_average, rate)
    proj_new = update(proj_weight, proj_share, proj_velocity, proj_average, rate)
    up_new = update(up_weight, up_share, up_velocity, up_average, rate)
    down_new = update(down_weight, down_share, down_velocity, down_average, rate)
    vec_new = update(vec_params, vec_share, vec_velocity, vec_average, rate)
    return (
        output,
        tokens_grad,
        query_share,
        proj_share,
        up_share,
        down_share,
        vec_share,
        qkv_new[0],
        proj_new[0],
        up_new[0],
        down_new[0],
        vec_new[0],
        qkv_new[1],
        proj_new[1],
        up_new[1],
        down_new[1],
        vec_new[1],
        qkv_new[2],
        proj_new[2],
        up_new[2],
        down_new[2],
        vec_new[2],
        qkv_new[0].astype(jnp.bfloat16),
        proj_new[0].astype(jnp.bfloat16),
        up_new[0].astype(jnp.bfloat16),
        down_new[0].astype(jnp.bfloat16),
        vec_new[0].astype(jnp.bfloat16),
    )


PIECE = (48, 384)
NP = 12
Z, Y, X, C = 4, 2, 2, 2
AHEAD = 2
TILE = 128
IMG_MAX = 198
REACH = (IMG_MAX - 1 + 15) // 16 * 16
SPAN = TILE + 2 * REACH
GATHER_SPLIT = ((0, NP, 2),)
PAIRS = HEADS // 2
MESH = pl.DeviceIdType.MESH
F32, BF16 = jnp.float32, jnp.bfloat16
NT = (((1,), (1,)), ((), ()))
TN = (((0,), (0,)), ((), ()))


def place():
    d, x = lax.axis_index("dp"), lax.axis_index("blk")
    return d // (2 * Y), (d // 2) % Y, d % 2, x


def ident(z, y, c, x):
    return ((z * Y + y) * 2 + c, x)


def greet(z, y, c, x):
    barrier = pltpu.get_barrier_semaphore()
    peers = [ident((z + k) % Z, y, c, x) for k in range(1, Z)]
    peers += [ident(z, 1 - y, c, x), ident(z, y, c, 1 - x), ident(z, y, 1 - c, x)]
    for peer in peers:
        pl.semaphore_signal(barrier, inc=1, device_id=peer, device_id_type=MESH)
    pl.semaphore_wait(barrier, len(peers))


def remote(src, dst, send, recv, peer):
    return pltpu.make_async_remote_copy(
        src_ref=src, dst_ref=dst, send_sem=send, recv_sem=recv, device_id=peer, device_id_type=MESH
    )


def begin(copies):
    for copy in copies:
        copy.start()


def arrive(copies):
    for copy in copies:
        copy.wait_recv()


def within(index, low, high, run):
    if isinstance(index, int):
        if low <= index < high:
            run()
    else:
        pl.when(jnp.logical_and(index >= low, index < high))(run)


def loop(count, body):
    def step(i, carry):
        body(i)
        return carry

    lax.fori_loop(0, count, step, 0)


def cols(j, width):
    return pl.ds(pl.multiple_of(j * width, width), width)


def dot(a, b, dims=None):
    dims = (((1,), (0,)), ((), ())) if dims is None else dims
    return lax.dot_general(a, b, dims, preferred_element_type=F32)


class Vec:
    def __init__(self, at, now, got, send, recv):
        self.at, self.now, self.got, self.send, self.recv = at, now, got, send, recv

    def copies(self, step):
        z, y, c, x = self.at
        peers = [
            [ident(z, y, 1 - c, x)],
            [ident(z, y, c, 1 - x)],
            [ident(z, 1 - y, c, x)],
            [ident((z + k) % Z, y, c, x) for k in range(1, Z)],
        ][step]
        return [
            remote(self.now.at[step], self.got.at[step + k], self.send.at[step + k], self.recv.at[step + k], peer)
            for k, peer in enumerate(peers)
        ]

    def begin(self, step):
        begin(self.copies(step))

    def total(self, step):
        copies = self.copies(step)
        arrive(copies)
        total = self.now[step]
        for k in range(len(copies)):
            total = total + self.got[step + k]
        return total

    def sent(self):
        for step in range(4):
            for copy in self.copies(step):
                copy.wait_send()


def normal(value):
    mean = jnp.mean(value, axis=-1, keepdims=True)
    cent = value - mean
    var = jnp.mean(cent * cent, axis=-1, keepdims=True)
    scale = lax.rsqrt(var + 1e-06)
    return cent * scale, scale


def window_start(i, x, tiles):
    near = tiles * TILE + REACH
    first = max(i * TILE - REACH, 0)
    count = min((i + 1) * TILE + REACH, near) - first
    start = jnp.where(x == 0, first, near - first - count)
    return jnp.where(x == 0, i, tiles - 1 - i), start, count


def window(i, x, tiles):
    tile, start, count = window_start(i, x, tiles)
    return tile, pl.ds(pl.multiple_of(start, 16), count), count


def mask_fill(seg, seg_col, bias, x, tiles):
    length = seg.shape[1]
    for k in range(length // TILE):
        row = seg[0:1, k * TILE : k * TILE + TILE].astype(F32)
        seg_col[k * TILE : k * TILE + TILE, :] = jnp.transpose(jnp.broadcast_to(row, (TILE, TILE)))
    for i in range(tiles):
        tile, start, count = window_start(i, x, tiles)
        start = start + x * (length - tiles * TILE - REACH)
        row = seg[0:1, pl.ds(pl.multiple_of((x * tiles + tile) * TILE, TILE), TILE)].astype(F32)
        column = seg_col[pl.ds(pl.multiple_of(start, 16), count), :]
        bias[i, 0:count] = jnp.where(column == row, 0.0, -1e30).astype(F32)


def split_heads(pair_block):
    lane = lax.broadcasted_iota(jnp.int32, pair_block.shape, 1)
    zero = jnp.zeros_like(pair_block)
    return jnp.concatenate(
        [jnp.where(lane < HEAD_DIM, pair_block, zero), jnp.where(lane < HEAD_DIM, zero, pair_block)], axis=0
    )


def join_heads(both):
    own = jnp.concatenate([both[:HEAD_DIM, :TILE], both[HEAD_DIM:, TILE:]], axis=0)
    return jnp.transpose(own)


def rows_from_stage(stage, target, t):
    left, right = cols(2 * t, 384), cols(2 * t + 1, 384)

    def group(g):
        parts = [stage[c, g % Y, x, g // Y].astype(F32) for c in range(C) for x in range(X)]
        rows = pl.ds(pl.multiple_of(g * 96, 96), 96)
        target[rows, left] = jnp.concatenate([p[:24] for p in parts], axis=0).astype(BF16)
        target[rows, right] = jnp.concatenate([p[24:] for p in parts], axis=0).astype(BF16)

    loop(Z * Y, group)


def down_copies(full, target, t, sem):
    half, col = (t - 8) % 2 * 48, (t - 8) // 2 * 384

    def group(g):
        for c in range(C):
            for x in range(X):
                row = pl.multiple_of(g * 384 + (c * X + x) * 96 + half, 16)
                pltpu.make_async_copy(
                    full.at[c, g % Y, x, g // Y, t], target.at[pl.ds(row, 48), col : col + 384], sem
                ).start()

    loop(Z * Y, group)


class Gather:
    def __init__(self, at, unit, full, own, send, recv):
        self.at, self.unit, self.full, self.own, self.send, self.recv = at, unit, full, own, send, recv

    def mine(self, t):
        z, y, c, x = self.at
        return pltpu.make_async_copy(self.unit.at[t], self.full.at[c, y, x, z, t], self.own.at[t])

    def first(self, t):
        z, y, c, x = self.at
        return [
            remote(
                self.unit.at[t], self.full.at[c, y, x, z, t], self.send.at[t, k - 1], self.recv.at[t, k - 1],
                ident((z + k) % Z, y, c, x),
            )
            for k in range(1, Z)
        ]

    def second(self, t, low):
        z, y, c, x = self.at
        one, two = self.full.at[c, y, x, 0:low, t], self.full.at[c, y, x, low:Z, t]
        return [
            remote(one, one, self.send.at[t, 3], self.recv.at[t, 3], ident(z, y, c, 1 - x)),
            remote(two, two, self.send.at[t, 4], self.recv.at[t, 4], ident(z, 1 - y, c, x)),
        ]

    def third(self, t, low):
        z, y, c, x = self.at
        one, two = self.full.at[c, y, :, 0:low, t], self.full.at[c, :, x, low:Z, t]
        return [
            remote(one, one, self.send.at[t, 5], self.recv.at[t, 5], ident(z, 1 - y, c, x)),
            remote(two, two, self.send.at[t, 6], self.recv.at[t, 6], ident(z, y, c, 1 - x)),
        ]

    def last(self, t):
        z, y, c, x = self.at
        block = self.full.at[c, :, :, :, t]
        return [remote(block, block, self.send.at[t, 7], self.recv.at[t, 7], ident(z, y, 1 - c, x))]

    def start(self):
        loop(NP, lambda t: self.mine(t).start())
        loop(AHEAD, lambda t: begin(self.first(t)))

    def progress(self, i):
        def to_second(t, low):
            self.mine(t).wait()
            arrive(self.first(t))
            begin(self.second(t, low))

        def to_third(t, low):
            arrive(self.second(t, low))
            begin(self.third(t, low))

        def to_last(t, low):
            arrive(self.third(t, low))
            begin(self.last(t))

        for first, end, low in GATHER_SPLIT:
            within(i, first, end, lambda: to_second(i, low))
        for first, end, low in GATHER_SPLIT:
            within(i - 1, first, end, lambda: to_third(i - 1, low))
        for first, end, low in GATHER_SPLIT:
            within(i - 2, first, end, lambda: to_last(i - 2, low))
        within(i + AHEAD, AHEAD, NP, lambda: begin(self.first(i + AHEAD)))

    def sent(self):
        for first, end, low in GATHER_SPLIT:
            def one(t):
                for copy in self.first(t) + self.second(t, low) + self.third(t, low) + self.last(t):
                    copy.wait_send()

            lax.fori_loop(first, end, lambda t, carry: (one(t), carry)[1], 0)


def forward_kernel(
    w_qkv, w_proj, w_up, w_down, vec_in, tok, dy, seg,
    full, vec_out, out_o, q_o, k_o, v_o, o_o, stat_o, x2_o, a2_o, z_o, slope_o, grad_o, bias_o,
    unit, seg_col, near, a1, wbig, wdown, stage, vecf, bias, out_s, q_s, k_s, v_s, o_s, stat_s, x2_s, a2_s, z_s, slope_s, got,
    local, vec_now, vec_got, own, send, recv, vsend, vrecv, hsem, ssem, dsem, osem, gsend, grecv,
):
    z, y, c, x = at = place()
    block = tok.shape[0]
    tiles = block // TILE
    offset = pl.multiple_of(x * REACH, 16)
    vec_now[0] = vec_in[...]

    def pack(t, weight, j):
        left, right = weight[:, j * 768 : j * 768 + 384], weight[:, j * 768 + 384 : j * 768 + 768]
        unit[t] = jnp.concatenate([left, right], axis=0).astype(BF16)

    for t, j in enumerate((1, 2, 0)):
        pack(t, w_qkv, j)
    pack(3, w_proj, 0)
    for j in range(4):
        pack(4 + j, w_up, j)
        unit[8 + j] = w_down[j % 2 * 48 : j % 2 * 48 + 48, j // 2 * 384 : j // 2 * 384 + 384].astype(BF16)
    greet(*at)
    gather = Gather(at, unit, full, own, send, recv)
    gather.start()
    vec = Vec(at, vec_now, vec_got, vsend, vrecv)
    vec.begin(0)
    away = pl.multiple_of((1 - x) * (block - REACH), 16)
    land = pl.multiple_of(x * block, 16)
    halo = remote(
        tok.at[pl.ds(away, REACH)], near.at[pl.ds(land, REACH)], hsem.at[0], hsem.at[1], ident(z, y, c, 1 - x)
    )
    halo.start()
    near[pl.ds(offset, block), :] = tok[...]

    def put(k, src, dst):
        return pltpu.make_async_copy(src, dst, osem.at[k])

    def vec_step(step):
        total = vec.total(step)
        if step < 3:
            vec_now[step + 1] = total
            vec.begin(step + 1)
        else:
            vec_out[...] = total
            vecf[...] = total.astype(F32)

    def staged(t):
        return pltpu.make_async_copy(full.at[:, :, :, :, t], stage.at[t % 4], ssem.at[t % 4])

    def fetch(t):
        arrive(gather.last(t))
        staged(t).start()

    def take(t):
        staged(t).wait()
        rows_from_stage(stage.at[t % 4], wbig, t)

    def down_start(t):
        arrive(gather.last(t))
        down_copies(full, wdown, t, dsem.at[t - 8])

    def down_wait(t):
        pltpu.make_async_copy(full.at[:, :, :, :, t], stage.at[0], dsem.at[t - 8]).wait()

    gather.progress(0)
    vec_step(0)
    gather.progress(1)
    vec_step(1)
    gather.progress(2)
    vec_step(2)
    vec_step(3)
    halo.wait_recv()

    def norm_one(i):
        rows = cols(i, 240)
        value = normal(near[rows, :].astype(F32))[0]
        a1[rows, :] = (value * (1.0 + vecf[0:1, :]) + vecf[1:2, :]).astype(BF16)

    loop(near.shape[0] // 240, norm_one)
    mask_fill(seg, seg_col, bias, x, tiles)
    put(11, bias, bias_o).start()
    gather.progress(3)
    fetch(0)
    take(0)

    def keys(j):
        k_s[:, cols(j, 256)] = dot(a1[...], wbig[:, cols(j, 256)]).astype(BF16)

    loop(3, keys)
    gather.progress(4)
    fetch(1)
    take(1)
    fetch(2)

    def values(j):
        v_s[:, cols(j, 256)] = (dot(a1[...], wbig[:, cols(j + 3, 256)]) + vecf[3:4, cols(j, 256)]).astype(BF16)

    loop(3, values)
    gather.progress(5)
    take(2)

    def queries(j):
        value = dot(a1[pl.ds(offset, block), :], wbig[:, cols(j + 6, 256)]) + vecf[2:3, cols(j, 256)]
        q_s[:, cols(j, 256)] = value.astype(BF16) * HEAD_DIM ** (-0.5)

    loop(3, queries)
    put(0, k_s, k_o).start()
    put(1, v_s, v_o).start()
    put(2, q_s, q_o).start()

    def attend(pair):
        pl.when(pair % 2 == 0)(lambda: gather.progress(6 + pair // 2))
        pl.when(pair % 2 == 1)(lambda: fetch(3 + pair // 2))
        lanes = cols(pair, 128)

        for i in range(tiles):
            tile, span, count = window(i, x, tiles)
            rows = cols(tile, TILE)
            both = split_heads(q_s[rows, lanes])
            fill = bias[i, 0:count]
            scores = dot(k_s[span, lanes], both, NT) + jnp.concatenate([fill, fill], axis=1)
            top = jnp.max(scores, axis=0, keepdims=True)
            weights = jnp.exp(scores - top)
            total = jnp.sum(weights, axis=0, keepdims=True)
            mixed = dot(v_s[span, lanes], weights.astype(BF16), TN) / total
            o_s[rows, lanes] = join_heads(mixed).astype(BF16)
            stat_s[pair * tiles + i] = jnp.broadcast_to(top + jnp.log(total), (8, 2 * TILE))
        pl.when(pair % 2 == 1)(lambda: take(3 + pair // 2))

    loop(PAIRS, attend)
    put(3, o_s, o_o).start()
    put(4, stat_s, stat_o).start()
    gather.progress(9)
    fetch(6)

    def project(j):
        value = dot(o_s[...], wbig[:, cols(j + 9, 256)])
        x2_s[:, cols(j, 256)] = tok[:, cols(j, 256)].astype(F32) + value + vecf[4:5, cols(j, 256)]

    loop(3, project)

    def norm_two(i):
        rows = pl.ds(pl.multiple_of(i * 256, 256), 256)
        value = normal(x2_s[rows, :])[0]
        a2_s[rows, :] = (value * (1.0 + vecf[5:6, :]) + vecf[6:7, :]).astype(BF16)

    loop(block // 256, norm_two)
    put(5, x2_s, x2_o).start()
    put(6, a2_s, a2_o).start()
    gather.progress(10)
    take(6)
    fetch(7)

    def expand(j):
        u = dot(a2_s[...], wbig[:, cols(j + 12, 256)])
        u = u + vecf[pl.ds(8 + j // 3, 1), pl.ds(pl.multiple_of((j % 3) * 256, 256), 256)]
        half = 0.5 + 0.5 * lax.erf(u * math.sqrt(0.5))
        z_s[:, cols(j, 256)] = (u * half).astype(BF16)
        slope = half + u * (jnp.exp(-0.5 * u * u) * (1.0 / math.sqrt(2.0 * math.pi)))
        slope_s[:, cols(j, 256)] = slope.astype(BF16)

    loop(5, expand)
    gather.progress(11)
    take(7)
    loop(5, lambda j: expand(j + 5))
    gather.progress(12)
    down_start(8)
    loop(2, lambda j: expand(j + 10))
    put(7, z_s, z_o).start()
    put(8, slope_s, slope_o).start()

    def core(t):
        peer = ident(z, y, 1 - c, x)
        return remote(local.at[1 - c, :, :, :, t], got.at[t], gsend.at[t], grecv.at[t], peer)

    for half in range(2):
        def down_grad(g):
            value = dot(z_s[:, cols(g, 384)], dy[:, half * 384 : half * 384 + 384], TN).astype(BF16)
            for k in range(4):
                for row in range(2):
                    part = value[k * 96 + row * 48 : k * 96 + row * 48 + 48]
                    local[k // 2, g % Y, k % 2, g // Y, 2 * half + row] = part

        loop(Z * Y, down_grad)
        core(2 * half).start()
        core(2 * half + 1).start()
        if half == 0:
            gather.progress(13)
            down_start(9)
    down_start(10)

    def contract(half):
        col = slice(half * 384, half * 384 + 384)
        value = dot(z_s[...], wdown[:, col])
        out_s[:, col] = (x2_s[:, col] + value + vecf[7:8, col]).astype(BF16)

    def gain(t):
        core(t).wait_recv()
        for a in range(Y):
            for b in range(X):
                own_part = local[c, a, b, :, t].astype(F32)
                got[t, a, b] = (own_part + got[t, a, b].astype(F32)).astype(BF16)

    loop(4, gain)
    put(10, got, grad_o).start()
    down_wait(8)
    down_wait(9)
    contract(0)
    down_start(11)
    down_wait(10)
    down_wait(11)
    contract(1)
    put(9, out_s, out_o).start()
    pairs = [(k_s, k_o), (v_s, v_o), (q_s, q_o), (o_s, o_o), (stat_s, stat_o), (x2_s, x2_o), (a2_s, a2_o)]
    for k, (src, dst) in enumerate(pairs + [(z_s, z_o), (slope_s, slope_o), (out_s, out_o)]):
        put(k, src, dst).wait()
    put(10, got, grad_o).wait()
    put(11, bias, bias_o).wait()
    gather.sent()
    vec.sent()
    halo.wait_send()
    loop(4, lambda t: core(t).wait_send())


def forward_all(weights, vec_placed, tok, dy, seg):
    block = tok.shape[0]
    near = block + REACH
    ff = 4 * D
    tiles = block // TILE
    shapes = [
        ((block, D), BF16),
        ((block, D), BF16),
        ((near, D), BF16),
        ((near, D), BF16),
        ((block, D), BF16),
        ((PAIRS * tiles, 8, 2 * TILE), F32),
        ((block, D), F32),
        ((block, D), BF16),
        ((block, ff), BF16),
        ((block, ff), BF16),
        ((4, Y, X, Z) + PIECE, BF16),
        ((tiles, SPAN, TILE), F32),
    ]
    hbm, vmem = pl.BlockSpec(memory_space=pl.ANY), pl.BlockSpec(memory_space=pltpu.VMEM)
    outs = [((C, Y, X, Z, NP) + PIECE, BF16), (vec_placed.shape, BF16)] + shapes
    return pl.pallas_call(
        forward_kernel,
        out_shape=tuple(jax.ShapeDtypeStruct(*one) for one in outs),
        in_specs=[vmem] * 8,
        out_specs=tuple([hbm, vmem] + [hbm] * len(shapes)),
        scratch_shapes=[
            pltpu.VMEM((NP,) + PIECE, BF16),
            pltpu.VMEM((seg.shape[1], TILE), F32),
            pltpu.VMEM((near, D), BF16),
            pltpu.VMEM((near, D), BF16),
            pltpu.VMEM((D, 8 * D), BF16),
            pltpu.VMEM((ff, D), BF16),
            pltpu.VMEM((4, C, Y, X, Z) + PIECE, BF16),
            pltpu.VMEM(vec_placed.shape, F32),
            *[pltpu.VMEM(*one) for one in shapes[-1:] + shapes[:-1]],
            pltpu.VMEM((C, Y, X, Z, 4) + PIECE, BF16),
            pltpu.VMEM((4,) + vec_placed.shape, BF16),
            pltpu.VMEM((6,) + vec_placed.shape, BF16),
            pltpu.SemaphoreType.DMA((NP,)),
            pltpu.SemaphoreType.DMA((NP, 8)),
            pltpu.SemaphoreType.DMA((NP, 8)),
            pltpu.SemaphoreType.DMA((6,)),
            pltpu.SemaphoreType.DMA((6,)),
            pltpu.SemaphoreType.DMA((2,)),
            pltpu.SemaphoreType.DMA((4,)),
            pltpu.SemaphoreType.DMA((4,)),
            pltpu.SemaphoreType.DMA((12,)),
            pltpu.SemaphoreType.DMA((4,)),
            pltpu.SemaphoreType.DMA((4,)),
        ],
        compiler_params=pltpu.CompilerParams(
            collective_id=0, has_side_effects=True, vmem_limit_bytes=60 << 20
        ),
        name="forward_all",
    )(*weights, vec_placed, tok, dy, seg)


SCATTER_SPLIT = ((0, 4, 3), (4, NP, 2))


class Scatter:
    def __init__(self, at, local, got_core, got_two, got_one, got_z, out, send, recv):
        self.at, self.local, self.out, self.send, self.recv = at, local, out, send, recv
        self.got = got_core, got_two, got_one, got_z

    def core(self, t):
        z, y, c, x = self.at
        peer = ident(z, y, 1 - c, x)
        return [remote(self.local.at[1 - c, :, :, :, t], self.got[0].at[t - 4], self.send.at[t, 0], self.recv.at[t, 0], peer)]

    def two(self, t, low):
        z, y, c, x = self.at
        one, other = self.local.at[c, 1 - y, :, 0:low, t], self.local.at[c, :, 1 - x, low:Z, t]
        got = self.got[1].at[t]
        return [
            remote(one, got.at[:, 0:low], self.send.at[t, 1], self.recv.at[t, 1], ident(z, 1 - y, c, x)),
            remote(other, got.at[:, low:Z], self.send.at[t, 2], self.recv.at[t, 2], ident(z, y, c, 1 - x)),
        ]

    def one(self, t, low):
        z, y, c, x = self.at
        one, other = self.local.at[c, y, 1 - x, 0:low, t], self.local.at[c, 1 - y, x, low:Z, t]
        got = self.got[2].at[t]
        return [
            remote(one, got.at[0:low], self.send.at[t, 3], self.recv.at[t, 3], ident(z, y, c, 1 - x)),
            remote(other, got.at[low:Z], self.send.at[t, 4], self.recv.at[t, 4], ident(z, 1 - y, c, x)),
        ]

    def along(self, t):
        z, y, c, x = self.at
        return [
            remote(
                self.local.at[c, y, x, (z + k) % Z, t], self.got[3].at[t, k - 1], self.send.at[t, 4 + k],
                self.recv.at[t, 4 + k], ident((z + k) % Z, y, c, x),
            )
            for k in range(1, Z)
        ]

    def add(self, where, value):
        self.local[where] = (self.local[where].astype(F32) + value.astype(F32)).astype(BF16)

    def take_core(self, t):
        c = self.at[2]
        arrive(self.core(t))
        for a in range(Y):
            for b in range(X):
                self.add((c, a, b, slice(None), t), self.got[0][t - 4, a, b])

    def after_core(self, t):
        self.take_core(t)
        self.go_two(t)

    def after_two(self, t, low):
        z, y, c, x = self.at
        arrive(self.two(t, low))
        for b in range(2):
            self.add((c, y, b, slice(0, low), t), self.got[1][t, b, 0:low])
            self.add((c, b, x, slice(low, Z), t), self.got[1][t, b, low:Z])
        begin(self.one(t, low))

    def after_one(self, t, low):
        z, y, c, x = self.at
        arrive(self.one(t, low))
        self.add((c, y, x, slice(None), t), self.got[2][t])
        begin(self.along(t))

    def after_z(self, t):
        z, y, c, x = self.at
        arrive(self.along(t))
        total = self.local[c, y, x, z, t].astype(F32)
        for k in range(Z - 1):
            total = total + self.got[3][t, k].astype(F32)
        self.out[t] = total

    def go_two(self, t):
        for first, end, low in SCATTER_SPLIT:
            within(t, first, end, lambda: begin(self.two(t, low)))

    def go_one(self, t):
        for first, end, low in SCATTER_SPLIT:
            within(t, first, end, lambda: self.after_two(t, low))

    def go_z(self, t):
        arrive_one = self.after_one
        for first, end, low in SCATTER_SPLIT:
            within(t, first, end, lambda: arrive_one(t, low))

    def sent(self):
        loop(NP - 4, lambda t: self.core(t + 4)[0].wait_send())
        for first, end, low in SCATTER_SPLIT:
            def each(t):
                for copy in self.two(t, low) + self.one(t, low) + self.along(t):
                    copy.wait_send()

            lax.fori_loop(first, end, lambda t, carry: (each(t), carry)[1], 0)


def total_rows(value):
    return jnp.sum(value.astype(F32), axis=0, keepdims=True)


def norm_back(value, grad, gain):
    unit_value, scale = normal(value)
    inner = grad * (1.0 + gain)
    mean_one = jnp.mean(inner, axis=-1, keepdims=True)
    mean_two = jnp.mean(inner * unit_value, axis=-1, keepdims=True)
    back = scale * (inner - mean_one - unit_value * mean_two)
    return back, total_rows(grad * unit_value), total_rows(grad)


def backward_kernel(
    full, vec_in, tok_o, dy_o, grad_o, bias_o, q_o, k_o, v_o, o_o, stat_o, x2_o, a2_o, slope_o,
    out, vec_out, tok_grad,
    local, got_core, got_two, got_one, got_z, wbuf, stage, bias, vecf, tok, dy, q_s, k_s, v_s, o_s, stat_s, x2_s, a2_s, z_s,
    slope_s, dx, da, acc_k, acc_v, halo_s, halo_r, vec_now, vec_got, send, recv, vsend, vrecv, hsend, hrecv, isem, ssem, dsem, gsem,
):
    z, y, c, x = at = place()
    block = tok.shape[0]
    tiles = block // TILE
    offset = pl.multiple_of(x * REACH, 16)
    away = pl.multiple_of((1 - x) * (block - REACH), 16)
    outside = pl.multiple_of((1 - x) * block, 16)
    order = [4, 5, 6, 7, 3, 2, 0, 1]

    def fetch(n):
        return pltpu.make_async_copy(full.at[:, :, :, :, order[n]], stage.at[n % 2], ssem.at[n % 2])

    def take(n, use):
        fetch(n).wait()
        use(stage.at[n % 2])
        if n + 2 < len(order):
            fetch(n + 2).start()

    pairs = [
        (dy_o, dy), (slope_o, slope_s), (a2_o, a2_s), (x2_o, x2_s), (o_o, o_s), (k_o, k_s), (v_o, v_s), (q_o, q_s),
        (stat_o, stat_s), (tok_o, tok), (bias_o, bias),
    ]

    def inward(k):
        return pltpu.make_async_copy(pairs[k][0], pairs[k][1], isem.at[k])

    def grads(t):
        return pltpu.make_async_copy(grad_o.at[t], local.at[c, :, :, :, t], gsem.at[t])

    for t in range(4):
        grads(t).start()
    inward(0).start()
    for t in range(8, 12):
        down_copies(full, wbuf, t, dsem.at[t - 8])
    for n in range(2):
        fetch(n).start()
    for k in range(1, len(pairs)):
        inward(k).start()
    greet(*at)
    scatter = Scatter(at, local, got_core, got_two, got_one, got_z, out, send, recv)
    vec = Vec(at, vec_now, vec_got, vsend, vrecv)
    vec_now[0] = jnp.zeros(vec_now.shape[1:], F32)
    vecf[...] = vec_in[...].astype(F32)

    def vec_step(step):
        total = vec.total(step)
        if step < 3:
            vec_now[step + 1] = total
            vec.begin(step + 1)
        else:
            vec_out[...] = total

    def gain_row(row, where, value):
        vec_now[0, row : row + 1, where] = vec_now[0, row : row + 1, where] + value

    def weight_grad(left, right, t):
        def half(h):
            value = dot(left[:, cols(h, 384)], right[...], TN)
            for g in range(4):
                for k in range(4):
                    part = value[g * 96 + k * 24 : g * 96 + k * 24 + 24]
                    part = jnp.concatenate([part[:, :384], part[:, 384:]], axis=0).astype(BF16)
                    local[k // 2, g % 2, k % 2, 2 * h + g // 2, t] = part

        loop(2, half)
        begin(scatter.core(t))

    for t in range(4):
        grads(t).wait()
        scatter.go_two(t)
    inward(0).wait()
    gain_row(7, slice(None), total_rows(dy[...]))
    for t in range(8, 12):
        pltpu.make_async_copy(full.at[:, :, :, :, t], stage.at[0], dsem.at[t - 8]).wait()
    inward(1).wait()

    def hidden(n):
        rows = pl.ds(pl.multiple_of(n * 256, 256), 256)
        grad = dot(dy[...], wbuf[rows, :], NT) * slope_s[:, cols(n, 256)].astype(F32)
        low = grad.astype(BF16)
        slope_s[:, cols(n, 256)] = low
        where = pl.ds(pl.multiple_of((n % 3) * 256, 256), 256)
        vec_now[0, pl.ds(8 + n // 3, 1), where] = total_rows(low)

    loop(12, hidden)
    scatter.go_one(0)
    inward(2).wait()
    for t in range(2):
        take(t, lambda part: rows_from_stage(part, wbuf.at[pl.ds(t * D, D)], 0))
    for t in range(4):
        weight_grad(a2_s, slope_s.at[:, t * D : t * D + D], 4 + t)
    scatter.go_one(1)
    scatter.go_one(2)
    for t in range(2, 4):
        take(t, lambda part: rows_from_stage(part, wbuf.at[pl.ds(t * D, D)], 0))

    def inner_grad(n):
        value = None
        for t in range(4):
            rows = pl.ds(pl.multiple_of(t * D + n * 256, 256), 256)
            part = dot(slope_s[:, t * D : t * D + D], wbuf[rows, :], NT)
            value = part if value is None else value + part
        dx[:, cols(n, 256)] = value

    loop(3, inner_grad)
    scatter.after_core(4)
    scatter.after_core(5)
    scatter.go_one(3)
    scatter.go_z(0)
    inward(3).wait()

    def norm_two(i):
        rows = cols(i, 128)
        grad = dx[rows, :]
        back, gain, shift = norm_back(x2_s[rows, :], grad, vecf[5:6, :])
        total = dy[rows, :].astype(F32) + back
        low = total.astype(BF16)
        dx[rows, :] = total
        da[rows, :] = low
        gain_row(5, slice(None), gain)
        gain_row(6, slice(None), shift)
        gain_row(4, slice(None), total_rows(low))

    loop(block // 128, norm_two)
    scatter.after_core(6)
    scatter.after_core(7)
    scatter.go_z(1)
    inward(4).wait()
    weight_grad(o_s, da, 8)
    take(4, lambda part: rows_from_stage(part, wbuf.at[pl.ds(3 * D, D)], 0))

    def mixed_grad(n):
        rows = pl.ds(pl.multiple_of(3 * D + n * 256, 256), 256)
        o_s[:, cols(n, 256)] = dot(da[...], wbuf[rows, :], NT).astype(BF16)

    loop(3, mixed_grad)
    scatter.after_core(8)
    for k in range(5, 11):
        inward(k).wait()

    def halo(pair):
        return remote(halo_s.at[pair], halo_r.at[pair], hsend.at[pair], hrecv.at[pair], ident(z, y, c, 1 - x))

    def attend(pair):
        lanes = cols(pair, 128)
        scatter.go_z(2 + pair)
        within(pair, 0, 5, lambda: scatter.go_one(4 + pair))
        scatter.after_z(pair)
        acc_k[...] = jnp.zeros(acc_k.shape, F32)
        acc_v[...] = jnp.zeros(acc_v.shape, F32)

        for i in range(tiles):
            tile, span, count = window(i, x, tiles)
            rows = cols(tile, TILE)
            both, grads = split_heads(q_s[rows, lanes]), split_heads(o_s[rows, lanes])
            fill = bias[i, 0:count]
            scores = dot(k_s[span, lanes], both, NT) + jnp.concatenate([fill, fill], axis=1)
            probs = jnp.exp(scores - stat_s[pair * tiles + i][0:1])
            low = probs.astype(BF16)
            back = dot(v_s[span, lanes], grads, NT)
            mean = jnp.sum(probs * back, axis=0, keepdims=True)
            inner = (probs * (back - mean)).astype(BF16)
            acc_v[span, :] = acc_v[span, :] + dot(low, grads)
            acc_k[span, :] = acc_k[span, :] + dot(inner, both)
            query = join_heads(dot(k_s[span, lanes], inner, TN)) * HEAD_DIM ** (-0.5)
            z_s[rows, lanes] = query.astype(BF16)

        for k, acc in ((0, acc_k), (1, acc_v)):
            where = pl.ds(pl.multiple_of((k + 1) * D + pair * 128, 128), 128)
            z_s[:, where] = acc[pl.ds(offset, block), :].astype(BF16)
            halo_s[pair, k] = acc[pl.ds(outside, REACH), :].astype(BF16)
        halo(pair).start()

    loop(PAIRS, attend)

    def norm_one(i):
        rows = cols(i, 128)
        value = normal(tok[rows, :].astype(F32))[0]
        a2_s[rows, :] = (value * (1.0 + vecf[0:1, :]) + vecf[1:2, :]).astype(BF16)

    loop(block // 128, norm_one)
    weight_grad(a2_s, z_s.at[:, 0:D], 9)

    def add_halo(pair):
        halo(pair).wait_recv()
        for k in range(2):
            where = pl.ds(pl.multiple_of((k + 1) * D + pair * 128, 128), 128)
            rows = pl.ds(away, REACH)
            z_s[rows, where] = (z_s[rows, where].astype(F32) + halo_r[pair, k].astype(F32)).astype(BF16)

    loop(PAIRS, add_halo)
    weight_grad(a2_s, z_s.at[:, D : 2 * D], 10)
    scatter.after_core(9)
    weight_grad(a2_s, z_s.at[:, 2 * D : 3 * D], 11)
    scatter.after_core(10)
    scatter.go_z(8)
    scatter.after_core(11)
    for n in range(5, 8):
        take(n, lambda part: rows_from_stage(part, wbuf.at[pl.ds((n - 5) * D, D)], 0))

    def first_grad(n):
        value = None
        for t in range(3):
            rows = pl.ds(pl.multiple_of(t * D + n * 256, 256), 256)
            part = dot(z_s[:, t * D : t * D + D], wbuf[rows, :], NT)
            value = part if value is None else value + part
        x2_s[:, cols(n, 256)] = value

    loop(3, first_grad)
    scatter.go_one(9)
    gain_row(2, slice(None), total_rows(z_s[:, 0:D]))
    gain_row(3, slice(None), total_rows(z_s[:, 2 * D : 3 * D]))

    def norm_first(i):
        rows = cols(i, 128)
        back, gain, shift = norm_back(tok[rows, :].astype(F32), x2_s[rows, :], vecf[0:1, :])
        tok_grad[rows, :] = (dx[rows, :] + back).astype(BF16)
        gain_row(0, slice(None), gain)
        gain_row(1, slice(None), shift)

    loop(block // 128, norm_first)
    vec.begin(0)
    scatter.go_one(10)
    scatter.go_z(9)
    scatter.after_z(6)
    vec_step(0)
    scatter.go_one(11)
    scatter.go_z(10)
    scatter.after_z(7)
    vec_step(1)
    scatter.go_z(11)
    scatter.after_z(8)
    vec_step(2)
    scatter.after_z(9)
    vec_step(3)
    scatter.after_z(10)
    scatter.after_z(11)
    scatter.sent()
    vec.sent()
    loop(PAIRS, lambda pair: halo(pair).wait_send())


def backward_all(full, vec_low, tok, dy, grad, fill, *saved):
    block = tok.shape[0]
    near = block + REACH
    tiles = block // TILE
    hbm, vmem = pl.BlockSpec(memory_space=pl.ANY), pl.BlockSpec(memory_space=pltpu.VMEM)
    vec_shape = vec_low.shape
    rows = (block, D)
    buffers = [
        ((C, Y, X, Z, NP) + PIECE, BF16),
        ((NP - 4, Y, X, Z) + PIECE, BF16),
        ((NP, 2, Z) + PIECE, BF16),
        ((NP, Z) + PIECE, BF16),
        ((NP, Z - 1) + PIECE, BF16),
        ((4 * D, D), BF16),
        ((2, C, Y, X, Z) + PIECE, BF16),
        ((tiles, SPAN, TILE), F32),
        (vec_shape, F32),
        (rows, BF16),
        (rows, BF16),
        *[(array.shape, array.dtype) for array in saved[:-1]],
        ((block, 3 * D), BF16),
        ((block, 4 * D), BF16),
        (rows, F32),
        (rows, BF16),
        ((near, 128), F32),
        ((near, 128), F32),
        ((PAIRS, 2, REACH, 128), BF16),
        ((PAIRS, 2, REACH, 128), BF16),
        ((4,) + vec_shape, F32),
        ((6,) + vec_shape, F32),
    ]
    semaphores = [(NP, 8), (NP, 8), (6,), (6,), (PAIRS,), (PAIRS,), (11,), (2,), (4,), (4,)]
    return pl.pallas_call(
        backward_kernel,
        out_shape=(
            jax.ShapeDtypeStruct((NP,) + PIECE, F32),
            jax.ShapeDtypeStruct(vec_shape, F32),
            jax.ShapeDtypeStruct(rows, BF16),
        ),
        in_specs=[hbm, vmem, hbm, hbm, hbm, hbm] + [hbm] * len(saved),
        out_specs=(vmem, vmem, vmem),
        scratch_shapes=[pltpu.VMEM(*one) for one in buffers] + [pltpu.SemaphoreType.DMA(one) for one in semaphores],
        compiler_params=pltpu.CompilerParams(
            collective_id=1, has_side_effects=True, vmem_limit_bytes=60 << 20
        ),
        name="backward_all",
    )(full, vec_low, tok, dy, grad, fill, *saved)


def update_kernel(rate, pieces, *refs):
    masters, velocities, averages, grads, news, moving, means, copies = [refs[k : k + 4] for k in range(0, 32, 4)]

    def one(k, rows, where, grad):
        new, velocity, average = update(
            masters[k][rows, where], grad, velocities[k][rows, where], averages[k][rows, where], rate
        )
        grads[k][rows, where] = grad
        news[k][rows, where] = new
        moving[k][rows, where] = velocity
        means[k][rows, where] = average

    for t in range(NP):
        piece = pieces[t]
        if t < 4:
            one(3, slice(t % 2 * 48, t % 2 * 48 + 48), slice(t // 2 * 384, t // 2 * 384 + 384), piece)
            continue
        k, j = (2, t - 4) if t < 8 else (1, 0) if t == 8 else (0, t - 9)
        for half in range(2):
            col = (2 * j + half) * 384
            one(k, slice(0, 24), slice(col, col + 384), piece[half * 24 : half * 24 + 24])
    for k in range(4):
        copies[k][...] = news[k][...].astype(BF16)


def update_all(rate, pieces, masters, velocities, averages):
    shapes = [jax.ShapeDtypeStruct(w.shape, F32) for w in masters] * 4
    shapes += [jax.ShapeDtypeStruct(w.shape, BF16) for w in masters]
    vmem = pl.BlockSpec(memory_space=pltpu.VMEM)
    return pl.pallas_call(
        functools.partial(update_kernel, rate),
        out_shape=tuple(shapes),
        in_specs=[vmem] * 13,
        out_specs=tuple([vmem] * 20),
        name="update_all",
    )(pieces, *masters, *velocities, *averages)


def on_device_fast(
    tokens,
    segments,
    cotangent,
    qkv_weight,
    proj_weight,
    up_weight,
    down_weight,
    vec_params,
    qkv_velocity,
    proj_velocity,
    up_velocity,
    down_velocity,
    vec_velocity,
    qkv_average,
    proj_average,
    up_average,
    down_average,
    vec_average,
):
    block = tokens.shape[1]
    total_tokens = lax.axis_size("dp") * segments.shape[1]
    rate = 0.05 / math.sqrt(total_tokens)
    position = lax.axis_index("blk")
    shard = lax.axis_index("dp") * lax.axis_size("blk") + position
    masters = (qkv_weight, proj_weight, up_weight, down_weight)
    vec_placed = lax.dynamic_update_slice(
        jnp.zeros((16, D), jnp.bfloat16), vec_params.astype(jnp.bfloat16), (0, shard * vec_params.shape[1])
    )
    full, vec_low, result, *saved, act, slope, down, fill = forward_all(
        masters, vec_placed, tokens[0], cotangent[0], segments
    )
    pieces, vec_sum, back = backward_all(full, vec_low, tokens[0], cotangent[0], down, fill, *saved, slope)
    output, tokens_grad = result[None], back[None]
    velocities = (qkv_velocity, proj_velocity, up_velocity, down_velocity)
    averages = (qkv_average, proj_average, up_average, down_average)
    done = update_all(rate, pieces, masters, velocities, averages)
    vec_share = lax.dynamic_slice(vec_sum, (0, shard * vec_params.shape[1]), vec_params.shape)
    vec_new = update(vec_params, vec_share, vec_velocity, vec_average, rate)
    return (
        output,
        tokens_grad,
        *done[0:4],
        vec_share,
        *done[4:8],
        vec_new[0],
        *done[8:12],
        vec_new[1],
        *done[12:16],
        vec_new[2],
        *done[16:20],
        vec_new[0].astype(jnp.bfloat16),
    )


def solution(mesh):
    fits = mesh.shape["dp"] == Z * Y * C and mesh.shape["blk"] == X
    return jax.shard_map(
        on_device_fast if fits else on_device,
        mesh=mesh,
        in_specs=(
            P("dp", "blk", None),
            P("dp", None),
            P("dp", "blk", None),
            P(("dp", "blk"), None),
            P(("dp", "blk"), None),
            P(("dp", "blk"), None),
            P(("dp", "blk"), None),
            P(None, ("dp", "blk")),
            P(("dp", "blk"), None),
            P(("dp", "blk"), None),
            P(("dp", "blk"), None),
            P(("dp", "blk"), None),
            P(None, ("dp", "blk")),
            P(("dp", "blk"), None),
            P(("dp", "blk"), None),
            P(("dp", "blk"), None),
            P(("dp", "blk"), None),
            P(None, ("dp", "blk")),
        ),
        out_specs=(
            P("dp", "blk", None),
            P("dp", "blk", None),
            P(("dp", "blk"), None),
            P(("dp", "blk"), None),
            P(("dp", "blk"), None),
            P(("dp", "blk"), None),
            P(None, ("dp", "blk")),
            P(("dp", "blk"), None),
            P(("dp", "blk"), None),
            P(("dp", "blk"), None),
            P(("dp", "blk"), None),
            P(None, ("dp", "blk")),
            P(("dp", "blk"), None),
            P(("dp", "blk"), None),
            P(("dp", "blk"), None),
            P(("dp", "blk"), None),
            P(None, ("dp", "blk")),
            P(("dp", "blk"), None),
            P(("dp", "blk"), None),
            P(("dp", "blk"), None),
            P(("dp", "blk"), None),
            P(None, ("dp", "blk")),
            P(("dp", "blk"), None),
            P(("dp", "blk"), None),
            P(("dp", "blk"), None),
            P(("dp", "blk"), None),
            P(None, ("dp", "blk")),
        ),
        check_vma=False,
    )
```

```python
import functools
import math

import jax
import jax.numpy as jnp
from jax import lax
from jax.experimental import pallas as pl
from jax.experimental.pallas import tpu as pltpu
from jax.sharding import PartitionSpec as P

D = 768
HEADS = 12
HEAD_DIM = 64


def layer_norm(value, gain, shift):
    mean = jnp.mean(value, axis=-1, keepdims=True)
    cent = value - mean
    var = jnp.mean(cent * cent, axis=-1, keepdims=True)
    return cent * lax.rsqrt(var + 1e-06) * (1.0 + gain) + shift


def gelu_exact(value):
    return jax.nn.gelu(value, approximate=False)


def contract_tokens(left, right):
    return lax.dot_general(
        left.reshape(-1, left.shape[-1]),
        right.reshape(-1, right.shape[-1]),
        (((0,), (0,)), ((), ())),
        preferred_element_type=jnp.float32,
    )


def times_transpose(left, weight):
    return lax.dot_general(
        left, weight, (((left.ndim - 1,), (1,)), ((), ())), preferred_element_type=jnp.float32
    )


def group_size(rows, block):
    limit = max(1, 512 // block)
    best = 1
    for cand in range(1, rows + 1):
        if rows % cand == 0 and cand <= limit:
            best = cand
    return best


def scores_of(query, keys, seg_query, seg_keys):
    scores = jnp.einsum(
        "gqhd,gkhd->ghqk", query, keys, preferred_element_type=jnp.float32
    ) * HEAD_DIM ** (-0.5)
    allowed = (seg_query[:, :, None] == seg_keys[:, None, :])[:, None]
    return (scores, allowed)


def attend_back(query, kv_all, grad_out, seg_query, segments, group):
    rows, block = (query.shape[0], query.shape[1])
    length = kv_all.shape[1]
    keys = kv_all[0:group, :, :D].reshape(group, length, HEADS, HEAD_DIM)
    values = kv_all[0:group, :, D:].reshape(group, length, HEADS, HEAD_DIM)
    scores, allowed = scores_of(query, keys, seg_query, segments)
    probs = jax.nn.softmax(jnp.where(allowed, scores, -1e30), axis=-1)
    probs_low = probs.astype(jnp.bfloat16)
    prob_grad = jnp.einsum("gqhd,gkhd->ghqk", grad_out, values, preferred_element_type=jnp.float32)
    score_grad = probs * (prob_grad - jnp.sum(probs * prob_grad, axis=-1, keepdims=True))
    score_low = score_grad.astype(jnp.bfloat16)
    dq_part = jnp.einsum(
        "ghqk,gkhd->gqhd", score_low, keys, preferred_element_type=jnp.float32
    ) * HEAD_DIM ** (-0.5)
    dk_part = jnp.einsum(
        "ghqk,gqhd->gkhd", score_low, query, preferred_element_type=jnp.float32
    ) * HEAD_DIM ** (-0.5)
    dv_part = jnp.einsum("ghqk,gqhd->gkhd", probs_low, grad_out, preferred_element_type=jnp.float32)
    dq_parts = dq_part.reshape(group, block, D)
    dkv_parts = jnp.concatenate(
        [dk_part.reshape(group, length, D), dv_part.reshape(group, length, D)], axis=-1
    )
    return (dq_parts, dkv_parts)


def update(weight, grad, velocity, average, rate):
    step_value = grad + 0.0005 * weight
    velocity_new = 0.9 * velocity + step_value
    weight_new = weight - rate * (step_value + 0.9 * velocity_new)
    average_new = 0.9 * average + 0.1 * weight_new
    return (weight_new, velocity_new, average_new)


def on_device(
    tokens,
    segments,
    cotangent,
    qkv_weight,
    proj_weight,
    up_weight,
    down_weight,
    vec_params,
    qkv_velocity,
    proj_velocity,
    up_velocity,
    down_velocity,
    vec_velocity,
    qkv_average,
    proj_average,
    up_average,
    down_average,
    vec_average,
):
    rows, block = (tokens.shape[0], tokens.shape[1])
    length = segments.shape[1]
    total_tokens = rows * lax.axis_size("dp") * length
    rate = 0.05 / math.sqrt(total_tokens)
    group = group_size(rows, block)
    gathered = (
        lax.all_gather(qkv_weight.astype(jnp.bfloat16), ("dp", "blk"), axis=0, tiled=True),
        lax.all_gather(proj_weight.astype(jnp.bfloat16), ("dp", "blk"), axis=0, tiled=True),
        lax.all_gather(up_weight.astype(jnp.bfloat16), ("dp", "blk"), axis=0, tiled=True),
        lax.all_gather(down_weight.astype(jnp.bfloat16), ("dp", "blk"), axis=0, tiled=True),
        lax.all_gather(vec_params.astype(jnp.bfloat16), ("dp", "blk"), axis=1, tiled=True),
    )
    w_query, w_proj, w_up, w_down, vec_low = gathered
    vec = vec_low.astype(jnp.float32)
    bias_up = vec[8:12].reshape(-1)
    position = lax.axis_index("blk")
    seg_query = lax.dynamic_slice_in_dim(segments, position * block, block, 1)
    inputs = tokens.astype(jnp.float32)
    a_one = layer_norm(inputs, vec[0], vec[1]).astype(jnp.bfloat16)
    zero_bias = jnp.zeros_like(vec[2])
    pre = jnp.dot(a_one, w_query, preferred_element_type=jnp.float32) + jnp.concatenate(
        [vec[2], zero_bias, vec[3]]
    )
    qkv = pre.astype(jnp.bfloat16)
    query = qkv[..., :D].reshape(rows, block, HEADS, HEAD_DIM)
    key_value = qkv[..., D:]
    piece = lax.all_gather(key_value, "blk", axis=1, tiled=True)
    top = jnp.full((rows, HEADS, block), -1e30, jnp.float32)
    count = piece.shape[1]
    keys = piece[0:group, :, :D].reshape(group, count, HEADS, HEAD_DIM)
    values = piece[0:group, :, D:].reshape(group, count, HEADS, HEAD_DIM)
    scores, allowed = scores_of(query, keys, seg_query, segments)
    scores = jnp.where(allowed, scores, -1e30)
    new_top = jnp.maximum(top, jnp.max(scores, axis=-1))
    weights = jnp.where(allowed, jnp.exp(scores - new_top[..., None]), 0.0)
    denoms = jnp.sum(weights, axis=-1)
    added = jnp.einsum(
        "ghqk,gkhd->gqhd", weights.astype(jnp.bfloat16), values, preferred_element_type=jnp.float32
    )
    mixed = (added / jnp.transpose(denoms, (0, 2, 1))[..., None]).reshape(rows, block, D)
    mixed_low = mixed.astype(jnp.bfloat16)
    second = inputs + jnp.dot(mixed_low, w_proj, preferred_element_type=jnp.float32) + vec[4]
    second_norm, norm_two_back = jax.vjp(layer_norm, second, vec[5], vec[6])
    a_two = second_norm.astype(jnp.bfloat16)
    hidden = jnp.dot(a_two, w_up, preferred_element_type=jnp.float32) + bias_up
    act_value, gelu_back = jax.vjp(gelu_exact, hidden)
    act = act_value.astype(jnp.bfloat16)
    result = second + jnp.dot(act, w_down, preferred_element_type=jnp.float32) + vec[7]
    output = result.astype(jnp.bfloat16)
    out_grad = cotangent.astype(jnp.float32)
    grad_down = contract_tokens(act, cotangent)
    bias_down_grad = jnp.sum(out_grad, axis=(0, 1))
    act_grad = times_transpose(cotangent, w_down)
    hidden_grad = gelu_back(act_grad)[0].astype(jnp.bfloat16)
    bias_up_grad = jnp.sum(hidden_grad.astype(jnp.float32), axis=(0, 1))
    grad_up = contract_tokens(a_two, hidden_grad)
    a_two_grad = times_transpose(hidden_grad, w_up)
    second_part, gain_two_grad, shift_two_grad = norm_two_back(a_two_grad)
    second_grad = out_grad + second_part
    attn_grad = second_grad.astype(jnp.bfloat16)
    bias_proj_grad = jnp.sum(attn_grad.astype(jnp.float32), axis=(0, 1))
    grad_proj = contract_tokens(mixed_low, attn_grad)
    mixed_grad = (
        times_transpose(attn_grad, w_proj)
        .astype(jnp.bfloat16)
        .reshape(rows, block, HEADS, HEAD_DIM)
    )
    kv_again = lax.all_gather(key_value, "blk", axis=1, tiled=True)
    query_grad, kv_terms = attend_back(query, kv_again, mixed_grad, seg_query, segments, group)
    kv_grad = lax.psum_scatter(
        kv_terms.astype(jnp.bfloat16), "blk", scatter_dimension=1, tiled=True
    ).astype(jnp.float32)
    qkv_grad_low = jnp.concatenate([query_grad, kv_grad], axis=-1).astype(jnp.bfloat16)
    qkv_sums = jnp.sum(qkv_grad_low.astype(jnp.float32), axis=(0, 1))
    grad_query = contract_tokens(a_one, qkv_grad_low)
    a_one_grad = times_transpose(qkv_grad_low, w_query)
    norm_one_back = jax.vjp(layer_norm, inputs, vec[0], vec[1])[1]
    first_part, gain_one_grad, shift_one_grad = norm_one_back(a_one_grad)
    tokens_grad = (second_grad + first_part).astype(jnp.bfloat16)
    vec_local = jnp.concatenate(
        [
            jnp.stack(
                [
                    gain_one_grad,
                    shift_one_grad,
                    qkv_sums[:D],
                    qkv_sums[2 * D :],
                    bias_proj_grad,
                    gain_two_grad,
                    shift_two_grad,
                    bias_down_grad,
                ]
            ),
            bias_up_grad.reshape(4, D),
        ],
        axis=0,
    )
    query_share, proj_share, up_share, down_share, vec_share = (
        lax.psum_scatter(grad_query, ("dp", "blk"), scatter_dimension=0, tiled=True),
        lax.psum_scatter(grad_proj, ("dp", "blk"), scatter_dimension=0, tiled=True),
        lax.psum_scatter(grad_up, ("dp", "blk"), scatter_dimension=0, tiled=True),
        lax.psum_scatter(grad_down, ("dp", "blk"), scatter_dimension=0, tiled=True),
        lax.psum_scatter(vec_local, ("dp", "blk"), scatter_dimension=1, tiled=True),
    )
    qkv_new = update(qkv_weight, query_share, qkv_velocity, qkv_average, rate)
    proj_new = update(proj_weight, proj_share, proj_velocity, proj_average, rate)
    up_new = update(up_weight, up_share, up_velocity, up_average, rate)
    down_new = update(down_weight, down_share, down_velocity, down_average, rate)
    vec_new = update(vec_params, vec_share, vec_velocity, vec_average, rate)
    return (
        output,
        tokens_grad,
        query_share,
        proj_share,
        up_share,
        down_share,
        vec_share,
        qkv_new[0],
        proj_new[0],
        up_new[0],
        down_new[0],
        vec_new[0],
        qkv_new[1],
        proj_new[1],
        up_new[1],
        down_new[1],
        vec_new[1],
        qkv_new[2],
        proj_new[2],
        up_new[2],
        down_new[2],
        vec_new[2],
        qkv_new[0].astype(jnp.bfloat16),
        proj_new[0].astype(jnp.bfloat16),
        up_new[0].astype(jnp.bfloat16),
        down_new[0].astype(jnp.bfloat16),
        vec_new[0].astype(jnp.bfloat16),
    )


PIECE = (48, 384)
NP = 12
Z, Y, X, C = 4, 2, 2, 2
AHEAD = 2
TILE = 128
IMG_MAX = 198
REACH = (IMG_MAX - 1 + 15) // 16 * 16
SPAN = TILE + 2 * REACH
GATHER_SPLIT = ((0, NP, 2),)
PAIRS = HEADS // 2
MESH = pl.DeviceIdType.MESH
F32, BF16 = jnp.float32, jnp.bfloat16
NT = (((1,), (1,)), ((), ()))
TN = (((0,), (0,)), ((), ()))


def place():
    d, x = lax.axis_index("dp"), lax.axis_index("blk")
    return d // (2 * Y), (d // 2) % Y, d % 2, x


def ident(z, y, c, x):
    return ((z * Y + y) * 2 + c, x)


def greet(z, y, c, x):
    barrier = pltpu.get_barrier_semaphore()
    peers = [ident((z + k) % Z, y, c, x) for k in range(1, Z)]
    peers += [ident(z, 1 - y, c, x), ident(z, y, c, 1 - x), ident(z, y, 1 - c, x)]
    for peer in peers:
        pl.semaphore_signal(barrier, inc=1, device_id=peer, device_id_type=MESH)
    pl.semaphore_wait(barrier, len(peers))


def remote(src, dst, send, recv, peer):
    return pltpu.make_async_remote_copy(
        src_ref=src, dst_ref=dst, send_sem=send, recv_sem=recv, device_id=peer, device_id_type=MESH
    )


def begin(copies):
    for copy in copies:
        copy.start()


def arrive(copies):
    for copy in copies:
        copy.wait_recv()


def within(index, low, high, run):
    if isinstance(index, int):
        if low <= index < high:
            run()
    else:
        pl.when(jnp.logical_and(index >= low, index < high))(run)


def loop(count, body):
    def step(i, carry):
        body(i)
        return carry

    lax.fori_loop(0, count, step, 0)


def cols(j, width):
    return pl.ds(pl.multiple_of(j * width, width), width)


def dot(a, b, dims=None):
    dims = (((1,), (0,)), ((), ())) if dims is None else dims
    return lax.dot_general(a, b, dims, preferred_element_type=F32)


class Vec:
    def __init__(self, at, now, got, send, recv):
        self.at, self.now, self.got, self.send, self.recv = at, now, got, send, recv

    def copies(self, step):
        z, y, c, x = self.at
        peers = [
            [ident(z, y, 1 - c, x)],
            [ident(z, y, c, 1 - x)],
            [ident(z, 1 - y, c, x)],
            [ident((z + k) % Z, y, c, x) for k in range(1, Z)],
        ][step]
        return [
            remote(self.now.at[step], self.got.at[step + k], self.send.at[step + k], self.recv.at[step + k], peer)
            for k, peer in enumerate(peers)
        ]

    def begin(self, step):
        begin(self.copies(step))

    def total(self, step):
        copies = self.copies(step)
        arrive(copies)
        total = self.now[step]
        for k in range(len(copies)):
            total = total + self.got[step + k]
        return total

    def sent(self):
        for step in range(4):
            for copy in self.copies(step):
                copy.wait_send()


def normal(value):
    mean = jnp.mean(value, axis=-1, keepdims=True)
    cent = value - mean
    var = jnp.mean(cent * cent, axis=-1, keepdims=True)
    scale = lax.rsqrt(var + 1e-06)
    return cent * scale, scale


def window_start(i, x, tiles):
    near = tiles * TILE + REACH
    first = max(i * TILE - REACH, 0)
    count = min((i + 1) * TILE + REACH, near) - first
    start = jnp.where(x == 0, first, near - first - count)
    return jnp.where(x == 0, i, tiles - 1 - i), start, count


def window(i, x, tiles):
    tile, start, count = window_start(i, x, tiles)
    return tile, pl.ds(pl.multiple_of(start, 16), count), count


def mask_fill(seg, seg_col, bias, x, tiles):
    length = seg.shape[1]
    for k in range(length // TILE):
        row = seg[0:1, k * TILE : k * TILE + TILE].astype(F32)
        seg_col[k * TILE : k * TILE + TILE, :] = jnp.transpose(jnp.broadcast_to(row, (TILE, TILE)))
    for i in range(tiles):
        tile, start, count = window_start(i, x, tiles)
        start = start + x * (length - tiles * TILE - REACH)
        row = seg[0:1, pl.ds(pl.multiple_of((x * tiles + tile) * TILE, TILE), TILE)].astype(F32)
        column = seg_col[pl.ds(pl.multiple_of(start, 16), count), :]
        bias[i, 0:count] = jnp.where(column == row, 0.0, -1e30).astype(F32)


def split_heads(pair_block):
    lane = lax.broadcasted_iota(jnp.int32, pair_block.shape, 1)
    zero = jnp.zeros_like(pair_block)
    return jnp.concatenate(
        [jnp.where(lane < HEAD_DIM, pair_block, zero), jnp.where(lane < HEAD_DIM, zero, pair_block)], axis=0
    )


def join_heads(both):
    own = jnp.concatenate([both[:HEAD_DIM, :TILE], both[HEAD_DIM:, TILE:]], axis=0)
    return jnp.transpose(own)


def rows_from_stage(stage, target, t):
    left, right = cols(2 * t, 384), cols(2 * t + 1, 384)

    def group(g):
        parts = [stage[c, g % Y, x, g // Y].astype(F32) for c in range(C) for x in range(X)]
        rows = pl.ds(pl.multiple_of(g * 96, 96), 96)
        target[rows, left] = jnp.concatenate([p[:24] for p in parts], axis=0).astype(BF16)
        target[rows, right] = jnp.concatenate([p[24:] for p in parts], axis=0).astype(BF16)

    loop(Z * Y, group)


def down_copies(full, target, t, sem):
    half, col = (t - 8) % 2 * 48, (t - 8) // 2 * 384

    def group(g):
        for c in range(C):
            for x in range(X):
                row = pl.multiple_of(g * 384 + (c * X + x) * 96 + half, 16)
                pltpu.make_async_copy(
                    full.at[c, g % Y, x, g // Y, t], target.at[pl.ds(row, 48), col : col + 384], sem
                ).start()

    loop(Z * Y, group)


def qkv_columns(j, half):
    if half == 0:
        return (256 * j, 256), (D + 256 * j, 128)
    return (D + 256 * j + 128, 128), (2 * D + 256 * j, 256)


class Gather:
    def __init__(self, at, unit, full, own, send, recv):
        self.at, self.unit, self.full, self.own, self.send, self.recv = at, unit, full, own, send, recv

    def mine(self, t):
        z, y, c, x = self.at
        return pltpu.make_async_copy(self.unit.at[t], self.full.at[c, y, x, z, t], self.own.at[t])

    def first(self, t):
        z, y, c, x = self.at
        return [
            remote(
                self.unit.at[t], self.full.at[c, y, x, z, t], self.send.at[t, k - 1], self.recv.at[t, k - 1],
                ident((z + k) % Z, y, c, x),
            )
            for k in range(1, Z)
        ]

    def second(self, t, low):
        z, y, c, x = self.at
        one, two = self.full.at[c, y, x, 0:low, t], self.full.at[c, y, x, low:Z, t]
        return [
            remote(one, one, self.send.at[t, 3], self.recv.at[t, 3], ident(z, y, c, 1 - x)),
            remote(two, two, self.send.at[t, 4], self.recv.at[t, 4], ident(z, 1 - y, c, x)),
        ]

    def third(self, t, low):
        z, y, c, x = self.at
        one, two = self.full.at[c, y, :, 0:low, t], self.full.at[c, :, x, low:Z, t]
        return [
            remote(one, one, self.send.at[t, 5], self.recv.at[t, 5], ident(z, 1 - y, c, x)),
            remote(two, two, self.send.at[t, 6], self.recv.at[t, 6], ident(z, y, c, 1 - x)),
        ]

    def last(self, t):
        z, y, c, x = self.at
        block = self.full.at[c, :, :, :, t]
        return [remote(block, block, self.send.at[t, 7], self.recv.at[t, 7], ident(z, y, 1 - c, x))]

    def start(self):
        loop(NP, lambda t: self.mine(t).start())
        loop(AHEAD, lambda t: begin(self.first(t)))

    def progress(self, i):
        def to_second(t, low):
            self.mine(t).wait()
            arrive(self.first(t))
            begin(self.second(t, low))

        def to_third(t, low):
            arrive(self.second(t, low))
            begin(self.third(t, low))

        def to_last(t, low):
            arrive(self.third(t, low))
            begin(self.last(t))

        for first, end, low in GATHER_SPLIT:
            within(i, first, end, lambda: to_second(i, low))
        for first, end, low in GATHER_SPLIT:
            within(i - 1, first, end, lambda: to_third(i - 1, low))
        for first, end, low in GATHER_SPLIT:
            within(i - 2, first, end, lambda: to_last(i - 2, low))
        within(i + AHEAD, AHEAD, NP, lambda: begin(self.first(i + AHEAD)))

    def sent(self):
        for first, end, low in GATHER_SPLIT:
            def one(t):
                for copy in self.first(t) + self.second(t, low) + self.third(t, low) + self.last(t):
                    copy.wait_send()

            lax.fori_loop(first, end, lambda t, carry: (one(t), carry)[1], 0)


def forward_kernel(
    w_qkv, w_proj, w_up, w_down, vec_in, tok, dy, seg,
    full, vec_out, out_o, q_o, k_o, v_o, o_o, stat_o, x2_o, a2_o, z_o, slope_o, grad_o, bias_o,
    unit, seg_col, near, a1, wbig, wdown, stage, vecf, bias, out_s, q_s, k_s, v_s, o_s, stat_s, x2_s, a2_s, z_s, slope_s, got,
    local, vec_now, vec_got, own, send, recv, vsend, vrecv, hsem, ssem, dsem, osem, gsend, grecv,
):
    z, y, c, x = at = place()
    block = tok.shape[0]
    tiles = block // TILE
    offset = pl.multiple_of(x * REACH, 16)
    vec_now[0] = vec_in[...]

    def pack(t, weight, j):
        left, right = weight[:, j * 768 : j * 768 + 384], weight[:, j * 768 + 384 : j * 768 + 768]
        unit[t] = jnp.concatenate([left, right], axis=0).astype(BF16)

    for j in range(3):
        sides = []
        for half in range(2):
            parts = [w_qkv[:, start : start + width] for start, width in qkv_columns(j, half)]
            sides.append(jnp.concatenate(parts, axis=1))
        unit[j] = jnp.concatenate(sides, axis=0).astype(BF16)
    pack(3, w_proj, 0)
    for j in range(4):
        pack(4 + j, w_up, j)
        unit[8 + j] = w_down[j % 2 * 48 : j % 2 * 48 + 48, j // 2 * 384 : j // 2 * 384 + 384].astype(BF16)
    greet(*at)
    gather = Gather(at, unit, full, own, send, recv)
    gather.start()
    vec = Vec(at, vec_now, vec_got, vsend, vrecv)
    vec.begin(0)
    away = pl.multiple_of((1 - x) * (block - REACH), 16)
    land = pl.multiple_of(x * block, 16)
    halo = remote(
        tok.at[pl.ds(away, REACH)], near.at[pl.ds(land, REACH)], hsem.at[0], hsem.at[1], ident(z, y, c, 1 - x)
    )
    halo.start()
    near[pl.ds(offset, block), :] = tok[...]

    def put(k, src, dst):
        return pltpu.make_async_copy(src, dst, osem.at[k])

    def vec_step(step):
        total = vec.total(step)
        if step < 3:
            vec_now[step + 1] = total
            vec.begin(step + 1)
        else:
            vec_out[...] = total
            vecf[...] = total.astype(F32)

    def staged(t):
        return pltpu.make_async_copy(full.at[:, :, :, :, t], stage.at[t % 4], ssem.at[t % 4])

    def fetch(t):
        arrive(gather.last(t))
        staged(t).start()

    def take(t):
        staged(t).wait()
        rows_from_stage(stage.at[t % 4], wbig, t)

    def down_start(t):
        arrive(gather.last(t))
        down_copies(full, wdown, t, dsem.at[t - 8])

    def down_wait(t):
        pltpu.make_async_copy(full.at[:, :, :, :, t], stage.at[0], dsem.at[t - 8]).wait()

    gather.progress(0)
    vec_step(0)
    gather.progress(1)
    vec_step(1)
    gather.progress(2)
    vec_step(2)
    vec_step(3)
    halo.wait_recv()

    def norm_one(i):
        rows = cols(i, 240)
        value = normal(near[rows, :].astype(F32))[0]
        a1[rows, :] = (value * (1.0 + vecf[0:1, :]) + vecf[1:2, :]).astype(BF16)

    loop(near.shape[0] // 240, norm_one)
    mask_fill(seg, seg_col, bias, x, tiles)
    put(11, bias, bias_o).start()
    def attend(pair):
        lanes = cols(pair, 128)

        for i in range(tiles):
            tile, span, count = window(i, x, tiles)
            rows = cols(tile, TILE)
            both = split_heads(q_s[rows, lanes])
            fill = bias[i, 0:count]
            scores = dot(k_s[span, lanes], both, NT) + jnp.concatenate([fill, fill], axis=1)
            top = jnp.max(scores, axis=0, keepdims=True)
            weights = jnp.exp(scores - top)
            total = jnp.sum(weights, axis=0, keepdims=True)
            mixed = dot(v_s[span, lanes], weights.astype(BF16), TN) / total
            o_s[rows, lanes] = join_heads(mixed).astype(BF16)
            stat_s[pair * tiles + i] = jnp.broadcast_to(top + jnp.log(total), (8, 2 * TILE))

    def third(j):
        fetch(j)
        gather.progress(3 + 2 * j)
        take(j)
        where = cols(j, 256)
        value = dot(a1[pl.ds(offset, block), :], wbig[:, cols(3 * j, 256)]) + vecf[2:3, where]
        q_s[:, where] = value.astype(BF16) * HEAD_DIM ** (-0.5)
        k_s[:, where] = dot(a1[...], wbig[:, cols(3 * j + 1, 256)]).astype(BF16)
        v_s[:, where] = (dot(a1[...], wbig[:, cols(3 * j + 2, 256)]) + vecf[3:4, where]).astype(BF16)
        attend(2 * j)
        gather.progress(4 + 2 * j)
        attend(2 * j + 1)

    loop(3, third)
    put(0, k_s, k_o).start()
    put(1, v_s, v_o).start()
    put(2, q_s, q_o).start()
    put(3, o_s, o_o).start()
    put(4, stat_s, stat_o).start()
    fetch(3)
    take(3)
    fetch(4)
    fetch(5)
    gather.progress(9)

    def project(j):
        value = dot(o_s[...], wbig[:, cols(j + 9, 256)])
        x2_s[:, cols(j, 256)] = tok[:, cols(j, 256)].astype(F32) + value + vecf[4:5, cols(j, 256)]

    loop(3, project)

    def norm_two(i):
        rows = pl.ds(pl.multiple_of(i * 256, 256), 256)
        value = normal(x2_s[rows, :])[0]
        a2_s[rows, :] = (value * (1.0 + vecf[5:6, :]) + vecf[6:7, :]).astype(BF16)

    loop(block // 256, norm_two)
    put(5, x2_s, x2_o).start()
    put(6, a2_s, a2_o).start()
    gather.progress(10)
    take(4)
    take(5)
    fetch(6)
    fetch(7)

    def expand(j):
        u = dot(a2_s[...], wbig[:, cols(j + 12, 256)])
        u = u + vecf[pl.ds(8 + j // 3, 1), pl.ds(pl.multiple_of((j % 3) * 256, 256), 256)]
        half = 0.5 + 0.5 * lax.erf(u * math.sqrt(0.5))
        z_s[:, cols(j, 256)] = (u * half).astype(BF16)
        slope = half + u * (jnp.exp(-0.5 * u * u) * (1.0 / math.sqrt(2.0 * math.pi)))
        slope_s[:, cols(j, 256)] = slope.astype(BF16)

    loop(5, expand)
    gather.progress(11)
    take(6)
    take(7)
    loop(5, lambda j: expand(j + 5))
    gather.progress(12)
    down_start(8)
    loop(2, lambda j: expand(j + 10))
    put(7, z_s, z_o).start()
    put(8, slope_s, slope_o).start()

    def core(t):
        peer = ident(z, y, 1 - c, x)
        return remote(local.at[1 - c, :, :, :, t], got.at[t], gsend.at[t], grecv.at[t], peer)

    for half in range(2):
        def down_grad(g):
            value = dot(z_s[:, cols(g, 384)], dy[:, half * 384 : half * 384 + 384], TN).astype(BF16)
            for k in range(4):
                for row in range(2):
                    part = value[k * 96 + row * 48 : k * 96 + row * 48 + 48]
                    local[k // 2, g % Y, k % 2, g // Y, 2 * half + row] = part

        loop(Z * Y, down_grad)
        core(2 * half).start()
        core(2 * half + 1).start()
        if half == 0:
            gather.progress(13)
            down_start(9)
    down_start(10)

    def contract(half):
        col = slice(half * 384, half * 384 + 384)
        value = dot(z_s[...], wdown[:, col])
        out_s[:, col] = (x2_s[:, col] + value + vecf[7:8, col]).astype(BF16)

    def gain(t):
        core(t).wait_recv()
        for a in range(Y):
            for b in range(X):
                own_part = local[c, a, b, :, t].astype(F32)
                got[t, a, b] = (own_part + got[t, a, b].astype(F32)).astype(BF16)

    loop(4, gain)
    put(10, got, grad_o).start()
    down_wait(8)
    down_wait(9)
    contract(0)
    down_start(11)
    down_wait(10)
    down_wait(11)
    contract(1)
    put(9, out_s, out_o).start()
    pairs = [(k_s, k_o), (v_s, v_o), (q_s, q_o), (o_s, o_o), (stat_s, stat_o), (x2_s, x2_o), (a2_s, a2_o)]
    for k, (src, dst) in enumerate(pairs + [(z_s, z_o), (slope_s, slope_o), (out_s, out_o)]):
        put(k, src, dst).wait()
    put(10, got, grad_o).wait()
    put(11, bias, bias_o).wait()
    gather.sent()
    vec.sent()
    halo.wait_send()
    loop(4, lambda t: core(t).wait_send())


def forward_all(weights, vec_placed, tok, dy, seg):
    block = tok.shape[0]
    near = block + REACH
    ff = 4 * D
    tiles = block // TILE
    shapes = [
        ((block, D), BF16),
        ((block, D), BF16),
        ((near, D), BF16),
        ((near, D), BF16),
        ((block, D), BF16),
        ((PAIRS * tiles, 8, 2 * TILE), F32),
        ((block, D), F32),
        ((block, D), BF16),
        ((block, ff), BF16),
        ((block, ff), BF16),
        ((4, Y, X, Z) + PIECE, BF16),
        ((tiles, SPAN, TILE), F32),
    ]
    hbm, vmem = pl.BlockSpec(memory_space=pl.ANY), pl.BlockSpec(memory_space=pltpu.VMEM)
    outs = [((C, Y, X, Z, NP) + PIECE, BF16), (vec_placed.shape, BF16)] + shapes
    return pl.pallas_call(
        forward_kernel,
        out_shape=tuple(jax.ShapeDtypeStruct(*one) for one in outs),
        in_specs=[vmem] * 8,
        out_specs=tuple([hbm, vmem] + [hbm] * len(shapes)),
        scratch_shapes=[
            pltpu.VMEM((NP,) + PIECE, BF16),
            pltpu.VMEM((seg.shape[1], TILE), F32),
            pltpu.VMEM((near, D), BF16),
            pltpu.VMEM((near, D), BF16),
            pltpu.VMEM((D, 8 * D), BF16),
            pltpu.VMEM((ff, D), BF16),
            pltpu.VMEM((4, C, Y, X, Z) + PIECE, BF16),
            pltpu.VMEM(vec_placed.shape, F32),
            *[pltpu.VMEM(*one) for one in shapes[-1:] + shapes[:-1]],
            pltpu.VMEM((C, Y, X, Z, 4) + PIECE, BF16),
            pltpu.VMEM((4,) + vec_placed.shape, BF16),
            pltpu.VMEM((6,) + vec_placed.shape, BF16),
            pltpu.SemaphoreType.DMA((NP,)),
            pltpu.SemaphoreType.DMA((NP, 8)),
            pltpu.SemaphoreType.DMA((NP, 8)),
            pltpu.SemaphoreType.DMA((6,)),
            pltpu.SemaphoreType.DMA((6,)),
            pltpu.SemaphoreType.DMA((2,)),
            pltpu.SemaphoreType.DMA((4,)),
            pltpu.SemaphoreType.DMA((4,)),
            pltpu.SemaphoreType.DMA((12,)),
            pltpu.SemaphoreType.DMA((4,)),
            pltpu.SemaphoreType.DMA((4,)),
        ],
        compiler_params=pltpu.CompilerParams(
            collective_id=0, has_side_effects=True, vmem_limit_bytes=60 << 20
        ),
        name="forward_all",
    )(*weights, vec_placed, tok, dy, seg)


SCATTER_SPLIT = ((0, NP, 2),)


class Scatter:
    def __init__(self, at, local, got_core, got_two, got_one, got_z, out, send, recv):
        self.at, self.local, self.out, self.send, self.recv = at, local, out, send, recv
        self.got = got_core, got_two, got_one, got_z

    def core(self, t):
        z, y, c, x = self.at
        peer = ident(z, y, 1 - c, x)
        return [remote(self.local.at[1 - c, :, :, :, t], self.got[0].at[t - 4], self.send.at[t, 0], self.recv.at[t, 0], peer)]

    def two(self, t, low):
        z, y, c, x = self.at
        one, other = self.local.at[c, 1 - y, :, 0:low, t], self.local.at[c, :, 1 - x, low:Z, t]
        got = self.got[1].at[t]
        return [
            remote(one, got.at[:, 0:low], self.send.at[t, 1], self.recv.at[t, 1], ident(z, 1 - y, c, x)),
            remote(other, got.at[:, low:Z], self.send.at[t, 2], self.recv.at[t, 2], ident(z, y, c, 1 - x)),
        ]

    def one(self, t, low):
        z, y, c, x = self.at
        one, other = self.local.at[c, y, 1 - x, 0:low, t], self.local.at[c, 1 - y, x, low:Z, t]
        got = self.got[2].at[t]
        return [
            remote(one, got.at[0:low], self.send.at[t, 3], self.recv.at[t, 3], ident(z, y, c, 1 - x)),
            remote(other, got.at[low:Z], self.send.at[t, 4], self.recv.at[t, 4], ident(z, 1 - y, c, x)),
        ]

    def along(self, t):
        z, y, c, x = self.at
        return [
            remote(
                self.local.at[c, y, x, (z + k) % Z, t], self.got[3].at[t, k - 1], self.send.at[t, 4 + k],
                self.recv.at[t, 4 + k], ident((z + k) % Z, y, c, x),
            )
            for k in range(1, Z)
        ]

    def add(self, where, value):
        self.local[where] = (self.local[where].astype(F32) + value.astype(F32)).astype(BF16)

    def take_core(self, t):
        c = self.at[2]
        arrive(self.core(t))
        for a in range(Y):
            for b in range(X):
                self.add((c, a, b, slice(None), t), self.got[0][t - 4, a, b])

    def after_core(self, t):
        self.take_core(t)
        self.go_two(t)

    def after_two(self, t, low):
        z, y, c, x = self.at
        arrive(self.two(t, low))
        for b in range(2):
            self.add((c, y, b, slice(0, low), t), self.got[1][t, b, 0:low])
            self.add((c, b, x, slice(low, Z), t), self.got[1][t, b, low:Z])
        begin(self.one(t, low))

    def after_one(self, t, low):
        z, y, c, x = self.at
        arrive(self.one(t, low))
        self.add((c, y, x, slice(None), t), self.got[2][t])
        begin(self.along(t))

    def after_z(self, t):
        z, y, c, x = self.at
        arrive(self.along(t))
        total = self.local[c, y, x, z, t].astype(F32)
        for k in range(Z - 1):
            total = total + self.got[3][t, k].astype(F32)
        self.out[t] = total

    def go_two(self, t):
        for first, end, low in SCATTER_SPLIT:
            within(t, first, end, lambda: begin(self.two(t, low)))

    def go_one(self, t):
        for first, end, low in SCATTER_SPLIT:
            within(t, first, end, lambda: self.after_two(t, low))

    def go_z(self, t):
        arrive_one = self.after_one
        for first, end, low in SCATTER_SPLIT:
            within(t, first, end, lambda: arrive_one(t, low))

    def sent(self):
        loop(NP - 4, lambda t: self.core(t + 4)[0].wait_send())
        for first, end, low in SCATTER_SPLIT:
            def each(t):
                for copy in self.two(t, low) + self.one(t, low) + self.along(t):
                    copy.wait_send()

            lax.fori_loop(first, end, lambda t, carry: (each(t), carry)[1], 0)


def total_rows(value):
    return jnp.sum(value.astype(F32), axis=0, keepdims=True)


def norm_back(value, grad, gain):
    unit_value, scale = normal(value)
    inner = grad * (1.0 + gain)
    mean_one = jnp.mean(inner, axis=-1, keepdims=True)
    mean_two = jnp.mean(inner * unit_value, axis=-1, keepdims=True)
    back = scale * (inner - mean_one - unit_value * mean_two)
    return back, total_rows(grad * unit_value), total_rows(grad)


def backward_kernel(
    full, vec_in, tok_o, dy_o, grad_o, bias_o, q_o, k_o, v_o, o_o, stat_o, x2_o, a2_o, slope_o,
    out, vec_out, tok_grad,
    local, got_core, got_two, got_one, got_z, wbuf, stage, bias, vecf, tok, dy, q_s, k_s, v_s, o_s, stat_s, x2_s, a2_s, z_s,
    slope_s, dx, da, acc_k, acc_v, halo_s, halo_r, vec_now, vec_got, send, recv, vsend, vrecv, hsend, hrecv, isem, ssem, dsem, gsem,
):
    z, y, c, x = at = place()
    block = tok.shape[0]
    tiles = block // TILE
    offset = pl.multiple_of(x * REACH, 16)
    away = pl.multiple_of((1 - x) * (block - REACH), 16)
    outside = pl.multiple_of((1 - x) * block, 16)
    order = [4, 5, 6, 7, 3, 0, 1, 2]

    def fetch(n):
        return pltpu.make_async_copy(full.at[:, :, :, :, order[n]], stage.at[n % 2], ssem.at[n % 2])

    def take(n, use):
        fetch(n).wait()
        use(stage.at[n % 2])
        if n + 2 < len(order):
            fetch(n + 2).start()

    pairs = [
        (dy_o, dy), (slope_o, slope_s), (a2_o, a2_s), (x2_o, x2_s), (o_o, o_s), (k_o, k_s), (v_o, v_s), (q_o, q_s),
        (stat_o, stat_s), (tok_o, tok), (bias_o, bias),
    ]

    def inward(k):
        return pltpu.make_async_copy(pairs[k][0], pairs[k][1], isem.at[k])

    def grads(t):
        return pltpu.make_async_copy(grad_o.at[t], local.at[c, :, :, :, t], gsem.at[t])

    for t in range(4):
        grads(t).start()
    inward(0).start()
    for t in range(8, 12):
        down_copies(full, wbuf, t, dsem.at[t - 8])
    for n in range(2):
        fetch(n).start()
    for k in range(1, len(pairs)):
        inward(k).start()
    greet(*at)
    scatter = Scatter(at, local, got_core, got_two, got_one, got_z, out, send, recv)
    vec = Vec(at, vec_now, vec_got, vsend, vrecv)
    vec_now[0] = jnp.zeros(vec_now.shape[1:], F32)
    vecf[...] = vec_in[...].astype(F32)

    def vec_step(step):
        total = vec.total(step)
        if step < 3:
            vec_now[step + 1] = total
            vec.begin(step + 1)
        else:
            vec_out[...] = total

    def gain_row(row, where, value):
        vec_now[0, row : row + 1, where] = vec_now[0, row : row + 1, where] + value

    def weight_grad(left, right, t):
        def half(h):
            value = dot(left[:, cols(h, 384)], right[...], TN)
            for g in range(4):
                for k in range(4):
                    part = value[g * 96 + k * 24 : g * 96 + k * 24 + 24]
                    part = jnp.concatenate([part[:, :384], part[:, 384:]], axis=0).astype(BF16)
                    local[k // 2, g % 2, k % 2, 2 * h + g // 2, t] = part

        loop(2, half)
        begin(scatter.core(t))

    for t in range(4):
        grads(t).wait()
        scatter.go_two(t)
    inward(0).wait()
    gain_row(7, slice(None), total_rows(dy[...]))
    for t in range(8, 12):
        pltpu.make_async_copy(full.at[:, :, :, :, t], stage.at[0], dsem.at[t - 8]).wait()
    inward(1).wait()

    def hidden(n):
        rows = pl.ds(pl.multiple_of(n * 256, 256), 256)
        grad = dot(dy[...], wbuf[rows, :], NT) * slope_s[:, cols(n, 256)].astype(F32)
        low = grad.astype(BF16)
        slope_s[:, cols(n, 256)] = low
        where = pl.ds(pl.multiple_of((n % 3) * 256, 256), 256)
        vec_now[0, pl.ds(8 + n // 3, 1), where] = total_rows(low)

    loop(12, hidden)
    scatter.go_one(0)
    inward(2).wait()
    for t in range(2):
        take(t, lambda part: rows_from_stage(part, wbuf.at[pl.ds(t * D, D)], 0))
    for t in range(4):
        weight_grad(a2_s, slope_s.at[:, t * D : t * D + D], 4 + t)
    scatter.go_one(1)
    scatter.go_one(2)
    for t in range(2, 4):
        take(t, lambda part: rows_from_stage(part, wbuf.at[pl.ds(t * D, D)], 0))

    def inner_grad(n):
        value = None
        for t in range(4):
            rows = pl.ds(pl.multiple_of(t * D + n * 256, 256), 256)
            part = dot(slope_s[:, t * D : t * D + D], wbuf[rows, :], NT)
            value = part if value is None else value + part
        dx[:, cols(n, 256)] = value

    loop(3, inner_grad)
    scatter.after_core(4)
    scatter.after_core(5)
    scatter.go_one(3)
    scatter.go_z(0)
    inward(3).wait()

    def norm_two(i):
        rows = cols(i, 128)
        grad = dx[rows, :]
        back, gain, shift = norm_back(x2_s[rows, :], grad, vecf[5:6, :])
        total = dy[rows, :].astype(F32) + back
        low = total.astype(BF16)
        dx[rows, :] = total
        da[rows, :] = low
        gain_row(5, slice(None), gain)
        gain_row(6, slice(None), shift)
        gain_row(4, slice(None), total_rows(low))

    loop(block // 128, norm_two)
    scatter.after_core(6)
    scatter.after_core(7)
    scatter.go_z(1)
    inward(4).wait()
    weight_grad(o_s, da, 8)
    take(4, lambda part: rows_from_stage(part, wbuf.at[pl.ds(3 * D, D)], 0))

    def mixed_grad(n):
        rows = pl.ds(pl.multiple_of(3 * D + n * 256, 256), 256)
        o_s[:, cols(n, 256)] = dot(da[...], wbuf[rows, :], NT).astype(BF16)

    loop(3, mixed_grad)
    scatter.after_core(8)
    for k in range(5, 11):
        inward(k).wait()

    def halo(pair):
        return remote(halo_s.at[pair], halo_r.at[pair], hsend.at[pair], hrecv.at[pair], ident(z, y, c, 1 - x))

    def spot(pair, kind):
        return pl.ds(pl.multiple_of(pair // 2 * D + kind * 256 + pair % 2 * 128, 128), 128)

    def attend(pair):
        lanes = cols(pair, 128)
        scatter.go_z(2 + pair)
        within(pair, 0, 5, lambda: scatter.go_one(4 + pair))
        scatter.after_z(pair)
        acc_k[...] = jnp.zeros(acc_k.shape, F32)
        acc_v[...] = jnp.zeros(acc_v.shape, F32)

        for i in range(tiles):
            tile, span, count = window(i, x, tiles)
            rows = cols(tile, TILE)
            both, grads = split_heads(q_s[rows, lanes]), split_heads(o_s[rows, lanes])
            fill = bias[i, 0:count]
            scores = dot(k_s[span, lanes], both, NT) + jnp.concatenate([fill, fill], axis=1)
            probs = jnp.exp(scores - stat_s[pair * tiles + i][0:1])
            low = probs.astype(BF16)
            back = dot(v_s[span, lanes], grads, NT)
            mean = jnp.sum(probs * back, axis=0, keepdims=True)
            inner = (probs * (back - mean)).astype(BF16)
            acc_v[span, :] = acc_v[span, :] + dot(low, grads)
            acc_k[span, :] = acc_k[span, :] + dot(inner, both)
            query = join_heads(dot(k_s[span, lanes], inner, TN)) * HEAD_DIM ** (-0.5)
            z_s[rows, spot(pair, 0)] = query.astype(BF16)

        for k, acc in ((0, acc_k), (1, acc_v)):
            z_s[:, spot(pair, k + 1)] = acc[pl.ds(offset, block), :].astype(BF16)
            halo_s[pair, k] = acc[pl.ds(outside, REACH), :].astype(BF16)
        halo(pair).start()

    def add_halo(pair):
        halo(pair).wait_recv()
        for k in range(2):
            where = spot(pair, k + 1)
            rows = pl.ds(away, REACH)
            z_s[rows, where] = (z_s[rows, where].astype(F32) + halo_r[pair, k].astype(F32)).astype(BF16)

    def finish(j):
        add_halo(2 * j)
        add_halo(2 * j + 1)
        weight_grad(a2_s, z_s.at[:, pl.ds(pl.multiple_of(j * D, D), D)], 9 + j)

    def norm_one(i):
        rows = cols(i, 128)
        value = normal(tok[rows, :].astype(F32))[0]
        a2_s[rows, :] = (value * (1.0 + vecf[0:1, :]) + vecf[1:2, :]).astype(BF16)

    loop(block // 128, norm_one)

    def third(j):
        loop(2, lambda i: attend(2 * j + i))
        within(j, 2, 3, lambda: scatter.after_core(9))
        within(j, 1, 3, lambda: finish(j - 1))

    loop(3, third)
    finish(2)
    scatter.after_core(10)
    scatter.go_z(8)
    scatter.after_core(11)
    for n in range(5, 8):
        take(n, lambda part: rows_from_stage(part, wbuf.at[pl.ds((n - 5) * D, D)], 0))

    def first_grad(n):
        value = None
        for t in range(3):
            rows = pl.ds(pl.multiple_of(t * D + n * 256, 256), 256)
            part = dot(z_s[:, t * D : t * D + D], wbuf[rows, :], NT)
            value = part if value is None else value + part
        x2_s[:, cols(n, 256)] = value

    loop(3, first_grad)
    scatter.go_one(9)
    for j in range(3):
        where = slice(j * 256, j * 256 + 256)
        gain_row(2, where, total_rows(z_s[:, j * D : j * D + 256]))
        gain_row(3, where, total_rows(z_s[:, j * D + 512 : j * D + 768]))

    def norm_first(i):
        rows = cols(i, 128)
        back, gain, shift = norm_back(tok[rows, :].astype(F32), x2_s[rows, :], vecf[0:1, :])
        tok_grad[rows, :] = (dx[rows, :] + back).astype(BF16)
        gain_row(0, slice(None), gain)
        gain_row(1, slice(None), shift)

    loop(block // 128, norm_first)
    vec.begin(0)
    scatter.go_one(10)
    scatter.go_z(9)
    scatter.after_z(6)
    vec_step(0)
    scatter.go_one(11)
    scatter.go_z(10)
    scatter.after_z(7)
    vec_step(1)
    scatter.go_z(11)
    scatter.after_z(8)
    vec_step(2)
    scatter.after_z(9)
    vec_step(3)
    scatter.after_z(10)
    scatter.after_z(11)
    scatter.sent()
    vec.sent()
    loop(PAIRS, lambda pair: halo(pair).wait_send())


def backward_all(full, vec_low, tok, dy, grad, fill, *saved):
    block = tok.shape[0]
    near = block + REACH
    tiles = block // TILE
    hbm, vmem = pl.BlockSpec(memory_space=pl.ANY), pl.BlockSpec(memory_space=pltpu.VMEM)
    vec_shape = vec_low.shape
    rows = (block, D)
    buffers = [
        ((C, Y, X, Z, NP) + PIECE, BF16),
        ((NP - 4, Y, X, Z) + PIECE, BF16),
        ((NP, 2, Z) + PIECE, BF16),
        ((NP, Z) + PIECE, BF16),
        ((NP, Z - 1) + PIECE, BF16),
        ((4 * D, D), BF16),
        ((2, C, Y, X, Z) + PIECE, BF16),
        ((tiles, SPAN, TILE), F32),
        (vec_shape, F32),
        (rows, BF16),
        (rows, BF16),
        *[(array.shape, array.dtype) for array in saved[:-1]],
        ((block, 3 * D), BF16),
        ((block, 4 * D), BF16),
        (rows, F32),
        (rows, BF16),
        ((near, 128), F32),
        ((near, 128), F32),
        ((PAIRS, 2, REACH, 128), BF16),
        ((PAIRS, 2, REACH, 128), BF16),
        ((4,) + vec_shape, F32),
        ((6,) + vec_shape, F32),
    ]
    semaphores = [(NP, 8), (NP, 8), (6,), (6,), (PAIRS,), (PAIRS,), (11,), (2,), (4,), (4,)]
    return pl.pallas_call(
        backward_kernel,
        out_shape=(
            jax.ShapeDtypeStruct((NP,) + PIECE, F32),
            jax.ShapeDtypeStruct(vec_shape, F32),
            jax.ShapeDtypeStruct(rows, BF16),
        ),
        in_specs=[hbm, vmem, hbm, hbm, hbm, hbm] + [hbm] * len(saved),
        out_specs=(vmem, vmem, vmem),
        scratch_shapes=[pltpu.VMEM(*one) for one in buffers] + [pltpu.SemaphoreType.DMA(one) for one in semaphores],
        compiler_params=pltpu.CompilerParams(
            collective_id=1, has_side_effects=True, vmem_limit_bytes=60 << 20
        ),
        name="backward_all",
    )(full, vec_low, tok, dy, grad, fill, *saved)


def update_kernel(rate, pieces, *refs):
    masters, velocities, averages, grads, news, moving, means, copies = [refs[k : k + 4] for k in range(0, 32, 4)]

    def one(k, rows, where, grad):
        new, velocity, average = update(
            masters[k][rows, where], grad, velocities[k][rows, where], averages[k][rows, where], rate
        )
        grads[k][rows, where] = grad
        news[k][rows, where] = new
        moving[k][rows, where] = velocity
        means[k][rows, where] = average

    for t in range(NP):
        piece = pieces[t]
        if t < 4:
            one(3, slice(t % 2 * 48, t % 2 * 48 + 48), slice(t // 2 * 384, t // 2 * 384 + 384), piece)
            continue
        k, j = (2, t - 4) if t < 8 else (1, 0)
        for half in range(2):
            if t > 8:
                part, col = piece[half * 24 : half * 24 + 24], 0
                for start, width in qkv_columns(t - 9, half):
                    one(0, slice(0, 24), slice(start, start + width), part[:, col : col + width])
                    col += width
                continue
            col = (2 * j + half) * 384
            one(k, slice(0, 24), slice(col, col + 384), piece[half * 24 : half * 24 + 24])
    for k in range(4):
        copies[k][...] = news[k][...].astype(BF16)


def update_all(rate, pieces, masters, velocities, averages):
    shapes = [jax.ShapeDtypeStruct(w.shape, F32) for w in masters] * 4
    shapes += [jax.ShapeDtypeStruct(w.shape, BF16) for w in masters]
    vmem = pl.BlockSpec(memory_space=pltpu.VMEM)
    return pl.pallas_call(
        functools.partial(update_kernel, rate),
        out_shape=tuple(shapes),
        in_specs=[vmem] * 13,
        out_specs=tuple([vmem] * 20),
        name="update_all",
    )(pieces, *masters, *velocities, *averages)


def on_device_fast(
    tokens,
    segments,
    cotangent,
    qkv_weight,
    proj_weight,
    up_weight,
    down_weight,
    vec_params,
    qkv_velocity,
    proj_velocity,
    up_velocity,
    down_velocity,
    vec_velocity,
    qkv_average,
    proj_average,
    up_average,
    down_average,
    vec_average,
):
    block = tokens.shape[1]
    total_tokens = lax.axis_size("dp") * segments.shape[1]
    rate = 0.05 / math.sqrt(total_tokens)
    position = lax.axis_index("blk")
    shard = lax.axis_index("dp") * lax.axis_size("blk") + position
    masters = (qkv_weight, proj_weight, up_weight, down_weight)
    vec_placed = lax.dynamic_update_slice(
        jnp.zeros((16, D), jnp.bfloat16), vec_params.astype(jnp.bfloat16), (0, shard * vec_params.shape[1])
    )
    full, vec_low, result, *saved, act, slope, down, fill = forward_all(
        masters, vec_placed, tokens[0], cotangent[0], segments
    )
    pieces, vec_sum, back = backward_all(full, vec_low, tokens[0], cotangent[0], down, fill, *saved, slope)
    output, tokens_grad = result[None], back[None]
    velocities = (qkv_velocity, proj_velocity, up_velocity, down_velocity)
    averages = (qkv_average, proj_average, up_average, down_average)
    done = update_all(rate, pieces, masters, velocities, averages)
    vec_share = lax.dynamic_slice(vec_sum, (0, shard * vec_params.shape[1]), vec_params.shape)
    vec_new = update(vec_params, vec_share, vec_velocity, vec_average, rate)
    return (
        output,
        tokens_grad,
        *done[0:4],
        vec_share,
        *done[4:8],
        vec_new[0],
        *done[8:12],
        vec_new[1],
        *done[12:16],
        vec_new[2],
        *done[16:20],
        vec_new[0].astype(jnp.bfloat16),
    )


def solution(mesh):
    fits = mesh.shape["dp"] == Z * Y * C and mesh.shape["blk"] == X
    return jax.shard_map(
        on_device_fast if fits else on_device,
        mesh=mesh,
        in_specs=(
            P("dp", "blk", None),
            P("dp", None),
            P("dp", "blk", None),
            P(("dp", "blk"), None),
            P(("dp", "blk"), None),
            P(("dp", "blk"), None),
            P(("dp", "blk"), None),
            P(None, ("dp", "blk")),
            P(("dp", "blk"), None),
            P(("dp", "blk"), None),
            P(("dp", "blk"), None),
            P(("dp", "blk"), None),
            P(None, ("dp", "blk")),
            P(("dp", "blk"), None),
            P(("dp", "blk"), None),
            P(("dp", "blk"), None),
            P(("dp", "blk"), None),
            P(None, ("dp", "blk")),
        ),
        out_specs=(
            P("dp", "blk", None),
            P("dp", "blk", None),
            P(("dp", "blk"), None),
            P(("dp", "blk"), None),
            P(("dp", "blk"), None),
            P(("dp", "blk"), None),
            P(None, ("dp", "blk")),
            P(("dp", "blk"), None),
            P(("dp", "blk"), None),
            P(("dp", "blk"), None),
            P(("dp", "blk"), None),
            P(None, ("dp", "blk")),
            P(("dp", "blk"), None),
            P(("dp", "blk"), None),
            P(("dp", "blk"), None),
            P(("dp", "blk"), None),
            P(None, ("dp", "blk")),
            P(("dp", "blk"), None),
            P(("dp", "blk"), None),
            P(("dp", "blk"), None),
            P(("dp", "blk"), None),
            P(None, ("dp", "blk")),
            P(("dp", "blk"), None),
            P(("dp", "blk"), None),
            P(("dp", "blk"), None),
            P(("dp", "blk"), None),
            P(None, ("dp", "blk")),
        ),
        check_vma=False,
    )
```

```python
import functools
import math

import jax
import jax.numpy as jnp
from jax import lax
from jax.experimental import pallas as pl
from jax.experimental.pallas import tpu as pltpu
from jax.sharding import PartitionSpec as P

D = 768
HEADS = 12
HEAD_DIM = 64


def layer_norm(value, gain, shift):
    mean = jnp.mean(value, axis=-1, keepdims=True)
    cent = value - mean
    var = jnp.mean(cent * cent, axis=-1, keepdims=True)
    return cent * lax.rsqrt(var + 1e-06) * (1.0 + gain) + shift


def gelu_exact(value):
    return jax.nn.gelu(value, approximate=False)


def contract_tokens(left, right):
    return lax.dot_general(
        left.reshape(-1, left.shape[-1]),
        right.reshape(-1, right.shape[-1]),
        (((0,), (0,)), ((), ())),
        preferred_element_type=jnp.float32,
    )


def times_transpose(left, weight):
    return lax.dot_general(
        left, weight, (((left.ndim - 1,), (1,)), ((), ())), preferred_element_type=jnp.float32
    )


def group_size(rows, block):
    limit = max(1, 512 // block)
    best = 1
    for cand in range(1, rows + 1):
        if rows % cand == 0 and cand <= limit:
            best = cand
    return best


def scores_of(query, keys, seg_query, seg_keys):
    scores = jnp.einsum(
        "gqhd,gkhd->ghqk", query, keys, preferred_element_type=jnp.float32
    ) * HEAD_DIM ** (-0.5)
    allowed = (seg_query[:, :, None] == seg_keys[:, None, :])[:, None]
    return (scores, allowed)


def attend_back(query, kv_all, grad_out, seg_query, segments, group):
    rows, block = (query.shape[0], query.shape[1])
    length = kv_all.shape[1]
    keys = kv_all[0:group, :, :D].reshape(group, length, HEADS, HEAD_DIM)
    values = kv_all[0:group, :, D:].reshape(group, length, HEADS, HEAD_DIM)
    scores, allowed = scores_of(query, keys, seg_query, segments)
    probs = jax.nn.softmax(jnp.where(allowed, scores, -1e30), axis=-1)
    probs_low = probs.astype(jnp.bfloat16)
    prob_grad = jnp.einsum("gqhd,gkhd->ghqk", grad_out, values, preferred_element_type=jnp.float32)
    score_grad = probs * (prob_grad - jnp.sum(probs * prob_grad, axis=-1, keepdims=True))
    score_low = score_grad.astype(jnp.bfloat16)
    dq_part = jnp.einsum(
        "ghqk,gkhd->gqhd", score_low, keys, preferred_element_type=jnp.float32
    ) * HEAD_DIM ** (-0.5)
    dk_part = jnp.einsum(
        "ghqk,gqhd->gkhd", score_low, query, preferred_element_type=jnp.float32
    ) * HEAD_DIM ** (-0.5)
    dv_part = jnp.einsum("ghqk,gqhd->gkhd", probs_low, grad_out, preferred_element_type=jnp.float32)
    dq_parts = dq_part.reshape(group, block, D)
    dkv_parts = jnp.concatenate(
        [dk_part.reshape(group, length, D), dv_part.reshape(group, length, D)], axis=-1
    )
    return (dq_parts, dkv_parts)


def update(weight, grad, velocity, average, rate):
    step_value = grad + 0.0005 * weight
    velocity_new = 0.9 * velocity + step_value
    weight_new = weight - rate * (step_value + 0.9 * velocity_new)
    average_new = 0.9 * average + 0.1 * weight_new
    return (weight_new, velocity_new, average_new)


def on_device(
    tokens,
    segments,
    cotangent,
    qkv_weight,
    proj_weight,
    up_weight,
    down_weight,
    vec_params,
    qkv_velocity,
    proj_velocity,
    up_velocity,
    down_velocity,
    vec_velocity,
    qkv_average,
    proj_average,
    up_average,
    down_average,
    vec_average,
):
    rows, block = (tokens.shape[0], tokens.shape[1])
    length = segments.shape[1]
    total_tokens = rows * lax.axis_size("dp") * length
    rate = 0.05 / math.sqrt(total_tokens)
    group = group_size(rows, block)
    gathered = (
        lax.all_gather(qkv_weight.astype(jnp.bfloat16), ("dp", "blk"), axis=0, tiled=True),
        lax.all_gather(proj_weight.astype(jnp.bfloat16), ("dp", "blk"), axis=0, tiled=True),
        lax.all_gather(up_weight.astype(jnp.bfloat16), ("dp", "blk"), axis=0, tiled=True),
        lax.all_gather(down_weight.astype(jnp.bfloat16), ("dp", "blk"), axis=0, tiled=True),
        lax.all_gather(vec_params.astype(jnp.bfloat16), ("dp", "blk"), axis=1, tiled=True),
    )
    w_query, w_proj, w_up, w_down, vec_low = gathered
    vec = vec_low.astype(jnp.float32)
    bias_up = vec[8:12].reshape(-1)
    position = lax.axis_index("blk")
    seg_query = lax.dynamic_slice_in_dim(segments, position * block, block, 1)
    inputs = tokens.astype(jnp.float32)
    a_one = layer_norm(inputs, vec[0], vec[1]).astype(jnp.bfloat16)
    zero_bias = jnp.zeros_like(vec[2])
    pre = jnp.dot(a_one, w_query, preferred_element_type=jnp.float32) + jnp.concatenate(
        [vec[2], zero_bias, vec[3]]
    )
    qkv = pre.astype(jnp.bfloat16)
    query = qkv[..., :D].reshape(rows, block, HEADS, HEAD_DIM)
    key_value = qkv[..., D:]
    piece = lax.all_gather(key_value, "blk", axis=1, tiled=True)
    top = jnp.full((rows, HEADS, block), -1e30, jnp.float32)
    count = piece.shape[1]
    keys = piece[0:group, :, :D].reshape(group, count, HEADS, HEAD_DIM)
    values = piece[0:group, :, D:].reshape(group, count, HEADS, HEAD_DIM)
    scores, allowed = scores_of(query, keys, seg_query, segments)
    scores = jnp.where(allowed, scores, -1e30)
    new_top = jnp.maximum(top, jnp.max(scores, axis=-1))
    weights = jnp.where(allowed, jnp.exp(scores - new_top[..., None]), 0.0)
    denoms = jnp.sum(weights, axis=-1)
    added = jnp.einsum(
        "ghqk,gkhd->gqhd", weights.astype(jnp.bfloat16), values, preferred_element_type=jnp.float32
    )
    mixed = (added / jnp.transpose(denoms, (0, 2, 1))[..., None]).reshape(rows, block, D)
    mixed_low = mixed.astype(jnp.bfloat16)
    second = inputs + jnp.dot(mixed_low, w_proj, preferred_element_type=jnp.float32) + vec[4]
    second_norm, norm_two_back = jax.vjp(layer_norm, second, vec[5], vec[6])
    a_two = second_norm.astype(jnp.bfloat16)
    hidden = jnp.dot(a_two, w_up, preferred_element_type=jnp.float32) + bias_up
    act_value, gelu_back = jax.vjp(gelu_exact, hidden)
    act = act_value.astype(jnp.bfloat16)
    result = second + jnp.dot(act, w_down, preferred_element_type=jnp.float32) + vec[7]
    output = result.astype(jnp.bfloat16)
    out_grad = cotangent.astype(jnp.float32)
    grad_down = contract_tokens(act, cotangent)
    bias_down_grad = jnp.sum(out_grad, axis=(0, 1))
    act_grad = times_transpose(cotangent, w_down)
    hidden_grad = gelu_back(act_grad)[0].astype(jnp.bfloat16)
    bias_up_grad = jnp.sum(hidden_grad.astype(jnp.float32), axis=(0, 1))
    grad_up = contract_tokens(a_two, hidden_grad)
    a_two_grad = times_transpose(hidden_grad, w_up)
    second_part, gain_two_grad, shift_two_grad = norm_two_back(a_two_grad)
    second_grad = out_grad + second_part
    attn_grad = second_grad.astype(jnp.bfloat16)
    bias_proj_grad = jnp.sum(attn_grad.astype(jnp.float32), axis=(0, 1))
    grad_proj = contract_tokens(mixed_low, attn_grad)
    mixed_grad = (
        times_transpose(attn_grad, w_proj)
        .astype(jnp.bfloat16)
        .reshape(rows, block, HEADS, HEAD_DIM)
    )
    kv_again = lax.all_gather(key_value, "blk", axis=1, tiled=True)
    query_grad, kv_terms = attend_back(query, kv_again, mixed_grad, seg_query, segments, group)
    kv_grad = lax.psum_scatter(
        kv_terms.astype(jnp.bfloat16), "blk", scatter_dimension=1, tiled=True
    ).astype(jnp.float32)
    qkv_grad_low = jnp.concatenate([query_grad, kv_grad], axis=-1).astype(jnp.bfloat16)
    qkv_sums = jnp.sum(qkv_grad_low.astype(jnp.float32), axis=(0, 1))
    grad_query = contract_tokens(a_one, qkv_grad_low)
    a_one_grad = times_transpose(qkv_grad_low, w_query)
    norm_one_back = jax.vjp(layer_norm, inputs, vec[0], vec[1])[1]
    first_part, gain_one_grad, shift_one_grad = norm_one_back(a_one_grad)
    tokens_grad = (second_grad + first_part).astype(jnp.bfloat16)
    vec_local = jnp.concatenate(
        [
            jnp.stack(
                [
                    gain_one_grad,
                    shift_one_grad,
                    qkv_sums[:D],
                    qkv_sums[2 * D :],
                    bias_proj_grad,
                    gain_two_grad,
                    shift_two_grad,
                    bias_down_grad,
                ]
            ),
            bias_up_grad.reshape(4, D),
        ],
        axis=0,
    )
    query_share, proj_share, up_share, down_share, vec_share = (
        lax.psum_scatter(grad_query, ("dp", "blk"), scatter_dimension=0, tiled=True),
        lax.psum_scatter(grad_proj, ("dp", "blk"), scatter_dimension=0, tiled=True),
        lax.psum_scatter(grad_up, ("dp", "blk"), scatter_dimension=0, tiled=True),
        lax.psum_scatter(grad_down, ("dp", "blk"), scatter_dimension=0, tiled=True),
        lax.psum_scatter(vec_local, ("dp", "blk"), scatter_dimension=1, tiled=True),
    )
    qkv_new = update(qkv_weight, query_share, qkv_velocity, qkv_average, rate)
    proj_new = update(proj_weight, proj_share, proj_velocity, proj_average, rate)
    up_new = update(up_weight, up_share, up_velocity, up_average, rate)
    down_new = update(down_weight, down_share, down_velocity, down_average, rate)
    vec_new = update(vec_params, vec_share, vec_velocity, vec_average, rate)
    return (
        output,
        tokens_grad,
        query_share,
        proj_share,
        up_share,
        down_share,
        vec_share,
        qkv_new[0],
        proj_new[0],
        up_new[0],
        down_new[0],
        vec_new[0],
        qkv_new[1],
        proj_new[1],
        up_new[1],
        down_new[1],
        vec_new[1],
        qkv_new[2],
        proj_new[2],
        up_new[2],
        down_new[2],
        vec_new[2],
        qkv_new[0].astype(jnp.bfloat16),
        proj_new[0].astype(jnp.bfloat16),
        up_new[0].astype(jnp.bfloat16),
        down_new[0].astype(jnp.bfloat16),
        vec_new[0].astype(jnp.bfloat16),
    )


PIECE = (48, 384)
NP = 12
Z, Y, X, C = 4, 2, 2, 2
AHEAD = 2
TILE = 128
IMG_MAX = 198
REACH = (IMG_MAX - 1 + 15) // 16 * 16
SPAN = TILE + 2 * REACH
GATHER_SPLIT = ((0, NP, 2),)
PAIRS = HEADS // 2
MESH = pl.DeviceIdType.MESH
F32, BF16 = jnp.float32, jnp.bfloat16
NT = (((1,), (1,)), ((), ()))
TN = (((0,), (0,)), ((), ()))


def place():
    d, x = lax.axis_index("dp"), lax.axis_index("blk")
    return d // (2 * Y), (d // 2) % Y, d % 2, x


def ident(z, y, c, x):
    return ((z * Y + y) * 2 + c, x)


def greet(z, y, c, x):
    barrier = pltpu.get_barrier_semaphore()
    peers = [ident((z + k) % Z, y, c, x) for k in range(1, Z)]
    peers += [ident(z, 1 - y, c, x), ident(z, y, c, 1 - x), ident(z, y, 1 - c, x)]
    for peer in peers:
        pl.semaphore_signal(barrier, inc=1, device_id=peer, device_id_type=MESH)
    return lambda: pl.semaphore_wait(barrier, len(peers))


def remote(src, dst, send, recv, peer):
    return pltpu.make_async_remote_copy(
        src_ref=src, dst_ref=dst, send_sem=send, recv_sem=recv, device_id=peer, device_id_type=MESH
    )


def begin(copies):
    for copy in copies:
        copy.start()


def arrive(copies):
    for copy in copies:
        copy.wait_recv()


def within(index, low, high, run):
    if isinstance(index, int):
        if low <= index < high:
            run()
    else:
        pl.when(jnp.logical_and(index >= low, index < high))(run)


def loop(count, body):
    def step(i, carry):
        body(i)
        return carry

    lax.fori_loop(0, count, step, 0)


def cols(j, width):
    return pl.ds(pl.multiple_of(j * width, width), width)


def dot(a, b, dims=None):
    dims = (((1,), (0,)), ((), ())) if dims is None else dims
    return lax.dot_general(a, b, dims, preferred_element_type=F32)


class Vec:
    def __init__(self, at, now, got, send, recv):
        self.at, self.now, self.got, self.send, self.recv = at, now, got, send, recv

    def copies(self, step):
        z, y, c, x = self.at
        peers = [
            [ident(z, y, 1 - c, x)],
            [ident(z, y, c, 1 - x)],
            [ident(z, 1 - y, c, x)],
            [ident((z + k) % Z, y, c, x) for k in range(1, Z)],
        ][step]
        return [
            remote(self.now.at[step], self.got.at[step + k], self.send.at[step + k], self.recv.at[step + k], peer)
            for k, peer in enumerate(peers)
        ]

    def begin(self, step):
        begin(self.copies(step))

    def total(self, step):
        copies = self.copies(step)
        arrive(copies)
        total = self.now[step]
        for k in range(len(copies)):
            total = total + self.got[step + k]
        return total

    def sent(self):
        for step in range(4):
            for copy in self.copies(step):
                copy.wait_send()


def normal(value):
    mean = jnp.mean(value, axis=-1, keepdims=True)
    cent = value - mean
    var = jnp.mean(cent * cent, axis=-1, keepdims=True)
    scale = lax.rsqrt(var + 1e-06)
    return cent * scale, scale


def window_start(i, x, tiles):
    near = tiles * TILE + REACH
    first = max(i * TILE - REACH, 0)
    count = min((i + 1) * TILE + REACH, near) - first
    start = jnp.where(x == 0, first, near - first - count)
    return jnp.where(x == 0, i, tiles - 1 - i), start, count


def window(i, x, tiles):
    tile, start, count = window_start(i, x, tiles)
    return tile, pl.ds(pl.multiple_of(start, 16), count), count


def mask_fill(seg, seg_col, bias, x, tiles):
    length = seg.shape[1]
    for k in range(length // TILE):
        row = seg[0:1, k * TILE : k * TILE + TILE].astype(F32)
        seg_col[k * TILE : k * TILE + TILE, :] = jnp.transpose(jnp.broadcast_to(row, (TILE, TILE)))
    for i in range(tiles):
        tile, start, count = window_start(i, x, tiles)
        start = start + x * (length - tiles * TILE - REACH)
        row = seg[0:1, pl.ds(pl.multiple_of((x * tiles + tile) * TILE, TILE), TILE)].astype(F32)
        column = seg_col[pl.ds(pl.multiple_of(start, 16), count), :]
        bias[i, 0:count] = jnp.where(column == row, 0.0, -1e30).astype(F32)


def split_heads(pair_block):
    lane = lax.broadcasted_iota(jnp.int32, pair_block.shape, 1)
    zero = jnp.zeros_like(pair_block)
    return jnp.concatenate(
        [jnp.where(lane < HEAD_DIM, pair_block, zero), jnp.where(lane < HEAD_DIM, zero, pair_block)], axis=0
    )


def join_heads(both):
    own = jnp.concatenate([both[:HEAD_DIM, :TILE], both[HEAD_DIM:, TILE:]], axis=0)
    return jnp.transpose(own)


def rows_from_stage(stage, target, t):
    left, right = cols(2 * t, 384), cols(2 * t + 1, 384)

    def group(g):
        parts = [stage[c, g % Y, x, g // Y].astype(F32) for c in range(C) for x in range(X)]
        rows = pl.ds(pl.multiple_of(g * 96, 96), 96)
        target[rows, left] = jnp.concatenate([p[:24] for p in parts], axis=0).astype(BF16)
        target[rows, right] = jnp.concatenate([p[24:] for p in parts], axis=0).astype(BF16)

    loop(Z * Y, group)


def down_copies(full, target, t, sem):
    half, col = (t - 8) % 2 * 48, (t - 8) // 2 * 384

    def group(g):
        for c in range(C):
            for x in range(X):
                row = pl.multiple_of(g * 384 + (c * X + x) * 96 + half, 16)
                pltpu.make_async_copy(
                    full.at[c, g % Y, x, g // Y, t], target.at[pl.ds(row, 48), col : col + 384], sem
                ).start()

    loop(Z * Y, group)


def qkv_columns(j, half):
    if half == 0:
        return (256 * j, 256), (D + 256 * j, 128)
    return (D + 256 * j + 128, 128), (2 * D + 256 * j, 256)


class Gather:
    def __init__(self, at, unit, full, own, send, recv):
        self.at, self.unit, self.full, self.own, self.send, self.recv = at, unit, full, own, send, recv

    def mine(self, t):
        z, y, c, x = self.at
        return pltpu.make_async_copy(self.unit.at[t], self.full.at[c, y, x, z, t], self.own.at[t])

    def first(self, t):
        z, y, c, x = self.at
        return [
            remote(
                self.unit.at[t], self.full.at[c, y, x, z, t], self.send.at[t, k - 1], self.recv.at[t, k - 1],
                ident((z + k) % Z, y, c, x),
            )
            for k in range(1, Z)
        ]

    def second(self, t, low):
        z, y, c, x = self.at
        one, two = self.full.at[c, y, x, 0:low, t], self.full.at[c, y, x, low:Z, t]
        return [
            remote(one, one, self.send.at[t, 3], self.recv.at[t, 3], ident(z, y, c, 1 - x)),
            remote(two, two, self.send.at[t, 4], self.recv.at[t, 4], ident(z, 1 - y, c, x)),
        ]

    def third(self, t, low):
        z, y, c, x = self.at
        one, two = self.full.at[c, y, :, 0:low, t], self.full.at[c, :, x, low:Z, t]
        return [
            remote(one, one, self.send.at[t, 5], self.recv.at[t, 5], ident(z, 1 - y, c, x)),
            remote(two, two, self.send.at[t, 6], self.recv.at[t, 6], ident(z, y, c, 1 - x)),
        ]

    def last(self, t):
        z, y, c, x = self.at
        block = self.full.at[c, :, :, :, t]
        return [remote(block, block, self.send.at[t, 7], self.recv.at[t, 7], ident(z, y, 1 - c, x))]

    def start(self):
        loop(NP, lambda t: self.mine(t).start())
        loop(AHEAD, lambda t: begin(self.first(t)))

    def progress(self, i):
        def to_second(t, low):
            self.mine(t).wait()
            arrive(self.first(t))
            begin(self.second(t, low))

        def to_third(t, low):
            arrive(self.second(t, low))
            begin(self.third(t, low))

        def to_last(t, low):
            arrive(self.third(t, low))
            begin(self.last(t))

        for first, end, low in GATHER_SPLIT:
            within(i, first, end, lambda: to_second(i, low))
        for first, end, low in GATHER_SPLIT:
            within(i - 1, first, end, lambda: to_third(i - 1, low))
        for first, end, low in GATHER_SPLIT:
            within(i - 2, first, end, lambda: to_last(i - 2, low))
        within(i + AHEAD, AHEAD, NP, lambda: begin(self.first(i + AHEAD)))

    def sent(self):
        for first, end, low in GATHER_SPLIT:
            def one(t):
                for copy in self.first(t) + self.second(t, low) + self.third(t, low) + self.last(t):
                    copy.wait_send()

            lax.fori_loop(first, end, lambda t, carry: (one(t), carry)[1], 0)


def forward_kernel(
    w_qkv, w_proj, w_up, w_down, vec_in, tok, dy, seg,
    full, vec_out, out_o, q_o, k_o, v_o, o_o, stat_o, x2_o, a2_o, z_o, slope_o, grad_o, bias_o,
    unit, seg_col, near, a1, wbig, wdown, stage, vecf, bias, out_s, q_s, k_s, v_s, o_s, stat_s, x2_s, a2_s, z_s, slope_s, got,
    local, two, vec_now, vec_got, own, send, recv, vsend, vrecv, hsem, ssem, dsem, osem, gsend, grecv, tsend, trecv,
):
    z, y, c, x = at = place()
    block = tok.shape[0]
    tiles = block // TILE
    offset = pl.multiple_of(x * REACH, 16)
    greeted = greet(*at)
    vec_now[0] = vec_in[...]

    def pack(t, weight, j):
        left, right = weight[:, j * 768 : j * 768 + 384], weight[:, j * 768 + 384 : j * 768 + 768]
        unit[t] = jnp.concatenate([left, right], axis=0).astype(BF16)

    for j in range(3):
        sides = []
        for half in range(2):
            parts = [w_qkv[:, start : start + width] for start, width in qkv_columns(j, half)]
            sides.append(jnp.concatenate(parts, axis=1))
        unit[j] = jnp.concatenate(sides, axis=0).astype(BF16)
    pack(3, w_proj, 0)
    for j in range(4):
        pack(4 + j, w_up, j)
        unit[8 + j] = w_down[j % 2 * 48 : j % 2 * 48 + 48, j // 2 * 384 : j // 2 * 384 + 384].astype(BF16)
    greeted()
    gather = Gather(at, unit, full, own, send, recv)
    gather.start()
    vec = Vec(at, vec_now, vec_got, vsend, vrecv)
    vec.begin(0)
    away = pl.multiple_of((1 - x) * (block - REACH), 16)
    land = pl.multiple_of(x * block, 16)
    halo = remote(
        tok.at[pl.ds(away, REACH)], near.at[pl.ds(land, REACH)], hsem.at[0], hsem.at[1], ident(z, y, c, 1 - x)
    )
    halo.start()
    near[pl.ds(offset, block), :] = tok[...]

    def put(k, src, dst):
        return pltpu.make_async_copy(src, dst, osem.at[k])

    def vec_step(step):
        total = vec.total(step)
        if step < 3:
            vec_now[step + 1] = total
            vec.begin(step + 1)
        else:
            vec_out[...] = total
            vecf[...] = total.astype(F32)

    def staged(t):
        return pltpu.make_async_copy(full.at[:, :, :, :, t], stage.at[t % 4], ssem.at[t % 4])

    def fetch(t):
        arrive(gather.last(t))
        staged(t).start()

    def take(t):
        staged(t).wait()
        rows_from_stage(stage.at[t % 4], wbig, t)

    def down_start(t):
        arrive(gather.last(t))
        down_copies(full, wdown, t, dsem.at[t - 8])

    def down_wait(t):
        pltpu.make_async_copy(full.at[:, :, :, :, t], stage.at[0], dsem.at[t - 8]).wait()

    gather.progress(0)
    vec_step(0)
    gather.progress(1)
    vec_step(1)
    gather.progress(2)
    vec_step(2)
    vec_step(3)
    halo.wait_recv()

    def norm_one(i):
        rows = cols(i, 240)
        value = normal(near[rows, :].astype(F32))[0]
        a1[rows, :] = (value * (1.0 + vecf[0:1, :]) + vecf[1:2, :]).astype(BF16)

    loop(near.shape[0] // 240, norm_one)
    mask_fill(seg, seg_col, bias, x, tiles)
    put(11, bias, bias_o).start()
    def attend(pair):
        lanes = cols(pair, 128)

        for i in range(tiles):
            tile, span, count = window(i, x, tiles)
            rows = cols(tile, TILE)
            both = split_heads(q_s[rows, lanes])
            fill = bias[i, 0:count]
            scores = dot(k_s[span, lanes], both, NT) + jnp.concatenate([fill, fill], axis=1)
            top = jnp.max(scores, axis=0, keepdims=True)
            weights = jnp.exp(scores - top)
            total = jnp.sum(weights, axis=0, keepdims=True)
            mixed = dot(v_s[span, lanes], weights.astype(BF16), TN) / total
            o_s[rows, lanes] = join_heads(mixed).astype(BF16)
            stat_s[pair * tiles + i] = jnp.broadcast_to(top + jnp.log(total), (8, 2 * TILE))

    def third(j):
        fetch(j)
        gather.progress(3 + 2 * j)
        take(j)
        where = cols(j, 256)
        value = dot(a1[pl.ds(offset, block), :], wbig[:, cols(3 * j, 256)]) + vecf[2:3, where]
        q_s[:, where] = value.astype(BF16) * HEAD_DIM ** (-0.5)
        k_s[:, where] = dot(a1[...], wbig[:, cols(3 * j + 1, 256)]).astype(BF16)
        v_s[:, where] = (dot(a1[...], wbig[:, cols(3 * j + 2, 256)]) + vecf[3:4, where]).astype(BF16)
        attend(2 * j)
        gather.progress(4 + 2 * j)
        attend(2 * j + 1)

    loop(3, third)
    put(0, k_s, k_o).start()
    put(1, v_s, v_o).start()
    put(2, q_s, q_o).start()
    put(3, o_s, o_o).start()
    put(4, stat_s, stat_o).start()
    fetch(3)
    take(3)
    fetch(4)
    fetch(5)
    gather.progress(9)

    def project(j):
        value = dot(o_s[...], wbig[:, cols(j + 9, 256)])
        x2_s[:, cols(j, 256)] = tok[:, cols(j, 256)].astype(F32) + value + vecf[4:5, cols(j, 256)]

    loop(3, project)

    def norm_two(i):
        rows = pl.ds(pl.multiple_of(i * 256, 256), 256)
        value = normal(x2_s[rows, :])[0]
        a2_s[rows, :] = (value * (1.0 + vecf[5:6, :]) + vecf[6:7, :]).astype(BF16)

    loop(block // 256, norm_two)
    put(5, x2_s, x2_o).start()
    put(6, a2_s, a2_o).start()
    gather.progress(10)
    take(4)
    take(5)
    fetch(6)
    fetch(7)

    def expand(j):
        u = dot(a2_s[...], wbig[:, cols(j + 12, 256)])
        u = u + vecf[pl.ds(8 + j // 3, 1), pl.ds(pl.multiple_of((j % 3) * 256, 256), 256)]
        half = 0.5 + 0.5 * lax.erf(u * math.sqrt(0.5))
        z_s[:, cols(j, 256)] = (u * half).astype(BF16)
        slope = half + u * (jnp.exp(-0.5 * u * u) * (1.0 / math.sqrt(2.0 * math.pi)))
        slope_s[:, cols(j, 256)] = slope.astype(BF16)

    loop(5, expand)
    gather.progress(11)
    take(6)
    take(7)
    loop(5, lambda j: expand(j + 5))
    gather.progress(12)
    down_start(8)
    loop(2, lambda j: expand(j + 10))
    put(7, z_s, z_o).start()
    put(8, slope_s, slope_o).start()

    def core(t):
        peer = ident(z, y, 1 - c, x)
        return remote(local.at[1 - c, :, :, :, t], got.at[t], gsend.at[t], grecv.at[t], peer)

    for half in range(2):
        def down_grad(g):
            value = dot(z_s[:, cols(g, 384)], dy[:, half * 384 : half * 384 + 384], TN).astype(BF16)
            for k in range(4):
                for row in range(2):
                    part = value[k * 96 + row * 48 : k * 96 + row * 48 + 48]
                    local[k // 2, g % Y, k % 2, g // Y, 2 * half + row] = part

        loop(Z * Y, down_grad)
        core(2 * half).start()
        core(2 * half + 1).start()
        if half == 0:
            gather.progress(13)
            down_start(9)
    down_start(10)

    def contract(half):
        col = slice(half * 384, half * 384 + 384)
        value = dot(z_s[...], wdown[:, col])
        out_s[:, col] = (x2_s[:, col] + value + vecf[7:8, col]).astype(BF16)

    def gain(t):
        core(t).wait_recv()
        for a in range(Y):
            for b in range(X):
                own_part = local[c, a, b, :, t].astype(F32)
                got[t, a, b] = (own_part + got[t, a, b].astype(F32)).astype(BF16)

    def ahead(t):
        along_y, along_x = ident(z, 1 - y, c, x), ident(z, y, c, 1 - x)
        return [
            remote(got.at[t, 1 - y, :, 0:2], two.at[t, :, 0:2], tsend.at[t, 0], trecv.at[t, 0], along_y),
            remote(got.at[t, :, 1 - x, 2:Z], two.at[t, :, 2:Z], tsend.at[t, 1], trecv.at[t, 1], along_x),
        ]

    for t in range(4):
        gain(t)
        if t < 2:
            begin(ahead(t))
    late = pltpu.make_async_copy(got.at[2:4], grad_o.at[2:4], osem.at[10])
    late.start()
    down_wait(8)
    down_wait(9)
    contract(0)
    down_start(11)
    down_wait(10)
    down_wait(11)
    contract(1)
    put(9, out_s, out_o).start()
    pairs = [(k_s, k_o), (v_s, v_o), (q_s, q_o), (o_s, o_o), (stat_s, stat_o), (x2_s, x2_o), (a2_s, a2_o)]
    for k, (src, dst) in enumerate(pairs + [(z_s, z_o), (slope_s, slope_o), (out_s, out_o)]):
        put(k, src, dst).wait()
    for t in range(2):
        arrive(ahead(t))
        for b in range(2):
            low, high = got[t, y, b, 0:2].astype(F32), got[t, b, x, 2:Z].astype(F32)
            got[t, y, b, 0:2] = (low + two[t, b, 0:2].astype(F32)).astype(BF16)
            got[t, b, x, 2:Z] = (high + two[t, b, 2:Z].astype(F32)).astype(BF16)
        for copy in ahead(t):
            copy.wait_send()
    soon = pltpu.make_async_copy(got.at[0:2], grad_o.at[0:2], osem.at[12])
    soon.start()
    late.wait()
    soon.wait()
    put(11, bias, bias_o).wait()
    gather.sent()
    vec.sent()
    halo.wait_send()
    loop(4, lambda t: core(t).wait_send())


def forward_all(weights, vec_placed, tok, dy, seg):
    block = tok.shape[0]
    near = block + REACH
    ff = 4 * D
    tiles = block // TILE
    shapes = [
        ((block, D), BF16),
        ((block, D), BF16),
        ((near, D), BF16),
        ((near, D), BF16),
        ((block, D), BF16),
        ((PAIRS * tiles, 8, 2 * TILE), F32),
        ((block, D), F32),
        ((block, D), BF16),
        ((block, ff), BF16),
        ((block, ff), BF16),
        ((4, Y, X, Z) + PIECE, BF16),
        ((tiles, SPAN, TILE), F32),
    ]
    hbm, vmem = pl.BlockSpec(memory_space=pl.ANY), pl.BlockSpec(memory_space=pltpu.VMEM)
    outs = [((C, Y, X, Z, NP) + PIECE, BF16), (vec_placed.shape, BF16)] + shapes
    return pl.pallas_call(
        forward_kernel,
        out_shape=tuple(jax.ShapeDtypeStruct(*one) for one in outs),
        in_specs=[vmem] * 8,
        out_specs=tuple([hbm, vmem] + [hbm] * len(shapes)),
        scratch_shapes=[
            pltpu.VMEM((NP,) + PIECE, BF16),
            pltpu.VMEM((seg.shape[1], TILE), F32),
            pltpu.VMEM((near, D), BF16),
            pltpu.VMEM((near, D), BF16),
            pltpu.VMEM((D, 8 * D), BF16),
            pltpu.VMEM((ff, D), BF16),
            pltpu.VMEM((4, C, Y, X, Z) + PIECE, BF16),
            pltpu.VMEM(vec_placed.shape, F32),
            *[pltpu.VMEM(*one) for one in shapes[-1:] + shapes[:-1]],
            pltpu.VMEM((C, Y, X, Z, 4) + PIECE, BF16),
            pltpu.VMEM((2, 2, Z) + PIECE, BF16),
            pltpu.VMEM((4,) + vec_placed.shape, BF16),
            pltpu.VMEM((6,) + vec_placed.shape, BF16),
            pltpu.SemaphoreType.DMA((NP,)),
            pltpu.SemaphoreType.DMA((NP, 8)),
            pltpu.SemaphoreType.DMA((NP, 8)),
            pltpu.SemaphoreType.DMA((6,)),
            pltpu.SemaphoreType.DMA((6,)),
            pltpu.SemaphoreType.DMA((2,)),
            pltpu.SemaphoreType.DMA((4,)),
            pltpu.SemaphoreType.DMA((4,)),
            pltpu.SemaphoreType.DMA((13,)),
            pltpu.SemaphoreType.DMA((4,)),
            pltpu.SemaphoreType.DMA((4,)),
            pltpu.SemaphoreType.DMA((2, 2)),
            pltpu.SemaphoreType.DMA((2, 2)),
        ],
        compiler_params=pltpu.CompilerParams(
            collective_id=0, has_side_effects=True, vmem_limit_bytes=60 << 20
        ),
        name="forward_all",
    )(*weights, vec_placed, tok, dy, seg)


SCATTER_SPLIT = ((0, NP, 2),)


class Scatter:
    def __init__(self, at, local, got_core, got_two, got_one, got_z, out, send, recv):
        self.at, self.local, self.out, self.send, self.recv = at, local, out, send, recv
        self.got = got_core, got_two, got_one, got_z

    def core(self, t):
        z, y, c, x = self.at
        peer = ident(z, y, 1 - c, x)
        return [remote(self.local.at[1 - c, :, :, :, t], self.got[0].at[t - 4], self.send.at[t, 0], self.recv.at[t, 0], peer)]

    def two(self, t, low):
        z, y, c, x = self.at
        one, other = self.local.at[c, 1 - y, :, 0:low, t], self.local.at[c, :, 1 - x, low:Z, t]
        got = self.got[1].at[t]
        return [
            remote(one, got.at[:, 0:low], self.send.at[t, 1], self.recv.at[t, 1], ident(z, 1 - y, c, x)),
            remote(other, got.at[:, low:Z], self.send.at[t, 2], self.recv.at[t, 2], ident(z, y, c, 1 - x)),
        ]

    def one(self, t, low):
        z, y, c, x = self.at
        one, other = self.local.at[c, y, 1 - x, 0:low, t], self.local.at[c, 1 - y, x, low:Z, t]
        got = self.got[2].at[t]
        return [
            remote(one, got.at[0:low], self.send.at[t, 3], self.recv.at[t, 3], ident(z, y, c, 1 - x)),
            remote(other, got.at[low:Z], self.send.at[t, 4], self.recv.at[t, 4], ident(z, 1 - y, c, x)),
        ]

    def along(self, t):
        z, y, c, x = self.at
        return [
            remote(
                self.local.at[c, y, x, (z + k) % Z, t], self.got[3].at[t, k - 1], self.send.at[t, 4 + k],
                self.recv.at[t, 4 + k], ident((z + k) % Z, y, c, x),
            )
            for k in range(1, Z)
        ]

    def add(self, where, value):
        self.local[where] = (self.local[where].astype(F32) + value.astype(F32)).astype(BF16)

    def take_core(self, t):
        c = self.at[2]
        arrive(self.core(t))
        for a in range(Y):
            for b in range(X):
                self.add((c, a, b, slice(None), t), self.got[0][t - 4, a, b])

    def after_core(self, t):
        self.take_core(t)
        self.go_two(t)

    def after_two(self, t, low):
        z, y, c, x = self.at
        arrive(self.two(t, low))
        for b in range(2):
            self.add((c, y, b, slice(0, low), t), self.got[1][t, b, 0:low])
            self.add((c, b, x, slice(low, Z), t), self.got[1][t, b, low:Z])
        begin(self.one(t, low))

    def after_one(self, t, low):
        z, y, c, x = self.at
        arrive(self.one(t, low))
        self.add((c, y, x, slice(None), t), self.got[2][t])
        begin(self.along(t))

    def after_z(self, t):
        z, y, c, x = self.at
        arrive(self.along(t))
        total = self.local[c, y, x, z, t].astype(F32)
        for k in range(Z - 1):
            total = total + self.got[3][t, k].astype(F32)
        self.out[t] = total

    def go_two(self, t):
        for first, end, low in SCATTER_SPLIT:
            within(t, first, end, lambda: begin(self.two(t, low)))

    def go_one(self, t):
        for first, end, low in SCATTER_SPLIT:
            within(t, first, end, lambda: self.after_two(t, low))

    def go_z(self, t):
        arrive_one = self.after_one
        for first, end, low in SCATTER_SPLIT:
            within(t, first, end, lambda: arrive_one(t, low))

    def sent(self):
        loop(NP - 4, lambda t: self.core(t + 4)[0].wait_send())
        for first, end, low in SCATTER_SPLIT:
            def each(t):
                for copy in self.one(t, low) + self.along(t):
                    copy.wait_send()
                within(t, 2, NP, lambda: [copy.wait_send() for copy in self.two(t, low)] and None)

            lax.fori_loop(first, end, lambda t, carry: (each(t), carry)[1], 0)


def total_rows(value):
    return jnp.sum(value.astype(F32), axis=0, keepdims=True)


def norm_back(value, grad, gain):
    unit_value, scale = normal(value)
    inner = grad * (1.0 + gain)
    mean_one = jnp.mean(inner, axis=-1, keepdims=True)
    mean_two = jnp.mean(inner * unit_value, axis=-1, keepdims=True)
    back = scale * (inner - mean_one - unit_value * mean_two)
    return back, total_rows(grad * unit_value), total_rows(grad)


def backward_kernel(
    full, vec_in, tok_o, dy_o, grad_o, bias_o, q_o, k_o, v_o, o_o, stat_o, x2_o, a2_o, slope_o,
    out, vec_out, tok_grad,
    local, got_core, got_two, got_one, got_z, wbuf, stage, bias, vecf, tok, dy, q_s, k_s, v_s, o_s, stat_s, x2_s, a2_s, z_s,
    slope_s, dx, da, acc_k, acc_v, halo_s, halo_r, vec_now, vec_got, send, recv, vsend, vrecv, hsend, hrecv, isem, ssem, dsem, gsem,
):
    z, y, c, x = at = place()
    greeted = greet(*at)
    block = tok.shape[0]
    tiles = block // TILE
    offset = pl.multiple_of(x * REACH, 16)
    away = pl.multiple_of((1 - x) * (block - REACH), 16)
    outside = pl.multiple_of((1 - x) * block, 16)
    order = [4, 5, 6, 7, 3, 0, 1, 2]

    def fetch(n):
        return pltpu.make_async_copy(full.at[:, :, :, :, order[n]], stage.at[n % 2], ssem.at[n % 2])

    def take(n, use):
        fetch(n).wait()
        use(stage.at[n % 2])
        if n + 2 < len(order):
            fetch(n + 2).start()

    pairs = [
        (dy_o, dy), (slope_o, slope_s), (a2_o, a2_s), (x2_o, x2_s), (o_o, o_s), (k_o, k_s), (v_o, v_s), (q_o, q_s),
        (stat_o, stat_s), (tok_o, tok), (bias_o, bias),
    ]

    def inward(k):
        return pltpu.make_async_copy(pairs[k][0], pairs[k][1], isem.at[k])

    def grads(t):
        return pltpu.make_async_copy(grad_o.at[t], local.at[c, :, :, :, t], gsem.at[t])

    for t in range(4):
        grads(t).start()
    inward(0).start()
    for t in range(8, 12):
        down_copies(full, wbuf, t, dsem.at[t - 8])
    for n in range(2):
        fetch(n).start()
    for k in range(1, len(pairs)):
        inward(k).start()
    greeted()
    scatter = Scatter(at, local, got_core, got_two, got_one, got_z, out, send, recv)
    vec = Vec(at, vec_now, vec_got, vsend, vrecv)
    vec_now[0] = jnp.zeros(vec_now.shape[1:], F32)
    vecf[...] = vec_in[...].astype(F32)

    def vec_step(step):
        total = vec.total(step)
        if step < 3:
            vec_now[step + 1] = total
            vec.begin(step + 1)
        else:
            vec_out[...] = total

    def gain_row(row, where, value):
        vec_now[0, row : row + 1, where] = vec_now[0, row : row + 1, where] + value

    def weight_grad(left, right, t):
        def half(h):
            value = dot(left[:, cols(h, 384)], right[...], TN)
            for g in range(4):
                for k in range(4):
                    part = value[g * 96 + k * 24 : g * 96 + k * 24 + 24]
                    part = jnp.concatenate([part[:, :384], part[:, 384:]], axis=0).astype(BF16)
                    local[k // 2, g % 2, k % 2, 2 * h + g // 2, t] = part

        loop(2, half)
        begin(scatter.core(t))

    for t in range(4):
        grads(t).wait()
        if t < 2:
            begin(scatter.one(t, 2))
        else:
            scatter.go_two(t)
    inward(0).wait()
    gain_row(7, slice(None), total_rows(dy[...]))
    for t in range(8, 12):
        pltpu.make_async_copy(full.at[:, :, :, :, t], stage.at[0], dsem.at[t - 8]).wait()
    inward(1).wait()

    def hidden(n):
        rows = pl.ds(pl.multiple_of(n * 256, 256), 256)
        grad = dot(dy[...], wbuf[rows, :], NT) * slope_s[:, cols(n, 256)].astype(F32)
        low = grad.astype(BF16)
        slope_s[:, cols(n, 256)] = low
        where = pl.ds(pl.multiple_of((n % 3) * 256, 256), 256)
        vec_now[0, pl.ds(8 + n // 3, 1), where] = total_rows(low)

    loop(12, hidden)
    inward(2).wait()
    for t in range(2):
        take(t, lambda part: rows_from_stage(part, wbuf.at[pl.ds(t * D, D)], 0))
    for t in range(4):
        weight_grad(a2_s, slope_s.at[:, t * D : t * D + D], 4 + t)
    scatter.after_core(4)
    scatter.go_one(2)
    scatter.go_z(0)
    for t in range(2, 4):
        take(t, lambda part: rows_from_stage(part, wbuf.at[pl.ds(t * D, D)], 0))

    def inner_grad(n):
        value = None
        for t in range(4):
            rows = pl.ds(pl.multiple_of(t * D + n * 256, 256), 256)
            part = dot(slope_s[:, t * D : t * D + D], wbuf[rows, :], NT)
            value = part if value is None else value + part
        dx[:, cols(n, 256)] = value

    loop(3, inner_grad)
    scatter.after_core(5)
    scatter.go_one(3)
    inward(3).wait()

    def norm_two(i):
        rows = cols(i, 128)
        grad = dx[rows, :]
        back, gain, shift = norm_back(x2_s[rows, :], grad, vecf[5:6, :])
        total = dy[rows, :].astype(F32) + back
        low = total.astype(BF16)
        dx[rows, :] = total
        da[rows, :] = low
        gain_row(5, slice(None), gain)
        gain_row(6, slice(None), shift)
        gain_row(4, slice(None), total_rows(low))

    loop(block // 128, norm_two)
    scatter.after_core(6)
    scatter.after_core(7)
    scatter.go_z(1)
    inward(4).wait()
    weight_grad(o_s, da, 8)
    take(4, lambda part: rows_from_stage(part, wbuf.at[pl.ds(3 * D, D)], 0))

    def mixed_grad(n):
        rows = pl.ds(pl.multiple_of(3 * D + n * 256, 256), 256)
        o_s[:, cols(n, 256)] = dot(da[...], wbuf[rows, :], NT).astype(BF16)

    loop(3, mixed_grad)
    scatter.after_core(8)
    for k in range(5, 11):
        inward(k).wait()

    def halo(pair):
        return remote(halo_s.at[pair], halo_r.at[pair], hsend.at[pair], hrecv.at[pair], ident(z, y, c, 1 - x))

    def spot(pair, kind):
        return pl.ds(pl.multiple_of(pair // 2 * D + kind * 256 + pair % 2 * 128, 128), 128)

    def attend(pair):
        lanes = cols(pair, 128)
        scatter.go_z(2 + pair)
        within(pair, 0, 5, lambda: scatter.go_one(4 + pair))
        scatter.after_z(pair)
        acc_k[...] = jnp.zeros(acc_k.shape, F32)
        acc_v[...] = jnp.zeros(acc_v.shape, F32)

        for i in range(tiles):
            tile, span, count = window(i, x, tiles)
            rows = cols(tile, TILE)
            both, grads = split_heads(q_s[rows, lanes]), split_heads(o_s[rows, lanes])
            fill = bias[i, 0:count]
            scores = dot(k_s[span, lanes], both, NT) + jnp.concatenate([fill, fill], axis=1)
            probs = jnp.exp(scores - stat_s[pair * tiles + i][0:1])
            low = probs.astype(BF16)
            back = dot(v_s[span, lanes], grads, NT)
            mean = jnp.sum(probs * back, axis=0, keepdims=True)
            inner = (probs * (back - mean)).astype(BF16)
            acc_v[span, :] = acc_v[span, :] + dot(low, grads)
            acc_k[span, :] = acc_k[span, :] + dot(inner, both)
            query = join_heads(dot(k_s[span, lanes], inner, TN)) * HEAD_DIM ** (-0.5)
            z_s[rows, spot(pair, 0)] = query.astype(BF16)

        for k, acc in ((0, acc_k), (1, acc_v)):
            z_s[:, spot(pair, k + 1)] = acc[pl.ds(offset, block), :].astype(BF16)
            halo_s[pair, k] = acc[pl.ds(outside, REACH), :].astype(BF16)
        halo(pair).start()

    def add_halo(pair):
        halo(pair).wait_recv()
        for k in range(2):
            where = spot(pair, k + 1)
            rows = pl.ds(away, REACH)
            z_s[rows, where] = (z_s[rows, where].astype(F32) + halo_r[pair, k].astype(F32)).astype(BF16)

    def finish(j):
        add_halo(2 * j)
        add_halo(2 * j + 1)
        weight_grad(a2_s, z_s.at[:, pl.ds(pl.multiple_of(j * D, D), D)], 9 + j)

    def norm_one(i):
        rows = cols(i, 128)
        value = normal(tok[rows, :].astype(F32))[0]
        a2_s[rows, :] = (value * (1.0 + vecf[0:1, :]) + vecf[1:2, :]).astype(BF16)

    loop(block // 128, norm_one)

    def third(j):
        loop(2, lambda i: attend(2 * j + i))
        within(j, 2, 3, lambda: scatter.after_core(9))
        within(j, 1, 3, lambda: finish(j - 1))

    loop(3, third)
    finish(2)
    scatter.after_core(10)
    scatter.go_z(8)
    scatter.after_core(11)
    for n in range(5, 8):
        take(n, lambda part: rows_from_stage(part, wbuf.at[pl.ds((n - 5) * D, D)], 0))

    def first_grad(n):
        value = None
        for t in range(3):
            rows = pl.ds(pl.multiple_of(t * D + n * 256, 256), 256)
            part = dot(z_s[:, t * D : t * D + D], wbuf[rows, :], NT)
            value = part if value is None else value + part
        x2_s[:, cols(n, 256)] = value

    loop(3, first_grad)
    scatter.go_one(9)
    for j in range(3):
        where = slice(j * 256, j * 256 + 256)
        gain_row(2, where, total_rows(z_s[:, j * D : j * D + 256]))
        gain_row(3, where, total_rows(z_s[:, j * D + 512 : j * D + 768]))

    def norm_first(i):
        rows = cols(i, 128)
        back, gain, shift = norm_back(tok[rows, :].astype(F32), x2_s[rows, :], vecf[0:1, :])
        tok_grad[rows, :] = (dx[rows, :] + back).astype(BF16)
        gain_row(0, slice(None), gain)
        gain_row(1, slice(None), shift)

    loop(block // 128, norm_first)
    vec.begin(0)
    scatter.go_one(10)
    scatter.go_z(9)
    scatter.after_z(6)
    vec_step(0)
    scatter.go_one(11)
    scatter.go_z(10)
    scatter.after_z(7)
    vec_step(1)
    scatter.go_z(11)
    scatter.after_z(8)
    vec_step(2)
    scatter.after_z(9)
    vec_step(3)
    scatter.after_z(10)
    scatter.after_z(11)
    scatter.sent()
    vec.sent()
    loop(PAIRS, lambda pair: halo(pair).wait_send())


def backward_all(full, vec_low, tok, dy, grad, fill, *saved):
    block = tok.shape[0]
    near = block + REACH
    tiles = block // TILE
    hbm, vmem = pl.BlockSpec(memory_space=pl.ANY), pl.BlockSpec(memory_space=pltpu.VMEM)
    vec_shape = vec_low.shape
    rows = (block, D)
    buffers = [
        ((C, Y, X, Z, NP) + PIECE, BF16),
        ((NP - 4, Y, X, Z) + PIECE, BF16),
        ((NP, 2, Z) + PIECE, BF16),
        ((NP, Z) + PIECE, BF16),
        ((NP, Z - 1) + PIECE, BF16),
        ((4 * D, D), BF16),
        ((2, C, Y, X, Z) + PIECE, BF16),
        ((tiles, SPAN, TILE), F32),
        (vec_shape, F32),
        (rows, BF16),
        (rows, BF16),
        *[(array.shape, array.dtype) for array in saved[:-1]],
        ((block, 3 * D), BF16),
        ((block, 4 * D), BF16),
        (rows, F32),
        (rows, BF16),
        ((near, 128), F32),
        ((near, 128), F32),
        ((PAIRS, 2, REACH, 128), BF16),
        ((PAIRS, 2, REACH, 128), BF16),
        ((4,) + vec_shape, F32),
        ((6,) + vec_shape, F32),
    ]
    semaphores = [(NP, 8), (NP, 8), (6,), (6,), (PAIRS,), (PAIRS,), (11,), (2,), (4,), (4,)]
    return pl.pallas_call(
        backward_kernel,
        out_shape=(
            jax.ShapeDtypeStruct((NP,) + PIECE, F32),
            jax.ShapeDtypeStruct(vec_shape, F32),
            jax.ShapeDtypeStruct(rows, BF16),
        ),
        in_specs=[hbm, vmem, hbm, hbm, hbm, hbm] + [hbm] * len(saved),
        out_specs=(vmem, vmem, vmem),
        scratch_shapes=[pltpu.VMEM(*one) for one in buffers] + [pltpu.SemaphoreType.DMA(one) for one in semaphores],
        compiler_params=pltpu.CompilerParams(
            collective_id=1, has_side_effects=True, vmem_limit_bytes=60 << 20
        ),
        name="backward_all",
    )(full, vec_low, tok, dy, grad, fill, *saved)


def update_kernel(rate, pieces, result, back, *refs):
    masters, velocities, averages, grads, news, moving, means, copies = [refs[k : k + 4] for k in range(0, 32, 4)]
    refs[32][...] = result[...]
    refs[33][...] = back[...]

    def one(k, rows, where, grad):
        new, velocity, average = update(
            masters[k][rows, where], grad, velocities[k][rows, where], averages[k][rows, where], rate
        )
        grads[k][rows, where] = grad
        news[k][rows, where] = new
        moving[k][rows, where] = velocity
        means[k][rows, where] = average

    for t in range(NP):
        piece = pieces[t]
        if t < 4:
            one(3, slice(t % 2 * 48, t % 2 * 48 + 48), slice(t // 2 * 384, t // 2 * 384 + 384), piece)
            continue
        k, j = (2, t - 4) if t < 8 else (1, 0)
        for half in range(2):
            if t > 8:
                part, col = piece[half * 24 : half * 24 + 24], 0
                for start, width in qkv_columns(t - 9, half):
                    one(0, slice(0, 24), slice(start, start + width), part[:, col : col + width])
                    col += width
                continue
            col = (2 * j + half) * 384
            one(k, slice(0, 24), slice(col, col + 384), piece[half * 24 : half * 24 + 24])
    for k in range(4):
        copies[k][...] = news[k][...].astype(BF16)


def update_all(rate, pieces, result, back, masters, velocities, averages):
    shapes = [jax.ShapeDtypeStruct(w.shape, F32) for w in masters] * 4
    shapes += [jax.ShapeDtypeStruct(w.shape, BF16) for w in masters]
    shapes += [jax.ShapeDtypeStruct(result.shape, BF16), jax.ShapeDtypeStruct(back.shape, BF16)]
    vmem = pl.BlockSpec(memory_space=pltpu.VMEM)
    return pl.pallas_call(
        functools.partial(update_kernel, rate),
        out_shape=tuple(shapes),
        in_specs=[vmem] * 15,
        out_specs=tuple([vmem] * 22),
        name="update_all",
    )(pieces, result, back, *masters, *velocities, *averages)


def on_device_fast(
    tokens,
    segments,
    cotangent,
    qkv_weight,
    proj_weight,
    up_weight,
    down_weight,
    vec_params,
    qkv_velocity,
    proj_velocity,
    up_velocity,
    down_velocity,
    vec_velocity,
    qkv_average,
    proj_average,
    up_average,
    down_average,
    vec_average,
):
    block = tokens.shape[1]
    total_tokens = lax.axis_size("dp") * segments.shape[1]
    rate = 0.05 / math.sqrt(total_tokens)
    position = lax.axis_index("blk")
    shard = lax.axis_index("dp") * lax.axis_size("blk") + position
    masters = (qkv_weight, proj_weight, up_weight, down_weight)
    vec_placed = lax.dynamic_update_slice(
        jnp.zeros((16, D), jnp.bfloat16), vec_params.astype(jnp.bfloat16), (0, shard * vec_params.shape[1])
    )
    full, vec_low, result, *saved, act, slope, down, fill = forward_all(
        masters, vec_placed, tokens[0], cotangent[0], segments
    )
    pieces, vec_sum, back = backward_all(full, vec_low, tokens[0], cotangent[0], down, fill, *saved, slope)
    velocities = (qkv_velocity, proj_velocity, up_velocity, down_velocity)
    averages = (qkv_average, proj_average, up_average, down_average)
    done = update_all(rate, pieces, result, back, masters, velocities, averages)
    vec_share = lax.dynamic_slice(vec_sum, (0, shard * vec_params.shape[1]), vec_params.shape)
    vec_new = update(vec_params, vec_share, vec_velocity, vec_average, rate)
    return (
        done[20][None],
        done[21][None],
        *done[0:4],
        vec_share,
        *done[4:8],
        vec_new[0],
        *done[8:12],
        vec_new[1],
        *done[12:16],
        vec_new[2],
        *done[16:20],
        vec_new[0].astype(jnp.bfloat16),
    )


def solution(mesh):
    fits = mesh.shape["dp"] == Z * Y * C and mesh.shape["blk"] == X
    return jax.shard_map(
        on_device_fast if fits else on_device,
        mesh=mesh,
        in_specs=(
            P("dp", "blk", None),
            P("dp", None),
            P("dp", "blk", None),
            P(("dp", "blk"), None),
            P(("dp", "blk"), None),
            P(("dp", "blk"), None),
            P(("dp", "blk"), None),
            P(None, ("dp", "blk")),
            P(("dp", "blk"), None),
            P(("dp", "blk"), None),
            P(("dp", "blk"), None),
            P(("dp", "blk"), None),
            P(None, ("dp", "blk")),
            P(("dp", "blk"), None),
            P(("dp", "blk"), None),
            P(("dp", "blk"), None),
            P(("dp", "blk"), None),
            P(None, ("dp", "blk")),
        ),
        out_specs=(
            P("dp", "blk", None),
            P("dp", "blk", None),
            P(("dp", "blk"), None),
            P(("dp", "blk"), None),
            P(("dp", "blk"), None),
            P(("dp", "blk"), None),
            P(None, ("dp", "blk")),
            P(("dp", "blk"), None),
            P(("dp", "blk"), None),
            P(("dp", "blk"), None),
            P(("dp", "blk"), None),
            P(None, ("dp", "blk")),
            P(("dp", "blk"), None),
            P(("dp", "blk"), None),
            P(("dp", "blk"), None),
            P(("dp", "blk"), None),
            P(None, ("dp", "blk")),
            P(("dp", "blk"), None),
            P(("dp", "blk"), None),
            P(("dp", "blk"), None),
            P(("dp", "blk"), None),
            P(None, ("dp", "blk")),
            P(("dp", "blk"), None),
            P(("dp", "blk"), None),
            P(("dp", "blk"), None),
            P(("dp", "blk"), None),
            P(None, ("dp", "blk")),
        ),
        check_vma=False,
    )
```

```python
import functools
import math

import jax
import jax.numpy as jnp
from jax import lax
from jax.experimental import pallas as pl
from jax.experimental.pallas import tpu as pltpu
from jax.sharding import PartitionSpec as P

D = 768
HEADS = 12
HEAD_DIM = 64


def layer_norm(value, gain, shift):
    mean = jnp.mean(value, axis=-1, keepdims=True)
    cent = value - mean
    var = jnp.mean(cent * cent, axis=-1, keepdims=True)
    return cent * lax.rsqrt(var + 1e-06) * (1.0 + gain) + shift


def gelu_exact(value):
    return jax.nn.gelu(value, approximate=False)


def contract_tokens(left, right):
    return lax.dot_general(
        left.reshape(-1, left.shape[-1]),
        right.reshape(-1, right.shape[-1]),
        (((0,), (0,)), ((), ())),
        preferred_element_type=jnp.float32,
    )


def times_transpose(left, weight):
    return lax.dot_general(
        left, weight, (((left.ndim - 1,), (1,)), ((), ())), preferred_element_type=jnp.float32
    )


def group_size(rows, block):
    limit = max(1, 512 // block)
    best = 1
    for cand in range(1, rows + 1):
        if rows % cand == 0 and cand <= limit:
            best = cand
    return best


def scores_of(query, keys, seg_query, seg_keys):
    scores = jnp.einsum(
        "gqhd,gkhd->ghqk", query, keys, preferred_element_type=jnp.float32
    ) * HEAD_DIM ** (-0.5)
    allowed = (seg_query[:, :, None] == seg_keys[:, None, :])[:, None]
    return (scores, allowed)


def attend_back(query, kv_all, grad_out, seg_query, segments, group):
    rows, block = (query.shape[0], query.shape[1])
    length = kv_all.shape[1]
    keys = kv_all[0:group, :, :D].reshape(group, length, HEADS, HEAD_DIM)
    values = kv_all[0:group, :, D:].reshape(group, length, HEADS, HEAD_DIM)
    scores, allowed = scores_of(query, keys, seg_query, segments)
    probs = jax.nn.softmax(jnp.where(allowed, scores, -1e30), axis=-1)
    probs_low = probs.astype(jnp.bfloat16)
    prob_grad = jnp.einsum("gqhd,gkhd->ghqk", grad_out, values, preferred_element_type=jnp.float32)
    score_grad = probs * (prob_grad - jnp.sum(probs * prob_grad, axis=-1, keepdims=True))
    score_low = score_grad.astype(jnp.bfloat16)
    dq_part = jnp.einsum(
        "ghqk,gkhd->gqhd", score_low, keys, preferred_element_type=jnp.float32
    ) * HEAD_DIM ** (-0.5)
    dk_part = jnp.einsum(
        "ghqk,gqhd->gkhd", score_low, query, preferred_element_type=jnp.float32
    ) * HEAD_DIM ** (-0.5)
    dv_part = jnp.einsum("ghqk,gqhd->gkhd", probs_low, grad_out, preferred_element_type=jnp.float32)
    dq_parts = dq_part.reshape(group, block, D)
    dkv_parts = jnp.concatenate(
        [dk_part.reshape(group, length, D), dv_part.reshape(group, length, D)], axis=-1
    )
    return (dq_parts, dkv_parts)


def update(weight, grad, velocity, average, rate):
    step_value = grad + 0.0005 * weight
    velocity_new = 0.9 * velocity + step_value
    weight_new = weight - rate * (step_value + 0.9 * velocity_new)
    average_new = 0.9 * average + 0.1 * weight_new
    return (weight_new, velocity_new, average_new)


def on_device(
    tokens,
    segments,
    cotangent,
    qkv_weight,
    proj_weight,
    up_weight,
    down_weight,
    vec_params,
    qkv_velocity,
    proj_velocity,
    up_velocity,
    down_velocity,
    vec_velocity,
    qkv_average,
    proj_average,
    up_average,
    down_average,
    vec_average,
):
    rows, block = (tokens.shape[0], tokens.shape[1])
    length = segments.shape[1]
    total_tokens = rows * lax.axis_size("dp") * length
    rate = 0.05 / math.sqrt(total_tokens)
    group = group_size(rows, block)
    gathered = (
        lax.all_gather(qkv_weight.astype(jnp.bfloat16), ("dp", "blk"), axis=0, tiled=True),
        lax.all_gather(proj_weight.astype(jnp.bfloat16), ("dp", "blk"), axis=0, tiled=True),
        lax.all_gather(up_weight.astype(jnp.bfloat16), ("dp", "blk"), axis=0, tiled=True),
        lax.all_gather(down_weight.astype(jnp.bfloat16), ("dp", "blk"), axis=0, tiled=True),
        lax.all_gather(vec_params.astype(jnp.bfloat16), ("dp", "blk"), axis=1, tiled=True),
    )
    w_query, w_proj, w_up, w_down, vec_low = gathered
    vec = vec_low.astype(jnp.float32)
    bias_up = vec[8:12].reshape(-1)
    position = lax.axis_index("blk")
    seg_query = lax.dynamic_slice_in_dim(segments, position * block, block, 1)
    inputs = tokens.astype(jnp.float32)
    a_one = layer_norm(inputs, vec[0], vec[1]).astype(jnp.bfloat16)
    zero_bias = jnp.zeros_like(vec[2])
    pre = jnp.dot(a_one, w_query, preferred_element_type=jnp.float32) + jnp.concatenate(
        [vec[2], zero_bias, vec[3]]
    )
    qkv = pre.astype(jnp.bfloat16)
    query = qkv[..., :D].reshape(rows, block, HEADS, HEAD_DIM)
    key_value = qkv[..., D:]
    piece = lax.all_gather(key_value, "blk", axis=1, tiled=True)
    top = jnp.full((rows, HEADS, block), -1e30, jnp.float32)
    count = piece.shape[1]
    keys = piece[0:group, :, :D].reshape(group, count, HEADS, HEAD_DIM)
    values = piece[0:group, :, D:].reshape(group, count, HEADS, HEAD_DIM)
    scores, allowed = scores_of(query, keys, seg_query, segments)
    scores = jnp.where(allowed, scores, -1e30)
    new_top = jnp.maximum(top, jnp.max(scores, axis=-1))
    weights = jnp.where(allowed, jnp.exp(scores - new_top[..., None]), 0.0)
    denoms = jnp.sum(weights, axis=-1)
    added = jnp.einsum(
        "ghqk,gkhd->gqhd", weights.astype(jnp.bfloat16), values, preferred_element_type=jnp.float32
    )
    mixed = (added / jnp.transpose(denoms, (0, 2, 1))[..., None]).reshape(rows, block, D)
    mixed_low = mixed.astype(jnp.bfloat16)
    second = inputs + jnp.dot(mixed_low, w_proj, preferred_element_type=jnp.float32) + vec[4]
    second_norm, norm_two_back = jax.vjp(layer_norm, second, vec[5], vec[6])
    a_two = second_norm.astype(jnp.bfloat16)
    hidden = jnp.dot(a_two, w_up, preferred_element_type=jnp.float32) + bias_up
    act_value, gelu_back = jax.vjp(gelu_exact, hidden)
    act = act_value.astype(jnp.bfloat16)
    result = second + jnp.dot(act, w_down, preferred_element_type=jnp.float32) + vec[7]
    output = result.astype(jnp.bfloat16)
    out_grad = cotangent.astype(jnp.float32)
    grad_down = contract_tokens(act, cotangent)
    bias_down_grad = jnp.sum(out_grad, axis=(0, 1))
    act_grad = times_transpose(cotangent, w_down)
    hidden_grad = gelu_back(act_grad)[0].astype(jnp.bfloat16)
    bias_up_grad = jnp.sum(hidden_grad.astype(jnp.float32), axis=(0, 1))
    grad_up = contract_tokens(a_two, hidden_grad)
    a_two_grad = times_transpose(hidden_grad, w_up)
    second_part, gain_two_grad, shift_two_grad = norm_two_back(a_two_grad)
    second_grad = out_grad + second_part
    attn_grad = second_grad.astype(jnp.bfloat16)
    bias_proj_grad = jnp.sum(attn_grad.astype(jnp.float32), axis=(0, 1))
    grad_proj = contract_tokens(mixed_low, attn_grad)
    mixed_grad = (
        times_transpose(attn_grad, w_proj)
        .astype(jnp.bfloat16)
        .reshape(rows, block, HEADS, HEAD_DIM)
    )
    kv_again = lax.all_gather(key_value, "blk", axis=1, tiled=True)
    query_grad, kv_terms = attend_back(query, kv_again, mixed_grad, seg_query, segments, group)
    kv_grad = lax.psum_scatter(
        kv_terms.astype(jnp.bfloat16), "blk", scatter_dimension=1, tiled=True
    ).astype(jnp.float32)
    qkv_grad_low = jnp.concatenate([query_grad, kv_grad], axis=-1).astype(jnp.bfloat16)
    qkv_sums = jnp.sum(qkv_grad_low.astype(jnp.float32), axis=(0, 1))
    grad_query = contract_tokens(a_one, qkv_grad_low)
    a_one_grad = times_transpose(qkv_grad_low, w_query)
    norm_one_back = jax.vjp(layer_norm, inputs, vec[0], vec[1])[1]
    first_part, gain_one_grad, shift_one_grad = norm_one_back(a_one_grad)
    tokens_grad = (second_grad + first_part).astype(jnp.bfloat16)
    vec_local = jnp.concatenate(
        [
            jnp.stack(
                [
                    gain_one_grad,
                    shift_one_grad,
                    qkv_sums[:D],
                    qkv_sums[2 * D :],
                    bias_proj_grad,
                    gain_two_grad,
                    shift_two_grad,
                    bias_down_grad,
                ]
            ),
            bias_up_grad.reshape(4, D),
        ],
        axis=0,
    )
    query_share, proj_share, up_share, down_share, vec_share = (
        lax.psum_scatter(grad_query, ("dp", "blk"), scatter_dimension=0, tiled=True),
        lax.psum_scatter(grad_proj, ("dp", "blk"), scatter_dimension=0, tiled=True),
        lax.psum_scatter(grad_up, ("dp", "blk"), scatter_dimension=0, tiled=True),
        lax.psum_scatter(grad_down, ("dp", "blk"), scatter_dimension=0, tiled=True),
        lax.psum_scatter(vec_local, ("dp", "blk"), scatter_dimension=1, tiled=True),
    )
    qkv_new = update(qkv_weight, query_share, qkv_velocity, qkv_average, rate)
    proj_new = update(proj_weight, proj_share, proj_velocity, proj_average, rate)
    up_new = update(up_weight, up_share, up_velocity, up_average, rate)
    down_new = update(down_weight, down_share, down_velocity, down_average, rate)
    vec_new = update(vec_params, vec_share, vec_velocity, vec_average, rate)
    return (
        output,
        tokens_grad,
        query_share,
        proj_share,
        up_share,
        down_share,
        vec_share,
        qkv_new[0],
        proj_new[0],
        up_new[0],
        down_new[0],
        vec_new[0],
        qkv_new[1],
        proj_new[1],
        up_new[1],
        down_new[1],
        vec_new[1],
        qkv_new[2],
        proj_new[2],
        up_new[2],
        down_new[2],
        vec_new[2],
        qkv_new[0].astype(jnp.bfloat16),
        proj_new[0].astype(jnp.bfloat16),
        up_new[0].astype(jnp.bfloat16),
        down_new[0].astype(jnp.bfloat16),
        vec_new[0].astype(jnp.bfloat16),
    )


PIECE = (48, 384)
NP = 12
Z, Y, X, C = 4, 2, 2, 2
AHEAD = 2
TILE = 128
IMG_MAX = 198
REACH = (IMG_MAX - 1 + 15) // 16 * 16
SPAN = TILE + 2 * REACH
GATHER_SPLIT = ((0, NP, 2),)
PAIRS = HEADS // 2
MESH = pl.DeviceIdType.MESH
F32, BF16 = jnp.float32, jnp.bfloat16
NT = (((1,), (1,)), ((), ()))
TN = (((0,), (0,)), ((), ()))


def place():
    d, x = lax.axis_index("dp"), lax.axis_index("blk")
    return d // (2 * Y), (d // 2) % Y, d % 2, x


def ident(z, y, c, x):
    return ((z * Y + y) * 2 + c, x)


def greet(z, y, c, x):
    barrier = pltpu.get_barrier_semaphore()
    peers = [ident((z + k) % Z, y, c, x) for k in range(1, Z)]
    peers += [ident(z, 1 - y, c, x), ident(z, y, c, 1 - x), ident(z, y, 1 - c, x)]
    for peer in peers:
        pl.semaphore_signal(barrier, inc=1, device_id=peer, device_id_type=MESH)
    return lambda: pl.semaphore_wait(barrier, len(peers))


def remote(src, dst, send, recv, peer):
    return pltpu.make_async_remote_copy(
        src_ref=src, dst_ref=dst, send_sem=send, recv_sem=recv, device_id=peer, device_id_type=MESH
    )


def begin(copies):
    for copy in copies:
        copy.start()


def arrive(copies):
    for copy in copies:
        copy.wait_recv()


def within(index, low, high, run):
    if isinstance(index, int):
        if low <= index < high:
            run()
    else:
        pl.when(jnp.logical_and(index >= low, index < high))(run)


def loop(count, body):
    def step(i, carry):
        body(i)
        return carry

    lax.fori_loop(0, count, step, 0)


def cols(j, width):
    return pl.ds(pl.multiple_of(j * width, width), width)


def dot(a, b, dims=None):
    dims = (((1,), (0,)), ((), ())) if dims is None else dims
    return lax.dot_general(a, b, dims, preferred_element_type=F32)


class Vec:
    def __init__(self, at, now, got, send, recv):
        self.at, self.now, self.got, self.send, self.recv = at, now, got, send, recv

    def copies(self, step):
        z, y, c, x = self.at
        peers = [
            [ident(z, y, 1 - c, x)],
            [ident(z, y, c, 1 - x)],
            [ident(z, 1 - y, c, x)],
            [ident((z + k) % Z, y, c, x) for k in range(1, Z)],
        ][step]
        return [
            remote(self.now.at[step], self.got.at[step + k], self.send.at[step + k], self.recv.at[step + k], peer)
            for k, peer in enumerate(peers)
        ]

    def begin(self, step):
        begin(self.copies(step))

    def total(self, step):
        copies = self.copies(step)
        arrive(copies)
        total = self.now[step]
        for k in range(len(copies)):
            total = total + self.got[step + k]
        return total

    def sent(self):
        for step in range(4):
            for copy in self.copies(step):
                copy.wait_send()


def normal(value):
    mean = jnp.mean(value, axis=-1, keepdims=True)
    cent = value - mean
    var = jnp.mean(cent * cent, axis=-1, keepdims=True)
    scale = lax.rsqrt(var + 1e-06)
    return cent * scale, scale


def window_start(i, x, tiles):
    near = tiles * TILE + REACH
    first = max(i * TILE - REACH, 0)
    count = min((i + 1) * TILE + REACH, near) - first
    start = jnp.where(x == 0, first, near - first - count)
    return jnp.where(x == 0, i, tiles - 1 - i), start, count


def window(i, x, tiles):
    tile, start, count = window_start(i, x, tiles)
    return tile, pl.ds(pl.multiple_of(start, 16), count), count


def mask_fill(seg, seg_col, bias, x, tiles):
    length = seg.shape[1]
    for k in range(length // TILE):
        row = seg[0:1, k * TILE : k * TILE + TILE].astype(F32)
        seg_col[k * TILE : k * TILE + TILE, :] = jnp.transpose(jnp.broadcast_to(row, (TILE, TILE)))
    for i in range(tiles):
        tile, start, count = window_start(i, x, tiles)
        start = start + x * (length - tiles * TILE - REACH)
        row = seg[0:1, pl.ds(pl.multiple_of((x * tiles + tile) * TILE, TILE), TILE)].astype(F32)
        column = seg_col[pl.ds(pl.multiple_of(start, 16), count), :]
        bias[i, 0:count] = jnp.where(column == row, 0.0, -1e30).astype(F32)


def split_heads(pair_block):
    lane = lax.broadcasted_iota(jnp.int32, pair_block.shape, 1)
    zero = jnp.zeros_like(pair_block)
    return jnp.concatenate(
        [jnp.where(lane < HEAD_DIM, pair_block, zero), jnp.where(lane < HEAD_DIM, zero, pair_block)], axis=0
    )


def join_heads(both):
    own = jnp.concatenate([both[:HEAD_DIM, :TILE], both[HEAD_DIM:, TILE:]], axis=0)
    return jnp.transpose(own)


def rows_from_stage(stage, target, t):
    left, right = cols(2 * t, 384), cols(2 * t + 1, 384)

    def group(g):
        parts = [stage[c, g % Y, x, g // Y].astype(F32) for c in range(C) for x in range(X)]
        rows = pl.ds(pl.multiple_of(g * 96, 96), 96)
        target[rows, left] = jnp.concatenate([p[:24] for p in parts], axis=0).astype(BF16)
        target[rows, right] = jnp.concatenate([p[24:] for p in parts], axis=0).astype(BF16)

    loop(Z * Y, group)


def down_copies(full, target, t, sem):
    half, col = (t - 8) % 2 * 48, (t - 8) // 2 * 384

    def group(g):
        for c in range(C):
            for x in range(X):
                row = pl.multiple_of(g * 384 + (c * X + x) * 96 + half, 16)
                pltpu.make_async_copy(
                    full.at[c, g % Y, x, g // Y, t], target.at[pl.ds(row, 48), col : col + 384], sem
                ).start()

    loop(Z * Y, group)


def qkv_columns(j, half):
    if half == 0:
        return (256 * j, 256), (D + 256 * j, 128)
    return (D + 256 * j + 128, 128), (2 * D + 256 * j, 256)


class Gather:
    def __init__(self, at, unit, full, own, send, recv):
        self.at, self.unit, self.full, self.own, self.send, self.recv = at, unit, full, own, send, recv

    def mine(self, t):
        z, y, c, x = self.at
        return pltpu.make_async_copy(self.unit.at[t], self.full.at[c, y, x, z, t], self.own.at[t])

    def first(self, t):
        z, y, c, x = self.at
        return [
            remote(
                self.unit.at[t], self.full.at[c, y, x, z, t], self.send.at[t, k - 1], self.recv.at[t, k - 1],
                ident((z + k) % Z, y, c, x),
            )
            for k in range(1, Z)
        ]

    def second(self, t, low):
        z, y, c, x = self.at
        one, two = self.full.at[c, y, x, 0:low, t], self.full.at[c, y, x, low:Z, t]
        return [
            remote(one, one, self.send.at[t, 3], self.recv.at[t, 3], ident(z, y, c, 1 - x)),
            remote(two, two, self.send.at[t, 4], self.recv.at[t, 4], ident(z, 1 - y, c, x)),
        ]

    def third(self, t, low):
        z, y, c, x = self.at
        one, two = self.full.at[c, y, :, 0:low, t], self.full.at[c, :, x, low:Z, t]
        return [
            remote(one, one, self.send.at[t, 5], self.recv.at[t, 5], ident(z, 1 - y, c, x)),
            remote(two, two, self.send.at[t, 6], self.recv.at[t, 6], ident(z, y, c, 1 - x)),
        ]

    def last(self, t):
        z, y, c, x = self.at
        block = self.full.at[c, :, :, :, t]
        return [remote(block, block, self.send.at[t, 7], self.recv.at[t, 7], ident(z, y, 1 - c, x))]

    def start(self):
        loop(NP, lambda t: self.mine(t).start())
        loop(AHEAD, lambda t: begin(self.first(t)))

    def progress(self, i):
        def to_second(t, low):
            self.mine(t).wait()
            arrive(self.first(t))
            begin(self.second(t, low))

        def to_third(t, low):
            arrive(self.second(t, low))
            begin(self.third(t, low))

        def to_last(t, low):
            arrive(self.third(t, low))
            begin(self.last(t))

        for first, end, low in GATHER_SPLIT:
            within(i, first, end, lambda: to_second(i, low))
        for first, end, low in GATHER_SPLIT:
            within(i - 1, first, end, lambda: to_third(i - 1, low))
        for first, end, low in GATHER_SPLIT:
            within(i - 2, first, end, lambda: to_last(i - 2, low))
        within(i + AHEAD, AHEAD, NP, lambda: begin(self.first(i + AHEAD)))

    def sent(self):
        for first, end, low in GATHER_SPLIT:
            def one(t):
                for copy in self.first(t) + self.second(t, low) + self.third(t, low) + self.last(t):
                    copy.wait_send()

            lax.fori_loop(first, end, lambda t, carry: (one(t), carry)[1], 0)


def forward_kernel(
    w_qkv, w_proj, w_up, w_down, vec_in, tok, dy, seg,
    full, vec_out, out_o, q_o, k_o, v_o, o_o, stat_o, x2_o, a2_o, z_o, slope_o, grad_o, bias_o,
    unit, seg_col, near, a1, wbig, wdown, stage, vecf, bias, out_s, q_s, k_s, v_s, o_s, stat_s, x2_s, a2_s, z_s, slope_s, got,
    local, two, vec_now, vec_got, own, send, recv, vsend, vrecv, hsem, ssem, dsem, osem, gsend, grecv, tsend, trecv,
):
    z, y, c, x = at = place()
    block = tok.shape[0]
    tiles = block // TILE
    offset = pl.multiple_of(x * REACH, 16)
    greeted = greet(*at)
    vec_now[0] = vec_in[...]

    def pack(t, weight, j):
        left, right = weight[:, j * 768 : j * 768 + 384], weight[:, j * 768 + 384 : j * 768 + 768]
        unit[t] = jnp.concatenate([left, right], axis=0).astype(BF16)

    for j in range(3):
        sides = []
        for half in range(2):
            parts = [w_qkv[:, start : start + width] for start, width in qkv_columns(j, half)]
            sides.append(jnp.concatenate(parts, axis=1))
        unit[j] = jnp.concatenate(sides, axis=0).astype(BF16)
    pack(3, w_proj, 0)
    for j in range(4):
        pack(4 + j, w_up, j)
        unit[8 + j] = w_down[j % 2 * 48 : j % 2 * 48 + 48, j // 2 * 384 : j // 2 * 384 + 384].astype(BF16)
    greeted()
    gather = Gather(at, unit, full, own, send, recv)
    gather.start()
    vec = Vec(at, vec_now, vec_got, vsend, vrecv)
    vec.begin(0)
    away = pl.multiple_of((1 - x) * (block - REACH), 16)
    land = pl.multiple_of(x * block, 16)
    halo = remote(
        tok.at[pl.ds(away, REACH)], near.at[pl.ds(land, REACH)], hsem.at[0], hsem.at[1], ident(z, y, c, 1 - x)
    )
    halo.start()
    near[pl.ds(offset, block), :] = tok[...]

    def put(k, src, dst):
        return pltpu.make_async_copy(src, dst, osem.at[k])

    def vec_step(step):
        total = vec.total(step)
        if step < 3:
            vec_now[step + 1] = total
            vec.begin(step + 1)
        else:
            vec_out[...] = total
            vecf[...] = total.astype(F32)

    def staged(t):
        return pltpu.make_async_copy(full.at[:, :, :, :, t], stage.at[t % 4], ssem.at[t % 4])

    def fetch(t):
        arrive(gather.last(t))
        staged(t).start()

    def take(t):
        staged(t).wait()
        rows_from_stage(stage.at[t % 4], wbig, t)

    def down_start(t):
        arrive(gather.last(t))
        down_copies(full, wdown, t, dsem.at[t - 8])

    def down_wait(t):
        pltpu.make_async_copy(full.at[:, :, :, :, t], stage.at[0], dsem.at[t - 8]).wait()

    gather.progress(0)
    vec_step(0)
    gather.progress(1)
    vec_step(1)
    gather.progress(2)
    vec_step(2)
    vec_step(3)
    halo.wait_recv()

    def norm_one(i):
        rows = cols(i, 240)
        value = normal(near[rows, :].astype(F32))[0]
        a1[rows, :] = (value * (1.0 + vecf[0:1, :]) + vecf[1:2, :]).astype(BF16)

    loop(near.shape[0] // 240, norm_one)
    mask_fill(seg, seg_col, bias, x, tiles)
    put(11, bias, bias_o).start()
    def attend(pair):
        lanes = cols(pair, 128)

        for i in range(tiles):
            tile, span, count = window(i, x, tiles)
            rows = cols(tile, TILE)
            both = split_heads(q_s[rows, lanes])
            fill = bias[i, 0:count]
            scores = dot(k_s[span, lanes], both, NT) + jnp.concatenate([fill, fill], axis=1)
            top = jnp.max(scores, axis=0, keepdims=True)
            weights = jnp.exp(scores - top)
            total = jnp.sum(weights, axis=0, keepdims=True)
            mixed = dot(v_s[span, lanes], weights.astype(BF16), TN) / total
            o_s[rows, lanes] = join_heads(mixed).astype(BF16)
            stat_s[pair * tiles + i] = jnp.broadcast_to(top + jnp.log(total), (8, 2 * TILE))

    def third(j):
        fetch(j)
        gather.progress(3 + 2 * j)
        take(j)
        where = cols(j, 256)
        value = dot(a1[pl.ds(offset, block), :], wbig[:, cols(3 * j, 256)]) + vecf[2:3, where]
        q_s[:, where] = value.astype(BF16) * HEAD_DIM ** (-0.5)
        k_s[:, where] = dot(a1[...], wbig[:, cols(3 * j + 1, 256)]).astype(BF16)
        v_s[:, where] = (dot(a1[...], wbig[:, cols(3 * j + 2, 256)]) + vecf[3:4, where]).astype(BF16)
        attend(2 * j)
        gather.progress(4 + 2 * j)
        attend(2 * j + 1)

    loop(3, third)
    put(0, k_s, k_o).start()
    put(1, v_s, v_o).start()
    put(2, q_s, q_o).start()
    put(3, o_s, o_o).start()
    put(4, stat_s, stat_o).start()
    fetch(3)
    take(3)
    fetch(4)
    fetch(5)
    gather.progress(9)

    def project(j):
        value = dot(o_s[...], wbig[:, cols(j + 9, 256)])
        x2_s[:, cols(j, 256)] = tok[:, cols(j, 256)].astype(F32) + value + vecf[4:5, cols(j, 256)]

    loop(3, project)

    def norm_two(i):
        rows = pl.ds(pl.multiple_of(i * 256, 256), 256)
        value = normal(x2_s[rows, :])[0]
        a2_s[rows, :] = (value * (1.0 + vecf[5:6, :]) + vecf[6:7, :]).astype(BF16)

    loop(block // 256, norm_two)
    put(5, x2_s, x2_o).start()
    put(6, a2_s, a2_o).start()
    gather.progress(10)
    take(4)
    take(5)
    fetch(6)
    fetch(7)

    def expand(j):
        u = dot(a2_s[...], wbig[:, cols(j + 12, 256)])
        u = u + vecf[pl.ds(8 + j // 3, 1), pl.ds(pl.multiple_of((j % 3) * 256, 256), 256)]
        half = 0.5 + 0.5 * lax.erf(u * math.sqrt(0.5))
        z_s[:, cols(j, 256)] = (u * half).astype(BF16)
        slope = half + u * (jnp.exp(-0.5 * u * u) * (1.0 / math.sqrt(2.0 * math.pi)))
        slope_s[:, cols(j, 256)] = slope.astype(BF16)

    loop(5, expand)
    gather.progress(11)
    take(6)
    take(7)
    loop(5, lambda j: expand(j + 5))
    gather.progress(12)
    down_start(8)
    loop(2, lambda j: expand(j + 10))
    put(7, z_s, z_o).start()
    put(8, slope_s, slope_o).start()

    def core(t):
        peer = ident(z, y, 1 - c, x)
        return remote(local.at[1 - c, :, :, :, t], got.at[t], gsend.at[t], grecv.at[t], peer)

    for half in range(2):
        def down_grad(g):
            value = dot(z_s[:, cols(g, 384)], dy[:, half * 384 : half * 384 + 384], TN).astype(BF16)
            for k in range(4):
                for row in range(2):
                    part = value[k * 96 + row * 48 : k * 96 + row * 48 + 48]
                    local[k // 2, g % Y, k % 2, g // Y, 2 * half + row] = part

        loop(Z * Y, down_grad)
        core(2 * half).start()
        core(2 * half + 1).start()
        if half == 0:
            gather.progress(13)
            down_start(9)
    down_start(10)

    def contract(half):
        col = slice(half * 384, half * 384 + 384)
        value = dot(z_s[...], wdown[:, col])
        out_s[:, col] = (x2_s[:, col] + value + vecf[7:8, col]).astype(BF16)

    def gain(t):
        core(t).wait_recv()
        for a in range(Y):
            for b in range(X):
                own_part = local[c, a, b, :, t].astype(F32)
                got[t, a, b] = (own_part + got[t, a, b].astype(F32)).astype(BF16)

    def ahead(t):
        along_y, along_x = ident(z, 1 - y, c, x), ident(z, y, c, 1 - x)
        return [
            remote(got.at[t, 1 - y, :, 0:2], two.at[t, :, 0:2], tsend.at[t, 0], trecv.at[t, 0], along_y),
            remote(got.at[t, :, 1 - x, 2:Z], two.at[t, :, 2:Z], tsend.at[t, 1], trecv.at[t, 1], along_x),
        ]

    down_wait(8)
    down_wait(9)
    contract(0)
    for t in range(4):
        gain(t)
        if t < 2:
            begin(ahead(t))
    late = pltpu.make_async_copy(got.at[2:4], grad_o.at[2:4], osem.at[10])
    late.start()
    down_start(11)
    down_wait(10)
    down_wait(11)
    contract(1)
    put(9, out_s, out_o).start()
    pairs = [(k_s, k_o), (v_s, v_o), (q_s, q_o), (o_s, o_o), (stat_s, stat_o), (x2_s, x2_o), (a2_s, a2_o)]
    for k, (src, dst) in enumerate(pairs + [(z_s, z_o), (slope_s, slope_o), (out_s, out_o)]):
        put(k, src, dst).wait()
    for t in range(2):
        arrive(ahead(t))
        for b in range(2):
            low, high = got[t, y, b, 0:2].astype(F32), got[t, b, x, 2:Z].astype(F32)
            got[t, y, b, 0:2] = (low + two[t, b, 0:2].astype(F32)).astype(BF16)
            got[t, b, x, 2:Z] = (high + two[t, b, 2:Z].astype(F32)).astype(BF16)
        for copy in ahead(t):
            copy.wait_send()
    soon = pltpu.make_async_copy(got.at[0:2], grad_o.at[0:2], osem.at[12])
    soon.start()
    late.wait()
    soon.wait()
    put(11, bias, bias_o).wait()
    gather.sent()
    vec.sent()
    halo.wait_send()
    loop(4, lambda t: core(t).wait_send())


def forward_all(weights, vec_placed, tok, dy, seg):
    block = tok.shape[0]
    near = block + REACH
    ff = 4 * D
    tiles = block // TILE
    shapes = [
        ((block, D), BF16),
        ((block, D), BF16),
        ((near, D), BF16),
        ((near, D), BF16),
        ((block, D), BF16),
        ((PAIRS * tiles, 8, 2 * TILE), F32),
        ((block, D), F32),
        ((block, D), BF16),
        ((block, ff), BF16),
        ((block, ff), BF16),
        ((4, Y, X, Z) + PIECE, BF16),
        ((tiles, SPAN, TILE), F32),
    ]
    hbm, vmem = pl.BlockSpec(memory_space=pl.ANY), pl.BlockSpec(memory_space=pltpu.VMEM)
    outs = [((C, Y, X, Z, NP) + PIECE, BF16), (vec_placed.shape, BF16)] + shapes
    return pl.pallas_call(
        forward_kernel,
        out_shape=tuple(jax.ShapeDtypeStruct(*one) for one in outs),
        in_specs=[vmem] * 8,
        out_specs=tuple([hbm, vmem] + [hbm] * len(shapes)),
        scratch_shapes=[
            pltpu.VMEM((NP,) + PIECE, BF16),
            pltpu.VMEM((seg.shape[1], TILE), F32),
            pltpu.VMEM((near, D), BF16),
            pltpu.VMEM((near, D), BF16),
            pltpu.VMEM((D, 8 * D), BF16),
            pltpu.VMEM((ff, D), BF16),
            pltpu.VMEM((4, C, Y, X, Z) + PIECE, BF16),
            pltpu.VMEM(vec_placed.shape, F32),
            *[pltpu.VMEM(*one) for one in shapes[-1:] + shapes[:-1]],
            pltpu.VMEM((C, Y, X, Z, 4) + PIECE, BF16),
            pltpu.VMEM((2, 2, Z) + PIECE, BF16),
            pltpu.VMEM((4,) + vec_placed.shape, BF16),
            pltpu.VMEM((6,) + vec_placed.shape, BF16),
            pltpu.SemaphoreType.DMA((NP,)),
            pltpu.SemaphoreType.DMA((NP, 8)),
            pltpu.SemaphoreType.DMA((NP, 8)),
            pltpu.SemaphoreType.DMA((6,)),
            pltpu.SemaphoreType.DMA((6,)),
            pltpu.SemaphoreType.DMA((2,)),
            pltpu.SemaphoreType.DMA((4,)),
            pltpu.SemaphoreType.DMA((4,)),
            pltpu.SemaphoreType.DMA((13,)),
            pltpu.SemaphoreType.DMA((4,)),
            pltpu.SemaphoreType.DMA((4,)),
            pltpu.SemaphoreType.DMA((2, 2)),
            pltpu.SemaphoreType.DMA((2, 2)),
        ],
        compiler_params=pltpu.CompilerParams(
            collective_id=0, has_side_effects=True, vmem_limit_bytes=60 << 20
        ),
        name="forward_all",
    )(*weights, vec_placed, tok, dy, seg)


SCATTER_SPLIT = ((0, NP, 2),)


class Scatter:
    def __init__(self, at, local, got_core, got_two, got_one, got_z, out, send, recv):
        self.at, self.local, self.out, self.send, self.recv = at, local, out, send, recv
        self.got = got_core, got_two, got_one, got_z

    def core(self, t):
        z, y, c, x = self.at
        peer = ident(z, y, 1 - c, x)
        return [remote(self.local.at[1 - c, :, :, :, t], self.got[0].at[t - 4], self.send.at[t, 0], self.recv.at[t, 0], peer)]

    def two(self, t, low):
        z, y, c, x = self.at
        one, other = self.local.at[c, 1 - y, :, 0:low, t], self.local.at[c, :, 1 - x, low:Z, t]
        got = self.got[1].at[t]
        return [
            remote(one, got.at[:, 0:low], self.send.at[t, 1], self.recv.at[t, 1], ident(z, 1 - y, c, x)),
            remote(other, got.at[:, low:Z], self.send.at[t, 2], self.recv.at[t, 2], ident(z, y, c, 1 - x)),
        ]

    def one(self, t, low):
        z, y, c, x = self.at
        one, other = self.local.at[c, y, 1 - x, 0:low, t], self.local.at[c, 1 - y, x, low:Z, t]
        got = self.got[2].at[t]
        return [
            remote(one, got.at[0:low], self.send.at[t, 3], self.recv.at[t, 3], ident(z, y, c, 1 - x)),
            remote(other, got.at[low:Z], self.send.at[t, 4], self.recv.at[t, 4], ident(z, 1 - y, c, x)),
        ]

    def along(self, t):
        z, y, c, x = self.at
        return [
            remote(
                self.local.at[c, y, x, (z + k) % Z, t], self.got[3].at[t, k - 1], self.send.at[t, 4 + k],
                self.recv.at[t, 4 + k], ident((z + k) % Z, y, c, x),
            )
            for k in range(1, Z)
        ]

    def add(self, where, value):
        self.local[where] = (self.local[where].astype(F32) + value.astype(F32)).astype(BF16)

    def take_core(self, t):
        c = self.at[2]
        arrive(self.core(t))
        for a in range(Y):
            for b in range(X):
                self.add((c, a, b, slice(None), t), self.got[0][t - 4, a, b])

    def after_core(self, t):
        self.take_core(t)
        self.go_two(t)

    def after_two(self, t, low):
        z, y, c, x = self.at
        arrive(self.two(t, low))
        for b in range(2):
            self.add((c, y, b, slice(0, low), t), self.got[1][t, b, 0:low])
            self.add((c, b, x, slice(low, Z), t), self.got[1][t, b, low:Z])
        begin(self.one(t, low))

    def after_one(self, t, low):
        z, y, c, x = self.at
        arrive(self.one(t, low))
        self.add((c, y, x, slice(None), t), self.got[2][t])
        begin(self.along(t))

    def after_z(self, t):
        z, y, c, x = self.at
        arrive(self.along(t))
        total = self.local[c, y, x, z, t].astype(F32)
        for k in range(Z - 1):
            total = total + self.got[3][t, k].astype(F32)
        self.out[t] = total

    def go_two(self, t):
        for first, end, low in SCATTER_SPLIT:
            within(t, first, end, lambda: begin(self.two(t, low)))

    def go_one(self, t):
        for first, end, low in SCATTER_SPLIT:
            within(t, first, end, lambda: self.after_two(t, low))

    def go_z(self, t):
        arrive_one = self.after_one
        for first, end, low in SCATTER_SPLIT:
            within(t, first, end, lambda: arrive_one(t, low))

    def sent(self):
        loop(NP - 4, lambda t: self.core(t + 4)[0].wait_send())
        for first, end, low in SCATTER_SPLIT:
            def each(t):
                for copy in self.one(t, low) + self.along(t):
                    copy.wait_send()
                within(t, 2, NP, lambda: [copy.wait_send() for copy in self.two(t, low)] and None)

            lax.fori_loop(first, end, lambda t, carry: (each(t), carry)[1], 0)


def total_rows(value):
    return jnp.sum(value.astype(F32), axis=0, keepdims=True)


def norm_back(value, grad, gain):
    unit_value, scale = normal(value)
    inner = grad * (1.0 + gain)
    mean_one = jnp.mean(inner, axis=-1, keepdims=True)
    mean_two = jnp.mean(inner * unit_value, axis=-1, keepdims=True)
    back = scale * (inner - mean_one - unit_value * mean_two)
    return back, total_rows(grad * unit_value), total_rows(grad)


def backward_kernel(
    full, vec_in, tok_o, dy_o, grad_o, bias_o, q_o, k_o, v_o, o_o, stat_o, x2_o, a2_o, slope_o,
    out, vec_out, tok_grad,
    local, got_core, got_two, got_one, got_z, wbuf, stage, bias, vecf, tok, dy, q_s, k_s, v_s, o_s, stat_s, x2_s, a2_s, z_s,
    slope_s, dx, da, acc_k, acc_v, halo_s, halo_r, vec_now, vec_got, send, recv, vsend, vrecv, hsend, hrecv, isem, ssem, dsem, gsem,
):
    z, y, c, x = at = place()
    greeted = greet(*at)
    block = tok.shape[0]
    tiles = block // TILE
    offset = pl.multiple_of(x * REACH, 16)
    away = pl.multiple_of((1 - x) * (block - REACH), 16)
    outside = pl.multiple_of((1 - x) * block, 16)
    order = [4, 5, 6, 7, 3, 0, 1, 2]

    def fetch(n):
        return pltpu.make_async_copy(full.at[:, :, :, :, order[n]], stage.at[n % 2], ssem.at[n % 2])

    def take(n, use):
        fetch(n).wait()
        use(stage.at[n % 2])
        if n + 2 < len(order):
            fetch(n + 2).start()

    pairs = [
        (dy_o, dy), (slope_o, slope_s), (a2_o, a2_s), (x2_o, x2_s), (o_o, o_s), (k_o, k_s), (v_o, v_s), (q_o, q_s),
        (stat_o, stat_s), (tok_o, tok), (bias_o, bias),
    ]

    def inward(k):
        return pltpu.make_async_copy(pairs[k][0], pairs[k][1], isem.at[k])

    def grads(t):
        return pltpu.make_async_copy(grad_o.at[t], local.at[c, :, :, :, t], gsem.at[t])

    for t in range(4):
        grads(t).start()
    inward(0).start()
    for t in range(8, 12):
        down_copies(full, wbuf, t, dsem.at[t - 8])
    for n in range(2):
        fetch(n).start()
    for k in range(1, len(pairs)):
        inward(k).start()
    greeted()
    scatter = Scatter(at, local, got_core, got_two, got_one, got_z, out, send, recv)
    vec = Vec(at, vec_now, vec_got, vsend, vrecv)
    vec_now[0] = jnp.zeros(vec_now.shape[1:], F32)
    vecf[...] = vec_in[...].astype(F32)

    def vec_step(step):
        total = vec.total(step)
        if step < 3:
            vec_now[step + 1] = total
            vec.begin(step + 1)
        else:
            vec_out[...] = total

    def gain_row(row, where, value):
        vec_now[0, row : row + 1, where] = vec_now[0, row : row + 1, where] + value

    def weight_grad(left, right, t):
        def half(h):
            value = dot(left[:, cols(h, 384)], right[...], TN)
            for g in range(4):
                for k in range(4):
                    part = value[g * 96 + k * 24 : g * 96 + k * 24 + 24]
                    part = jnp.concatenate([part[:, :384], part[:, 384:]], axis=0).astype(BF16)
                    local[k // 2, g % 2, k % 2, 2 * h + g // 2, t] = part

        loop(2, half)
        begin(scatter.core(t))

    for t in range(4):
        grads(t).wait()
        if t < 2:
            begin(scatter.one(t, 2))
        else:
            scatter.go_two(t)
    inward(0).wait()
    gain_row(7, slice(None), total_rows(dy[...]))
    for t in range(8, 12):
        pltpu.make_async_copy(full.at[:, :, :, :, t], stage.at[0], dsem.at[t - 8]).wait()
    inward(1).wait()

    def hidden(n):
        rows = pl.ds(pl.multiple_of(n * 256, 256), 256)
        grad = dot(dy[...], wbuf[rows, :], NT) * slope_s[:, cols(n, 256)].astype(F32)
        low = grad.astype(BF16)
        slope_s[:, cols(n, 256)] = low
        where = pl.ds(pl.multiple_of((n % 3) * 256, 256), 256)
        vec_now[0, pl.ds(8 + n // 3, 1), where] = total_rows(low)

    loop(12, hidden)
    inward(2).wait()
    for t in range(2):
        take(t, lambda part: rows_from_stage(part, wbuf.at[pl.ds(t * D, D)], 0))
    for t in range(4):
        weight_grad(a2_s, slope_s.at[:, t * D : t * D + D], 4 + t)
    scatter.after_core(4)
    scatter.go_one(2)
    scatter.go_z(0)
    for t in range(2, 4):
        take(t, lambda part: rows_from_stage(part, wbuf.at[pl.ds(t * D, D)], 0))

    def inner_grad(n):
        value = None
        for t in range(4):
            rows = pl.ds(pl.multiple_of(t * D + n * 256, 256), 256)
            part = dot(slope_s[:, t * D : t * D + D], wbuf[rows, :], NT)
            value = part if value is None else value + part
        dx[:, cols(n, 256)] = value

    loop(3, inner_grad)
    scatter.after_core(5)
    scatter.go_one(3)
    inward(3).wait()

    def norm_two(i):
        rows = cols(i, 128)
        grad = dx[rows, :]
        back, gain, shift = norm_back(x2_s[rows, :], grad, vecf[5:6, :])
        total = dy[rows, :].astype(F32) + back
        low = total.astype(BF16)
        dx[rows, :] = total
        da[rows, :] = low
        gain_row(5, slice(None), gain)
        gain_row(6, slice(None), shift)
        gain_row(4, slice(None), total_rows(low))

    loop(block // 128, norm_two)
    scatter.after_core(6)
    scatter.after_core(7)
    scatter.go_z(1)
    inward(4).wait()
    weight_grad(o_s, da, 8)
    take(4, lambda part: rows_from_stage(part, wbuf.at[pl.ds(3 * D, D)], 0))

    def mixed_grad(n):
        rows = pl.ds(pl.multiple_of(3 * D + n * 256, 256), 256)
        o_s[:, cols(n, 256)] = dot(da[...], wbuf[rows, :], NT).astype(BF16)

    loop(3, mixed_grad)
    scatter.after_core(8)
    for k in range(5, 11):
        inward(k).wait()

    def halo(pair):
        return remote(halo_s.at[pair], halo_r.at[pair], hsend.at[pair], hrecv.at[pair], ident(z, y, c, 1 - x))

    def spot(pair, kind):
        return pl.ds(pl.multiple_of(pair // 2 * D + kind * 256 + pair % 2 * 128, 128), 128)

    def attend(pair):
        lanes = cols(pair, 128)
        scatter.go_z(2 + pair)
        within(pair, 0, 5, lambda: scatter.go_one(4 + pair))
        scatter.after_z(pair)
        acc_k[...] = jnp.zeros(acc_k.shape, F32)
        acc_v[...] = jnp.zeros(acc_v.shape, F32)

        for i in range(tiles):
            tile, span, count = window(i, x, tiles)
            rows = cols(tile, TILE)
            both, grads = split_heads(q_s[rows, lanes]), split_heads(o_s[rows, lanes])
            fill = bias[i, 0:count]
            scores = dot(k_s[span, lanes], both, NT) + jnp.concatenate([fill, fill], axis=1)
            probs = jnp.exp(scores - stat_s[pair * tiles + i][0:1])
            low = probs.astype(BF16)
            back = dot(v_s[span, lanes], grads, NT)
            mean = jnp.sum(probs * back, axis=0, keepdims=True)
            inner = (probs * (back - mean)).astype(BF16)
            acc_v[span, :] = acc_v[span, :] + dot(low, grads)
            acc_k[span, :] = acc_k[span, :] + dot(inner, both)
            query = join_heads(dot(k_s[span, lanes], inner, TN)) * HEAD_DIM ** (-0.5)
            z_s[rows, spot(pair, 0)] = query.astype(BF16)

        for k, acc in ((0, acc_k), (1, acc_v)):
            z_s[:, spot(pair, k + 1)] = acc[pl.ds(offset, block), :].astype(BF16)
            halo_s[pair, k] = acc[pl.ds(outside, REACH), :].astype(BF16)
        halo(pair).start()

    def add_halo(pair):
        halo(pair).wait_recv()
        for k in range(2):
            where = spot(pair, k + 1)
            rows = pl.ds(away, REACH)
            z_s[rows, where] = (z_s[rows, where].astype(F32) + halo_r[pair, k].astype(F32)).astype(BF16)

    def finish(j):
        add_halo(2 * j)
        add_halo(2 * j + 1)
        weight_grad(a2_s, z_s.at[:, pl.ds(pl.multiple_of(j * D, D), D)], 9 + j)

    def norm_one(i):
        rows = cols(i, 128)
        value = normal(tok[rows, :].astype(F32))[0]
        a2_s[rows, :] = (value * (1.0 + vecf[0:1, :]) + vecf[1:2, :]).astype(BF16)

    loop(block // 128, norm_one)

    def third(j):
        loop(2, lambda i: attend(2 * j + i))
        within(j, 2, 3, lambda: scatter.after_core(9))
        within(j, 1, 3, lambda: finish(j - 1))

    loop(3, third)
    finish(2)
    scatter.after_core(10)
    scatter.go_z(8)
    scatter.after_core(11)
    for n in range(5, 8):
        take(n, lambda part: rows_from_stage(part, wbuf.at[pl.ds((n - 5) * D, D)], 0))

    def first_grad(n):
        value = None
        for t in range(3):
            rows = pl.ds(pl.multiple_of(t * D + n * 256, 256), 256)
            part = dot(z_s[:, t * D : t * D + D], wbuf[rows, :], NT)
            value = part if value is None else value + part
        x2_s[:, cols(n, 256)] = value

    loop(3, first_grad)
    scatter.go_one(9)
    for j in range(3):
        where = slice(j * 256, j * 256 + 256)
        gain_row(2, where, total_rows(z_s[:, j * D : j * D + 256]))
        gain_row(3, where, total_rows(z_s[:, j * D + 512 : j * D + 768]))

    def norm_first(i):
        rows = cols(i, 128)
        back, gain, shift = norm_back(tok[rows, :].astype(F32), x2_s[rows, :], vecf[0:1, :])
        tok_grad[rows, :] = (dx[rows, :] + back).astype(BF16)
        gain_row(0, slice(None), gain)
        gain_row(1, slice(None), shift)

    loop(block // 128, norm_first)
    vec.begin(0)
    scatter.go_one(10)
    scatter.go_z(9)
    scatter.after_z(6)
    vec_step(0)
    scatter.go_one(11)
    scatter.go_z(10)
    scatter.after_z(7)
    vec_step(1)
    scatter.go_z(11)
    scatter.after_z(8)
    vec_step(2)
    scatter.after_z(9)
    vec_step(3)
    scatter.after_z(10)
    scatter.after_z(11)
    scatter.sent()
    vec.sent()
    loop(PAIRS, lambda pair: halo(pair).wait_send())


def backward_all(full, vec_low, tok, dy, grad, fill, *saved):
    block = tok.shape[0]
    near = block + REACH
    tiles = block // TILE
    hbm, vmem = pl.BlockSpec(memory_space=pl.ANY), pl.BlockSpec(memory_space=pltpu.VMEM)
    vec_shape = vec_low.shape
    rows = (block, D)
    buffers = [
        ((C, Y, X, Z, NP) + PIECE, BF16),
        ((NP - 4, Y, X, Z) + PIECE, BF16),
        ((NP, 2, Z) + PIECE, BF16),
        ((NP, Z) + PIECE, BF16),
        ((NP, Z - 1) + PIECE, BF16),
        ((4 * D, D), BF16),
        ((2, C, Y, X, Z) + PIECE, BF16),
        ((tiles, SPAN, TILE), F32),
        (vec_shape, F32),
        (rows, BF16),
        (rows, BF16),
        *[(array.shape, array.dtype) for array in saved[:-1]],
        ((block, 3 * D), BF16),
        ((block, 4 * D), BF16),
        (rows, F32),
        (rows, BF16),
        ((near, 128), F32),
        ((near, 128), F32),
        ((PAIRS, 2, REACH, 128), BF16),
        ((PAIRS, 2, REACH, 128), BF16),
        ((4,) + vec_shape, F32),
        ((6,) + vec_shape, F32),
    ]
    semaphores = [(NP, 8), (NP, 8), (6,), (6,), (PAIRS,), (PAIRS,), (11,), (2,), (4,), (4,)]
    return pl.pallas_call(
        backward_kernel,
        out_shape=(
            jax.ShapeDtypeStruct((NP,) + PIECE, F32),
            jax.ShapeDtypeStruct(vec_shape, F32),
            jax.ShapeDtypeStruct(rows, BF16),
        ),
        in_specs=[hbm, vmem, hbm, hbm, hbm, hbm] + [hbm] * len(saved),
        out_specs=(vmem, vmem, vmem),
        scratch_shapes=[pltpu.VMEM(*one) for one in buffers] + [pltpu.SemaphoreType.DMA(one) for one in semaphores],
        compiler_params=pltpu.CompilerParams(
            collective_id=1, has_side_effects=True, vmem_limit_bytes=60 << 20
        ),
        name="backward_all",
    )(full, vec_low, tok, dy, grad, fill, *saved)


def update_kernel(rate, pieces, result, back, *refs):
    masters, velocities, averages, grads, news, moving, means, copies = [refs[k : k + 4] for k in range(0, 32, 4)]
    refs[32][...] = result[...]
    refs[33][...] = back[...]

    def one(k, rows, where, grad):
        new, velocity, average = update(
            masters[k][rows, where], grad, velocities[k][rows, where], averages[k][rows, where], rate
        )
        grads[k][rows, where] = grad
        news[k][rows, where] = new
        moving[k][rows, where] = velocity
        means[k][rows, where] = average

    for t in range(NP):
        piece = pieces[t]
        if t < 4:
            one(3, slice(t % 2 * 48, t % 2 * 48 + 48), slice(t // 2 * 384, t // 2 * 384 + 384), piece)
            continue
        k, j = (2, t - 4) if t < 8 else (1, 0)
        for half in range(2):
            if t > 8:
                part, col = piece[half * 24 : half * 24 + 24], 0
                for start, width in qkv_columns(t - 9, half):
                    one(0, slice(0, 24), slice(start, start + width), part[:, col : col + width])
                    col += width
                continue
            col = (2 * j + half) * 384
            one(k, slice(0, 24), slice(col, col + 384), piece[half * 24 : half * 24 + 24])
    for k in range(4):
        copies[k][...] = news[k][...].astype(BF16)


def update_all(rate, pieces, result, back, masters, velocities, averages):
    shapes = [jax.ShapeDtypeStruct(w.shape, F32) for w in masters] * 4
    shapes += [jax.ShapeDtypeStruct(w.shape, BF16) for w in masters]
    shapes += [jax.ShapeDtypeStruct(result.shape, BF16), jax.ShapeDtypeStruct(back.shape, BF16)]
    vmem = pl.BlockSpec(memory_space=pltpu.VMEM)
    return pl.pallas_call(
        functools.partial(update_kernel, rate),
        out_shape=tuple(shapes),
        in_specs=[vmem] * 15,
        out_specs=tuple([vmem] * 22),
        name="update_all",
    )(pieces, result, back, *masters, *velocities, *averages)


def on_device_fast(
    tokens,
    segments,
    cotangent,
    qkv_weight,
    proj_weight,
    up_weight,
    down_weight,
    vec_params,
    qkv_velocity,
    proj_velocity,
    up_velocity,
    down_velocity,
    vec_velocity,
    qkv_average,
    proj_average,
    up_average,
    down_average,
    vec_average,
):
    block = tokens.shape[1]
    total_tokens = lax.axis_size("dp") * segments.shape[1]
    rate = 0.05 / math.sqrt(total_tokens)
    position = lax.axis_index("blk")
    shard = lax.axis_index("dp") * lax.axis_size("blk") + position
    masters = (qkv_weight, proj_weight, up_weight, down_weight)
    vec_placed = lax.dynamic_update_slice(
        jnp.zeros((16, D), jnp.bfloat16), vec_params.astype(jnp.bfloat16), (0, shard * vec_params.shape[1])
    )
    full, vec_low, result, *saved, act, slope, down, fill = forward_all(
        masters, vec_placed, tokens[0], cotangent[0], segments
    )
    pieces, vec_sum, back = backward_all(full, vec_low, tokens[0], cotangent[0], down, fill, *saved, slope)
    velocities = (qkv_velocity, proj_velocity, up_velocity, down_velocity)
    averages = (qkv_average, proj_average, up_average, down_average)
    done = update_all(rate, pieces, result, back, masters, velocities, averages)
    vec_share = lax.dynamic_slice(vec_sum, (0, shard * vec_params.shape[1]), vec_params.shape)
    vec_new = update(vec_params, vec_share, vec_velocity, vec_average, rate)
    return (
        done[20][None],
        done[21][None],
        *done[0:4],
        vec_share,
        *done[4:8],
        vec_new[0],
        *done[8:12],
        vec_new[1],
        *done[12:16],
        vec_new[2],
        *done[16:20],
        vec_new[0].astype(jnp.bfloat16),
    )


def solution(mesh):
    fits = mesh.shape["dp"] == Z * Y * C and mesh.shape["blk"] == X
    return jax.shard_map(
        on_device_fast if fits else on_device,
        mesh=mesh,
        in_specs=(
            P("dp", "blk", None),
            P("dp", None),
            P("dp", "blk", None),
            P(("dp", "blk"), None),
            P(("dp", "blk"), None),
            P(("dp", "blk"), None),
            P(("dp", "blk"), None),
            P(None, ("dp", "blk")),
            P(("dp", "blk"), None),
            P(("dp", "blk"), None),
            P(("dp", "blk"), None),
            P(("dp", "blk"), None),
            P(None, ("dp", "blk")),
            P(("dp", "blk"), None),
            P(("dp", "blk"), None),
            P(("dp", "blk"), None),
            P(("dp", "blk"), None),
            P(None, ("dp", "blk")),
        ),
        out_specs=(
            P("dp", "blk", None),
            P("dp", "blk", None),
            P(("dp", "blk"), None),
            P(("dp", "blk"), None),
            P(("dp", "blk"), None),
            P(("dp", "blk"), None),
            P(None, ("dp", "blk")),
            P(("dp", "blk"), None),
            P(("dp", "blk"), None),
            P(("dp", "blk"), None),
            P(("dp", "blk"), None),
            P(None, ("dp", "blk")),
            P(("dp", "blk"), None),
            P(("dp", "blk"), None),
            P(("dp", "blk"), None),
            P(("dp", "blk"), None),
            P(None, ("dp", "blk")),
            P(("dp", "blk"), None),
            P(("dp", "blk"), None),
            P(("dp", "blk"), None),
            P(("dp", "blk"), None),
            P(None, ("dp", "blk")),
            P(("dp", "blk"), None),
            P(("dp", "blk"), None),
            P(("dp", "blk"), None),
            P(("dp", "blk"), None),
            P(None, ("dp", "blk")),
        ),
        check_vma=False,
    )
```

```python
import functools
import math

import jax
import jax.numpy as jnp
from jax import lax
from jax.experimental import pallas as pl
from jax.experimental.pallas import tpu as pltpu
from jax.sharding import PartitionSpec as P

D = 768
HEADS = 12
HEAD_DIM = 64


def layer_norm(value, gain, shift):
    mean = jnp.mean(value, axis=-1, keepdims=True)
    cent = value - mean
    var = jnp.mean(cent * cent, axis=-1, keepdims=True)
    return cent * lax.rsqrt(var + 1e-06) * (1.0 + gain) + shift


def gelu_exact(value):
    return jax.nn.gelu(value, approximate=False)


def contract_tokens(left, right):
    return lax.dot_general(
        left.reshape(-1, left.shape[-1]),
        right.reshape(-1, right.shape[-1]),
        (((0,), (0,)), ((), ())),
        preferred_element_type=jnp.float32,
    )


def times_transpose(left, weight):
    return lax.dot_general(
        left, weight, (((left.ndim - 1,), (1,)), ((), ())), preferred_element_type=jnp.float32
    )


def group_size(rows, block):
    limit = max(1, 512 // block)
    best = 1
    for cand in range(1, rows + 1):
        if rows % cand == 0 and cand <= limit:
            best = cand
    return best


def scores_of(query, keys, seg_query, seg_keys):
    scores = jnp.einsum(
        "gqhd,gkhd->ghqk", query, keys, preferred_element_type=jnp.float32
    ) * HEAD_DIM ** (-0.5)
    allowed = (seg_query[:, :, None] == seg_keys[:, None, :])[:, None]
    return (scores, allowed)


def attend_back(query, kv_all, grad_out, seg_query, segments, group):
    rows, block = (query.shape[0], query.shape[1])
    length = kv_all.shape[1]
    keys = kv_all[0:group, :, :D].reshape(group, length, HEADS, HEAD_DIM)
    values = kv_all[0:group, :, D:].reshape(group, length, HEADS, HEAD_DIM)
    scores, allowed = scores_of(query, keys, seg_query, segments)
    probs = jax.nn.softmax(jnp.where(allowed, scores, -1e30), axis=-1)
    probs_low = probs.astype(jnp.bfloat16)
    prob_grad = jnp.einsum("gqhd,gkhd->ghqk", grad_out, values, preferred_element_type=jnp.float32)
    score_grad = probs * (prob_grad - jnp.sum(probs * prob_grad, axis=-1, keepdims=True))
    score_low = score_grad.astype(jnp.bfloat16)
    dq_part = jnp.einsum(
        "ghqk,gkhd->gqhd", score_low, keys, preferred_element_type=jnp.float32
    ) * HEAD_DIM ** (-0.5)
    dk_part = jnp.einsum(
        "ghqk,gqhd->gkhd", score_low, query, preferred_element_type=jnp.float32
    ) * HEAD_DIM ** (-0.5)
    dv_part = jnp.einsum("ghqk,gqhd->gkhd", probs_low, grad_out, preferred_element_type=jnp.float32)
    dq_parts = dq_part.reshape(group, block, D)
    dkv_parts = jnp.concatenate(
        [dk_part.reshape(group, length, D), dv_part.reshape(group, length, D)], axis=-1
    )
    return (dq_parts, dkv_parts)


def update(weight, grad, velocity, average, rate):
    step_value = grad + 0.0005 * weight
    velocity_new = 0.9 * velocity + step_value
    weight_new = weight - rate * (step_value + 0.9 * velocity_new)
    average_new = 0.9 * average + 0.1 * weight_new
    return (weight_new, velocity_new, average_new)


def on_device(
    tokens,
    segments,
    cotangent,
    qkv_weight,
    proj_weight,
    up_weight,
    down_weight,
    vec_params,
    qkv_velocity,
    proj_velocity,
    up_velocity,
    down_velocity,
    vec_velocity,
    qkv_average,
    proj_average,
    up_average,
    down_average,
    vec_average,
):
    rows, block = (tokens.shape[0], tokens.shape[1])
    length = segments.shape[1]
    total_tokens = rows * lax.axis_size("dp") * length
    rate = 0.05 / math.sqrt(total_tokens)
    group = group_size(rows, block)
    gathered = (
        lax.all_gather(qkv_weight.astype(jnp.bfloat16), ("dp", "blk"), axis=0, tiled=True),
        lax.all_gather(proj_weight.astype(jnp.bfloat16), ("dp", "blk"), axis=0, tiled=True),
        lax.all_gather(up_weight.astype(jnp.bfloat16), ("dp", "blk"), axis=0, tiled=True),
        lax.all_gather(down_weight.astype(jnp.bfloat16), ("dp", "blk"), axis=0, tiled=True),
        lax.all_gather(vec_params.astype(jnp.bfloat16), ("dp", "blk"), axis=1, tiled=True),
    )
    w_query, w_proj, w_up, w_down, vec_low = gathered
    vec = vec_low.astype(jnp.float32)
    bias_up = vec[8:12].reshape(-1)
    position = lax.axis_index("blk")
    seg_query = lax.dynamic_slice_in_dim(segments, position * block, block, 1)
    inputs = tokens.astype(jnp.float32)
    a_one = layer_norm(inputs, vec[0], vec[1]).astype(jnp.bfloat16)
    zero_bias = jnp.zeros_like(vec[2])
    pre = jnp.dot(a_one, w_query, preferred_element_type=jnp.float32) + jnp.concatenate(
        [vec[2], zero_bias, vec[3]]
    )
    qkv = pre.astype(jnp.bfloat16)
    query = qkv[..., :D].reshape(rows, block, HEADS, HEAD_DIM)
    key_value = qkv[..., D:]
    piece = lax.all_gather(key_value, "blk", axis=1, tiled=True)
    top = jnp.full((rows, HEADS, block), -1e30, jnp.float32)
    count = piece.shape[1]
    keys = piece[0:group, :, :D].reshape(group, count, HEADS, HEAD_DIM)
    values = piece[0:group, :, D:].reshape(group, count, HEADS, HEAD_DIM)
    scores, allowed = scores_of(query, keys, seg_query, segments)
    scores = jnp.where(allowed, scores, -1e30)
    new_top = jnp.maximum(top, jnp.max(scores, axis=-1))
    weights = jnp.where(allowed, jnp.exp(scores - new_top[..., None]), 0.0)
    denoms = jnp.sum(weights, axis=-1)
    added = jnp.einsum(
        "ghqk,gkhd->gqhd", weights.astype(jnp.bfloat16), values, preferred_element_type=jnp.float32
    )
    mixed = (added / jnp.transpose(denoms, (0, 2, 1))[..., None]).reshape(rows, block, D)
    mixed_low = mixed.astype(jnp.bfloat16)
    second = inputs + jnp.dot(mixed_low, w_proj, preferred_element_type=jnp.float32) + vec[4]
    second_norm, norm_two_back = jax.vjp(layer_norm, second, vec[5], vec[6])
    a_two = second_norm.astype(jnp.bfloat16)
    hidden = jnp.dot(a_two, w_up, preferred_element_type=jnp.float32) + bias_up
    act_value, gelu_back = jax.vjp(gelu_exact, hidden)
    act = act_value.astype(jnp.bfloat16)
    result = second + jnp.dot(act, w_down, preferred_element_type=jnp.float32) + vec[7]
    output = result.astype(jnp.bfloat16)
    out_grad = cotangent.astype(jnp.float32)
    grad_down = contract_tokens(act, cotangent)
    bias_down_grad = jnp.sum(out_grad, axis=(0, 1))
    act_grad = times_transpose(cotangent, w_down)
    hidden_grad = gelu_back(act_grad)[0].astype(jnp.bfloat16)
    bias_up_grad = jnp.sum(hidden_grad.astype(jnp.float32), axis=(0, 1))
    grad_up = contract_tokens(a_two, hidden_grad)
    a_two_grad = times_transpose(hidden_grad, w_up)
    second_part, gain_two_grad, shift_two_grad = norm_two_back(a_two_grad)
    second_grad = out_grad + second_part
    attn_grad = second_grad.astype(jnp.bfloat16)
    bias_proj_grad = jnp.sum(attn_grad.astype(jnp.float32), axis=(0, 1))
    grad_proj = contract_tokens(mixed_low, attn_grad)
    mixed_grad = (
        times_transpose(attn_grad, w_proj)
        .astype(jnp.bfloat16)
        .reshape(rows, block, HEADS, HEAD_DIM)
    )
    kv_again = lax.all_gather(key_value, "blk", axis=1, tiled=True)
    query_grad, kv_terms = attend_back(query, kv_again, mixed_grad, seg_query, segments, group)
    kv_grad = lax.psum_scatter(
        kv_terms.astype(jnp.bfloat16), "blk", scatter_dimension=1, tiled=True
    ).astype(jnp.float32)
    qkv_grad_low = jnp.concatenate([query_grad, kv_grad], axis=-1).astype(jnp.bfloat16)
    qkv_sums = jnp.sum(qkv_grad_low.astype(jnp.float32), axis=(0, 1))
    grad_query = contract_tokens(a_one, qkv_grad_low)
    a_one_grad = times_transpose(qkv_grad_low, w_query)
    norm_one_back = jax.vjp(layer_norm, inputs, vec[0], vec[1])[1]
    first_part, gain_one_grad, shift_one_grad = norm_one_back(a_one_grad)
    tokens_grad = (second_grad + first_part).astype(jnp.bfloat16)
    vec_local = jnp.concatenate(
        [
            jnp.stack(
                [
                    gain_one_grad,
                    shift_one_grad,
                    qkv_sums[:D],
                    qkv_sums[2 * D :],
                    bias_proj_grad,
                    gain_two_grad,
                    shift_two_grad,
                    bias_down_grad,
                ]
            ),
            bias_up_grad.reshape(4, D),
        ],
        axis=0,
    )
    query_share, proj_share, up_share, down_share, vec_share = (
        lax.psum_scatter(grad_query, ("dp", "blk"), scatter_dimension=0, tiled=True),
        lax.psum_scatter(grad_proj, ("dp", "blk"), scatter_dimension=0, tiled=True),
        lax.psum_scatter(grad_up, ("dp", "blk"), scatter_dimension=0, tiled=True),
        lax.psum_scatter(grad_down, ("dp", "blk"), scatter_dimension=0, tiled=True),
        lax.psum_scatter(vec_local, ("dp", "blk"), scatter_dimension=1, tiled=True),
    )
    qkv_new = update(qkv_weight, query_share, qkv_velocity, qkv_average, rate)
    proj_new = update(proj_weight, proj_share, proj_velocity, proj_average, rate)
    up_new = update(up_weight, up_share, up_velocity, up_average, rate)
    down_new = update(down_weight, down_share, down_velocity, down_average, rate)
    vec_new = update(vec_params, vec_share, vec_velocity, vec_average, rate)
    return (
        output,
        tokens_grad,
        query_share,
        proj_share,
        up_share,
        down_share,
        vec_share,
        qkv_new[0],
        proj_new[0],
        up_new[0],
        down_new[0],
        vec_new[0],
        qkv_new[1],
        proj_new[1],
        up_new[1],
        down_new[1],
        vec_new[1],
        qkv_new[2],
        proj_new[2],
        up_new[2],
        down_new[2],
        vec_new[2],
        qkv_new[0].astype(jnp.bfloat16),
        proj_new[0].astype(jnp.bfloat16),
        up_new[0].astype(jnp.bfloat16),
        down_new[0].astype(jnp.bfloat16),
        vec_new[0].astype(jnp.bfloat16),
    )


PIECE = (48, 384)
NP = 12
Z, Y, X, C = 4, 2, 2, 2
AHEAD = 2
TILE = 128
IMG_MAX = 198
REACH = (IMG_MAX - 1 + 15) // 16 * 16
SPAN = TILE + 2 * REACH
GATHER_SPLIT = ((0, NP, 2),)
PAIRS = HEADS // 2
MESH = pl.DeviceIdType.MESH
F32, BF16 = jnp.float32, jnp.bfloat16
NT = (((1,), (1,)), ((), ()))
TN = (((0,), (0,)), ((), ()))


def place():
    d, x = lax.axis_index("dp"), lax.axis_index("blk")
    return d // (2 * Y), (d // 2) % Y, d % 2, x


def ident(z, y, c, x):
    return ((z * Y + y) * 2 + c, x)


def greet(z, y, c, x):
    barrier = pltpu.get_barrier_semaphore()
    peers = [ident((z + k) % Z, y, c, x) for k in range(1, Z)]
    peers += [ident(z, 1 - y, c, x), ident(z, y, c, 1 - x), ident(z, y, 1 - c, x)]
    for peer in peers:
        pl.semaphore_signal(barrier, inc=1, device_id=peer, device_id_type=MESH)
    return lambda: pl.semaphore_wait(barrier, len(peers))


def remote(src, dst, send, recv, peer):
    return pltpu.make_async_remote_copy(
        src_ref=src, dst_ref=dst, send_sem=send, recv_sem=recv, device_id=peer, device_id_type=MESH
    )


def begin(copies):
    for copy in copies:
        copy.start()


def arrive(copies):
    for copy in copies:
        copy.wait_recv()


def within(index, low, high, run):
    if isinstance(index, int):
        if low <= index < high:
            run()
    else:
        pl.when(jnp.logical_and(index >= low, index < high))(run)


def loop(count, body):
    def step(i, carry):
        body(i)
        return carry

    lax.fori_loop(0, count, step, 0)


def cols(j, width):
    return pl.ds(pl.multiple_of(j * width, width), width)


def dot(a, b, dims=None):
    dims = (((1,), (0,)), ((), ())) if dims is None else dims
    return lax.dot_general(a, b, dims, preferred_element_type=F32)


class Vec:
    def __init__(self, at, now, got, send, recv):
        self.at, self.now, self.got, self.send, self.recv = at, now, got, send, recv

    def copies(self, step):
        z, y, c, x = self.at
        peers = [
            [ident(z, y, 1 - c, x)],
            [ident(z, y, c, 1 - x)],
            [ident(z, 1 - y, c, x)],
            [ident((z + k) % Z, y, c, x) for k in range(1, Z)],
        ][step]
        return [
            remote(self.now.at[step], self.got.at[step + k], self.send.at[step + k], self.recv.at[step + k], peer)
            for k, peer in enumerate(peers)
        ]

    def begin(self, step):
        begin(self.copies(step))

    def total(self, step):
        copies = self.copies(step)
        arrive(copies)
        total = self.now[step]
        for k in range(len(copies)):
            total = total + self.got[step + k]
        return total

    def sent(self):
        for step in range(4):
            for copy in self.copies(step):
                copy.wait_send()


def normal(value):
    mean = jnp.mean(value, axis=-1, keepdims=True)
    cent = value - mean
    var = jnp.mean(cent * cent, axis=-1, keepdims=True)
    scale = lax.rsqrt(var + 1e-06)
    return cent * scale, scale


def window_start(i, x, tiles):
    near = tiles * TILE + REACH
    first = max(i * TILE - REACH, 0)
    count = min((i + 1) * TILE + REACH, near) - first
    start = jnp.where(x == 0, first, near - first - count)
    return jnp.where(x == 0, i, tiles - 1 - i), start, count


def window(i, x, tiles):
    tile, start, count = window_start(i, x, tiles)
    return tile, pl.ds(pl.multiple_of(start, 16), count), count


def mask_fill(seg, seg_col, bias, x, tiles):
    length = seg.shape[1]
    for k in range(length // TILE):
        row = seg[0:1, k * TILE : k * TILE + TILE].astype(F32)
        seg_col[k * TILE : k * TILE + TILE, :] = jnp.transpose(jnp.broadcast_to(row, (TILE, TILE)))
    for i in range(tiles):
        tile, start, count = window_start(i, x, tiles)
        start = start + x * (length - tiles * TILE - REACH)
        row = seg[0:1, pl.ds(pl.multiple_of((x * tiles + tile) * TILE, TILE), TILE)].astype(F32)
        column = seg_col[pl.ds(pl.multiple_of(start, 16), count), :]
        bias[i, 0:count] = jnp.where(column == row, 0.0, -1e30).astype(F32)


def split_heads(pair_block):
    lane = lax.broadcasted_iota(jnp.int32, pair_block.shape, 1)
    zero = jnp.zeros_like(pair_block)
    return jnp.concatenate(
        [jnp.where(lane < HEAD_DIM, pair_block, zero), jnp.where(lane < HEAD_DIM, zero, pair_block)], axis=0
    )


def join_heads(both):
    own = jnp.concatenate([both[:HEAD_DIM, :TILE], both[HEAD_DIM:, TILE:]], axis=0)
    return jnp.transpose(own)


def rows_from_stage(stage, target, t):
    left, right = cols(2 * t, 384), cols(2 * t + 1, 384)

    def group(g):
        parts = [stage[c, g % Y, x, g // Y].astype(F32) for c in range(C) for x in range(X)]
        rows = pl.ds(pl.multiple_of(g * 96, 96), 96)
        target[rows, left] = jnp.concatenate([p[:24] for p in parts], axis=0).astype(BF16)
        target[rows, right] = jnp.concatenate([p[24:] for p in parts], axis=0).astype(BF16)

    loop(Z * Y, group)


def down_copies(full, target, t, sem):
    half, col = (t - 8) % 2 * 48, (t - 8) // 2 * 384

    def group(g):
        for c in range(C):
            for x in range(X):
                row = pl.multiple_of(g * 384 + (c * X + x) * 96 + half, 16)
                pltpu.make_async_copy(
                    full.at[c, g % Y, x, g // Y, t], target.at[pl.ds(row, 48), col : col + 384], sem
                ).start()

    loop(Z * Y, group)


def qkv_columns(j, half):
    if half == 0:
        return (256 * j, 256), (D + 256 * j, 128)
    return (D + 256 * j + 128, 128), (2 * D + 256 * j, 256)


class Gather:
    def __init__(self, at, unit, full, own, send, recv):
        self.at, self.unit, self.full, self.own, self.send, self.recv = at, unit, full, own, send, recv

    def mine(self, t):
        z, y, c, x = self.at
        return pltpu.make_async_copy(self.unit.at[t], self.full.at[c, y, x, z, t], self.own.at[t])

    def first(self, t):
        z, y, c, x = self.at
        return [
            remote(
                self.unit.at[t], self.full.at[c, y, x, z, t], self.send.at[t, k - 1], self.recv.at[t, k - 1],
                ident((z + k) % Z, y, c, x),
            )
            for k in range(1, Z)
        ]

    def second(self, t, low):
        z, y, c, x = self.at
        one, two = self.full.at[c, y, x, 0:low, t], self.full.at[c, y, x, low:Z, t]
        return [
            remote(one, one, self.send.at[t, 3], self.recv.at[t, 3], ident(z, y, c, 1 - x)),
            remote(two, two, self.send.at[t, 4], self.recv.at[t, 4], ident(z, 1 - y, c, x)),
        ]

    def third(self, t, low):
        z, y, c, x = self.at
        one, two = self.full.at[c, y, :, 0:low, t], self.full.at[c, :, x, low:Z, t]
        return [
            remote(one, one, self.send.at[t, 5], self.recv.at[t, 5], ident(z, 1 - y, c, x)),
            remote(two, two, self.send.at[t, 6], self.recv.at[t, 6], ident(z, y, c, 1 - x)),
        ]

    def last(self, t):
        z, y, c, x = self.at
        block = self.full.at[c, :, :, :, t]
        return [remote(block, block, self.send.at[t, 7], self.recv.at[t, 7], ident(z, y, 1 - c, x))]

    def start(self):
        loop(NP, lambda t: self.mine(t).start())
        loop(AHEAD, lambda t: begin(self.first(t)))

    def progress(self, i):
        def to_second(t, low):
            self.mine(t).wait()
            arrive(self.first(t))
            begin(self.second(t, low))

        def to_third(t, low):
            arrive(self.second(t, low))
            begin(self.third(t, low))

        def to_last(t, low):
            arrive(self.third(t, low))
            begin(self.last(t))

        for first, end, low in GATHER_SPLIT:
            within(i, first, end, lambda: to_second(i, low))
        for first, end, low in GATHER_SPLIT:
            within(i - 1, first, end, lambda: to_third(i - 1, low))
        for first, end, low in GATHER_SPLIT:
            within(i - 2, first, end, lambda: to_last(i - 2, low))
        within(i + AHEAD, AHEAD, NP, lambda: begin(self.first(i + AHEAD)))

    def sent(self):
        for first, end, low in GATHER_SPLIT:
            def one(t):
                for copy in self.first(t) + self.second(t, low) + self.third(t, low) + self.last(t):
                    copy.wait_send()

            lax.fori_loop(first, end, lambda t, carry: (one(t), carry)[1], 0)


def forward_kernel(
    w_qkv, w_proj, w_up, w_down, vec_in, tok, dy, seg,
    full, vec_out, out_o, q_o, k_o, v_o, o_o, stat_o, x2_o, a2_o, z_o, slope_o, grad_o, bias_o,
    unit, seg_col, near, a1, wbig, wdown, stage, vecf, bias, out_s, q_s, k_s, v_s, o_s, stat_s, x2_s, a2_s, z_s, slope_s, got,
    local, two, vec_now, vec_got, own, send, recv, vsend, vrecv, hsem, ssem, dsem, osem, gsend, grecv, tsend, trecv,
):
    z, y, c, x = at = place()
    block = tok.shape[0]
    tiles = block // TILE
    offset = pl.multiple_of(x * REACH, 16)
    greeted = greet(*at)
    vec_now[0] = vec_in[...]

    def pack(t, weight, j):
        left, right = weight[:, j * 768 : j * 768 + 384], weight[:, j * 768 + 384 : j * 768 + 768]
        unit[t] = jnp.concatenate([left, right], axis=0).astype(BF16)

    for j in range(3):
        sides = []
        for half in range(2):
            parts = [w_qkv[:, start : start + width] for start, width in qkv_columns(j, half)]
            sides.append(jnp.concatenate(parts, axis=1))
        unit[j] = jnp.concatenate(sides, axis=0).astype(BF16)
    pack(3, w_proj, 0)
    for j in range(4):
        pack(4 + j, w_up, j)
        unit[8 + j] = w_down[j % 2 * 48 : j % 2 * 48 + 48, j // 2 * 384 : j // 2 * 384 + 384].astype(BF16)
    greeted()
    gather = Gather(at, unit, full, own, send, recv)
    gather.start()
    vec = Vec(at, vec_now, vec_got, vsend, vrecv)
    vec.begin(0)
    away = pl.multiple_of((1 - x) * (block - REACH), 16)
    land = pl.multiple_of(x * block, 16)
    halo = remote(
        tok.at[pl.ds(away, REACH)], near.at[pl.ds(land, REACH)], hsem.at[0], hsem.at[1], ident(z, y, c, 1 - x)
    )
    halo.start()
    near[pl.ds(offset, block), :] = tok[...]

    def put(k, src, dst):
        return pltpu.make_async_copy(src, dst, osem.at[k])

    def vec_step(step):
        total = vec.total(step)
        if step < 3:
            vec_now[step + 1] = total
            vec.begin(step + 1)
        else:
            vec_out[...] = total
            vecf[...] = total.astype(F32)

    def staged(t):
        return pltpu.make_async_copy(full.at[:, :, :, :, t], stage.at[t % 4], ssem.at[t % 4])

    def fetch(t):
        arrive(gather.last(t))
        staged(t).start()

    def take(t):
        staged(t).wait()
        rows_from_stage(stage.at[t % 4], wbig, t)

    def down_start(t):
        arrive(gather.last(t))
        down_copies(full, wdown, t, dsem.at[t - 8])

    def down_wait(t):
        pltpu.make_async_copy(full.at[:, :, :, :, t], stage.at[0], dsem.at[t - 8]).wait()

    gather.progress(0)
    vec_step(0)
    gather.progress(1)
    vec_step(1)
    gather.progress(2)
    vec_step(2)
    vec_step(3)
    halo.wait_recv()

    def norm_one(i):
        rows = cols(i, 240)
        value = normal(near[rows, :].astype(F32))[0]
        a1[rows, :] = (value * (1.0 + vecf[0:1, :]) + vecf[1:2, :]).astype(BF16)

    loop(near.shape[0] // 240, norm_one)
    mask_fill(seg, seg_col, bias, x, tiles)
    put(11, bias, bias_o).start()
    def attend(pair):
        lanes = cols(pair, 128)

        for i in range(tiles):
            tile, span, count = window(i, x, tiles)
            rows = cols(tile, TILE)
            both = split_heads(q_s[rows, lanes])
            fill = bias[i, 0:count]
            scores = dot(k_s[span, lanes], both, NT) + jnp.concatenate([fill, fill], axis=1)
            top = jnp.max(scores, axis=0, keepdims=True)
            weights = jnp.exp(scores - top)
            total = jnp.sum(weights, axis=0, keepdims=True)
            mixed = dot(v_s[span, lanes], weights.astype(BF16), TN) / total
            o_s[rows, lanes] = join_heads(mixed).astype(BF16)
            stat_s[pair * tiles + i] = jnp.broadcast_to(top + jnp.log(total), (8, 2 * TILE))

    def third(j):
        fetch(j)
        gather.progress(3 + 2 * j)
        take(j)
        where = cols(j, 256)
        value = dot(a1[pl.ds(offset, block), :], wbig[:, cols(3 * j, 256)]) + vecf[2:3, where]
        q_s[:, where] = value.astype(BF16) * HEAD_DIM ** (-0.5)
        k_s[:, where] = dot(a1[...], wbig[:, cols(3 * j + 1, 256)]).astype(BF16)
        v_s[:, where] = (dot(a1[...], wbig[:, cols(3 * j + 2, 256)]) + vecf[3:4, where]).astype(BF16)
        attend(2 * j)
        gather.progress(4 + 2 * j)
        attend(2 * j + 1)

    loop(3, third)
    put(0, k_s, k_o).start()
    put(1, v_s, v_o).start()
    put(2, q_s, q_o).start()
    put(3, o_s, o_o).start()
    put(4, stat_s, stat_o).start()
    fetch(3)
    take(3)
    fetch(4)
    fetch(5)
    gather.progress(9)

    def project(j):
        value = dot(o_s[...], wbig[:, cols(j + 9, 256)])
        x2_s[:, cols(j, 256)] = tok[:, cols(j, 256)].astype(F32) + value + vecf[4:5, cols(j, 256)]

    loop(3, project)

    def norm_two(i):
        rows = pl.ds(pl.multiple_of(i * 256, 256), 256)
        value = normal(x2_s[rows, :])[0]
        a2_s[rows, :] = (value * (1.0 + vecf[5:6, :]) + vecf[6:7, :]).astype(BF16)

    loop(block // 256, norm_two)
    put(5, x2_s, x2_o).start()
    put(6, a2_s, a2_o).start()
    gather.progress(10)
    take(4)
    take(5)
    fetch(6)
    fetch(7)

    def expand(j):
        u = dot(a2_s[...], wbig[:, cols(j + 12, 256)])
        u = u + vecf[pl.ds(8 + j // 3, 1), pl.ds(pl.multiple_of((j % 3) * 256, 256), 256)]
        half = 0.5 + 0.5 * lax.erf(u * math.sqrt(0.5))
        z_s[:, cols(j, 256)] = (u * half).astype(BF16)
        slope = half + u * (jnp.exp(-0.5 * u * u) * (1.0 / math.sqrt(2.0 * math.pi)))
        slope_s[:, cols(j, 256)] = slope.astype(BF16)

    loop(5, expand)
    gather.progress(11)
    take(6)
    take(7)
    loop(5, lambda j: expand(j + 5))
    gather.progress(12)
    down_start(8)
    loop(2, lambda j: expand(j + 10))
    put(7, z_s, z_o).start()
    put(8, slope_s, slope_o).start()

    def core(t):
        peer = ident(z, y, 1 - c, x)
        return remote(local.at[1 - c, :, :, :, t], got.at[t], gsend.at[t], grecv.at[t], peer)

    for half in range(2):
        def down_grad(g):
            value = dot(z_s[:, cols(g, 384)], dy[:, half * 384 : half * 384 + 384], TN).astype(BF16)
            for k in range(4):
                for row in range(2):
                    part = value[k * 96 + row * 48 : k * 96 + row * 48 + 48]
                    local[k // 2, g % Y, k % 2, g // Y, 2 * half + row] = part

        loop(Z * Y, down_grad)
        core(2 * half).start()
        core(2 * half + 1).start()
        if half == 0:
            gather.progress(13)
            down_start(9)
    down_start(10)

    def contract(half):
        col = slice(half * 384, half * 384 + 384)
        value = dot(z_s[...], wdown[:, col])
        out_s[:, col] = (x2_s[:, col] + value + vecf[7:8, col]).astype(BF16)

    def gain(t):
        core(t).wait_recv()
        for a in range(Y):
            for b in range(X):
                own_part = local[c, a, b, :, t].astype(F32)
                got[t, a, b] = (own_part + got[t, a, b].astype(F32)).astype(BF16)

    def ahead(t):
        along_y, along_x = ident(z, 1 - y, c, x), ident(z, y, c, 1 - x)
        return [
            remote(got.at[t, 1 - y, :, 0:2], two.at[t, :, 0:2], tsend.at[t, 0], trecv.at[t, 0], along_y),
            remote(got.at[t, :, 1 - x, 2:Z], two.at[t, :, 2:Z], tsend.at[t, 1], trecv.at[t, 1], along_x),
        ]

    down_wait(8)
    down_wait(9)
    contract(0)
    for t in range(4):
        gain(t)
        if t < 2:
            begin(ahead(t))
    late = pltpu.make_async_copy(got.at[2:4], grad_o.at[2:4], osem.at[10])
    late.start()
    down_start(11)
    down_wait(10)
    down_wait(11)
    contract(1)
    put(9, out_s, out_o).start()
    pairs = [(k_s, k_o), (v_s, v_o), (q_s, q_o), (o_s, o_o), (stat_s, stat_o), (x2_s, x2_o), (a2_s, a2_o)]
    for k, (src, dst) in enumerate(pairs + [(z_s, z_o), (slope_s, slope_o), (out_s, out_o)]):
        put(k, src, dst).wait()
    for t in range(2):
        arrive(ahead(t))
        for b in range(2):
            low, high = got[t, y, b, 0:2].astype(F32), got[t, b, x, 2:Z].astype(F32)
            got[t, y, b, 0:2] = (low + two[t, b, 0:2].astype(F32)).astype(BF16)
            got[t, b, x, 2:Z] = (high + two[t, b, 2:Z].astype(F32)).astype(BF16)
        for copy in ahead(t):
            copy.wait_send()
    soon = pltpu.make_async_copy(got.at[0:2], grad_o.at[0:2], osem.at[12])
    soon.start()
    late.wait()
    soon.wait()
    put(11, bias, bias_o).wait()
    gather.sent()
    vec.sent()
    halo.wait_send()
    loop(4, lambda t: core(t).wait_send())


def forward_all(weights, vec_placed, tok, dy, seg):
    block = tok.shape[0]
    near = block + REACH
    ff = 4 * D
    tiles = block // TILE
    shapes = [
        ((block, D), BF16),
        ((block, D), BF16),
        ((near, D), BF16),
        ((near, D), BF16),
        ((block, D), BF16),
        ((PAIRS * tiles, 8, 2 * TILE), F32),
        ((block, D), F32),
        ((block, D), BF16),
        ((block, ff), BF16),
        ((block, ff), BF16),
        ((4, Y, X, Z) + PIECE, BF16),
        ((tiles, SPAN, TILE), F32),
    ]
    hbm, vmem = pl.BlockSpec(memory_space=pl.ANY), pl.BlockSpec(memory_space=pltpu.VMEM)
    outs = [((C, Y, X, Z, NP) + PIECE, BF16), (vec_placed.shape, BF16)] + shapes
    return pl.pallas_call(
        forward_kernel,
        out_shape=tuple(jax.ShapeDtypeStruct(*one) for one in outs),
        in_specs=[vmem] * 8,
        out_specs=tuple([hbm, vmem] + [hbm] * len(shapes)),
        scratch_shapes=[
            pltpu.VMEM((NP,) + PIECE, BF16),
            pltpu.VMEM((seg.shape[1], TILE), F32),
            pltpu.VMEM((near, D), BF16),
            pltpu.VMEM((near, D), BF16),
            pltpu.VMEM((D, 8 * D), BF16),
            pltpu.VMEM((ff, D), BF16),
            pltpu.VMEM((4, C, Y, X, Z) + PIECE, BF16),
            pltpu.VMEM(vec_placed.shape, F32),
            *[pltpu.VMEM(*one) for one in shapes[-1:] + shapes[:-1]],
            pltpu.VMEM((C, Y, X, Z, 4) + PIECE, BF16),
            pltpu.VMEM((2, 2, Z) + PIECE, BF16),
            pltpu.VMEM((4,) + vec_placed.shape, BF16),
            pltpu.VMEM((6,) + vec_placed.shape, BF16),
            pltpu.SemaphoreType.DMA((NP,)),
            pltpu.SemaphoreType.DMA((NP, 8)),
            pltpu.SemaphoreType.DMA((NP, 8)),
            pltpu.SemaphoreType.DMA((6,)),
            pltpu.SemaphoreType.DMA((6,)),
            pltpu.SemaphoreType.DMA((2,)),
            pltpu.SemaphoreType.DMA((4,)),
            pltpu.SemaphoreType.DMA((4,)),
            pltpu.SemaphoreType.DMA((13,)),
            pltpu.SemaphoreType.DMA((4,)),
            pltpu.SemaphoreType.DMA((4,)),
            pltpu.SemaphoreType.DMA((2, 2)),
            pltpu.SemaphoreType.DMA((2, 2)),
        ],
        compiler_params=pltpu.CompilerParams(
            collective_id=0, has_side_effects=True, vmem_limit_bytes=60 << 20
        ),
        name="forward_all",
    )(*weights, vec_placed, tok, dy, seg)


SCATTER_SPLIT = ((0, NP, 2),)


class Scatter:
    def __init__(self, at, local, got_core, got_two, got_one, got_z, out, send, recv):
        self.at, self.local, self.out, self.send, self.recv = at, local, out, send, recv
        self.got = got_core, got_two, got_one, got_z

    def core(self, t):
        z, y, c, x = self.at
        peer = ident(z, y, 1 - c, x)
        return [remote(self.local.at[1 - c, :, :, :, t], self.got[0].at[t - 4], self.send.at[t, 0], self.recv.at[t, 0], peer)]

    def two(self, t, low):
        z, y, c, x = self.at
        one, other = self.local.at[c, 1 - y, :, 0:low, t], self.local.at[c, :, 1 - x, low:Z, t]
        got = self.got[1].at[t]
        return [
            remote(one, got.at[:, 0:low], self.send.at[t, 1], self.recv.at[t, 1], ident(z, 1 - y, c, x)),
            remote(other, got.at[:, low:Z], self.send.at[t, 2], self.recv.at[t, 2], ident(z, y, c, 1 - x)),
        ]

    def one(self, t, low):
        z, y, c, x = self.at
        one, other = self.local.at[c, y, 1 - x, 0:low, t], self.local.at[c, 1 - y, x, low:Z, t]
        got = self.got[2].at[t]
        return [
            remote(one, got.at[0:low], self.send.at[t, 3], self.recv.at[t, 3], ident(z, y, c, 1 - x)),
            remote(other, got.at[low:Z], self.send.at[t, 4], self.recv.at[t, 4], ident(z, 1 - y, c, x)),
        ]

    def along(self, t):
        z, y, c, x = self.at
        return [
            remote(
                self.local.at[c, y, x, (z + k) % Z, t], self.got[3].at[t, k - 1], self.send.at[t, 4 + k],
                self.recv.at[t, 4 + k], ident((z + k) % Z, y, c, x),
            )
            for k in range(1, Z)
        ]

    def add(self, where, value):
        self.local[where] = (self.local[where].astype(F32) + value.astype(F32)).astype(BF16)

    def take_core(self, t):
        c = self.at[2]
        arrive(self.core(t))
        for a in range(Y):
            for b in range(X):
                self.add((c, a, b, slice(None), t), self.got[0][t - 4, a, b])

    def after_core(self, t):
        self.take_core(t)
        self.go_two(t)

    def after_two(self, t, low):
        z, y, c, x = self.at
        arrive(self.two(t, low))
        for b in range(2):
            self.add((c, y, b, slice(0, low), t), self.got[1][t, b, 0:low])
            self.add((c, b, x, slice(low, Z), t), self.got[1][t, b, low:Z])
        begin(self.one(t, low))

    def after_one(self, t, low):
        z, y, c, x = self.at
        arrive(self.one(t, low))
        self.add((c, y, x, slice(None), t), self.got[2][t])
        begin(self.along(t))

    def after_z(self, t):
        z, y, c, x = self.at
        arrive(self.along(t))
        total = self.local[c, y, x, z, t].astype(F32)
        for k in range(Z - 1):
            total = total + self.got[3][t, k].astype(F32)
        self.out[t] = total

    def go_two(self, t):
        for first, end, low in SCATTER_SPLIT:
            within(t, first, end, lambda: begin(self.two(t, low)))

    def go_one(self, t):
        for first, end, low in SCATTER_SPLIT:
            within(t, first, end, lambda: self.after_two(t, low))

    def go_z(self, t):
        arrive_one = self.after_one
        for first, end, low in SCATTER_SPLIT:
            within(t, first, end, lambda: arrive_one(t, low))

    def sent(self):
        loop(NP - 4, lambda t: self.core(t + 4)[0].wait_send())
        for first, end, low in SCATTER_SPLIT:
            def each(t):
                for copy in self.one(t, low) + self.along(t):
                    copy.wait_send()
                within(t, 2, NP, lambda: [copy.wait_send() for copy in self.two(t, low)] and None)

            lax.fori_loop(first, end, lambda t, carry: (each(t), carry)[1], 0)


def total_rows(value):
    return jnp.sum(value.astype(F32), axis=0, keepdims=True)


def norm_back(value, grad, gain):
    unit_value, scale = normal(value)
    inner = grad * (1.0 + gain)
    mean_one = jnp.mean(inner, axis=-1, keepdims=True)
    mean_two = jnp.mean(inner * unit_value, axis=-1, keepdims=True)
    back = scale * (inner - mean_one - unit_value * mean_two)
    return back, total_rows(grad * unit_value), total_rows(grad)


def backward_kernel(
    full, vec_in, tok_o, dy_o, grad_o, bias_o, q_o, k_o, v_o, o_o, stat_o, x2_o, a2_o, slope_o,
    out, vec_out, tok_grad,
    local, got_core, got_two, got_one, got_z, wbuf, stage, bias, vecf, tok, dy, q_s, k_s, v_s, o_s, stat_s, x2_s, a2_s, z_s,
    slope_s, dx, da, acc_k, acc_v, halo_s, halo_r, vec_now, vec_got, send, recv, vsend, vrecv, hsend, hrecv, isem, ssem, dsem, gsem,
):
    z, y, c, x = at = place()
    greeted = greet(*at)
    block = tok.shape[0]
    tiles = block // TILE
    offset = pl.multiple_of(x * REACH, 16)
    away = pl.multiple_of((1 - x) * (block - REACH), 16)
    outside = pl.multiple_of((1 - x) * block, 16)
    order = [4, 5, 6, 7, 3, 0, 1, 2]

    def fetch(n):
        return pltpu.make_async_copy(full.at[:, :, :, :, order[n]], stage.at[n % 2], ssem.at[n % 2])

    def take(n, use):
        fetch(n).wait()
        use(stage.at[n % 2])
        if n + 2 < len(order):
            fetch(n + 2).start()

    pairs = [
        (dy_o, dy), (slope_o, slope_s), (a2_o, a2_s), (x2_o, x2_s), (o_o, o_s), (k_o, k_s), (v_o, v_s), (q_o, q_s),
        (stat_o, stat_s), (tok_o, tok), (bias_o, bias),
    ]

    def inward(k):
        return pltpu.make_async_copy(pairs[k][0], pairs[k][1], isem.at[k])

    def grads(t):
        return pltpu.make_async_copy(grad_o.at[t], local.at[c, :, :, :, t], gsem.at[t])

    for t in range(4):
        grads(t).start()
    inward(0).start()
    for t in range(8, 12):
        down_copies(full, wbuf, t, dsem.at[t - 8])
    for n in range(2):
        fetch(n).start()
    for k in range(1, 3):
        inward(k).start()
    greeted()
    scatter = Scatter(at, local, got_core, got_two, got_one, got_z, out, send, recv)
    vec = Vec(at, vec_now, vec_got, vsend, vrecv)
    vec_now[0] = jnp.zeros(vec_now.shape[1:], F32)
    vecf[...] = vec_in[...].astype(F32)

    def vec_step(step):
        total = vec.total(step)
        if step < 3:
            vec_now[step + 1] = total
            vec.begin(step + 1)
        else:
            vec_out[...] = total

    def gain_row(row, where, value):
        vec_now[0, row : row + 1, where] = vec_now[0, row : row + 1, where] + value

    def weight_grad(left, right, t):
        def half(h):
            value = dot(left[:, cols(h, 384)], right[...], TN)
            for g in range(4):
                for k in range(4):
                    part = value[g * 96 + k * 24 : g * 96 + k * 24 + 24]
                    part = jnp.concatenate([part[:, :384], part[:, 384:]], axis=0).astype(BF16)
                    local[k // 2, g % 2, k % 2, 2 * h + g // 2, t] = part

        loop(2, half)
        begin(scatter.core(t))

    for t in range(4):
        grads(t).wait()
        if t < 2:
            begin(scatter.one(t, 2))
        else:
            scatter.go_two(t)
    for k in range(3, len(pairs)):
        inward(k).start()
    inward(0).wait()
    gain_row(7, slice(None), total_rows(dy[...]))
    for t in range(8, 12):
        pltpu.make_async_copy(full.at[:, :, :, :, t], stage.at[0], dsem.at[t - 8]).wait()
    inward(1).wait()

    def hidden(n):
        rows = pl.ds(pl.multiple_of(n * 256, 256), 256)
        grad = dot(dy[...], wbuf[rows, :], NT) * slope_s[:, cols(n, 256)].astype(F32)
        low = grad.astype(BF16)
        slope_s[:, cols(n, 256)] = low
        where = pl.ds(pl.multiple_of((n % 3) * 256, 256), 256)
        vec_now[0, pl.ds(8 + n // 3, 1), where] = total_rows(low)

    loop(12, hidden)
    inward(2).wait()
    for t in range(2):
        take(t, lambda part: rows_from_stage(part, wbuf.at[pl.ds(t * D, D)], 0))
    for t in range(4):
        weight_grad(a2_s, slope_s.at[:, t * D : t * D + D], 4 + t)
    scatter.after_core(4)
    scatter.go_one(2)
    scatter.go_z(0)
    for t in range(2, 4):
        take(t, lambda part: rows_from_stage(part, wbuf.at[pl.ds(t * D, D)], 0))

    def inner_grad(n):
        value = None
        for t in range(4):
            rows = pl.ds(pl.multiple_of(t * D + n * 256, 256), 256)
            part = dot(slope_s[:, t * D : t * D + D], wbuf[rows, :], NT)
            value = part if value is None else value + part
        dx[:, cols(n, 256)] = value

    loop(3, inner_grad)
    scatter.after_core(5)
    scatter.go_one(3)
    inward(3).wait()

    def norm_two(i):
        rows = cols(i, 128)
        grad = dx[rows, :]
        back, gain, shift = norm_back(x2_s[rows, :], grad, vecf[5:6, :])
        total = dy[rows, :].astype(F32) + back
        low = total.astype(BF16)
        dx[rows, :] = total
        da[rows, :] = low
        gain_row(5, slice(None), gain)
        gain_row(6, slice(None), shift)
        gain_row(4, slice(None), total_rows(low))

    loop(block // 128, norm_two)
    scatter.after_core(6)
    scatter.after_core(7)
    scatter.go_z(1)
    inward(4).wait()
    weight_grad(o_s, da, 8)
    take(4, lambda part: rows_from_stage(part, wbuf.at[pl.ds(3 * D, D)], 0))

    def mixed_grad(n):
        rows = pl.ds(pl.multiple_of(3 * D + n * 256, 256), 256)
        o_s[:, cols(n, 256)] = dot(da[...], wbuf[rows, :], NT).astype(BF16)

    loop(3, mixed_grad)
    scatter.after_core(8)
    for k in range(5, 11):
        inward(k).wait()

    def halo(pair):
        return remote(halo_s.at[pair], halo_r.at[pair], hsend.at[pair], hrecv.at[pair], ident(z, y, c, 1 - x))

    def spot(pair, kind):
        return pl.ds(pl.multiple_of(pair // 2 * D + kind * 256 + pair % 2 * 128, 128), 128)

    def attend(pair):
        lanes = cols(pair, 128)
        scatter.go_z(2 + pair)
        within(pair, 0, 5, lambda: scatter.go_one(4 + pair))
        scatter.after_z(pair)
        acc_k[...] = jnp.zeros(acc_k.shape, F32)
        acc_v[...] = jnp.zeros(acc_v.shape, F32)

        for i in range(tiles):
            tile, span, count = window(i, x, tiles)
            rows = cols(tile, TILE)
            both, grads = split_heads(q_s[rows, lanes]), split_heads(o_s[rows, lanes])
            fill = bias[i, 0:count]
            scores = dot(k_s[span, lanes], both, NT) + jnp.concatenate([fill, fill], axis=1)
            probs = jnp.exp(scores - stat_s[pair * tiles + i][0:1])
            low = probs.astype(BF16)
            back = dot(v_s[span, lanes], grads, NT)
            mean = jnp.sum(probs * back, axis=0, keepdims=True)
            inner = (probs * (back - mean)).astype(BF16)
            acc_v[span, :] = acc_v[span, :] + dot(low, grads)
            acc_k[span, :] = acc_k[span, :] + dot(inner, both)
            query = join_heads(dot(k_s[span, lanes], inner, TN)) * HEAD_DIM ** (-0.5)
            z_s[rows, spot(pair, 0)] = query.astype(BF16)

        for k, acc in ((0, acc_k), (1, acc_v)):
            z_s[:, spot(pair, k + 1)] = acc[pl.ds(offset, block), :].astype(BF16)
            halo_s[pair, k] = acc[pl.ds(outside, REACH), :].astype(BF16)
        halo(pair).start()

    def add_halo(pair):
        halo(pair).wait_recv()
        for k in range(2):
            where = spot(pair, k + 1)
            rows = pl.ds(away, REACH)
            z_s[rows, where] = (z_s[rows, where].astype(F32) + halo_r[pair, k].astype(F32)).astype(BF16)

    def finish(j):
        add_halo(2 * j)
        add_halo(2 * j + 1)
        weight_grad(a2_s, z_s.at[:, pl.ds(pl.multiple_of(j * D, D), D)], 9 + j)

    def norm_one(i):
        rows = cols(i, 128)
        value = normal(tok[rows, :].astype(F32))[0]
        a2_s[rows, :] = (value * (1.0 + vecf[0:1, :]) + vecf[1:2, :]).astype(BF16)

    loop(block // 128, norm_one)

    def third(j):
        loop(2, lambda i: attend(2 * j + i))
        within(j, 2, 3, lambda: scatter.after_core(9))
        within(j, 1, 3, lambda: finish(j - 1))

    loop(3, third)
    finish(2)
    scatter.after_core(10)
    scatter.after_core(11)
    scatter.go_z(8)
    for n in range(5, 8):
        take(n, lambda part: rows_from_stage(part, wbuf.at[pl.ds((n - 5) * D, D)], 0))

    def first_grad(n):
        value = None
        for t in range(3):
            rows = pl.ds(pl.multiple_of(t * D + n * 256, 256), 256)
            part = dot(z_s[:, t * D : t * D + D], wbuf[rows, :], NT)
            value = part if value is None else value + part
        x2_s[:, cols(n, 256)] = value

    loop(3, first_grad)
    scatter.go_one(9)
    for j in range(3):
        where = slice(j * 256, j * 256 + 256)
        gain_row(2, where, total_rows(z_s[:, j * D : j * D + 256]))
        gain_row(3, where, total_rows(z_s[:, j * D + 512 : j * D + 768]))

    def norm_first(i):
        rows = cols(i, 128)
        back, gain, shift = norm_back(tok[rows, :].astype(F32), x2_s[rows, :], vecf[0:1, :])
        tok_grad[rows, :] = (dx[rows, :] + back).astype(BF16)
        gain_row(0, slice(None), gain)
        gain_row(1, slice(None), shift)

    loop(block // 128, norm_first)
    vec.begin(0)
    scatter.go_one(10)
    scatter.go_z(9)
    scatter.after_z(6)
    vec_step(0)
    scatter.go_one(11)
    scatter.go_z(10)
    scatter.after_z(7)
    vec_step(1)
    scatter.go_z(11)
    scatter.after_z(8)
    vec_step(2)
    scatter.after_z(9)
    vec_step(3)
    scatter.after_z(10)
    scatter.after_z(11)
    scatter.sent()
    vec.sent()
    loop(PAIRS, lambda pair: halo(pair).wait_send())


def backward_all(full, vec_low, tok, dy, grad, fill, *saved):
    block = tok.shape[0]
    near = block + REACH
    tiles = block // TILE
    hbm, vmem = pl.BlockSpec(memory_space=pl.ANY), pl.BlockSpec(memory_space=pltpu.VMEM)
    vec_shape = vec_low.shape
    rows = (block, D)
    buffers = [
        ((C, Y, X, Z, NP) + PIECE, BF16),
        ((NP - 4, Y, X, Z) + PIECE, BF16),
        ((NP, 2, Z) + PIECE, BF16),
        ((NP, Z) + PIECE, BF16),
        ((NP, Z - 1) + PIECE, BF16),
        ((4 * D, D), BF16),
        ((2, C, Y, X, Z) + PIECE, BF16),
        ((tiles, SPAN, TILE), F32),
        (vec_shape, F32),
        (rows, BF16),
        (rows, BF16),
        *[(array.shape, array.dtype) for array in saved[:-1]],
        ((block, 3 * D), BF16),
        ((block, 4 * D), BF16),
        (rows, F32),
        (rows, BF16),
        ((near, 128), F32),
        ((near, 128), F32),
        ((PAIRS, 2, REACH, 128), BF16),
        ((PAIRS, 2, REACH, 128), BF16),
        ((4,) + vec_shape, F32),
        ((6,) + vec_shape, F32),
    ]
    semaphores = [(NP, 8), (NP, 8), (6,), (6,), (PAIRS,), (PAIRS,), (11,), (2,), (4,), (4,)]
    return pl.pallas_call(
        backward_kernel,
        out_shape=(
            jax.ShapeDtypeStruct((NP,) + PIECE, F32),
            jax.ShapeDtypeStruct(vec_shape, F32),
            jax.ShapeDtypeStruct(rows, BF16),
        ),
        in_specs=[hbm, vmem, hbm, hbm, hbm, hbm] + [hbm] * len(saved),
        out_specs=(vmem, vmem, vmem),
        scratch_shapes=[pltpu.VMEM(*one) for one in buffers] + [pltpu.SemaphoreType.DMA(one) for one in semaphores],
        compiler_params=pltpu.CompilerParams(
            collective_id=1, has_side_effects=True, vmem_limit_bytes=60 << 20
        ),
        name="backward_all",
    )(full, vec_low, tok, dy, grad, fill, *saved)


def update_kernel(rate, pieces, result, back, *refs):
    masters, velocities, averages, grads, news, moving, means, copies = [refs[k : k + 4] for k in range(0, 32, 4)]
    refs[32][...] = result[...]
    refs[33][...] = back[...]

    def one(k, rows, where, grad):
        new, velocity, average = update(
            masters[k][rows, where], grad, velocities[k][rows, where], averages[k][rows, where], rate
        )
        grads[k][rows, where] = grad
        news[k][rows, where] = new
        moving[k][rows, where] = velocity
        means[k][rows, where] = average

    for t in range(NP):
        piece = pieces[t]
        if t < 4:
            one(3, slice(t % 2 * 48, t % 2 * 48 + 48), slice(t // 2 * 384, t // 2 * 384 + 384), piece)
            continue
        k, j = (2, t - 4) if t < 8 else (1, 0)
        for half in range(2):
            if t > 8:
                part, col = piece[half * 24 : half * 24 + 24], 0
                for start, width in qkv_columns(t - 9, half):
                    one(0, slice(0, 24), slice(start, start + width), part[:, col : col + width])
                    col += width
                continue
            col = (2 * j + half) * 384
            one(k, slice(0, 24), slice(col, col + 384), piece[half * 24 : half * 24 + 24])
    for k in range(4):
        copies[k][...] = news[k][...].astype(BF16)


def update_all(rate, pieces, result, back, masters, velocities, averages):
    shapes = [jax.ShapeDtypeStruct(w.shape, F32) for w in masters] * 4
    shapes += [jax.ShapeDtypeStruct(w.shape, BF16) for w in masters]
    shapes += [jax.ShapeDtypeStruct(result.shape, BF16), jax.ShapeDtypeStruct(back.shape, BF16)]
    vmem = pl.BlockSpec(memory_space=pltpu.VMEM)
    return pl.pallas_call(
        functools.partial(update_kernel, rate),
        out_shape=tuple(shapes),
        in_specs=[vmem] * 15,
        out_specs=tuple([vmem] * 22),
        name="update_all",
    )(pieces, result, back, *masters, *velocities, *averages)


def on_device_fast(
    tokens,
    segments,
    cotangent,
    qkv_weight,
    proj_weight,
    up_weight,
    down_weight,
    vec_params,
    qkv_velocity,
    proj_velocity,
    up_velocity,
    down_velocity,
    vec_velocity,
    qkv_average,
    proj_average,
    up_average,
    down_average,
    vec_average,
):
    block = tokens.shape[1]
    total_tokens = lax.axis_size("dp") * segments.shape[1]
    rate = 0.05 / math.sqrt(total_tokens)
    position = lax.axis_index("blk")
    shard = lax.axis_index("dp") * lax.axis_size("blk") + position
    masters = (qkv_weight, proj_weight, up_weight, down_weight)
    vec_placed = lax.dynamic_update_slice(
        jnp.zeros((16, D), jnp.bfloat16), vec_params.astype(jnp.bfloat16), (0, shard * vec_params.shape[1])
    )
    full, vec_low, result, *saved, act, slope, down, fill = forward_all(
        masters, vec_placed, tokens[0], cotangent[0], segments
    )
    pieces, vec_sum, back = backward_all(full, vec_low, tokens[0], cotangent[0], down, fill, *saved, slope)
    velocities = (qkv_velocity, proj_velocity, up_velocity, down_velocity)
    averages = (qkv_average, proj_average, up_average, down_average)
    done = update_all(rate, pieces, result, back, masters, velocities, averages)
    vec_share = lax.dynamic_slice(vec_sum, (0, shard * vec_params.shape[1]), vec_params.shape)
    vec_new = update(vec_params, vec_share, vec_velocity, vec_average, rate)
    return (
        done[20][None],
        done[21][None],
        *done[0:4],
        vec_share,
        *done[4:8],
        vec_new[0],
        *done[8:12],
        vec_new[1],
        *done[12:16],
        vec_new[2],
        *done[16:20],
        vec_new[0].astype(jnp.bfloat16),
    )


def solution(mesh):
    fits = mesh.shape["dp"] == Z * Y * C and mesh.shape["blk"] == X
    return jax.shard_map(
        on_device_fast if fits else on_device,
        mesh=mesh,
        in_specs=(
            P("dp", "blk", None),
            P("dp", None),
            P("dp", "blk", None),
            P(("dp", "blk"), None),
            P(("dp", "blk"), None),
            P(("dp", "blk"), None),
            P(("dp", "blk"), None),
            P(None, ("dp", "blk")),
            P(("dp", "blk"), None),
            P(("dp", "blk"), None),
            P(("dp", "blk"), None),
            P(("dp", "blk"), None),
            P(None, ("dp", "blk")),
            P(("dp", "blk"), None),
            P(("dp", "blk"), None),
            P(("dp", "blk"), None),
            P(("dp", "blk"), None),
            P(None, ("dp", "blk")),
        ),
        out_specs=(
            P("dp", "blk", None),
            P("dp", "blk", None),
            P(("dp", "blk"), None),
            P(("dp", "blk"), None),
            P(("dp", "blk"), None),
            P(("dp", "blk"), None),
            P(None, ("dp", "blk")),
            P(("dp", "blk"), None),
            P(("dp", "blk"), None),
            P(("dp", "blk"), None),
            P(("dp", "blk"), None),
            P(None, ("dp", "blk")),
            P(("dp", "blk"), None),
            P(("dp", "blk"), None),
            P(("dp", "blk"), None),
            P(("dp", "blk"), None),
            P(None, ("dp", "blk")),
            P(("dp", "blk"), None),
            P(("dp", "blk"), None),
            P(("dp", "blk"), None),
            P(("dp", "blk"), None),
            P(None, ("dp", "blk")),
            P(("dp", "blk"), None),
            P(("dp", "blk"), None),
            P(("dp", "blk"), None),
            P(("dp", "blk"), None),
            P(None, ("dp", "blk")),
        ),
        check_vma=False,
    )
```
